32 devices in a mesh: dp: 2 (over x), shard: 16 (over z, y, core).
Axes of the slice: x: 2, y: 2, z: 4, core: 2. Of those that a mesh axis runs over, the one named last changes fastest.
Arguments:
- trajectories: float32 [2048, 32, 23], P(('dp', 'shard')), may hold values from -6 to 6
- noise: float32 [2048, 32, 23], P(('dp', 'shard')), may hold values from -6 to 6
- timesteps: int32 [2048], P(('dp', 'shard')), may hold values from 0 to 19
- valid: int32 [2048, 32], P(('dp', 'shard')), may hold values from 0 to 1, as said below
- owners: int32 [67], replicated, may hold values from 0 to 79, as said below
- mat_weight: float32 [67, 128, 256], P(None, 'shard')
- mat_ema: float32 [67, 128, 256], P(None, 'shard')
- soap_first: float32 [80, 128, 256], P('shard'), may hold values from -5.340576e-05 to 5.340576e-05
- soap_second: float32 [80, 128, 256], P('shard'), may hold values from 5.834243e-11 to 2.378576e-10
- left_stat: float32 [80, 128, 128], P('shard'), as said below
- right_stat: float32 [80, 256, 256], P('shard'), as said below
- left_basis: float32 [80, 128, 128], P('shard'), as said below
- right_basis: float32 [80, 256, 256], P('shard'), as said below
- vec_weight: float32 [128, 256], P('shard')
- vec_first: float32 [128, 256], P('shard'), may hold values from -0.00048828125 to 0.00048828125
- vec_second: float32 [128, 256], P('shard'), may hold values from 5.3854547e-09 to 2.1093031e-08
- vec_ema: float32 [128, 256], P('shard')
Outputs:
- loss_sum: float32 [], replicated
- count: float32 [], replicated
- grad_norm: float32 [], replicated
- new_mat: float32 [67, 128, 256], P(None, 'shard')
- new_mat_ema: float32 [67, 128, 256], P(None, 'shard')
- new_first: float32 [80, 128, 256], P('shard')
- new_second: float32 [80, 128, 256], P('shard')
- new_left_stat: float32 [80, 128, 128], P('shard')
- new_right_stat: float32 [80, 256, 256], P('shard')
- new_left_basis: float32 [80, 128, 128], P('shard')
- new_right_basis: float32 [80, 256, 256], P('shard')
- new_vec: float32 [128, 256], P('shard')
- new_vec_first: float32 [128, 256], P('shard')
- new_vec_second: float32 [128, 256], P('shard')
- new_vec_ema: float32 [128, 256], P('shard')
The draws below stay inside these ranges and needn't reach their ends.
Inputs may be any that keep to these rules, and one draw needn't show every extreme that they name: `valid`: the first frame of every trajectory counts. `owners`: distinct slots; the last slot always holds a block. `left_stat`: symmetric positive definite. `right_stat`: symmetric positive definite. `left_basis`: Nonsingular. `right_basis`: Nonsingular.
All inputs are finite; a program needn't handle non-finite values.
Results may differ from the reference program's by a relative error of at most 0.01.
Values may be sent and summed in bfloat16 or wider, within the bound.
A program may use at most 192 MiB of HBM per device.

```python
import math
import jax
import jax.numpy as jnp
from jax import lax

WIDTH = 256
KERNEL = 5
GROUPS = 8
TDIM = 128
FEAT = 23
FRAMES = 32
BLOCKS = 3
DSTEPS = 20
STEP = 10
TRAJ_DEV = 64
TRAJ = 2048
OWNED = 6
HALF = 128
UNITS = 67
SLOTS_DEV = 5
VROWS = 128
PARAMS = 2228224
N_DP = 2
N_SHARD = 16


def draw_valid(key, part):
    devices_all = N_DP * N_SHARD
    device_row = jnp.arange(TRAJ, dtype=jnp.int32) // TRAJ_DEV
    limit = 250 + 500 * device_row // max(devices_all - 1, 1)
    picks = jax.random.randint(key, (TRAJ, FRAMES), 0, 1000)
    marks = (picks < limit[:, None]).astype(jnp.int32)
    return marks.at[:, 0].set(1)


def draw_owners(key, part):
    slots = N_SHARD * SLOTS_DEV
    picks = jax.random.permutation(jax.random.fold_in(key, 11), slots - 1)[:UNITS - 1]
    listed = jnp.concatenate([picks.astype(jnp.int32), jnp.full((1,), slots - 1, jnp.int32)])
    order = jax.random.permutation(jax.random.fold_in(key, 12), UNITS)
    return listed[order].astype(jnp.int32)


def drawn_values(key, shape):
    return jax.random.normal(key, shape, jnp.float32)


def mat_draw(key):
    units = jnp.arange(UNITS, dtype=jnp.int32)[:, None, None]
    conv_scale = (KERNEL * WIDTH) ** (-0.5)
    scale = jnp.where(units < 2 * KERNEL * OWNED, conv_scale, jnp.where(units < UNITS - 1, WIDTH ** (-0.5), TDIM ** (-0.5)))
    return scale * drawn_values(key, (UNITS, HALF, WIDTH))


def draw_mat_weight(key, part):
    return mat_draw(jax.random.fold_in(key, 51))


def draw_mat_ema(key, part):
    return mat_draw(jax.random.fold_in(key, 52))


def stat_draw(key, size, scale):
    slots = N_SHARD * SLOTS_DEV
    spread = jax.random.uniform(jax.random.fold_in(key, 1), (slots, size), jnp.float32, 0.0, 1.0)
    diag = jnp.exp(spread * math.log(4.0))
    drawn = drawn_values(jax.random.fold_in(key, 2), (slots, size, size))
    gram = jnp.einsum('sij,skj->sik', drawn, drawn, precision=lax.Precision.HIGHEST) / size
    gram = 0.5 * (gram + jnp.swapaxes(gram, 1, 2))
    eye = jnp.eye(size, dtype=jnp.float32)[None, :, :]
    return scale * (eye * diag[:, None, :] + 0.6 * gram)


def draw_left_stat(key, part):
    return stat_draw(jax.random.fold_in(key, 21), HALF, 0.0001316 * WIDTH / PARAMS)


def draw_right_stat(key, part):
    return stat_draw(jax.random.fold_in(key, 22), WIDTH, 0.0001316 * HALF / PARAMS)


def basis_draw(key, size):
    slots = N_SHARD * SLOTS_DEV
    drawn = drawn_values(jax.random.fold_in(key, 1), (slots, size, size))
    rows = jnp.exp(jax.random.uniform(jax.random.fold_in(key, 2), (slots, size), jnp.float32, -0.2, 0.2))
    eye = jnp.eye(size, dtype=jnp.float32)[None, :, :]
    return rows[:, :, None] * (eye + 0.25 * drawn / math.sqrt(size))


def draw_left_basis(key, part):
    return basis_draw(jax.random.fold_in(key, 31), HALF)


def draw_right_basis(key, part):
    return basis_draw(jax.random.fold_in(key, 32), WIDTH)


def table_draw(key):
    rows = jnp.arange(VROWS, dtype=jnp.int32)[:, None]
    values = drawn_values(key, (VROWS, WIDTH))
    even = jax.random.uniform(jax.random.fold_in(key, 5), (VROWS, WIDTH), jnp.float32, -1.0, 1.0)
    base = 2 * FEAT
    scale = jnp.where(rows < FEAT, FEAT ** (-0.5), jnp.where(rows < 2 * FEAT, WIDTH ** (-0.5), 0.3))
    gain_rows = (rows >= base + 3 + OWNED) & (rows < base + 3 + 2 * OWNED)
    return jnp.where(gain_rows, 1.0 + 0.3 * even, scale * values)


def draw_vec_weight(key, part):
    return table_draw(jax.random.fold_in(key, 41))


def draw_vec_ema(key, part):
    return table_draw(jax.random.fold_in(key, 42))


def place_ends(entries, stream_key, low, high):
    index_at = [jax.random.randint(jax.random.fold_in(stream_key, axis), (), 0, length) for axis, length in enumerate(entries.shape)]
    longest = entries.shape.index(max(entries.shape))
    neighbour = index_at[:longest] + [(index_at[longest] + 1) % entries.shape[longest]] + index_at[longest + 1:]
    return entries.at[tuple(index_at)].set(low).at[tuple(neighbour)].set(high)


def block_levels(key, shape, shards, smallest, top_value):
    def one(position, parts):
        steps = jax.random.uniform(jax.random.fold_in(jax.random.fold_in(key, 6), position), (parts,), jnp.float32, smallest / len(shards), top_value / len(shards))
        return jnp.repeat(jnp.exp(steps), shape[position] // parts).reshape((-1,) + (1,) * (len(shape) - position - 1))

    level = one(*shards[0])
    for cut in shards[1:]:
        level = level * one(*cut)
    return level


def gaussian(stream_key, extent, scale, reach, cuts=(), kind=jnp.bfloat16):
    level = block_levels(stream_key, extent, cuts, -0.22, 0.18) if cuts else 1.0
    values = jax.random.normal(stream_key, extent, jnp.float32) * scale * level
    return jnp.minimum(jnp.maximum(values, -reach), reach).astype(kind)


def setup_inputs(seed: int = 0) -> dict:
    splits = jax.random.split(jax.random.key(seed), 18)
    trajectories = gaussian(splits[0], (TRAJ, FRAMES, FEAT), 1.0, 6.0, ((0, 32),), jnp.float32)
    noise = gaussian(splits[1], (TRAJ, FRAMES, FEAT), 1.0, 6.0, ((0, 32),), jnp.float32)
    timesteps = place_ends(jax.random.randint(splits[2], (TRAJ,), 0, DSTEPS), jax.random.fold_in(splits[2], 1), 0, DSTEPS - 1).astype(jnp.int32)
    valid = draw_valid(jax.random.fold_in(splits[17], 71), 0)
    owners = draw_owners(jax.random.fold_in(splits[17], 71), 0)
    mat_weight = draw_mat_weight(jax.random.fold_in(splits[17], 71), 0)
    mat_ema = draw_mat_ema(jax.random.fold_in(splits[17], 71), 0)
    soap_first = gaussian(splits[7], (N_SHARD * SLOTS_DEV, HALF, WIDTH), (0.0056 * PARAMS ** -0.5), 5.340576171875e-05, ((0, 16),), jnp.float32)
    soap_second = jnp.clip(jnp.exp(math.log(2.3785759473149426e-10) - 1.4053426 * jax.random.uniform(splits[8], (N_SHARD * SLOTS_DEV, HALF, WIDTH), jnp.float32) ** block_levels(splits[8], (N_SHARD * SLOTS_DEV, HALF, WIDTH), ((0, 16),), -0.2, 0.2)), 5.834242811086909e-11, 2.3785759473149426e-10)
    left_stat = draw_left_stat(jax.random.fold_in(splits[17], 71), 0)
    right_stat = draw_right_stat(jax.random.fold_in(splits[17], 71), 0)
    left_basis = draw_left_basis(jax.random.fold_in(splits[17], 71), 0)
    right_basis = draw_right_basis(jax.random.fold_in(splits[17], 71), 0)
    vec_weight = draw_vec_weight(jax.random.fold_in(splits[17], 71), 0)
    vec_first = gaussian(splits[14], (VROWS, WIDTH), (0.054 * PARAMS ** -0.5), 0.00048828125, ((0, 16),), jnp.float32)
    vec_second = jnp.clip(jnp.exp(math.log(2.109303132158402e-08) - 1.36524096 * jax.random.uniform(splits[15], (VROWS, WIDTH), jnp.float32) ** block_levels(splits[15], (VROWS, WIDTH), ((0, 16),), -0.2, 0.2)), 5.3854547488185744e-09, 2.109303132158402e-08)
    vec_ema = draw_vec_ema(jax.random.fold_in(splits[17], 71), 0)
    return dict(trajectories=trajectories, noise=noise, timesteps=timesteps, valid=valid, owners=owners, mat_weight=mat_weight, mat_ema=mat_ema, soap_first=soap_first, soap_second=soap_second, left_stat=left_stat, right_stat=right_stat, left_basis=left_basis, right_basis=right_basis, vec_weight=vec_weight, vec_first=vec_first, vec_second=vec_second, vec_ema=vec_ema)


HIGH = lax.Precision.HIGHEST
BETA_ONE = 0.9
BETA_TWO = 0.95
ADAM_EPS = 1e-08
LEARN = 0.05
TABLE_LEARN = 0.25
DECAY = 0.01
CLIP = 0.05
EMA_RATE = 0.8
NORM_EPS = 1e-05

@jax.custom_vjp
def low(v):
    return lax.optimization_barrier(v.astype(jnp.bfloat16)).astype(jnp.float32)

@jax.custom_vjp
def low_back(v):
    return v

def low_keep(v):
    return (low(v), None)

def low_pass(kept, grad):
    return (grad,)

def back_keep(v):
    return (v, None)

def back_low(kept, grad):
    return (low(grad),)
low.defvjp(low_keep, low_pass)
low_back.defvjp(back_keep, back_low)

def vec_base():
    return 2 * FEAT

def block_vectors(table, block):
    conv_row = vec_base() + 3 + 2 * block
    gain_row = conv_row + OWNED
    shift_row = conv_row + 2 * OWNED
    return (table[conv_row], table[gain_row], table[shift_row], table[conv_row + 1], table[gain_row + 1], table[shift_row + 1])

def bias_row(block):
    return vec_base() + 3 + 3 * OWNED + block

def conv_matrix(mats, index):
    taps = 2 * KERNEL
    return mats[index * taps:(index + 1) * taps].reshape(KERNEL * WIDTH, WIDTH)

def lin_matrix(mats, block):
    start = 2 * KERNEL * OWNED + 2 * block
    return mats[start:start + 2].reshape(WIDTH, WIDTH)

def mish_act(v):
    return v * jnp.tanh(jax.nn.softplus(v))

def group_norm(v, gain, shift):
    grouped = v.reshape(v.shape[0], v.shape[1], GROUPS, v.shape[2] // GROUPS)
    centre = lax.optimization_barrier(jnp.mean(grouped, axis=(1, 3), keepdims=True))
    spread = lax.optimization_barrier(jnp.mean((grouped - centre) ** 2, axis=(1, 3), keepdims=True))
    normed = ((grouped - centre) * lax.rsqrt(spread + NORM_EPS)).reshape(v.shape)
    return normed * gain + shift

def unfold_taps(v):
    margin = KERNEL // 2
    padded = jnp.pad(v, ((0, 0), (margin, margin), (0, 0)))
    frames = v.shape[1]
    return jnp.concatenate([padded[:, index:index + frames] for index in range(KERNEL)], axis=-1)

def noise_level(steps):
    offset = 0.008
    ratio = (steps.astype(jnp.float32) + 1.0) / DSTEPS
    upper = jnp.cos((ratio + offset) / (1.0 + offset) * math.pi / 2) ** 2
    return upper / math.cos(offset / (1.0 + offset) * math.pi / 2) ** 2

def time_embed(steps):
    halfway = TDIM // 2
    freqs = jnp.exp(-math.log(10000.0) * jnp.arange(halfway, dtype=jnp.float32) / (halfway - 1))
    angles = steps.astype(jnp.float32)[:, None] * freqs[None, :]
    return jnp.concatenate([jnp.sin(angles), jnp.cos(angles)], axis=-1)

def res_block(h_in, w_first, w_second, vectors, t_bias):
    pre_a = low_back(jnp.einsum('bfk,kw->bfw', unfold_taps(low(h_in)), w_first, precision=HIGH))
    middle = mish_act(group_norm(pre_a + vectors[0], vectors[1], vectors[2])) + t_bias[:, None, :]
    pre_b = low_back(jnp.einsum('bfk,kw->bfw', unfold_taps(low(middle)), w_second, precision=HIGH))
    return h_in + mish_act(group_norm(pre_b + vectors[3], vectors[4], vectors[5]))

def net_loss(mat_w, vec_w, traj, noise, steps, mask):
    mat_low = low(mat_w)
    vec_low = low(vec_w)
    base = vec_base()
    level = noise_level(steps)[:, None, None]
    noisy = jnp.sqrt(level) * traj + jnp.sqrt(1.0 - level) * noise
    emb = low(time_embed(steps))
    pre_time = low_back(jnp.dot(emb, mat_low[UNITS - 1], precision=HIGH))
    temb = low(mish_act(pre_time + vec_w[base + 1]))
    hidden = low_back(jnp.einsum('bfc,cw->bfw', low(noisy), vec_low[:FEAT], precision=HIGH)) + vec_w[base]
    skip = hidden
    for block in range(BLOCKS):
        t_bias = low_back(jnp.dot(temb, lin_matrix(mat_low, block), precision=HIGH)) + vec_w[bias_row(block)]
        if block == BLOCKS - 1:
            hidden = hidden + skip
        hidden = res_block(hidden, conv_matrix(mat_low, 2 * block), conv_matrix(mat_low, 2 * block + 1), block_vectors(vec_w, block), t_bias)
        if block == 0:
            skip = hidden
    pred = low_back(jnp.einsum('bfw,cw->bfc', low(hidden), vec_low[FEAT:2 * FEAT], precision=HIGH)) + vec_w[base + 2, :FEAT]
    error = pred - noise
    return jnp.sum(mask[:, :, None] * error * error)

def orthonormal(matrix):
    gram = jnp.dot(matrix.T, matrix, precision=HIGH)
    lower = jnp.linalg.cholesky(gram)
    return jax.scipy.linalg.solve_triangular(lower, matrix.T, lower=True).T

def rotate_in(matrix, left, right):
    return jnp.dot(jnp.dot(left.T, matrix, precision=HIGH), right, precision=HIGH)

def rotate_out(matrix, left, right):
    return jnp.dot(jnp.dot(left, matrix, precision=HIGH), right.T, precision=HIGH)

def soap_slot(grad, first, second, left_stat, right_stat, left_basis, right_basis):
    first_new = BETA_ONE * first + (1.0 - BETA_ONE) * grad
    turned = rotate_in(grad, left_basis, right_basis)
    second_new = BETA_TWO * second + (1.0 - BETA_TWO) * turned * turned
    moment = rotate_in(first_new, left_basis, right_basis)
    normed = moment / (1.0 - BETA_ONE ** STEP) / (jnp.sqrt(second_new / (1.0 - BETA_TWO ** STEP)) + ADAM_EPS)
    update = rotate_out(normed, left_basis, right_basis)
    left_new = BETA_TWO * left_stat + (1.0 - BETA_TWO) * jnp.dot(grad, grad.T, precision=HIGH)
    right_new = BETA_TWO * right_stat + (1.0 - BETA_TWO) * jnp.dot(grad.T, grad, precision=HIGH)
    left_next = orthonormal(jnp.dot(left_new, left_basis, precision=HIGH))
    right_next = orthonormal(jnp.dot(right_new, right_basis, precision=HIGH))
    return (update, first_new, second_new, left_new, right_new, left_next, right_next)

def reference(trajectories, noise, timesteps, valid, owners, mat_weight, mat_ema, soap_first, soap_second, left_stat, right_stat, left_basis, right_basis, vec_weight, vec_first, vec_second, vec_ema):
    mask = valid.astype(jnp.float32)
    rows_block = 4 * TRAJ_DEV
    blocks = TRAJ // rows_block

    def one_block(carry, index):
        start = (index * rows_block).astype(jnp.int32)

        def take(array):
            return lax.dynamic_slice_in_dim(array, start, rows_block, 0)

        def loss_of(mat_w, vec_w):
            return net_loss(mat_w, vec_w, take(trajectories), take(noise), take(timesteps), take(mask))
        loss, pull = jax.vjp(loss_of, mat_weight, vec_weight)
        grad_mat, grad_vec = pull(jnp.ones_like(loss))
        return ((carry[0] + grad_mat, carry[1] + grad_vec, carry[2] + loss), None)
    start_carry = (jnp.zeros_like(mat_weight), jnp.zeros_like(vec_weight), jnp.zeros((), jnp.float32))
    (grad_mat, grad_vec, loss_sum), _ = lax.scan(one_block, start_carry, jnp.arange(blocks, dtype=jnp.int32))
    count = FEAT * jnp.sum(mask)
    grad_mat = grad_mat / count
    grad_vec = grad_vec / count
    grad_norm = jnp.sqrt(jnp.sum(grad_mat * grad_mat) + jnp.sum(grad_vec * grad_vec))
    factor = jnp.minimum(1.0, CLIP / (grad_norm + 1e-06))
    grad_mat = grad_mat * factor
    grad_vec = grad_vec * factor
    slots = N_SHARD * SLOTS_DEV
    choose = (owners[None, :] == jnp.arange(slots, dtype=jnp.int32)[:, None]).astype(jnp.float32)
    slot_grad = jnp.einsum('sm,mrw->srw', choose, grad_mat, precision=HIGH)
    results = lax.map(lambda pack: soap_slot(*pack), (slot_grad, soap_first, soap_second, left_stat, right_stat, left_basis, right_basis))
    update = jnp.einsum('sm,srw->mrw', choose, results[0], precision=HIGH)
    new_mat = mat_weight * (1.0 - LEARN * DECAY) - LEARN * update
    new_mat_ema = EMA_RATE * mat_ema + (1.0 - EMA_RATE) * new_mat
    new_vec_first = BETA_ONE * vec_first + (1.0 - BETA_ONE) * grad_vec
    new_vec_second = BETA_TWO * vec_second + (1.0 - BETA_TWO) * grad_vec * grad_vec
    step_vec = new_vec_first / (1.0 - BETA_ONE ** STEP) / (jnp.sqrt(new_vec_second / (1.0 - BETA_TWO ** STEP)) + ADAM_EPS)
    new_vec = vec_weight * (1.0 - TABLE_LEARN * DECAY) - TABLE_LEARN * step_vec
    new_vec_ema = EMA_RATE * vec_ema + (1.0 - EMA_RATE) * new_vec
    return (loss_sum, count, grad_norm, new_mat, new_mat_ema, results[1], results[2], results[3], results[4], results[5], results[6], new_vec, new_vec_first, new_vec_second, new_vec_ema)
```

```python
import functools
import math

import jax
import jax.numpy as jnp
from jax import lax
from jax.experimental import pallas as pl
from jax.experimental.pallas import tpu as pltpu
from jax.sharding import PartitionSpec as P

WIDTH = 256
KERNEL = 5
GROUPS = 8
TDIM = 128
FEAT = 23
BLOCKS = 3
DSTEPS = 20
STEP = 10
OWNED = 6
UNITS = 67
VROWS = 128


HIGH = lax.Precision.HIGHEST
BETA_ONE = 0.9
BETA_TWO = 0.95
ADAM_EPS = 1e-08
LEARN = 0.05
TABLE_LEARN = 0.25
DECAY = 0.01
CLIP = 0.05
EMA_RATE = 0.8
NORM_EPS = 1e-05
PANEL = 32
LANES = 128
PAD = 8
CHUNK = 8
BASE = 2 * FEAT
F32 = jnp.float32
BF16 = jnp.bfloat16


def noise_level(steps):
    offset = 0.008
    ratio = (steps.astype(jnp.float32) + 1.0) / DSTEPS
    upper = jnp.cos((ratio + offset) / (1.0 + offset) * math.pi / 2) ** 2
    return upper / math.cos(offset / (1.0 + offset) * math.pi / 2) ** 2


def time_embed(steps):
    halfway = TDIM // 2
    freqs = jnp.exp(-math.log(10000.0) * jnp.arange(halfway, dtype=jnp.float32) / (halfway - 1))
    angles = steps.astype(jnp.float32)[:, None] * freqs[None, :]
    return jnp.concatenate([jnp.sin(angles), jnp.cos(angles)], axis=-1)


def mm(a, b, ca=1, cb=0):
    return lax.dot_general(a, b, (((ca,), (cb,)), ((), ())), precision=HIGH, preferred_element_type=jnp.float32)

def split3(v):
    hi = v.astype(jnp.bfloat16)
    rest = v - hi.astype(jnp.float32)
    mid = rest.astype(jnp.bfloat16)
    last = (rest - mid.astype(jnp.float32)).astype(jnp.bfloat16)
    return hi, mid, last

def factor_panels(chains, start):
    rows = lax.broadcasted_iota(jnp.int32, (PANEL, LANES), 0)
    lanes = lax.broadcasted_iota(jnp.int32, (PANEL, LANES), 1)
    unit = jnp.where(lanes - PANEL == rows, 1.0, 0.0).astype(jnp.float32)
    offset = lax.rem(start, LANES)
    tile = pl.multiple_of(start - offset, LANES)
    shift = lax.rem(LANES - offset, LANES)
    held = []
    for z, s, n in chains:
        block = z[s, pl.ds(start, PANEL), pl.ds(tile, LANES)]
        held.append(jnp.where(lanes < PANEL, pltpu.roll(block, shift, 1), unit))
    for k in range(PANEL):
        for c in range(len(chains)):
            e = held[c]
            column = jnp.broadcast_to(e[:, k : k + 1], (PANEL, LANES))
            pivot = column[k : k + 1, :]
            row = e[k : k + 1, :] * (1.0 / pivot)
            held[c] = e - jnp.where(rows > k, column, 0.0) * row
    for c, (z, s, n) in enumerate(chains):
        e = held[c]
        pivots = jnp.sum(jnp.where(lanes == rows, e, 0.0), axis=1, keepdims=True)
        inverse = e[:, PANEL : 2 * PANEL] * lax.rsqrt(pivots)
        panel = z[s, pl.ds(start, PANEL), :]
        done = mm(inverse, panel)
        z[s, pl.ds(start, PANEL), :] = done
        hi, mid, last = split3(done)
        lhs = jnp.concatenate([hi, hi, mid, hi, last, mid], axis=0)[:, :n]
        rhs = jnp.concatenate([hi, mid, hi, last, hi, mid], axis=0)
        for r in range(0, n, LANES):
            upd = lax.dot_general(lhs[:, r:r + LANES], rhs, (((0,), (0,)), ((), ())), preferred_element_type=jnp.float32)
            rowid = lax.broadcasted_iota(jnp.int32, (LANES, 2 * n), 0) + r
            z[s, pl.ds(r, LANES), :] = z[s, pl.ds(r, LANES), :] - jnp.where(rowid >= start + PANEL, upd, 0.0)

def soap_kernel(slots, scale, g, m, v, ls, rs, lb, rb, u_o, m_o, v_o, ls_o, rs_o, lb_o, rb_o, zl, zr):
    for s in range(slots):
        grad = g[s] * scale[0]
        left, right = lb[s], rb[s]
        first = BETA_ONE * m[s] + (1.0 - BETA_ONE) * grad
        m_o[s] = first
        turned = mm(mm(left, grad, 0, 0), right)
        second = BETA_TWO * v[s] + (1.0 - BETA_TWO) * turned * turned
        v_o[s] = second
        moment = mm(mm(left, first, 0, 0), right)
        normed = moment / (1.0 - BETA_ONE**STEP) / (jnp.sqrt(second / (1.0 - BETA_TWO**STEP)) + ADAM_EPS)
        u_o[s] = mm(mm(left, normed), right, 1, 1)
        lnew = BETA_TWO * ls[s] + (1.0 - BETA_TWO) * mm(grad, grad, 1, 1)
        rnew = BETA_TWO * rs[s] + (1.0 - BETA_TWO) * mm(grad, grad, 0, 0)
        ls_o[s] = lnew
        rs_o[s] = rnew
        xl = mm(left, lnew, 0, 1)
        xr = mm(right, rnew, 0, 1)
        zl[s, :, : LANES] = mm(xl, xl, 1, 1)
        zl[s, :, LANES:] = xl
        zr[s, :, : 2 * LANES] = mm(xr, xr, 1, 1)
        zr[s, :, 2 * LANES :] = xr
    lc = [(zl, s, LANES) for s in range(slots)]
    rc = [(zr, s, 2 * LANES) for s in range(slots)]
    def both(p, _):
        factor_panels(rc + lc, pl.multiple_of(p * PANEL, PANEL))
        return 0
    def only(p, _):
        factor_panels(rc, pl.multiple_of(p * PANEL, PANEL))
        return 0
    lax.fori_loop(0, LANES // PANEL, both, 0)
    lax.fori_loop(LANES // PANEL, 2 * LANES // PANEL, only, 0)
    for s in range(slots):
        lb_o[s] = zl[s, :, LANES:].T
        rb_o[s] = zr[s, :, 2 * LANES :].T

def soap(scale, g, m, v, ls, rs, lb, rb):
    slots = g.shape[0]
    f = jax.ShapeDtypeStruct
    vm = pl.BlockSpec(memory_space=pltpu.VMEM)
    outs = [f(x.shape, jnp.float32) for x in (g, m, v, ls, rs, lb, rb)]
    return pl.pallas_call(
        functools.partial(soap_kernel, slots),
        out_shape=outs,
        in_specs=[pl.BlockSpec(memory_space=pltpu.SMEM)] + [vm] * 7,
        out_specs=[vm] * 7,
        scratch_shapes=[pltpu.VMEM((slots, LANES, 2 * LANES), jnp.float32), pltpu.VMEM((slots, 2 * LANES, 4 * LANES), jnp.float32)],
        compiler_params=pltpu.CompilerParams(vmem_limit_bytes=56 * 2**20),
        name="soap",
    )(scale, g, m, v, ls, rs, lb, rb)


def dot(a, b, ca=1, cb=0):
    return lax.dot_general(a, b, (((ca,), (cb,)), ((), ())), preferred_element_type=F32)


def mish_parts(v):
    e = jnp.exp(jnp.minimum(v, 20.0))
    n = e * (e + 2.0)
    r = pl.reciprocal(n + 2.0)
    return e, r, n * r


def mish_slope(v, e, r, t):
    return t + v * (4.0 * e * (e + 1.0)) * (r * r)


def net_kernel(trajs, frames, emb, noisy, noise, mask, table, mats, gmat, mat_o, vec_o, loss_o,
               xin, xhat, h, skip, d, dskip, dy, u, xp, s_one, s_two, mean, rstd, xsum, q_one, q_two, g_one, g_two, tb, dtb, dpl, acc):
    rows_c = CHUNK * frames
    chunks = trajs // CHUNK
    low = table[: 2 * FEAT, :].astype(BF16)
    w_in, w_head = low[:FEAT], low[FEAT : 2 * FEAT]
    group = gmat[...]
    part = 1.0 / (frames * (WIDTH // GROUPS))

    def rows_of(c):
        return pl.ds(pl.multiple_of(c * rows_c, rows_c), rows_c)

    def trajs_of(c):
        return pl.ds(pl.multiple_of(c * CHUNK, CHUNK), CHUNK)

    def wide(v):
        return v.reshape(CHUNK, frames, WIDTH)

    def flat(v):
        return v.reshape(rows_c, WIDTH)

    def row(index):
        return table[index : index + 1, :]

    def gain(l):
        return row(BASE + 3 + OWNED + l), row(BASE + 3 + 2 * OWNED + l)

    def conv(l):
        return mats[2 * KERNEL * l : 2 * KERNEL * (l + 1)].reshape(KERNEL * WIDTH, WIDTH)

    def lin(j):
        start = 2 * KERNEL * OWNED + 2 * j
        return mats[start : start + 2].reshape(WIDTH, WIDTH)

    def group_sum(v):
        return lax.dot_general(v, group, (((1,), (0,)), ((), ())), precision=HIGH, preferred_element_type=F32)

    def spread(c, value, flip):
        for half in range(2):
            xp[half, :, PAD : PAD + frames, :] = value[:, half * LANES : (half + 1) * LANES].reshape(CHUNK, frames, LANES)
        for k in range(KERNEL):
            at = PAD + (KERNEL // 2 - k if flip else k - KERNEL // 2)
            for half in range(2):
                lane = k * WIDTH + half * LANES
                u[rows_of(c), lane : lane + LANES] = xp[half, :, at : at + frames, :].reshape(rows_c, LANES).astype(BF16)

    def pass_one(l, c, x):
        xin[l, rows_of(c), :] = x.astype(BF16)
        spread(c, x, False)
        p = dot(u[rows_of(c), :], conv(l)) + row(BASE + 3 + l)
        xhat[l, rows_of(c), :] = p
        p = wide(p)
        total = jnp.sum(p, axis=1)
        s_one[trajs_of(c), :] = total
        off = p - (total * (1.0 / frames))[:, None, :]
        s_two[trajs_of(c), :] = jnp.sum(off * off, axis=1)

    def stats(l):
        total = s_one[...]
        centre = group_sum(total) * part
        off = total * (1.0 / frames) - centre
        var = group_sum(s_two[...] + frames * off * off) * part
        scale = lax.rsqrt(var + NORM_EPS)
        mean[...] = centre
        rstd[l] = scale
        xsum[l] = frames * off * scale

    def normed(l, c):
        p = wide(xhat[l, rows_of(c), :])
        x = flat((p - mean[trajs_of(c), :][:, None, :]) * rstd[l, trajs_of(c), :][:, None, :])
        xhat[l, rows_of(c), :] = x
        g, s = gain(l)
        return x, x * g + s

    def pass_a(l, c, dm, x, v, parts):
        slope = dm * mish_slope(v, *parts)
        dy[rows_of(c), :] = slope
        q_one[trajs_of(c), :] = jnp.sum(wide(slope), axis=1)
        q_two[trajs_of(c), :] = jnp.sum(wide(slope * x), axis=1)

    def pass_a_load(l, c, dm):
        x = xhat[l, rows_of(c), :]
        g, s = gain(l)
        v = x * g + s
        pass_a(l, c, dm, x, v, mish_parts(v))

    def stats_back(l):
        g, s = gain(l)
        one, two = q_one[...], q_two[...]
        vec_o[BASE + 3 + OWNED + l : BASE + 4 + OWNED + l, :] = jnp.sum(two, axis=0, keepdims=True)
        vec_o[BASE + 3 + 2 * OWNED + l : BASE + 4 + 2 * OWNED + l, :] = jnp.sum(one, axis=0, keepdims=True)
        sums = group_sum(jnp.concatenate([one * g, two * g], axis=0)) * part
        first, second = sums[:trajs], sums[trajs:]
        g_one[...] = first
        g_two[...] = second
        dc = rstd[l] * (one * g - frames * first - xsum[l] * second)
        vec_o[BASE + 3 + l : BASE + 4 + l, :] = jnp.sum(dc, axis=0, keepdims=True)

    def loop(body):
        def step(c, carry):
            body(c)
            return carry

        lax.fori_loop(0, chunks, step, 0)

    vec_o[...] = jnp.zeros_like(vec_o)
    xp[...] = jnp.zeros_like(xp)
    acc[...] = jnp.zeros_like(acc)
    loss_o[...] = jnp.zeros_like(loss_o)
    pre_time = dot(emb[...], mats[UNITS - 1]) + row(BASE + 1)
    time_parts = mish_parts(pre_time)
    temb = (pre_time * time_parts[2]).astype(BF16)
    time_slope = mish_slope(pre_time, *time_parts)
    for j in range(BLOCKS):
        tb[j] = dot(temb, lin(j)) + row(BASE + 3 + 3 * OWNED + j)

    def enter(c):
        x = dot(noisy[rows_of(c), :], w_in) + row(BASE)
        h[rows_of(c), :] = x
        pass_one(0, c, x)

    loop(enter)
    for l in range(OWNED - 1):
        stats(l)

        def forward(c, l=l):
            _, v = normed(l, c)
            m = v * mish_parts(v)[2]
            if l % 2 == 0:
                m = flat(wide(m) + tb[l // 2, trajs_of(c), :][:, None, :])
            else:
                m = h[rows_of(c), :] + m
                if l == 1:
                    skip[rows_of(c), :] = m
                if l == 2 * BLOCKS - 3:
                    m = m + skip[rows_of(c), :]
                h[rows_of(c), :] = m
            pass_one(l + 1, c, m)

        loop(forward)
    stats(OWNED - 1)

    def turn(c):
        l = OWNED - 1
        x, v = normed(l, c)
        parts = mish_parts(v)
        top = (h[rows_of(c), :] + v * parts[2]).astype(BF16)
        xin[OWNED, rows_of(c), :] = top
        err = dot(top, w_head, 1, 1) + row(BASE + 2)[:, :FEAT] - noise[rows_of(c), :]
        weighted = mask[rows_of(c), :] * err
        loss_o[...] += jnp.sum(weighted * err, axis=0, keepdims=True)
        grad = 2.0 * weighted
        acc[0:1, :FEAT] += jnp.sum(grad, axis=0, keepdims=True)
        grad = grad.astype(BF16)
        dpl[rows_of(c), :] = grad
        dh = dot(grad, w_head)
        d[rows_of(c), :] = dh
        pass_a(l, c, dh, x, v, parts)

    loop(turn)
    vec_o[FEAT : 2 * FEAT, :] = dot(dpl[...], xin[OWNED], 0, 0)
    vec_o[BASE + 2 : BASE + 3, :] = acc[0:1, :]

    for l in reversed(range(OWNED)):
        stats_back(l)

        def backward(c, l=l):
            g, s = gain(l)
            at = trajs_of(c)
            x = wide(xhat[l, rows_of(c), :])
            dp = rstd[l, at, :][:, None, :] * (
                wide(dy[rows_of(c), :] * g) - g_one[at, :][:, None, :] - x * g_two[at, :][:, None, :]
            )
            spread(c, flat(dp), True)
            dx = None
            w = conv(l)
            for k in range(KERNEL):
                term = dot(u[rows_of(c), k * WIDTH : (k + 1) * WIDTH], w[k * WIDTH : (k + 1) * WIDTH], 1, 1)
                dx = term if dx is None else dx + term
            if l % 2 == 1:
                dtb[l // 2, at, :] = jnp.sum(wide(dx), axis=1)
                pass_a_load(l - 1, c, dx)
            else:
                dx = d[rows_of(c), :] + dx
                if l == OWNED - 2:
                    dskip[rows_of(c), :] = dx
                if l == 2:
                    dx = dx + dskip[rows_of(c), :]
                if l > 0:
                    d[rows_of(c), :] = dx
                    pass_a_load(l - 1, c, dx)
                else:
                    acc[8:16, :] += jnp.sum(dx.reshape(rows_c // 8, 8, WIDTH), axis=0)
                    xin[OWNED, rows_of(c), :] = dx.astype(BF16)

        loop(backward)
        w_grad = dot(xin[l], u[...], 0, 0)
        for k in range(KERNEL):
            for half in range(2):
                mat_o[2 * KERNEL * l + 2 * k + half] = w_grad[half * LANES : (half + 1) * LANES, k * WIDTH : (k + 1) * WIDTH].astype(mat_o.dtype)

    vec_o[BASE : BASE + 1, :] = jnp.sum(acc[8:16, :], axis=0, keepdims=True)
    vec_o[:FEAT, :] = dot(noisy[...], xin[OWNED], 0, 0)
    d_temb = None
    for j in range(BLOCKS):
        grads = dtb[j]
        vec_o[BASE + 3 + 3 * OWNED + j : BASE + 4 + 3 * OWNED + j, :] = jnp.sum(grads, axis=0, keepdims=True)
        grads = grads.astype(BF16)
        t_grad = dot(temb, grads, 0, 0)
        for half in range(2):
            mat_o[2 * KERNEL * OWNED + 2 * j + half] = t_grad[half * LANES : (half + 1) * LANES].astype(mat_o.dtype)
        term = dot(grads, lin(j), 1, 1)
        d_temb = term if d_temb is None else d_temb + term
    d_pre = d_temb * time_slope
    vec_o[BASE + 1 : BASE + 2, :] = jnp.sum(d_pre, axis=0, keepdims=True)
    mat_o[UNITS - 1] = dot(emb[...], d_pre.astype(BF16), 0, 0).astype(mat_o.dtype)


def net(emb, noisy, noise, mask, table, mats, frames):
    rows = noisy.shape[0]
    trajs = rows // frames
    lane = jnp.arange(WIDTH, dtype=jnp.int32) // (WIDTH // GROUPS)
    gmat = (lane[:, None] == lane[None, :]).astype(F32)
    vm = pl.BlockSpec(memory_space=pltpu.VMEM)
    f = jax.ShapeDtypeStruct
    big = pltpu.VMEM((rows, WIDTH), F32)
    small = pltpu.VMEM((trajs, WIDTH), F32)
    return pl.pallas_call(
        functools.partial(net_kernel, trajs, frames),
        out_shape=[f((UNITS, LANES, WIDTH), BF16), f((VROWS, WIDTH), F32), f((1, FEAT), F32)],
        in_specs=[vm] * 7,
        out_specs=[vm] * 3,
        scratch_shapes=[
            pltpu.VMEM((OWNED + 1, rows, WIDTH), BF16),
            pltpu.VMEM((OWNED, rows, WIDTH), F32),
            big, big, big, big, big,
            pltpu.VMEM((rows, KERNEL * WIDTH), BF16),
            pltpu.VMEM((2, CHUNK, frames + 2 * PAD, LANES), F32),
            small, small, small,
            pltpu.VMEM((OWNED, trajs, WIDTH), F32),
            pltpu.VMEM((OWNED, trajs, WIDTH), F32),
            small, small, small, small,
            pltpu.VMEM((BLOCKS, trajs, WIDTH), F32),
            pltpu.VMEM((BLOCKS, trajs, WIDTH), F32),
            pltpu.VMEM((rows, FEAT), BF16),
            pltpu.VMEM((16, WIDTH), F32),
        ],
        compiler_params=pltpu.CompilerParams(vmem_limit_bytes=60 * 2**20),
        name="net",
    )(emb, noisy, noise, mask, table, mats, gmat)


def body(
    trajectories,
    noise,
    timesteps,
    valid,
    owners,
    mat_weight,
    mat_ema,
    soap_first,
    soap_second,
    left_stat,
    right_stat,
    left_basis,
    right_basis,
    vec_weight,
    vec_first,
    vec_second,
    vec_ema,
):
    mask = valid.astype(jnp.float32)
    count_local = FEAT * jnp.sum(mask)
    count_total = lax.psum(count_local, ("dp", "shard"))
    mat_low = lax.all_gather(mat_weight.astype(jnp.bfloat16), "shard", axis=1, tiled=True)
    table = lax.all_gather(vec_weight, "shard", axis=0, tiled=True)
    level = noise_level(timesteps)[:, None, None]
    noisy = (jnp.sqrt(level) * trajectories + jnp.sqrt(1.0 - level) * noise).astype(jnp.bfloat16)
    emb = time_embed(timesteps).astype(jnp.bfloat16)
    frames = valid.shape[1]
    mat_grad, vec_grad, loss_parts = net(
        emb,
        noisy.reshape(-1, FEAT),
        noise.reshape(-1, FEAT),
        mask.reshape(-1, 1),
        table,
        mat_low,
        frames,
    )
    loss_local = jnp.sum(loss_parts)
    shards = lax.axis_size("shard")
    groups = lax.axis_size("dp")
    mat_part, vec_part = (
        lax.psum_scatter(
            mat_grad.astype(jnp.bfloat16), "shard", scatter_dimension=1, tiled=True
        ).astype(jnp.float32),
        lax.psum_scatter(
            vec_grad.astype(jnp.bfloat16), "shard", scatter_dimension=0, tiled=True
        ).astype(jnp.float32),
    )
    mat_part, vec_part = lax.psum((mat_part, vec_part), "dp")
    square_local = jnp.sum(mat_part * mat_part) + jnp.sum(vec_part * vec_part)
    loss_total, square_total = lax.psum((loss_local, square_local / groups), ("dp", "shard"))
    grad_norm = jnp.sqrt(square_total) / count_total
    factor = jnp.minimum(1.0, CLIP / (grad_norm + 1e-06))
    vec_part = vec_part / count_total * factor
    slots = shards * soap_first.shape[0]
    choose = (owners[None, :] == jnp.arange(slots, dtype=jnp.int32)[:, None]).astype(jnp.float32)
    outgoing = jnp.einsum("sm,mrw->srw", choose, mat_part, precision=HIGH)
    incoming = lax.all_to_all(outgoing, "shard", split_axis=0, concat_axis=1, tiled=True)
    scale = (factor / count_total).reshape(1)
    results = soap(
        scale, incoming, soap_first, soap_second, left_stat, right_stat, left_basis, right_basis
    )
    returned = lax.all_to_all(
        results[0].astype(jnp.bfloat16), "shard", split_axis=1, concat_axis=0, tiled=True
    ).astype(jnp.float32)
    update = jnp.einsum("sm,srw->mrw", choose, returned, precision=HIGH)
    new_mat = mat_weight * (1.0 - LEARN * DECAY) - LEARN * update
    new_mat_ema = EMA_RATE * mat_ema + (1.0 - EMA_RATE) * new_mat
    new_vec_first = BETA_ONE * vec_first + (1.0 - BETA_ONE) * vec_part
    new_vec_second = BETA_TWO * vec_second + (1.0 - BETA_TWO) * vec_part * vec_part
    step_vec = (
        new_vec_first
        / (1.0 - BETA_ONE**STEP)
        / (jnp.sqrt(new_vec_second / (1.0 - BETA_TWO**STEP)) + ADAM_EPS)
    )
    new_vec = vec_weight * (1.0 - TABLE_LEARN * DECAY) - TABLE_LEARN * step_vec
    new_vec_ema = EMA_RATE * vec_ema + (1.0 - EMA_RATE) * new_vec
    return (
        loss_total,
        count_total,
        grad_norm,
        new_mat,
        new_mat_ema,
        results[1],
        results[2],
        results[3],
        results[4],
        results[5],
        results[6],
        new_vec,
        new_vec_first,
        new_vec_second,
        new_vec_ema,
    )


def solution(mesh):
    placed = (
        P(("dp", "shard"), None, None),
        P(("dp", "shard"), None, None),
        P(("dp", "shard")),
        P(("dp", "shard"), None),
        P(),
        P(None, "shard", None),
        P(None, "shard", None),
        P("shard", None, None),
        P("shard", None, None),
        P("shard", None, None),
        P("shard", None, None),
        P("shard", None, None),
        P("shard", None, None),
        P("shard", None),
        P("shard", None),
        P("shard", None),
        P("shard", None),
    )
    return jax.shard_map(
        body,
        mesh=mesh,
        in_specs=placed,
        out_specs=(
            P(),
            P(),
            P(),
            P(None, "shard", None),
            P(None, "shard", None),
            P("shard", None, None),
            P("shard", None, None),
            P("shard", None, None),
            P("shard", None, None),
            P("shard", None, None),
            P("shard", None, None),
            P("shard", None),
            P("shard", None),
            P("shard", None),
            P("shard", None),
        ),
        check_vma=False,
    )
```

```python
import functools
import math

import jax
import jax.numpy as jnp
from jax import lax
from jax.experimental import pallas as pl
from jax.experimental.pallas import tpu as pltpu
from jax.sharding import PartitionSpec as P

WIDTH = 256
KERNEL = 5
GROUPS = 8
TDIM = 128
FEAT = 23
BLOCKS = 3
DSTEPS = 20
STEP = 10
OWNED = 6
UNITS = 67
VROWS = 128

HIGH = lax.Precision.HIGHEST
BETA_ONE = 0.9
BETA_TWO = 0.95
ADAM_EPS = 1e-08
LEARN = 0.05
TABLE_LEARN = 0.25
DECAY = 0.01
CLIP = 0.05
EMA_RATE = 0.8
NORM_EPS = 1e-05
PANEL = 32
LANES = 128
PAD = 8
CHUNK = 8
TILE = 16
BASE = 2 * FEAT
F32 = jnp.float32
BF16 = jnp.bfloat16
MESH = pl.DeviceIdType.MESH


def noise_level(steps):
    offset = 0.008
    ratio = (steps.astype(jnp.float32) + 1.0) / DSTEPS
    upper = jnp.cos((ratio + offset) / (1.0 + offset) * math.pi / 2) ** 2
    return upper / math.cos(offset / (1.0 + offset) * math.pi / 2) ** 2


def time_embed(steps):
    halfway = TDIM // 2
    freqs = jnp.exp(-math.log(10000.0) * jnp.arange(halfway, dtype=jnp.float32) / (halfway - 1))
    angles = steps.astype(jnp.float32)[:, None] * freqs[None, :]
    return jnp.concatenate([jnp.sin(angles), jnp.cos(angles)], axis=-1)


def mm(a, b, ca=1, cb=0):
    return lax.dot_general(a, b, (((ca,), (cb,)), ((), ())), precision=HIGH, preferred_element_type=jnp.float32)

def split3(v):
    hi = v.astype(jnp.bfloat16)
    rest = v - hi.astype(jnp.float32)
    mid = rest.astype(jnp.bfloat16)
    last = (rest - mid.astype(jnp.float32)).astype(jnp.bfloat16)
    return hi, mid, last

def factor_panels(chains, start):
    rows = lax.broadcasted_iota(jnp.int32, (PANEL, LANES), 0)
    lanes = lax.broadcasted_iota(jnp.int32, (PANEL, LANES), 1)
    unit = jnp.where(lanes - PANEL == rows, 1.0, 0.0).astype(jnp.float32)
    offset = lax.rem(start, LANES)
    tile = pl.multiple_of(start - offset, LANES)
    shift = lax.rem(LANES - offset, LANES)
    held = []
    for z, s, n in chains:
        block = z[s, pl.ds(start, PANEL), pl.ds(tile, LANES)]
        held.append(jnp.where(lanes < PANEL, pltpu.roll(block, shift, 1), unit))
    for k in range(PANEL):
        for c in range(len(chains)):
            e = held[c]
            column = jnp.broadcast_to(e[:, k : k + 1], (PANEL, LANES))
            pivot = column[k : k + 1, :]
            row = e[k : k + 1, :] * (1.0 / pivot)
            held[c] = e - jnp.where(rows > k, column, 0.0) * row
    for c, (z, s, n) in enumerate(chains):
        e = held[c]
        pivots = jnp.sum(jnp.where(lanes == rows, e, 0.0), axis=1, keepdims=True)
        inverse = e[:, PANEL : 2 * PANEL] * lax.rsqrt(pivots)
        panel = z[s, pl.ds(start, PANEL), :]
        done = mm(inverse, panel)
        z[s, pl.ds(start, PANEL), :] = done
        hi, mid, last = split3(done)
        lhs = jnp.concatenate([hi, hi, mid, hi, last, mid], axis=0)[:, :n]
        rhs = jnp.concatenate([hi, mid, hi, last, hi, mid], axis=0)
        for r in range(0, n, LANES):
            upd = lax.dot_general(lhs[:, r:r + LANES], rhs, (((0,), (0,)), ((), ())), preferred_element_type=jnp.float32)
            rowid = lax.broadcasted_iota(jnp.int32, (LANES, 2 * n), 0) + r
            z[s, pl.ds(r, LANES), :] = z[s, pl.ds(r, LANES), :] - jnp.where(rowid >= start + PANEL, upd, 0.0)


def split_shard(shards):
    return 4, shards // 8


def place(outer, inner):
    s = lax.axis_index("shard")
    return s // (2 * inner), lax.rem(s // 2, inner), lax.rem(s, 2)


def spot(inner, a, b, c):
    return (a * inner + b) * 2 + c


def greet(peers):
    barrier = pltpu.get_barrier_semaphore()
    for peer in peers:
        pl.semaphore_signal(barrier, inc=1, device_id=peer, device_id_type=MESH)
    pl.semaphore_wait(barrier, len(peers))


def chunk_rows(slots, groups):
    step = 2 * groups * TILE
    return -(-(slots * LANES + TILE) // step) * step


def reduce_kernel(groups, outer, inner, slots, vrows, inverse, present, grad, vec, scal, slot_o, vec_o, scal_o,
                  s_core, r_core, held, r_in_a, sum_a, r_dp_a, r_dp_b, sum_b, r_in_b, ready, r_out, final, sc,
                  sem_core, sem_in_a, sem_dp_a, sem_dp_b, sem_in_b, sem_out, sem_fin, sem_sc):
    d = lax.axis_index("dp")
    a, b, c = place(outer, inner)
    me = lax.axis_index("shard")
    rows = s_core.shape[1]
    half = rows // 2
    piece = half // groups
    core_peer = (d, spot(inner, a, b, 1 - c))
    in_peers = [(d, spot(inner, a, lax.rem(b + i, inner), c)) for i in range(1, inner)]
    dp_peers = [(lax.rem(d + i, groups), me) for i in range(1, groups)]
    out_peers = [(d, spot(inner, lax.rem(a + i, outer), b, c)) for i in range(1, outer)]
    greet([core_peer] + in_peers + dp_peers + out_peers)
    waits = []

    def send(src, dst, sems, index, peer):
        copy = pltpu.make_async_remote_copy(
            src_ref=src, dst_ref=dst, send_sem=sems.at[(0,) + index], recv_sem=sems.at[(1,) + index],
            device_id=peer, device_id_type=MESH)
        copy.start()
        waits.append(copy)
        return copy

    def load(aa, bb, cc):
        target = spot(inner, aa, bb, cc)
        parts = []
        for s in range(slots):
            at = target * slots + s
            parts.append(grad[inverse[at]].astype(F32) * present[at])
        tail = vec[target].astype(F32)
        parts.append(tail)
        parts.append(jnp.zeros((rows - slots * LANES - TILE, WIDTH), F32))
        return jnp.concatenate(parts, axis=0)

    sc[0, c] = scal[...]
    moves = [send(sc.at[0, c], sc.at[0, c], sem_sc, (0, 0), core_peer)]
    order = [lax.rem(a + i, outer) for i in range(1, outer + 1)]
    core_copies = []
    for i in range(outer):
        for j in range(inner):
            s_core[i * inner + j] = load(order[i], j, 1 - c).astype(BF16)
            core_copies.append(send(s_core.at[i * inner + j], r_core.at[i * inner + j], sem_core, (i * inner + j,), core_peer))

    def share(level, index, total, peers):
        sc[level, index] = total
        return [send(sc.at[level, index], sc.at[level, index], sem_sc, (level, k), p) for k, p in enumerate(peers)]

    def gathered(level, count):
        for m in moves:
            m.wait_recv()
        total = sc[level, 0]
        for k in range(1, count):
            total = total + sc[level, k]
        return total

    in_a, dp_b = [], []
    for i in range(outer):
        for j in range(inner):
            core_copies[i * inner + j].wait_recv()
            held[i * inner + j] = (load(order[i], j, c) + r_core[i * inner + j].astype(F32)).astype(BF16)
        in_a.append([send(held.at[i * inner + lax.rem(b + k, inner), pl.ds(0, half)], r_in_a.at[i, k - 1], sem_in_a, (i, k - 1), in_peers[k - 1])
                     for k in range(1, inner)])
        dp_b.append([send(held.at[i * inner + j, pl.ds(pl.multiple_of(half + lax.rem(d + k, groups) * piece, TILE), piece)],
                          r_dp_b.at[i, j, k - 1], sem_dp_b, (i, j, k - 1), dp_peers[k - 1])
                     for k in range(1, groups) for j in range(inner)])
        if i == 0:
            total = gathered(0, 2)
            moves = share(1, b, total, in_peers)
    dp_a, in_b = [], []
    for i in range(outer):
        for m in in_a[i]:
            m.wait_recv()
        total = held[i * inner + b, pl.ds(0, half)].astype(F32)
        for k in range(inner - 1):
            total = total + r_in_a[i, k].astype(F32)
        sum_a[i] = total.astype(BF16)
        dp_a.append([send(sum_a.at[i, pl.ds(pl.multiple_of(lax.rem(d + k, groups) * piece, TILE), piece)], r_dp_a.at[i, k - 1], sem_dp_a, (i, k - 1), dp_peers[k - 1])
                     for k in range(1, groups)])
        for m in dp_b[i]:
            m.wait_recv()
        for j in range(inner):
            total = held[i * inner + j, pl.ds(pl.multiple_of(half + d * piece, TILE), piece)].astype(F32)
            for k in range(groups - 1):
                total = total + r_dp_b[i, j, k].astype(F32)
            sum_b[i * inner + j] = total.astype(BF16)
        in_b.append([send(sum_b.at[i * inner + lax.rem(b + k, inner)], r_in_b.at[i, k - 1], sem_in_b, (i, k - 1), in_peers[k - 1])
                     for k in range(1, inner)])
        if i == 0:
            total = gathered(1, inner)
            moves = share(2, d, total, dp_peers)
    out = []
    for i in range(outer):
        for m in dp_a[i] + in_b[i]:
            m.wait_recv()
        first = sum_a[i, pl.ds(pl.multiple_of(d * piece, TILE), piece)].astype(F32)
        for k in range(groups - 1):
            first = first + r_dp_a[i, k].astype(F32)
        second = sum_b[i * inner + b].astype(F32)
        for k in range(inner - 1):
            second = second + r_in_b[i, k].astype(F32)
        ready[i, 0:piece] = first.astype(BF16)
        ready[i, piece : 2 * piece] = second.astype(BF16)
        if i < outer - 1:
            out.append(send(ready.at[i], r_out.at[i], sem_out, (i,), out_peers[i]))
        if i == 0:
            total = gathered(2, groups)
            moves = share(3, a, total, out_peers)
    total = ready[outer - 1].astype(F32)
    for i in range(outer - 1):
        out[i].wait_recv()
        total = total + r_out[i].astype(F32)
    final[d] = total.astype(BF16)
    last = [send(final.at[d], final.at[d], sem_fin, (k,), p) for k, p in enumerate(dp_peers)]
    total = gathered(3, outer)
    scal_o[...] = total
    scale = 1.0 / total[1:2, 0:1]
    for m in last:
        m.wait_recv()
    pieces = [final[k, 0:piece] for k in range(groups)] + [final[k, piece : 2 * piece] for k in range(groups)]
    whole = jnp.concatenate(pieces, axis=0).astype(F32) * scale
    for s in range(slots):
        slot_o[s] = whole[s * LANES : (s + 1) * LANES]
    vec_o[...] = whole[slots * LANES : slots * LANES + vrows]
    for m in waits:
        m.wait_send()


def reduce_grads(inverse, present, grad, vec, scal, slots, groups, shards):
    outer, inner = split_shard(shards)
    vrows = vec.shape[0] // shards
    tails = jnp.pad(vec.reshape(shards, vrows, WIDTH), ((0, 0), (0, TILE - vrows), (0, 0)))
    rows = chunk_rows(slots, groups)
    half = rows // 2
    piece = half // groups
    f = jax.ShapeDtypeStruct
    vm = pl.BlockSpec(memory_space=pltpu.VMEM)
    sm = pl.BlockSpec(memory_space=pltpu.SMEM)
    both = outer * inner

    def buf(*shape):
        return pltpu.VMEM(shape + (WIDTH,), BF16)

    dma = pltpu.SemaphoreType.DMA
    peers_in, peers_dp = max(inner - 1, 1), max(groups - 1, 1)
    return pl.pallas_call(
        functools.partial(reduce_kernel, groups, outer, inner, slots, vrows),
        out_shape=[f((slots, LANES, WIDTH), F32), f((vrows, WIDTH), F32), f((8, LANES), F32)],
        in_specs=[sm, sm, vm, vm, vm],
        out_specs=[vm] * 3,
        scratch_shapes=[
            buf(both, rows), buf(both, rows), buf(both, rows),
            buf(outer, peers_in, half), buf(outer, half), buf(outer, peers_dp, piece),
            buf(outer, inner, peers_dp, piece), buf(both, piece), buf(outer, peers_in, piece),
            buf(outer, 2 * piece), buf(outer - 1, 2 * piece), buf(groups, 2 * piece),
            pltpu.VMEM((4, 4, 8, LANES), F32),
            dma((2, both)), dma((2, outer, peers_in)), dma((2, outer, peers_dp)), dma((2, outer, inner, peers_dp)),
            dma((2, outer, peers_in)), dma((2, outer - 1)), dma((2, peers_dp)), dma((2, 4, 3)),
        ],
        compiler_params=pltpu.CompilerParams(collective_id=1, has_side_effects=True, vmem_limit_bytes=56 * 2**20),
        name="reduce",
    )(inverse, present, grad, tails, scal)


def soap_kernel(shards, slots, owners, scal, g, gvec, m, v, ls, rs, lb, rb, mat, ema, vw, vf, vs, ve,
                scal_o, mat_o, ema_o, m_o, v_o, ls_o, rs_o, lb_o, rb_o, vw_o, vf_o, vs_o, ve_o,
                zl, zr, turn, sent, got, back, norms, sem_n, sem_u):
    d = lax.axis_index("dp")
    me = lax.axis_index("shard")
    peers = [(d, lax.rem(me + i, shards)) for i in range(1, shards)]
    greet(peers)
    piece = mat.shape[1]

    def send(src, dst, sems, index, peer):
        copy = pltpu.make_async_remote_copy(
            src_ref=src, dst_ref=dst, send_sem=sems.at[0, index], recv_sem=sems.at[1, index],
            device_id=peer, device_id_type=MESH)
        copy.start()
        return copy

    square = jnp.sum(gvec[...] * gvec[...])
    for s in range(slots):
        square = square + jnp.sum(g[s] * g[s])
    norms[me] = jnp.full((8, LANES), square, F32)
    moves = [send(norms.at[me], norms.at[me], sem_n, k, p) for k, p in enumerate(peers)]
    for s in range(slots):
        left, right = lb[s], rb[s]
        turn[s] = mm(mm(left, g[s], 0, 0), right)
        v_o[s] = mm(mm(left, m[s], 0, 0), right)
    for move in moves:
        move.wait_recv()
    total = norms[0]
    for k in range(1, shards):
        total = total + norms[k]
    norm = jnp.sqrt(total)
    factor = jnp.minimum(1.0, CLIP / (norm + 1e-06))
    rowid = lax.broadcasted_iota(jnp.int32, (8, LANES), 0)
    scal_o[...] = jnp.where(rowid == 2, norm, scal[...])
    scale = factor[0:1, 0:1]
    for s in range(slots):
        turned = turn[s] * scale
        moment = BETA_ONE * v_o[s] + (1.0 - BETA_ONE) * turned
        second = BETA_TWO * v[s] + (1.0 - BETA_TWO) * turned * turned
        v_o[s] = second
        normed = moment / (1.0 - BETA_ONE**STEP) / (jnp.sqrt(second / (1.0 - BETA_TWO**STEP)) + ADAM_EPS)
        turn[s] = mm(mm(lb[s], normed), rb[s], 1, 1)
    used = slots * piece
    full = sent.shape[1]
    for t in range(shards):
        parts = [turn[s, t * piece : (t + 1) * piece, :] for s in range(slots)]
        if full > used:
            parts.append(jnp.zeros((full - used, WIDTH), F32))
        sent[t] = jnp.concatenate(parts, axis=0).astype(BF16)
    got[me] = sent[me]
    moves = moves + [send(sent.at[p[1]], got.at[me], sem_u, k, p) for k, p in enumerate(peers)]
    for s in range(slots):
        grad = g[s] * scale
        left, right = lb[s], rb[s]
        m_o[s] = BETA_ONE * m[s] + (1.0 - BETA_ONE) * grad
        lnew = BETA_TWO * ls[s] + (1.0 - BETA_TWO) * mm(grad, grad, 1, 1)
        rnew = BETA_TWO * rs[s] + (1.0 - BETA_TWO) * mm(grad, grad, 0, 0)
        ls_o[s] = lnew
        rs_o[s] = rnew
        xl = mm(left, lnew, 0, 1)
        xr = mm(right, rnew, 0, 1)
        zl[s, :, :LANES] = mm(xl, xl, 1, 1)
        zl[s, :, LANES:] = xl
        zr[s, :, : 2 * LANES] = mm(xr, xr, 1, 1)
        zr[s, :, 2 * LANES :] = xr
    grad = gvec[...] * scale
    first = BETA_ONE * vf[...] + (1.0 - BETA_ONE) * grad
    second = BETA_TWO * vs[...] + (1.0 - BETA_TWO) * grad * grad
    step = first / (1.0 - BETA_ONE**STEP) / (jnp.sqrt(second / (1.0 - BETA_TWO**STEP)) + ADAM_EPS)
    new = vw[...] * (1.0 - TABLE_LEARN * DECAY) - TABLE_LEARN * step
    vf_o[...] = first
    vs_o[...] = second
    vw_o[...] = new
    ve_o[...] = EMA_RATE * ve[...] + (1.0 - EMA_RATE) * new
    lc = [(zl, s, LANES) for s in range(slots)]
    rc = [(zr, s, 2 * LANES) for s in range(slots)]

    def both(p, _):
        factor_panels(rc + lc, pl.multiple_of(p * PANEL, PANEL))
        return 0

    def only(p, _):
        factor_panels(rc, pl.multiple_of(p * PANEL, PANEL))
        return 0

    lax.fori_loop(0, LANES // PANEL, both, 0)
    lax.fori_loop(LANES // PANEL, 2 * LANES // PANEL, only, 0)
    for s in range(slots):
        lb_o[s] = zl[s, :, LANES:].T
        rb_o[s] = zr[s, :, 2 * LANES :].T
    for move in moves[shards - 1 :]:
        move.wait_recv()
    for t in range(shards):
        piece_t = got[t].astype(F32)
        for s in range(slots):
            back[t * slots + s] = piece_t[s * piece : (s + 1) * piece]
    for unit in range(UNITS):
        new = mat[unit] * (1.0 - LEARN * DECAY) - LEARN * back[owners[unit]]
        mat_o[unit] = new
        ema_o[unit] = EMA_RATE * ema[unit] + (1.0 - EMA_RATE) * new
    for move in moves:
        move.wait_send()


def soap(owners, scal, g, gvec, m, v, ls, rs, lb, rb, mat, ema, vw, vf, vs, ve, shards):
    slots, piece = g.shape[0], mat.shape[1]
    full = -(-slots * piece // TILE) * TILE
    f = jax.ShapeDtypeStruct
    vm = pl.BlockSpec(memory_space=pltpu.VMEM)
    outs = [f(x.shape, F32) for x in (scal, mat, ema, m, v, ls, rs, lb, rb, vw, vf, vs, ve)]
    dma = pltpu.SemaphoreType.DMA
    return pl.pallas_call(
        functools.partial(soap_kernel, shards, slots),
        out_shape=outs,
        in_specs=[pl.BlockSpec(memory_space=pltpu.SMEM)] + [vm] * 15,
        out_specs=[vm] * 13,
        scratch_shapes=[
            pltpu.VMEM((slots, LANES, 2 * LANES), F32),
            pltpu.VMEM((slots, 2 * LANES, 4 * LANES), F32),
            pltpu.VMEM((slots, LANES, WIDTH), F32),
            pltpu.VMEM((shards, full, WIDTH), BF16),
            pltpu.VMEM((shards, full, WIDTH), BF16),
            pltpu.VMEM((shards * slots, piece, WIDTH), F32),
            pltpu.VMEM((shards, 8, LANES), F32),
            dma((2, shards - 1)),
            dma((2, shards - 1)),
        ],
        compiler_params=pltpu.CompilerParams(collective_id=2, has_side_effects=True, vmem_limit_bytes=58 * 2**20),
        name="soap",
    )(owners, scal, g, gvec, m, v, ls, rs, lb, rb, mat, ema, vw, vf, vs, ve)


def dot(a, b, ca=1, cb=0):
    return lax.dot_general(a, b, (((ca,), (cb,)), ((), ())), preferred_element_type=F32)


def mish_parts(v):
    e = jnp.exp(jnp.minimum(v, 20.0))
    n = e * (e + 2.0)
    r = pl.reciprocal(n + 2.0)
    return e, r, n * r


def mish_slope(v, e, r, t):
    return t + v * (4.0 * e * (e + 1.0)) * (r * r)


def net_kernel(trajs, frames, emb, noisy, noise, mask, mats, gmat, mat_o, vec_o, loss_o,
               xin, xhat, h, skip, d, dskip, dy, u, xp, s_one, s_two, mean, rstd, xsum, q_one, q_two, g_one, g_two, tb, dtb, dpl, acc, table):
    rows_c = CHUNK * frames
    chunks = trajs // CHUNK
    table[...] = (mats[UNITS].astype(F32) + mats[UNITS + 1].astype(F32)) + mats[UNITS + 2].astype(F32)
    low = mats[UNITS, : 2 * FEAT, :]
    w_in, w_head = low[:FEAT], low[FEAT : 2 * FEAT]
    group = gmat[...]
    part = 1.0 / (frames * (WIDTH // GROUPS))

    def rows_of(c):
        return pl.ds(pl.multiple_of(c * rows_c, rows_c), rows_c)

    def trajs_of(c):
        return pl.ds(pl.multiple_of(c * CHUNK, CHUNK), CHUNK)

    def wide(v):
        return v.reshape(CHUNK, frames, WIDTH)

    def flat(v):
        return v.reshape(rows_c, WIDTH)

    def row(index):
        return table[index : index + 1, :]

    def gain(l):
        return row(BASE + 3 + OWNED + l), row(BASE + 3 + 2 * OWNED + l)

    def conv(l):
        return mats[2 * KERNEL * l : 2 * KERNEL * (l + 1)].reshape(KERNEL * WIDTH, WIDTH)

    def lin(j):
        start = 2 * KERNEL * OWNED + 2 * j
        return mats[start : start + 2].reshape(WIDTH, WIDTH)

    def group_sum(v):
        return lax.dot_general(v, group, (((1,), (0,)), ((), ())), precision=HIGH, preferred_element_type=F32)

    def spread(c, value, flip):
        for half in range(2):
            xp[half, :, PAD : PAD + frames, :] = value[:, half * LANES : (half + 1) * LANES].reshape(CHUNK, frames, LANES)
        for k in range(KERNEL):
            at = PAD + (KERNEL // 2 - k if flip else k - KERNEL // 2)
            for half in range(2):
                lane = k * WIDTH + half * LANES
                u[rows_of(c), lane : lane + LANES] = xp[half, :, at : at + frames, :].reshape(rows_c, LANES).astype(BF16)

    def pass_one(l, c, x):
        xin[l, rows_of(c), :] = x.astype(BF16)
        spread(c, x, False)
        p = dot(u[rows_of(c), :], conv(l)) + row(BASE + 3 + l)
        xhat[l, rows_of(c), :] = p
        p = wide(p)
        total = jnp.sum(p, axis=1)
        s_one[trajs_of(c), :] = total
        off = p - (total * (1.0 / frames))[:, None, :]
        s_two[trajs_of(c), :] = jnp.sum(off * off, axis=1)

    def stats(l):
        total = s_one[...]
        centre = group_sum(total) * part
        off = total * (1.0 / frames) - centre
        var = group_sum(s_two[...] + frames * off * off) * part
        scale = lax.rsqrt(var + NORM_EPS)
        mean[...] = centre
        rstd[l] = scale
        xsum[l] = frames * off * scale

    def normed(l, c):
        p = wide(xhat[l, rows_of(c), :])
        x = flat((p - mean[trajs_of(c), :][:, None, :]) * rstd[l, trajs_of(c), :][:, None, :])
        xhat[l, rows_of(c), :] = x
        g, s = gain(l)
        return x, x * g + s

    def pass_a(l, c, dm, x, v, parts):
        slope = dm * mish_slope(v, *parts)
        dy[rows_of(c), :] = slope
        q_one[trajs_of(c), :] = jnp.sum(wide(slope), axis=1)
        q_two[trajs_of(c), :] = jnp.sum(wide(slope * x), axis=1)

    def pass_a_load(l, c, dm):
        x = xhat[l, rows_of(c), :]
        g, s = gain(l)
        v = x * g + s
        pass_a(l, c, dm, x, v, mish_parts(v))

    def stats_back(l):
        g, s = gain(l)
        one, two = q_one[...], q_two[...]
        vec_o[BASE + 3 + OWNED + l : BASE + 4 + OWNED + l, :] = jnp.sum(two, axis=0, keepdims=True)
        vec_o[BASE + 3 + 2 * OWNED + l : BASE + 4 + 2 * OWNED + l, :] = jnp.sum(one, axis=0, keepdims=True)
        sums = group_sum(jnp.concatenate([one * g, two * g], axis=0)) * part
        first, second = sums[:trajs], sums[trajs:]
        g_one[...] = first
        g_two[...] = second
        dc = rstd[l] * (one * g - frames * first - xsum[l] * second)
        vec_o[BASE + 3 + l : BASE + 4 + l, :] = jnp.sum(dc, axis=0, keepdims=True)

    def loop(body):
        def step(c, carry):
            body(c)
            return carry

        lax.fori_loop(0, chunks, step, 0)

    vec_o[...] = jnp.zeros_like(vec_o)
    xp[...] = jnp.zeros_like(xp)
    acc[...] = jnp.zeros_like(acc)
    pre_time = dot(emb[...], mats[UNITS - 1]) + row(BASE + 1)
    time_parts = mish_parts(pre_time)
    temb = (pre_time * time_parts[2]).astype(BF16)
    time_slope = mish_slope(pre_time, *time_parts)
    for j in range(BLOCKS):
        tb[j] = dot(temb, lin(j)) + row(BASE + 3 + 3 * OWNED + j)

    def enter(c):
        x = dot(noisy[rows_of(c), :], w_in) + row(BASE)
        h[rows_of(c), :] = x
        pass_one(0, c, x)

    loop(enter)
    for l in range(OWNED - 1):
        stats(l)

        def forward(c, l=l):
            _, v = normed(l, c)
            m = v * mish_parts(v)[2]
            if l % 2 == 0:
                m = flat(wide(m) + tb[l // 2, trajs_of(c), :][:, None, :])
            else:
                m = h[rows_of(c), :] + m
                if l == 1:
                    skip[rows_of(c), :] = m
                if l == 2 * BLOCKS - 3:
                    m = m + skip[rows_of(c), :]
                h[rows_of(c), :] = m
            pass_one(l + 1, c, m)

        loop(forward)
    stats(OWNED - 1)

    def turn(c):
        l = OWNED - 1
        x, v = normed(l, c)
        parts = mish_parts(v)
        top = (h[rows_of(c), :] + v * parts[2]).astype(BF16)
        xin[OWNED, rows_of(c), :] = top
        err = dot(top, w_head, 1, 1) + row(BASE + 2)[:, :FEAT] - noise[rows_of(c), :]
        weighted = mask[rows_of(c), :] * err
        acc[1:2, :FEAT] += jnp.sum(weighted * err, axis=0, keepdims=True)
        grad = 2.0 * weighted
        acc[0:1, :FEAT] += jnp.sum(grad, axis=0, keepdims=True)
        grad = grad.astype(BF16)
        dpl[rows_of(c), :] = grad
        dh = dot(grad, w_head)
        d[rows_of(c), :] = dh
        pass_a(l, c, dh, x, v, parts)

    loop(turn)
    vec_o[FEAT : 2 * FEAT, :] = dot(dpl[...], xin[OWNED], 0, 0)
    vec_o[BASE + 2 : BASE + 3, :] = acc[0:1, :]
    loss = jnp.sum(acc[1:2, :], axis=1, keepdims=True)
    count = FEAT * jnp.sum(mask[...], axis=0, keepdims=True)
    rowid = lax.broadcasted_iota(jnp.int32, (8, LANES), 0)
    loss_o[...] = jnp.where(rowid == 0, loss, jnp.where(rowid == 1, count, 0.0))

    for l in reversed(range(OWNED)):
        stats_back(l)

        def backward(c, l=l):
            g, s = gain(l)
            at = trajs_of(c)
            x = wide(xhat[l, rows_of(c), :])
            dp = rstd[l, at, :][:, None, :] * (
                wide(dy[rows_of(c), :] * g) - g_one[at, :][:, None, :] - x * g_two[at, :][:, None, :]
            )
            spread(c, flat(dp), True)
            dx = None
            w = conv(l)
            for k in range(KERNEL):
                term = dot(u[rows_of(c), k * WIDTH : (k + 1) * WIDTH], w[k * WIDTH : (k + 1) * WIDTH], 1, 1)
                dx = term if dx is None else dx + term
            if l % 2 == 1:
                dtb[l // 2, at, :] = jnp.sum(wide(dx), axis=1)
                pass_a_load(l - 1, c, dx)
            else:
                dx = d[rows_of(c), :] + dx
                if l == OWNED - 2:
                    dskip[rows_of(c), :] = dx
                if l == 2:
                    dx = dx + dskip[rows_of(c), :]
                if l > 0:
                    d[rows_of(c), :] = dx
                    pass_a_load(l - 1, c, dx)
                else:
                    acc[8:16, :] += jnp.sum(dx.reshape(rows_c // 8, 8, WIDTH), axis=0)
                    xin[OWNED, rows_of(c), :] = dx.astype(BF16)

        loop(backward)
        w_grad = dot(xin[l], u[...], 0, 0)
        for k in range(KERNEL):
            for half in range(2):
                mat_o[2 * KERNEL * l + 2 * k + half] = w_grad[half * LANES : (half + 1) * LANES, k * WIDTH : (k + 1) * WIDTH].astype(mat_o.dtype)

    vec_o[BASE : BASE + 1, :] = jnp.sum(acc[8:16, :], axis=0, keepdims=True)
    vec_o[:FEAT, :] = dot(noisy[...], xin[OWNED], 0, 0)
    d_temb = None
    for j in range(BLOCKS):
        grads = dtb[j]
        vec_o[BASE + 3 + 3 * OWNED + j : BASE + 4 + 3 * OWNED + j, :] = jnp.sum(grads, axis=0, keepdims=True)
        grads = grads.astype(BF16)
        t_grad = dot(temb, grads, 0, 0)
        for half in range(2):
            mat_o[2 * KERNEL * OWNED + 2 * j + half] = t_grad[half * LANES : (half + 1) * LANES].astype(mat_o.dtype)
        term = dot(grads, lin(j), 1, 1)
        d_temb = term if d_temb is None else d_temb + term
    d_pre = d_temb * time_slope
    vec_o[BASE + 1 : BASE + 2, :] = jnp.sum(d_pre, axis=0, keepdims=True)
    mat_o[UNITS - 1] = dot(emb[...], d_pre.astype(BF16), 0, 0).astype(mat_o.dtype)


def net(emb, noisy, noise, mask, mats, frames):
    rows = noisy.shape[0]
    trajs = rows // frames
    lane = jnp.arange(WIDTH, dtype=jnp.int32) // (WIDTH // GROUPS)
    gmat = (lane[:, None] == lane[None, :]).astype(F32)
    vm = pl.BlockSpec(memory_space=pltpu.VMEM)
    f = jax.ShapeDtypeStruct
    big = pltpu.VMEM((rows, WIDTH), F32)
    small = pltpu.VMEM((trajs, WIDTH), F32)
    return pl.pallas_call(
        functools.partial(net_kernel, trajs, frames),
        out_shape=[f((UNITS, LANES, WIDTH), BF16), f((VROWS, WIDTH), F32), f((8, LANES), F32)],
        in_specs=[vm] * 6,
        out_specs=[vm] * 3,
        scratch_shapes=[
            pltpu.VMEM((OWNED + 1, rows, WIDTH), BF16),
            pltpu.VMEM((OWNED, rows, WIDTH), F32),
            big, big, big, big, big,
            pltpu.VMEM((rows, KERNEL * WIDTH), BF16),
            pltpu.VMEM((2, CHUNK, frames + 2 * PAD, LANES), F32),
            small, small, small,
            pltpu.VMEM((OWNED, trajs, WIDTH), F32),
            pltpu.VMEM((OWNED, trajs, WIDTH), F32),
            small, small, small, small,
            pltpu.VMEM((BLOCKS, trajs, WIDTH), F32),
            pltpu.VMEM((BLOCKS, trajs, WIDTH), F32),
            pltpu.VMEM((rows, FEAT), BF16),
            pltpu.VMEM((16, WIDTH), F32),
            pltpu.VMEM((VROWS, WIDTH), F32),
        ],
        compiler_params=pltpu.CompilerParams(vmem_limit_bytes=60 * 2**20),
        name="net",
    )(emb, noisy, noise, mask, mats, gmat)


def split_table(v):
    hi = lax.optimization_barrier(v.astype(BF16))
    rest = v - hi.astype(F32)
    mid = lax.optimization_barrier(rest.astype(BF16))
    last = lax.optimization_barrier((rest - mid.astype(F32)).astype(BF16))
    return jnp.stack([hi, mid, last])


def body(
    trajectories,
    noise,
    timesteps,
    valid,
    owners,
    mat_weight,
    mat_ema,
    soap_first,
    soap_second,
    left_stat,
    right_stat,
    left_basis,
    right_basis,
    vec_weight,
    vec_first,
    vec_second,
    vec_ema,
):
    shards = lax.axis_size("shard")
    groups = lax.axis_size("dp")
    slots = soap_first.shape[0]
    mask = valid.astype(jnp.float32)
    parts = jnp.concatenate([mat_weight.astype(BF16), split_table(vec_weight)], axis=0)
    mats = lax.all_gather(parts, "shard", axis=1, tiled=True)
    level = noise_level(timesteps)[:, None, None]
    noisy = (jnp.sqrt(level) * trajectories + jnp.sqrt(1.0 - level) * noise).astype(jnp.bfloat16)
    emb = time_embed(timesteps).astype(jnp.bfloat16)
    mat_grad, vec_grad, scal = net(
        emb,
        noisy.reshape(-1, FEAT),
        noise.reshape(-1, FEAT),
        mask.reshape(-1, 1),
        mats,
        valid.shape[1],
    )
    choose = owners[None, :] == jnp.arange(shards * slots, dtype=jnp.int32)[:, None]
    order = jnp.arange(UNITS, dtype=jnp.int32)[None, :]
    inverse = jnp.sum(jnp.where(choose, order, 0), axis=1, dtype=jnp.int32)
    present = jnp.any(choose, axis=1).astype(F32)
    grads, grads_vec, scal = reduce_grads(inverse, present, mat_grad, vec_grad, scal, slots, groups, shards)
    results = soap(
        owners, scal, grads, grads_vec, soap_first, soap_second, left_stat, right_stat, left_basis, right_basis,
        mat_weight, mat_ema, vec_weight, vec_first, vec_second, vec_ema, shards,
    )
    scal = results[0]
    return (scal[0, 0], scal[1, 0], scal[2, 0]) + tuple(results[1:])


def solution(mesh):
    placed = (
        P(("dp", "shard"), None, None),
        P(("dp", "shard"), None, None),
        P(("dp", "shard")),
        P(("dp", "shard"), None),
        P(),
        P(None, "shard", None),
        P(None, "shard", None),
        P("shard", None, None),
        P("shard", None, None),
        P("shard", None, None),
        P("shard", None, None),
        P("shard", None, None),
        P("shard", None, None),
        P("shard", None),
        P("shard", None),
        P("shard", None),
        P("shard", None),
    )
    return jax.shard_map(
        body,
        mesh=mesh,
        in_specs=placed,
        out_specs=(
            P(),
            P(),
            P(),
            P(None, "shard", None),
            P(None, "shard", None),
            P("shard", None, None),
            P("shard", None, None),
            P("shard", None, None),
            P("shard", None, None),
            P("shard", None, None),
            P("shard", None, None),
            P("shard", None),
            P("shard", None),
            P("shard", None),
            P("shard", None),
        ),
        check_vma=False,
    )
```

```python
import functools
import math

import jax
import jax.numpy as jnp
import numpy as np
from jax import lax
from jax.experimental import pallas as pl
from jax.experimental.pallas import tpu as pltpu
from jax.sharding import PartitionSpec as P

WIDTH = 256
KERNEL = 5
GROUPS = 8
TDIM = 128
FEAT = 23
BLOCKS = 3
DSTEPS = 20
STEP = 10
OWNED = 6
UNITS = 67
VROWS = 128

HIGH = lax.Precision.HIGHEST
BETA_ONE = 0.9
BETA_TWO = 0.95
ADAM_EPS = 1e-08
LEARN = 0.05
TABLE_LEARN = 0.25
DECAY = 0.01
CLIP = 0.05
EMA_RATE = 0.8
NORM_EPS = 1e-05
PANEL = 32
LANES = 128
PAD = 8
CHUNK = 8
TILE = 16
BASE = 2 * FEAT
F32 = jnp.float32
BF16 = jnp.bfloat16
MESH = pl.DeviceIdType.MESH


def mm(a, b, ca=1, cb=0):
    return lax.dot_general(a, b, (((ca,), (cb,)), ((), ())), precision=HIGH, preferred_element_type=jnp.float32)

def split3(v):
    hi = v.astype(jnp.bfloat16)
    rest = v - hi.astype(jnp.float32)
    mid = rest.astype(jnp.bfloat16)
    last = (rest - mid.astype(jnp.float32)).astype(jnp.bfloat16)
    return hi, mid, last

def factor_panels(chains, start):
    rows = lax.broadcasted_iota(jnp.int32, (PANEL, LANES), 0)
    lanes = lax.broadcasted_iota(jnp.int32, (PANEL, LANES), 1)
    unit = jnp.where(lanes - PANEL == rows, 1.0, 0.0).astype(jnp.float32)
    offset = lax.rem(start, LANES)
    tile = pl.multiple_of(start - offset, LANES)
    shift = lax.rem(LANES - offset, LANES)
    held = []
    for z, s, n in chains:
        block = z[s, pl.ds(start, PANEL), pl.ds(tile, LANES)]
        held.append(jnp.where(lanes < PANEL, pltpu.roll(block, shift, 1), unit))
    for k in range(PANEL):
        for c in range(len(chains)):
            e = held[c]
            column = jnp.broadcast_to(e[:, k : k + 1], (PANEL, LANES))
            pivot = column[k : k + 1, :]
            row = e[k : k + 1, :] * (1.0 / pivot)
            held[c] = e - jnp.where(rows > k, column, 0.0) * row
    for c, (z, s, n) in enumerate(chains):
        e = held[c]
        pivots = jnp.sum(jnp.where(lanes == rows, e, 0.0), axis=1, keepdims=True)
        inverse = e[:, PANEL : 2 * PANEL] * lax.rsqrt(pivots)
        panel = z[s, pl.ds(start, PANEL), :]
        done = mm(inverse, panel)
        z[s, pl.ds(start, PANEL), :] = done
        hi, mid, last = split3(done)
        lhs = jnp.concatenate([hi, hi, mid, hi, last, mid], axis=0)[:, :n]
        rhs = jnp.concatenate([hi, mid, hi, last, hi, mid], axis=0)
        for r in range(0, n, LANES):
            upd = lax.dot_general(lhs[:, r:r + LANES], rhs, (((0,), (0,)), ((), ())), preferred_element_type=jnp.float32)
            rowid = lax.broadcasted_iota(jnp.int32, (LANES, 2 * n), 0) + r
            z[s, pl.ds(r, LANES), :] = z[s, pl.ds(r, LANES), :] - jnp.where(rowid >= start + PANEL, upd, 0.0)


def split_shard(shards):
    return 4, shards // 8


def place(outer, inner):
    s = lax.axis_index("shard")
    return s // (2 * inner), lax.rem(s // 2, inner), lax.rem(s, 2)


def spot(inner, a, b, c):
    return (a * inner + b) * 2 + c


def greet(peers):
    barrier = pltpu.get_barrier_semaphore()
    for peer in peers:
        pl.semaphore_signal(barrier, inc=1, device_id=peer, device_id_type=MESH)
    pl.semaphore_wait(barrier, len(peers))


def chunk_rows(slots, groups):
    step = 2 * groups * TILE
    return -(-(slots * LANES + TILE) // step) * step


def reduce_kernel(groups, outer, inner, slots, vrows, inverse, present, grad, vec, scal, slot_o, vec_o, scal_o,
                  s_core, r_core, held, r_in_a, sum_a, r_dp_a, r_dp_b, sum_b, r_in_b, ready, r_out, final, sc,
                  sem_core, sem_in_a, sem_dp_a, sem_dp_b, sem_in_b, sem_out, sem_fin, sem_sc):
    d = lax.axis_index("dp")
    a, b, c = place(outer, inner)
    me = lax.axis_index("shard")
    rows = s_core.shape[1]
    half = rows // 2
    piece = half // groups
    core_peer = (d, spot(inner, a, b, 1 - c))
    in_peers = [(d, spot(inner, a, lax.rem(b + i, inner), c)) for i in range(1, inner)]
    dp_peers = [(lax.rem(d + i, groups), me) for i in range(1, groups)]
    out_peers = [(d, spot(inner, lax.rem(a + i, outer), b, c)) for i in range(1, outer)]
    greet([core_peer] + in_peers + dp_peers + out_peers)
    waits = []

    def send(src, dst, sems, index, peer):
        copy = pltpu.make_async_remote_copy(
            src_ref=src, dst_ref=dst, send_sem=sems.at[(0,) + index], recv_sem=sems.at[(1,) + index],
            device_id=peer, device_id_type=MESH)
        copy.start()
        waits.append(copy)
        return copy

    def load(aa, bb, cc):
        target = spot(inner, aa, bb, cc)
        parts = []
        for s in range(slots):
            at = target * slots + s
            parts.append(grad[inverse[at]].astype(F32) * present[at])
        tail = vec[target].astype(F32)
        parts.append(tail)
        parts.append(jnp.zeros((rows - slots * LANES - TILE, WIDTH), F32))
        return jnp.concatenate(parts, axis=0)

    sc[0, c] = scal[...]
    moves = [send(sc.at[0, c], sc.at[0, c], sem_sc, (0, 0), core_peer)]
    order = [lax.rem(a + i, outer) for i in range(1, outer + 1)]
    core_copies = []
    for i in range(outer):
        for j in range(inner):
            s_core[i * inner + j] = load(order[i], j, 1 - c).astype(BF16)
            core_copies.append(send(s_core.at[i * inner + j], r_core.at[i * inner + j], sem_core, (i * inner + j,), core_peer))

    def share(level, index, total, peers):
        sc[level, index] = total
        return [send(sc.at[level, index], sc.at[level, index], sem_sc, (level, k), p) for k, p in enumerate(peers)]

    def gathered(level, count):
        for m in moves:
            m.wait_recv()
        total = sc[level, 0]
        for k in range(1, count):
            total = total + sc[level, k]
        return total

    in_a, dp_b = [], []
    for i in range(outer):
        for j in range(inner):
            core_copies[i * inner + j].wait_recv()
            held[i * inner + j] = (load(order[i], j, c) + r_core[i * inner + j].astype(F32)).astype(BF16)
        in_a.append([send(held.at[i * inner + lax.rem(b + k, inner), pl.ds(0, half)], r_in_a.at[i, k - 1], sem_in_a, (i, k - 1), in_peers[k - 1])
                     for k in range(1, inner)])
        dp_b.append([send(held.at[i * inner + j, pl.ds(pl.multiple_of(half + lax.rem(d + k, groups) * piece, TILE), piece)],
                          r_dp_b.at[i, j, k - 1], sem_dp_b, (i, j, k - 1), dp_peers[k - 1])
                     for k in range(1, groups) for j in range(inner)])
        if i == 0:
            total = gathered(0, 2)
            moves = share(1, b, total, in_peers)
    dp_a, in_b = [], []
    for i in range(outer):
        for m in in_a[i]:
            m.wait_recv()
        total = held[i * inner + b, pl.ds(0, half)].astype(F32)
        for k in range(inner - 1):
            total = total + r_in_a[i, k].astype(F32)
        sum_a[i] = total.astype(BF16)
        dp_a.append([send(sum_a.at[i, pl.ds(pl.multiple_of(lax.rem(d + k, groups) * piece, TILE), piece)], r_dp_a.at[i, k - 1], sem_dp_a, (i, k - 1), dp_peers[k - 1])
                     for k in range(1, groups)])
        for m in dp_b[i]:
            m.wait_recv()
        for j in range(inner):
            total = held[i * inner + j, pl.ds(pl.multiple_of(half + d * piece, TILE), piece)].astype(F32)
            for k in range(groups - 1):
                total = total + r_dp_b[i, j, k].astype(F32)
            sum_b[i * inner + j] = total.astype(BF16)
        in_b.append([send(sum_b.at[i * inner + lax.rem(b + k, inner)], r_in_b.at[i, k - 1], sem_in_b, (i, k - 1), in_peers[k - 1])
                     for k in range(1, inner)])
        if i == 0:
            total = gathered(1, inner)
            moves = share(2, d, total, dp_peers)
    out = []
    for i in range(outer):
        for m in dp_a[i] + in_b[i]:
            m.wait_recv()
        first = sum_a[i, pl.ds(pl.multiple_of(d * piece, TILE), piece)].astype(F32)
        for k in range(groups - 1):
            first = first + r_dp_a[i, k].astype(F32)
        second = sum_b[i * inner + b].astype(F32)
        for k in range(inner - 1):
            second = second + r_in_b[i, k].astype(F32)
        ready[i, 0:piece] = first.astype(BF16)
        ready[i, piece : 2 * piece] = second.astype(BF16)
        if i < outer - 1:
            out.append(send(ready.at[i], r_out.at[i], sem_out, (i,), out_peers[i]))
        if i == 0:
            total = gathered(2, groups)
            moves = share(3, a, total, out_peers)
    total = ready[outer - 1].astype(F32)
    for i in range(outer - 1):
        out[i].wait_recv()
        total = total + r_out[i].astype(F32)
    final[d] = total.astype(BF16)
    last = [send(final.at[d], final.at[d], sem_fin, (k,), p) for k, p in enumerate(dp_peers)]
    total = gathered(3, outer)
    scal_o[...] = total
    scale = 1.0 / total[1:2, 0:1]
    for m in last:
        m.wait_recv()
    pieces = [final[k, 0:piece] for k in range(groups)] + [final[k, piece : 2 * piece] for k in range(groups)]
    whole = jnp.concatenate(pieces, axis=0).astype(F32) * scale
    for s in range(slots):
        slot_o[s] = whole[s * LANES : (s + 1) * LANES]
    vec_o[...] = whole[slots * LANES : slots * LANES + vrows]
    for m in waits:
        m.wait_send()


def reduce_grads(inverse, present, grad, vec, scal, slots, groups, shards):
    outer, inner = split_shard(shards)
    vrows = vec.shape[0] // shards
    tails = jnp.pad(vec.reshape(shards, vrows, WIDTH), ((0, 0), (0, TILE - vrows), (0, 0)))
    rows = chunk_rows(slots, groups)
    half = rows // 2
    piece = half // groups
    f = jax.ShapeDtypeStruct
    vm = pl.BlockSpec(memory_space=pltpu.VMEM)
    sm = pl.BlockSpec(memory_space=pltpu.SMEM)
    both = outer * inner

    def buf(*shape):
        return pltpu.VMEM(shape + (WIDTH,), BF16)

    dma = pltpu.SemaphoreType.DMA
    peers_in, peers_dp = max(inner - 1, 1), max(groups - 1, 1)
    return pl.pallas_call(
        functools.partial(reduce_kernel, groups, outer, inner, slots, vrows),
        out_shape=[f((slots, LANES, WIDTH), F32), f((vrows, WIDTH), F32), f((8, LANES), F32)],
        in_specs=[sm, sm, vm, vm, vm],
        out_specs=[vm] * 3,
        scratch_shapes=[
            buf(both, rows), buf(both, rows), buf(both, rows),
            buf(outer, peers_in, half), buf(outer, half), buf(outer, peers_dp, piece),
            buf(outer, inner, peers_dp, piece), buf(both, piece), buf(outer, peers_in, piece),
            buf(outer, 2 * piece), buf(outer - 1, 2 * piece), buf(groups, 2 * piece),
            pltpu.VMEM((4, 4, 8, LANES), F32),
            dma((2, both)), dma((2, outer, peers_in)), dma((2, outer, peers_dp)), dma((2, outer, inner, peers_dp)),
            dma((2, outer, peers_in)), dma((2, outer - 1)), dma((2, peers_dp)), dma((2, 4, 3)),
        ],
        compiler_params=pltpu.CompilerParams(collective_id=1, has_side_effects=True, vmem_limit_bytes=56 * 2**20),
        name="reduce",
    )(inverse, present, grad, tails, scal)


def soap_kernel(shards, slots, owners, scal, g, gvec, m, v, ls, rs, lb, rb, mat, ema, vw, vf, vs, ve,
                scal_o, mat_o, ema_o, m_o, v_o, ls_o, rs_o, lb_o, rb_o, vw_o, vf_o, vs_o, ve_o,
                zl, zr, turn, sent, got, back, norms, sem_n, sem_u):
    d = lax.axis_index("dp")
    me = lax.axis_index("shard")
    peers = [(d, lax.rem(me + i, shards)) for i in range(1, shards)]
    greet(peers)
    piece = mat.shape[1]

    def send(src, dst, sems, index, peer):
        copy = pltpu.make_async_remote_copy(
            src_ref=src, dst_ref=dst, send_sem=sems.at[0, index], recv_sem=sems.at[1, index],
            device_id=peer, device_id_type=MESH)
        copy.start()
        return copy

    square = jnp.sum(gvec[...] * gvec[...])
    for s in range(slots):
        square = square + jnp.sum(g[s] * g[s])
    norms[me] = jnp.full((8, LANES), square, F32)
    moves = [send(norms.at[me], norms.at[me], sem_n, k, p) for k, p in enumerate(peers)]
    for s in range(slots):
        left, right = lb[s], rb[s]
        turn[s] = mm(mm(left, g[s], 0, 0), right)
        v_o[s] = mm(mm(left, m[s], 0, 0), right)
    for move in moves:
        move.wait_recv()
    total = norms[0]
    for k in range(1, shards):
        total = total + norms[k]
    norm = jnp.sqrt(total)
    factor = jnp.minimum(1.0, CLIP / (norm + 1e-06))
    rowid = lax.broadcasted_iota(jnp.int32, (8, LANES), 0)
    scal_o[...] = jnp.where(rowid == 2, norm, scal[...])
    scale = factor[0:1, 0:1]
    for s in range(slots):
        turned = turn[s] * scale
        moment = BETA_ONE * v_o[s] + (1.0 - BETA_ONE) * turned
        second = BETA_TWO * v[s] + (1.0 - BETA_TWO) * turned * turned
        v_o[s] = second
        normed = moment / (1.0 - BETA_ONE**STEP) / (jnp.sqrt(second / (1.0 - BETA_TWO**STEP)) + ADAM_EPS)
        turn[s] = mm(mm(lb[s], normed), rb[s], 1, 1)
    used = slots * piece
    full = sent.shape[1]
    for t in range(shards):
        parts = [turn[s, t * piece : (t + 1) * piece, :] for s in range(slots)]
        if full > used:
            parts.append(jnp.zeros((full - used, WIDTH), F32))
        sent[t] = jnp.concatenate(parts, axis=0).astype(BF16)
    got[me] = sent[me]
    moves = moves + [send(sent.at[p[1]], got.at[me], sem_u, k, p) for k, p in enumerate(peers)]
    for s in range(slots):
        grad = g[s] * scale
        left, right = lb[s], rb[s]
        m_o[s] = BETA_ONE * m[s] + (1.0 - BETA_ONE) * grad
        lnew = BETA_TWO * ls[s] + (1.0 - BETA_TWO) * mm(grad, grad, 1, 1)
        rnew = BETA_TWO * rs[s] + (1.0 - BETA_TWO) * mm(grad, grad, 0, 0)
        ls_o[s] = lnew
        rs_o[s] = rnew
        xl = mm(left, lnew, 0, 1)
        xr = mm(right, rnew, 0, 1)
        zl[s, :, :LANES] = mm(xl, xl, 1, 1)
        zl[s, :, LANES:] = xl
        zr[s, :, : 2 * LANES] = mm(xr, xr, 1, 1)
        zr[s, :, 2 * LANES :] = xr
    grad = gvec[...] * scale
    first = BETA_ONE * vf[...] + (1.0 - BETA_ONE) * grad
    second = BETA_TWO * vs[...] + (1.0 - BETA_TWO) * grad * grad
    step = first / (1.0 - BETA_ONE**STEP) / (jnp.sqrt(second / (1.0 - BETA_TWO**STEP)) + ADAM_EPS)
    new = vw[...] * (1.0 - TABLE_LEARN * DECAY) - TABLE_LEARN * step
    vf_o[...] = first
    vs_o[...] = second
    vw_o[...] = new
    ve_o[...] = EMA_RATE * ve[...] + (1.0 - EMA_RATE) * new
    lc = [(zl, s, LANES) for s in range(slots)]
    rc = [(zr, s, 2 * LANES) for s in range(slots)]

    def both(p, _):
        factor_panels(rc + lc, pl.multiple_of(p * PANEL, PANEL))
        return 0

    def only(p, _):
        factor_panels(rc, pl.multiple_of(p * PANEL, PANEL))
        return 0

    lax.fori_loop(0, LANES // PANEL, both, 0)
    lax.fori_loop(LANES // PANEL, 2 * LANES // PANEL, only, 0)
    for s in range(slots):
        lb_o[s] = zl[s, :, LANES:].T
        rb_o[s] = zr[s, :, 2 * LANES :].T
    for move in moves[shards - 1 :]:
        move.wait_recv()
    for t in range(shards):
        piece_t = got[t].astype(F32)
        for s in range(slots):
            back[t * slots + s] = piece_t[s * piece : (s + 1) * piece]
    for unit in range(UNITS):
        new = mat[unit] * (1.0 - LEARN * DECAY) - LEARN * back[owners[unit]]
        mat_o[unit] = new
        ema_o[unit] = EMA_RATE * ema[unit] + (1.0 - EMA_RATE) * new
    for move in moves:
        move.wait_send()


def soap(owners, scal, g, gvec, m, v, ls, rs, lb, rb, mat, ema, vw, vf, vs, ve, shards):
    slots, piece = g.shape[0], mat.shape[1]
    full = -(-slots * piece // TILE) * TILE
    f = jax.ShapeDtypeStruct
    vm = pl.BlockSpec(memory_space=pltpu.VMEM)
    outs = [f(x.shape, F32) for x in (scal, mat, ema, m, v, ls, rs, lb, rb, vw, vf, vs, ve)]
    dma = pltpu.SemaphoreType.DMA
    return pl.pallas_call(
        functools.partial(soap_kernel, shards, slots),
        out_shape=outs,
        in_specs=[pl.BlockSpec(memory_space=pltpu.SMEM)] + [vm] * 15,
        out_specs=[vm] * 13,
        scratch_shapes=[
            pltpu.VMEM((slots, LANES, 2 * LANES), F32),
            pltpu.VMEM((slots, 2 * LANES, 4 * LANES), F32),
            pltpu.VMEM((slots, LANES, WIDTH), F32),
            pltpu.VMEM((shards, full, WIDTH), BF16),
            pltpu.VMEM((shards, full, WIDTH), BF16),
            pltpu.VMEM((shards * slots, piece, WIDTH), F32),
            pltpu.VMEM((shards, 8, LANES), F32),
            dma((2, shards - 1)),
            dma((2, shards - 1)),
        ],
        compiler_params=pltpu.CompilerParams(collective_id=2, has_side_effects=True, vmem_limit_bytes=58 * 2**20),
        name="soap",
    )(owners, scal, g, gvec, m, v, ls, rs, lb, rb, mat, ema, vw, vf, vs, ve)


def time_table():
    steps = np.arange(32, dtype=np.float32)
    halfway = TDIM // 2
    freqs = np.exp(-math.log(10000.0) * np.arange(halfway, dtype=np.float32) / (halfway - 1)).astype(np.float32)
    angles = (freqs[:, None] * steps[None, :]).astype(np.float32)
    offset = 0.008
    ratio = (steps + 1.0) / DSTEPS
    upper = np.cos((ratio + offset) / (1.0 + offset) * math.pi / 2) ** 2
    level = upper / math.cos(offset / (1.0 + offset) * math.pi / 2) ** 2
    level = np.clip(np.where(steps < DSTEPS, level, 0.0), 0.0, 1.0)
    levels = np.stack([np.sqrt(level), np.sqrt(1.0 - level)] + [np.zeros(32)] * 6)
    return np.concatenate([np.sin(angles), np.cos(angles), levels]).astype(np.float32)


def dot(a, b, ca=1, cb=0):
    return lax.dot_general(a, b, (((ca,), (cb,)), ((), ())), preferred_element_type=F32)


def mish_parts(v):
    e = jnp.exp(jnp.minimum(v, 20.0))
    n = e * (e + 2.0)
    r = pl.reciprocal(n + 2.0)
    return e, r, n * r


def mish_slope(v, e, r, t):
    return t + v * (4.0 * e * (e + 1.0)) * (r * r)


def gather_parts():
    taps = 2 * KERNEL
    bounds = [3, 3 + taps, UNITS + 3 - (OWNED - 1) * taps]
    while bounds[-1] < UNITS + 3:
        bounds.append(bounds[-1] + taps)
    return [(0, bounds[1])] + list(zip(bounds[1:-1], bounds[2:]))


def net_kernel(trajs, frames, groups, outer, inner, traj, noise, steps, valid, times, gmat, mat, vec, mat_o, vec_o, loss_o,
               other, other_vec, mb, xin, xhat, h, skip, d, dskip, dy, dp, low, xt, s_one, s_two, mean, rstd, xsum, q_one, q_two,
               g_one, g_two, tb, dtb, noisy_t, noise_t, mask_t, dpl, acc, table, sem_c, sem_z, sem_y, sem_s, sem_t):
    dpi = lax.axis_index("dp")
    a, b, c = place(outer, inner)
    piece = mat.shape[1]
    chunks = trajs // TILE
    rows_c = TILE * frames
    rows = trajs * frames
    taps = 2 * KERNEL
    part = 1.0 / (frames * (WIDTH // GROUPS))
    group = gmat[...]
    core_peer = (dpi, spot(inner, a, b, 1 - c))
    in_peers = [(dpi, spot(inner, a, lax.rem(b + i, inner), c)) for i in range(1, inner)]
    out_peers = [(dpi, spot(inner, lax.rem(a + i, outer), b, c)) for i in range(1, outer)]
    greet([core_peer] + in_peers + out_peers)
    waits = []

    def send(src, dst, sems, index, peer):
        copy = pltpu.make_async_remote_copy(
            src_ref=src, dst_ref=dst, send_sem=sems.at[(0,) + index], recv_sem=sems.at[(1,) + index],
            device_id=peer, device_id_type=MESH)
        copy.start()
        waits.append(copy)
        return copy

    spans = [(0, taps), (taps * OWNED, UNITS), (taps, taps * OWNED)]
    first_copies = [send(vec, other_vec, sem_c, (3,), core_peer)]
    for k, (lo, hi) in enumerate(spans):
        first_copies.append(send(mat.at[pl.ds(lo, hi - lo)], other.at[pl.ds(lo, hi - lo)], sem_c, (k,), core_peer))
    parts = gather_parts()
    start_of = [3 if l == 0 else parts[l + 1][0] for l in range(OWNED)]
    time_at = parts[1][0]
    source = {0: 0, 1: taps * OWNED}
    for g in range(2, len(parts)):
        source[g] = taps * (g - 1)
    cols = pl.ds(pl.multiple_of(c * LANES, LANES), LANES)
    state = {}

    def chip_rows(mine, theirs):
        mine_first = jnp.where(c == 0, mine, theirs)
        then = jnp.where(c == 0, theirs, mine)
        return jnp.concatenate([mine_first, then], axis=mine.ndim - 2)

    def build(g):
        lo, hi = parts[g]
        count = hi - lo
        if g == 0:
            count -= 3
            first_copies[0].wait_recv()
            first_copies[1].wait_recv()
            rows_v = chip_rows(vec[...], other_vec[...])
            one, two, three = split3(rows_v)
            mb[0, a, b] = one.astype(mb.dtype)
            mb[1, a, b] = two.astype(mb.dtype)
            mb[2, a, b] = three.astype(mb.dtype)
        elif g == 1:
            first_copies[2].wait_recv()
        elif g == 2:
            first_copies[3].wait_recv()
        at = source[g]
        mb[hi - count : hi, a, b] = chip_rows(mat[at : at + count], other[at : at + count]).astype(BF16).astype(mb.dtype)
        region = mb.at[pl.ds(lo, hi - lo), a, b, :, cols]
        state[g] = [send(region, region, sem_z, (g, k), p) for k, p in enumerate(out_peers)]

    def along(g):
        lo, hi = parts[g]
        for copy in state[g]:
            copy.wait_recv()
        region = mb.at[pl.ds(lo, hi - lo), :, b, :, cols]
        nexts = [send(region, region, sem_y, (g, k), p) for k, p in enumerate(in_peers)]
        sib = []
        for i in range(1, outer):
            region = mb.at[pl.ds(lo, hi - lo), lax.rem(a + i, outer), b, :, cols]
            sib.append(send(region, region, sem_s, (g, i - 1), core_peer))
        state[g] = (nexts, sib)

    def across(g):
        lo, hi = parts[g]
        nexts, sib = state[g]
        for copy in nexts:
            copy.wait_recv()
        for i in range(1, inner):
            region = mb.at[pl.ds(lo, hi - lo), :, lax.rem(b + i, inner), :, cols]
            sib.append(send(region, region, sem_t, (g, i - 1), core_peer))
        state[g] = sib

    def whole(g):
        for copy in state[g]:
            copy.wait_recv()

    def chunk_of(n):
        return pl.ds(pl.multiple_of(n * TILE, TILE), TILE)

    def flat(v):
        return v.reshape(rows_c, WIDTH)

    def wide(v):
        return v.reshape(frames, TILE, WIDTH)

    def row(index):
        return table[index : index + 1, :]

    def gain(l):
        return row(BASE + 3 + OWNED + l), row(BASE + 3 + 2 * OWNED + l)

    def tap(l, k):
        at = start_of[l] + 2 * k
        return mb[at : at + 2].reshape(WIDTH, WIDTH).astype(BF16)

    def lin(j):
        at = time_at + 2 * j
        return mb[at : at + 2].reshape(WIDTH, WIDTH).astype(BF16)

    def group_sum(v):
        return lax.dot_general(v, group, (((1,), (0,)), ((), ())), precision=HIGH, preferred_element_type=F32)

    def loop(body):
        def step(n, carry):
            body(n)
            return carry

        lax.fori_loop(0, chunks, step, 0)

    def pass_one(l, n, x):
        at = chunk_of(n)
        xin[l, KERNEL // 2 : KERNEL // 2 + frames, at, :] = wide(x).astype(BF16)
        p = None
        for k in range(KERNEL):
            term = dot(flat(xin[l, k : k + frames, at, :]), tap(l, k))
            p = term if p is None else p + term
        p = wide(p + row(BASE + 3 + l))
        xhat[l, :, at, :] = p
        total = jnp.sum(p, axis=0)
        s_one[at, :] = total
        off = p - (total * (1.0 / frames))[None]
        s_two[at, :] = jnp.sum(off * off, axis=0)

    def stats(l):
        total = s_one[...]
        centre = group_sum(total) * part
        off = total * (1.0 / frames) - centre
        var = group_sum(s_two[...] + frames * off * off) * part
        scale = lax.rsqrt(var + NORM_EPS)
        mean[...] = centre
        rstd[l] = scale
        xsum[l] = frames * off * scale

    def normed(l, n):
        at = chunk_of(n)
        x = (xhat[l, :, at, :] - mean[at, :][None]) * rstd[l, at, :][None]
        xhat[l, :, at, :] = x
        g, s = gain(l)
        return x, x * g + s

    def pass_a(n, dm, x, v, pieces):
        at = chunk_of(n)
        slope = dm * mish_slope(v, *pieces)
        dy[:, at, :] = slope
        q_one[at, :] = jnp.sum(slope, axis=0)
        q_two[at, :] = jnp.sum(slope * x, axis=0)

    def pass_a_load(l, n, dm):
        x = xhat[l, :, chunk_of(n), :]
        g, s = gain(l)
        v = x * g + s
        pass_a(n, dm, x, v, mish_parts(v))

    def stats_back(l):
        g, s = gain(l)
        one, two = q_one[...], q_two[...]
        vec_o[BASE + 3 + OWNED + l : BASE + 4 + OWNED + l, :] = jnp.sum(two, axis=0, keepdims=True)
        vec_o[BASE + 3 + 2 * OWNED + l : BASE + 4 + 2 * OWNED + l, :] = jnp.sum(one, axis=0, keepdims=True)
        sums = group_sum(jnp.concatenate([one * g, two * g], axis=0)) * part
        first, second = sums[:trajs], sums[trajs:]
        g_one[...] = first
        g_two[...] = second
        dc = rstd[l] * (one * g - frames * first - xsum[l] * second)
        vec_o[BASE + 3 + l : BASE + 4 + l, :] = jnp.sum(dc, axis=0, keepdims=True)

    build(0)
    build(1)
    build(2)
    vec_o[...] = jnp.zeros_like(vec_o)
    edge = jnp.zeros((OWNED, KERNEL // 2, trajs, WIDTH), BF16)
    xin[:, : KERNEL // 2] = edge
    xin[:, KERNEL // 2 + frames :] = edge
    dp[: KERNEL // 2] = edge[0]
    dp[KERNEL // 2 + frames :] = edge[0]
    acc[...] = jnp.zeros_like(acc)
    stepid = lax.broadcasted_iota(jnp.int32, (32, trajs), 0)
    picked = mm(times[...], (stepid == steps[...]).astype(F32))
    emb = picked[:TDIM].astype(BF16)
    keep, add = picked[TDIM : TDIM + 1], picked[TDIM + 1 : TDIM + 2]
    for f in range(frames):
        at = slice(f * trajs, (f + 1) * trajs)
        raw = noise[:, f, :]
        noise_t[:, at] = raw
        noisy_t[:, at] = (keep * traj[:, f, :] + add * raw).astype(BF16)
        mask_t[:, at] = valid[f : f + 1, :].astype(F32)
    along(0)
    build(3)
    along(1)
    across(0)
    along(2)
    build(4)
    across(1)
    whole(0)
    full = [mb[k].reshape(VROWS, WIDTH).astype(F32) for k in range(3)]
    table[...] = (full[0] + full[1]) + full[2]
    low[...] = full[0].astype(BF16)
    w_in, w_head = low[:FEAT, :], low[FEAT : 2 * FEAT, :]
    h[...] = (dot(noisy_t[...], w_in, 0, 0) + row(BASE)).reshape(frames, trajs, WIDTH)

    def enter(n):
        pass_one(0, n, flat(h[:, chunk_of(n), :]))

    loop(enter)
    along(3)
    build(5)
    across(2)
    whole(1)
    pre_time = dot(emb, mb[time_at + 2 * BLOCKS].reshape(TDIM, WIDTH).astype(BF16), 0, 0) + row(BASE + 1)
    time_parts = mish_parts(pre_time)
    temb = (pre_time * time_parts[2]).astype(BF16)
    time_slope = mish_slope(pre_time, *time_parts)
    for j in range(BLOCKS):
        tb[j] = dot(temb, lin(j)) + row(BASE + 3 + 3 * OWNED + j)
    moves = {0: [(along, 4), (build, 6), (across, 3), (whole, 2)], 1: [(along, 5), (across, 4), (whole, 3)],
             2: [(along, 6), (across, 5), (whole, 4)], 3: [(across, 6), (whole, 5)], 4: [(whole, 6)]}
    for l in range(OWNED - 1):
        stats(l)
        for act, g in moves[l]:
            act(g)

        def forward(n, l=l):
            at = chunk_of(n)
            _, v = normed(l, n)
            m = v * mish_parts(v)[2]
            if l % 2 == 0:
                m = m + tb[l // 2, at, :][None]
            else:
                m = h[:, at, :] + m
                if l == 1:
                    skip[:, at, :] = m
                if l == 2 * BLOCKS - 3:
                    m = m + skip[:, at, :]
                h[:, at, :] = m
            pass_one(l + 1, n, flat(m))

        loop(forward)
    stats(OWNED - 1)
    head_bias = table[BASE + 2 : BASE + 3, :]

    def settle(n):
        at = chunk_of(n)
        _, v = normed(OWNED - 1, n)
        dp[KERNEL // 2 : KERNEL // 2 + frames, at, :] = (h[:, at, :] + v * mish_parts(v)[2]).astype(BF16)

    loop(settle)
    top = dp[KERNEL // 2 : KERNEL // 2 + frames].reshape(rows, WIDTH)
    pick = lax.broadcasted_iota(jnp.int32, (FEAT, WIDTH), 0) == lax.broadcasted_iota(jnp.int32, (FEAT, WIDTH), 1)
    bias = jnp.sum(jnp.where(pick, head_bias, 0.0), axis=1, keepdims=True)
    err = dot(w_head, top, 1, 1) + bias - noise_t[...]
    weighted = mask_t[...] * err
    loss = jnp.sum(jnp.sum(weighted * err, axis=0, keepdims=True), axis=1, keepdims=True)
    count = FEAT * jnp.sum(mask_t[...], axis=1, keepdims=True)
    rowid = lax.broadcasted_iota(jnp.int32, (8, LANES), 0)
    loss_o[...] = jnp.where(rowid == 0, loss, jnp.where(rowid == 1, count, 0.0))
    grad = 2.0 * weighted
    g_bias = jnp.sum(grad, axis=1, keepdims=True)
    vec_o[BASE + 2 : BASE + 3, :] = jnp.sum(jnp.where(pick, g_bias, 0.0), axis=0, keepdims=True)
    dpl[...] = grad.astype(BF16)
    vec_o[FEAT : 2 * FEAT, :] = dot(dpl[...], top)
    d[...] = dot(dpl[...], w_head, 0, 0).reshape(frames, trajs, WIDTH)

    def turn(n):
        pass_a_load(OWNED - 1, n, d[:, chunk_of(n), :])

    loop(turn)
    for l in reversed(range(OWNED)):
        stats_back(l)

        def backward(n, l=l):
            g, s = gain(l)
            at = chunk_of(n)
            x = xhat[l, :, at, :]
            back = rstd[l, at, :][None] * (dy[:, at, :] * g - g_one[at, :][None] - x * g_two[at, :][None])
            dp[KERNEL // 2 : KERNEL // 2 + frames, at, :] = back.astype(BF16)
            dx = None
            for k in range(KERNEL):
                shift = KERNEL - 1 - k
                term = dot(flat(dp[shift : shift + frames, at, :]), tap(l, k), 1, 1)
                dx = term if dx is None else dx + term
            dx = wide(dx)
            if l % 2 == 1:
                dtb[l // 2, at, :] = jnp.sum(dx, axis=0)
                pass_a_load(l - 1, n, dx)
            else:
                dx = d[:, at, :] + dx
                if l == OWNED - 2:
                    dskip[:, at, :] = dx
                if l == 2:
                    dx = dx + dskip[:, at, :]
                d[:, at, :] = dx
                if l > 0:
                    pass_a_load(l - 1, n, dx)

        loop(backward)
        xt[...] = xin[l, KERNEL // 2 : KERNEL // 2 + frames].reshape(rows, WIDTH).T
        for k in range(KERNEL):
            shift = KERNEL - 1 - k
            w_grad = dot(xt[...], dp[shift : shift + frames].reshape(rows, WIDTH))
            for half in range(2):
                mat_o[taps * l + 2 * k + half] = w_grad[half * LANES : (half + 1) * LANES].astype(mat_o.dtype)

    d_in = d[...].reshape(rows, WIDTH)
    vec_o[BASE : BASE + 1, :] = jnp.sum(d_in, axis=0, keepdims=True)
    vec_o[:FEAT, :] = dot(noisy_t[...], d_in.astype(BF16))
    d_temb = None
    for j in range(BLOCKS):
        grads = dtb[j]
        vec_o[BASE + 3 + 3 * OWNED + j : BASE + 4 + 3 * OWNED + j, :] = jnp.sum(grads, axis=0, keepdims=True)
        grads = grads.astype(BF16)
        t_grad = dot(temb, grads, 0, 0)
        for half in range(2):
            mat_o[taps * OWNED + 2 * j + half] = t_grad[half * LANES : (half + 1) * LANES].astype(mat_o.dtype)
        term = dot(grads, lin(j), 1, 1)
        d_temb = term if d_temb is None else d_temb + term
    d_pre = d_temb * time_slope
    vec_o[BASE + 1 : BASE + 2, :] = jnp.sum(d_pre, axis=0, keepdims=True)
    mat_o[UNITS - 1] = dot(emb, d_pre.astype(BF16)).astype(mat_o.dtype)
    for copy in waits:
        copy.wait_send()


def net(traj, noise, steps, valid, mat, vec, groups, shards):
    outer, inner = split_shard(shards)
    feats, frames, trajs = traj.shape
    rows = frames * trajs
    piece = mat.shape[1]
    lane = np.arange(WIDTH) // (WIDTH // GROUPS)
    gmat = jnp.asarray((lane[:, None] == lane[None, :]).astype(np.float32))
    times = jnp.asarray(time_table())
    wire = BF16 if (2 * piece) % TILE == 0 else F32
    vm = pl.BlockSpec(memory_space=pltpu.VMEM)
    f = jax.ShapeDtypeStruct
    big = pltpu.VMEM((frames, trajs, WIDTH), F32)
    small = pltpu.VMEM((trajs, WIDTH), F32)
    padded = frames + KERNEL - 1
    dma = pltpu.SemaphoreType.DMA
    count = len(gather_parts())
    return pl.pallas_call(
        functools.partial(net_kernel, trajs, frames, groups, outer, inner),
        out_shape=[f((UNITS, LANES, WIDTH), BF16), f((VROWS, WIDTH), F32), f((8, LANES), F32)],
        in_specs=[vm] * 8,
        out_specs=[vm] * 3,
        scratch_shapes=[
            pltpu.VMEM((UNITS, piece, WIDTH), F32),
            pltpu.VMEM((piece, WIDTH), F32),
            pltpu.VMEM((UNITS + 3, outer, inner, 2 * piece, WIDTH), wire),
            pltpu.VMEM((OWNED, padded, trajs, WIDTH), BF16),
            pltpu.VMEM((OWNED, frames, trajs, WIDTH), F32),
            big, big, big, big, big,
            pltpu.VMEM((padded, trajs, WIDTH), BF16),
            pltpu.VMEM((VROWS, WIDTH), BF16),
            pltpu.VMEM((WIDTH, rows), BF16),
            small, small, small,
            pltpu.VMEM((OWNED, trajs, WIDTH), F32),
            pltpu.VMEM((OWNED, trajs, WIDTH), F32),
            small, small, small, small,
            pltpu.VMEM((BLOCKS, trajs, WIDTH), F32),
            pltpu.VMEM((BLOCKS, trajs, WIDTH), F32),
            pltpu.VMEM((feats, rows), BF16),
            pltpu.VMEM((feats, rows), F32),
            pltpu.VMEM((1, rows), F32),
            pltpu.VMEM((feats, rows), BF16),
            pltpu.VMEM((16, WIDTH), F32),
            pltpu.VMEM((VROWS, WIDTH), F32),
            dma((2, 4)), dma((2, count, outer - 1)), dma((2, count, max(inner - 1, 1))),
            dma((2, count, outer - 1)), dma((2, count, max(inner - 1, 1))),
        ],
        compiler_params=pltpu.CompilerParams(collective_id=3, has_side_effects=True, vmem_limit_bytes=62 * 2**20),
        name="net",
    )(traj, noise, steps, valid, times, gmat, mat, vec)


def body(
    trajectories,
    noise,
    timesteps,
    valid,
    owners,
    mat_weight,
    mat_ema,
    soap_first,
    soap_second,
    left_stat,
    right_stat,
    left_basis,
    right_basis,
    vec_weight,
    vec_first,
    vec_second,
    vec_ema,
):
    shards = lax.axis_size("shard")
    groups = lax.axis_size("dp")
    slots = soap_first.shape[0]
    mat_grad, vec_grad, scal = net(
        trajectories.transpose(2, 1, 0),
        noise.transpose(2, 1, 0),
        timesteps.reshape(1, -1),
        valid.T,
        mat_weight,
        vec_weight,
        groups,
        shards,
    )
    choose = owners[None, :] == jnp.arange(shards * slots, dtype=jnp.int32)[:, None]
    order = jnp.arange(UNITS, dtype=jnp.int32)[None, :]
    inverse = jnp.sum(jnp.where(choose, order, 0), axis=1, dtype=jnp.int32)
    present = jnp.any(choose, axis=1).astype(F32)
    grads, grads_vec, scal = reduce_grads(inverse, present, mat_grad, vec_grad, scal, slots, groups, shards)
    results = soap(
        owners, scal, grads, grads_vec, soap_first, soap_second, left_stat, right_stat, left_basis, right_basis,
        mat_weight, mat_ema, vec_weight, vec_first, vec_second, vec_ema, shards,
    )
    scal = results[0]
    return (scal[0, 0], scal[1, 0], scal[2, 0]) + tuple(results[1:])


def solution(mesh):
    placed = (
        P(("dp", "shard"), None, None),
        P(("dp", "shard"), None, None),
        P(("dp", "shard")),
        P(("dp", "shard"), None),
        P(),
        P(None, "shard", None),
        P(None, "shard", None),
        P("shard", None, None),
        P("shard", None, None),
        P("shard", None, None),
        P("shard", None, None),
        P("shard", None, None),
        P("shard", None, None),
        P("shard", None),
        P("shard", None),
        P("shard", None),
        P("shard", None),
    )
    return jax.shard_map(
        body,
        mesh=mesh,
        in_specs=placed,
        out_specs=(
            P(),
            P(),
            P(),
            P(None, "shard", None),
            P(None, "shard", None),
            P("shard", None, None),
            P("shard", None, None),
            P("shard", None, None),
            P("shard", None, None),
            P("shard", None, None),
            P("shard", None, None),
            P("shard", None),
            P("shard", None),
            P("shard", None),
            P("shard", None),
        ),
        check_vma=False,
    )
```

```python
import functools
import math

import jax
import jax.numpy as jnp
import numpy as np
from jax import lax
from jax.experimental import pallas as pl
from jax.experimental.pallas import tpu as pltpu
from jax.sharding import PartitionSpec as P

WIDTH = 256
KERNEL = 5
GROUPS = 8
TDIM = 128
FEAT = 23
BLOCKS = 3
DSTEPS = 20
STEP = 10
OWNED = 6
UNITS = 67
VROWS = 128

HIGH = lax.Precision.HIGHEST
BETA_ONE = 0.9
BETA_TWO = 0.95
ADAM_EPS = 1e-08
LEARN = 0.05
TABLE_LEARN = 0.25
DECAY = 0.01
CLIP = 0.05
EMA_RATE = 0.8
NORM_EPS = 1e-05
PANEL = 32
LANES = 128
PAD = 8
CHUNK = 8
TILE = 16
BASE = 2 * FEAT
F32 = jnp.float32
BF16 = jnp.bfloat16
MESH = pl.DeviceIdType.MESH


def mm(a, b, ca=1, cb=0):
    return lax.dot_general(a, b, (((ca,), (cb,)), ((), ())), precision=HIGH, preferred_element_type=F32)

def mm3(a, b, ca=1, cb=0):
    ah = a.astype(BF16)
    al = (a - ah.astype(F32)).astype(BF16)
    bh = b.astype(BF16)
    bl = (b - bh.astype(F32)).astype(BF16)
    d = (((ca,), (cb,)), ((), ()))

    def product(p, q):
        return lax.dot_general(p, q, d, preferred_element_type=F32)

    return product(ah, bh) + (product(ah, bl) + product(al, bh))


def split3(v):
    hi = v.astype(BF16)
    rest = v - hi.astype(F32)
    mid = rest.astype(BF16)
    last = (rest - mid.astype(F32)).astype(BF16)
    return hi, mid, last

def eliminate(held):
    lanes = lax.broadcasted_iota(jnp.int32, (8, LANES), 1)
    sub = lax.broadcasted_iota(jnp.int32, (8, LANES), 0)
    tall = PANEL // 8

    def lane(v, k):
        return jnp.broadcast_to(v[:, k : k + 1], (8, LANES))

    for k in range(0, PANEL, 2):
        top, r = k // 8, k % 8
        for e in held:
            first = jnp.broadcast_to(e[top][r : r + 1, :], (8, LANES))
            second = jnp.broadcast_to(e[top][r + 1 : r + 2, :], (8, LANES))
            corner = lane(first, k + 1)
            one = pl.reciprocal(lane(first, k))
            ratio = corner * one
            two = pl.reciprocal(lane(second, k + 1) - corner * ratio)
            second = second - ratio * first
            by_first = first * one
            by_second = second * two
            for v in range(top, tall):
                left = lane(e[v], k)
                right = lane(e[v], k + 1) - left * ratio
                less = e[v] - left * by_first - right * by_second
                if v == top:
                    less = jnp.where(sub > r + 1, less, jnp.where(sub == r + 1, second, e[v]))
                e[v] = less
    results = []
    for e in held:
        parts = []
        for v in range(tall):
            pivots = jnp.sum(jnp.where(lanes == sub + 8 * v, e[v], 0.0), axis=1, keepdims=True)
            parts.append(e[v] * lax.rsqrt(pivots))
        results.append(jnp.concatenate(parts, axis=0)[:, PANEL : 2 * PANEL])
    return results


def factor_panels(chains, start):
    rows = lax.broadcasted_iota(jnp.int32, (PANEL, LANES), 0)
    lanes = lax.broadcasted_iota(jnp.int32, (PANEL, LANES), 1)
    unit = jnp.where(lanes - PANEL == rows, 1.0, 0.0).astype(F32)
    shift = lax.rem(LANES - start, LANES)
    at = pl.ds(start, PANEL)
    held = []
    for z, out, s in chains:
        block = jnp.where(lanes < PANEL, pltpu.roll(z[s, at, :LANES], shift, 1), unit)
        held.append([block[8 * v : 8 * v + 8] for v in range(PANEL // 8)])
    panels = [mm(inverse, z[s, at, :]) for (z, out, s), inverse in zip(chains, eliminate(held))]
    for (z, out, s), done in zip(chains, panels):
        out[s, at, :] = done[:, LANES:]
    for (z, out, s), done in zip(chains, panels):
        hi, mid, last = split3(done)
        lhs = jnp.concatenate([hi, hi, mid, hi, last, mid], axis=0)[:, :LANES]
        rhs = jnp.concatenate([hi, mid, hi, last, hi, mid], axis=0)
        z[s] = z[s] - lax.dot_general(lhs, rhs, (((0,), (0,)), ((), ())), preferred_element_type=F32)


def factor_all(chains):
    def step(p, carry):
        factor_panels(chains, pl.multiple_of(p * PANEL, PANEL))
        return carry

    lax.fori_loop(0, LANES // PANEL, step, 0)


def split_shard(shards):
    return 4, shards // 8


def place(outer, inner):
    s = lax.axis_index("shard")
    return s // (2 * inner), lax.rem(s // 2, inner), lax.rem(s, 2)


def spot(inner, a, b, c):
    return (a * inner + b) * 2 + c


def greet(peers):
    barrier = pltpu.get_barrier_semaphore()
    for peer in peers:
        pl.semaphore_signal(barrier, inc=1, device_id=peer, device_id_type=MESH)
    pl.semaphore_wait(barrier, len(peers))


def reduce_kernel(groups, outer, inner, slots, shards, inverse, grad, vec, scal, m, v, ls, rs, lb, rb,
                  grad_o, vec_o, scal_o, second_o, lnew_o, rnew_o, xl_o, xr_o, back_o,
                  s_core, r_core, held, r_in_a, sum_a, r_dp_a, r_dp_b, sum_b, r_in_b, ready, r_out, final, sc, turn, norms, sent, got,
                  w_core, w_in, w_dp, w_out, w_sum,
                  sem_core, sem_in_a, sem_dp_a, sem_dp_b, sem_in_b, sem_out, sem_fin, sem_sc, sem_n, sem_u):
    d = lax.axis_index("dp")
    a, b, c = place(outer, inner)
    me = lax.axis_index("shard")
    rows = slots * LANES
    half = rows // 2
    piece = half // groups
    core_peer = (d, spot(inner, a, b, 1 - c))
    in_peers = [(d, spot(inner, a, lax.rem(b + i, inner), c)) for i in range(1, inner)]
    dp_peers = [(lax.rem(d + i, groups), me) for i in range(1, groups)]
    out_peers = [(d, spot(inner, lax.rem(a + i, outer), b, c)) for i in range(1, outer)]
    peers = [(d, lax.rem(me + i, shards)) for i in range(1, shards)]
    greet(peers + dp_peers)
    waits = []

    def send(src, dst, sems, index, peer):
        copy = pltpu.make_async_remote_copy(
            src_ref=src, dst_ref=dst, send_sem=sems.at[(0,) + index], recv_sem=sems.at[(1,) + index],
            device_id=peer, device_id_type=MESH)
        copy.start()
        waits.append(copy)
        return copy

    def load(aa, bb, cc):
        first = spot(inner, aa, bb, cc) * slots
        return jnp.concatenate([grad[inverse[first + s]] for s in range(slots)], axis=0)

    order = [lax.rem(a + i, outer) for i in range(1, outer + 1)]
    core_copies = {}

    def begin(i):
        for j in range(inner):
            at = i * inner + j
            s_core[at] = load(order[i], j, 1 - c)
            core_copies[at] = send(s_core.at[at], r_core.at[at], sem_core, (at,), core_peer)

    begin(0)
    sc[0, c] = scal[...]
    small = [send(sc.at[0, c], sc.at[0, c], sem_sc, (0, 0), core_peer),
             send(vec.at[:, :, 1 - c], w_core, sem_sc, (0, 3), core_peer)]
    begin(1)
    in_a, dp_b, dp_a, in_b, out = {}, {}, {}, {}, {}

    def first_hop(i):
        for j in range(inner):
            at = i * inner + j
            core_copies[at].wait_recv()
            held[at] = (load(order[i], j, c).astype(F32) + r_core[at].astype(F32)).astype(BF16)
        in_a[i] = [send(held.at[i * inner + lax.rem(b + k, inner), pl.ds(0, half)], r_in_a.at[i, k - 1], sem_in_a, (i, k - 1), in_peers[k - 1])
                   for k in range(1, inner)]
        dp_b[i] = [send(held.at[i * inner + j, pl.ds(pl.multiple_of(half + lax.rem(d + k, groups) * piece, TILE), piece)],
                        r_dp_b.at[i, j, k - 1], sem_dp_b, (i, j, k - 1), dp_peers[k - 1])
                   for k in range(1, groups) for j in range(inner)]

    def second_hop(i):
        for copy in in_a[i]:
            copy.wait_recv()
        total = held[i * inner + b, pl.ds(0, half)].astype(F32)
        for k in range(inner - 1):
            total = total + r_in_a[i, k].astype(F32)
        sum_a[i] = total.astype(BF16)
        dp_a[i] = [send(sum_a.at[i, pl.ds(pl.multiple_of(lax.rem(d + k, groups) * piece, TILE), piece)], r_dp_a.at[i, k - 1], sem_dp_a, (i, k - 1), dp_peers[k - 1])
                   for k in range(1, groups)]
        for copy in dp_b[i]:
            copy.wait_recv()
        for j in range(inner):
            total = held[i * inner + j, pl.ds(pl.multiple_of(half + d * piece, TILE), piece)].astype(F32)
            for k in range(groups - 1):
                total = total + r_dp_b[i, j, k].astype(F32)
            sum_b[i * inner + j] = total.astype(BF16)
        in_b[i] = [send(sum_b.at[i * inner + lax.rem(b + k, inner)], r_in_b.at[i, k - 1], sem_in_b, (i, k - 1), in_peers[k - 1])
                   for k in range(1, inner)]

    def third_hop(i):
        for copy in dp_a[i] + in_b[i]:
            copy.wait_recv()
        first = sum_a[i, pl.ds(pl.multiple_of(d * piece, TILE), piece)].astype(F32)
        for k in range(groups - 1):
            first = first + r_dp_a[i, k].astype(F32)
        second = sum_b[i * inner + b].astype(F32)
        for k in range(inner - 1):
            second = second + r_in_b[i, k].astype(F32)
        ready[i, 0:piece] = first.astype(BF16)
        ready[i, piece : 2 * piece] = second.astype(BF16)
        if i < outer - 1:
            out[i] = send(ready.at[i], r_out.at[i], sem_out, (i,), out_peers[i])

    def gathered(level, count):
        for copy in small:
            copy.wait_recv()
        total = sc[level, 0]
        for k in range(1, count):
            total = total + sc[level, k]
        return total

    first_hop(0)
    if outer > 2:
        begin(2)
    first_hop(1)
    total = gathered(0, 2)
    sc[1, b] = total
    w_sum[0] = vec[:, :, c] + w_core[...]
    small = [send(sc.at[1, b], sc.at[1, b], sem_sc, (1, k), p) for k, p in enumerate(in_peers)]
    small += [send(w_sum.at[0, :, lax.rem(b + k, inner)], w_in.at[k - 1], sem_sc, (1, 2 + k), in_peers[k - 1]) for k in range(1, inner)]
    second_hop(0)
    for i in range(2, outer):
        if i + 1 < outer:
            begin(i + 1)
        first_hop(i)
        second_hop(i - 1)
        third_hop(i - 2)
    total = gathered(1, inner)
    sc[2, d] = total
    summed = w_sum[0, :, b]
    for k in range(inner - 1):
        summed = summed + w_in[k]
    w_dp[d] = summed
    small = [send(sc.at[2, d], sc.at[2, d], sem_sc, (2, k), p) for k, p in enumerate(dp_peers)]
    small += [send(w_dp.at[d], w_dp.at[d], sem_sc, (2, 3 + k), p) for k, p in enumerate(dp_peers)]
    second_hop(outer - 1)
    third_hop(outer - 2)
    for s in range(slots):
        second_o[s] = mm3(mm3(lb[s], m[s], 0, 0), rb[s])
    total = gathered(2, groups)
    sc[3, a] = total
    summed = w_dp[0]
    for k in range(1, groups):
        summed = summed + w_dp[k]
    w_sum[1, :, 0] = summed
    small = [send(sc.at[3, a], sc.at[3, a], sem_sc, (3, k), p) for k, p in enumerate(out_peers)]
    small += [send(w_sum.at[1, lax.rem(a + k, outer), 0], w_out.at[k - 1], sem_sc, (3, 2 + k), out_peers[k - 1]) for k in range(1, outer)]
    third_hop(outer - 1)
    total = ready[outer - 1].astype(F32)
    for i in range(outer - 1):
        out[i].wait_recv()
        total = total + r_out[i].astype(F32)
    final[d] = total.astype(BF16)
    last = [send(final.at[d], final.at[d], sem_fin, (k,), p) for k, p in enumerate(dp_peers)]
    counts = gathered(3, outer)
    scale = 1.0 / counts[1:2, 0:1]
    table = w_sum[1, a, 0]
    for k in range(outer - 1):
        table = table + w_out[k]
    table = table * scale
    for copy in last:
        copy.wait_recv()
    parts = [final[k, 0:piece] for k in range(groups)] + [final[k, piece : 2 * piece] for k in range(groups)]
    whole = jnp.concatenate(parts, axis=0).astype(F32) * scale
    squares = jnp.sum(table * table) + jnp.sum(whole * whole)
    norms[me] = jnp.full((8, LANES), squares, F32)
    moves = [send(norms.at[me], norms.at[me], sem_n, (k,), p) for k, p in enumerate(peers)]
    for s in range(slots):
        slot = whole[s * LANES : (s + 1) * LANES]
        grad_o[s] = slot
        turn[s] = mm3(mm3(lb[s], slot, 0, 0), rb[s])
    for copy in moves:
        copy.wait_recv()
    total = norms[0]
    for k in range(1, shards):
        total = total + norms[k]
    norm = jnp.sqrt(total)
    factor = jnp.minimum(1.0, CLIP / (norm + 1e-06))
    rowid = lax.broadcasted_iota(jnp.int32, (8, LANES), 0)
    scal_o[...] = jnp.where(rowid == 2, norm, counts)
    scale = factor[0:1, 0:1]
    vec_o[...] = table * scale
    for s in range(slots):
        turned = turn[s] * scale
        moment = BETA_ONE * second_o[s] + (1.0 - BETA_ONE) * turned
        second = BETA_TWO * v[s] + (1.0 - BETA_TWO) * turned * turned
        second_o[s] = second
        normed = moment / (1.0 - BETA_ONE**STEP) / (jnp.sqrt(second / (1.0 - BETA_TWO**STEP)) + ADAM_EPS)
        turn[s] = mm3(mm3(lb[s], normed), rb[s], 1, 1)
    width = back_o.shape[1]
    used = slots * width
    full = sent.shape[1]
    for t in range(shards):
        parts = [turn[s, t * width : (t + 1) * width, :] for s in range(slots)]
        if full > used:
            parts.append(jnp.zeros((full - used, WIDTH), F32))
        sent[t] = jnp.concatenate(parts, axis=0).astype(BF16)
    got[me] = sent[me]
    moves = [send(sent.at[p[1]], got.at[me], sem_u, (k,), p) for k, p in enumerate(peers)]
    for s in range(slots):
        slot = grad_o[s] * scale
        grad_o[s] = slot
        lnew = BETA_TWO * ls[s] + (1.0 - BETA_TWO) * mm3(slot, slot, 1, 1)
        rnew = BETA_TWO * rs[s] + (1.0 - BETA_TWO) * mm3(slot, slot, 0, 0)
        lnew_o[s] = lnew
        rnew_o[s] = rnew
        xl_o[s] = mm3(lb[s], lnew, 0, 1)
        xr_o[s] = mm3(rb[s], rnew, 0, 1)
    for copy in moves:
        copy.wait_recv()
    for t in range(shards):
        rows_t = got[t].astype(F32)
        for s in range(slots):
            back_o[t * slots + s] = rows_t[s * width : (s + 1) * width]
    for copy in waits:
        copy.wait_send()


def reduce_grads(inverse, grad, vec, scal, m, v, ls, rs, lb, rb, groups, shards):
    outer, inner = split_shard(shards)
    slots = m.shape[0]
    width = LANES // shards
    full = -(-slots * width // TILE) * TILE
    rows = slots * LANES
    half = rows // 2
    piece = half // groups
    f = jax.ShapeDtypeStruct
    vm = pl.BlockSpec(memory_space=pltpu.VMEM)
    sm = pl.BlockSpec(memory_space=pltpu.SMEM)
    both = outer * inner
    table = vec.reshape(outer, inner, 2, width, WIDTH)

    def buf(*shape):
        return pltpu.VMEM(shape + (WIDTH,), BF16)

    def wide(*shape):
        return pltpu.VMEM(shape + (WIDTH,), F32)

    dma = pltpu.SemaphoreType.DMA
    peers_in, peers_dp = max(inner - 1, 1), max(groups - 1, 1)
    outs = [f(m.shape, F32), f((width, WIDTH), F32), f((8, LANES), F32)]
    outs += [f(x.shape, F32) for x in (v, ls, rs, lb, rb)] + [f((shards * slots, width, WIDTH), F32)]
    return pl.pallas_call(
        functools.partial(reduce_kernel, groups, outer, inner, slots, shards),
        out_shape=outs,
        in_specs=[sm] + [vm] * 9,
        out_specs=[vm] * 9,
        scratch_shapes=[
            buf(both, rows), buf(both, rows), buf(both, rows),
            buf(outer, peers_in, half), buf(outer, half), buf(outer, peers_dp, piece),
            buf(outer, inner, peers_dp, piece), buf(both, piece), buf(outer, peers_in, piece),
            buf(outer, 2 * piece), buf(outer - 1, 2 * piece), buf(groups, 2 * piece),
            pltpu.VMEM((4, 4, 8, LANES), F32),
            wide(slots, LANES), pltpu.VMEM((shards, 8, LANES), F32), buf(shards, full), buf(shards, full),
            wide(outer, inner, width), wide(peers_in, outer, width), wide(groups, outer, width), wide(outer - 1, width),
            wide(2, outer, inner, width),
            dma((2, both)), dma((2, outer, peers_in)), dma((2, outer, peers_dp)), dma((2, outer, inner, peers_dp)),
            dma((2, outer, peers_in)), dma((2, outer - 1)), dma((2, peers_dp)), dma((2, 4, 6)),
            dma((2, shards - 1)), dma((2, shards - 1)),
        ],
        compiler_params=pltpu.CompilerParams(collective_id=1, has_side_effects=True, vmem_limit_bytes=56 * 2**20),
        name="reduce",
    )(inverse, grad, table, scal, m, v, ls, rs, lb, rb)


def soap_kernel(slots, owners, g, gvec, second, lnew, rnew, xl, xr, back, m, mat, ema, vw, vf, vs, ve,
                mat_o, ema_o, m_o, v_o, ls_o, rs_o, lb_o, rb_o, vw_o, vf_o, vs_o, ve_o, zl, ol, zw, ow, xa):
    eye = (lax.broadcasted_iota(jnp.int32, (LANES, LANES), 0) == lax.broadcasted_iota(jnp.int32, (LANES, LANES), 1)).astype(F32)
    for s in range(slots):
        zl[s, :, :LANES] = mm(xl[s], xl[s], 1, 1)
        zl[s, :, LANES:] = xl[s]
        gram = mm(xr[s], xr[s], 1, 1)
        zw[s, :, :LANES] = gram[:LANES, :LANES]
        zw[s, :, LANES:] = eye
        xa[s, :LANES, :LANES] = gram[:LANES, LANES:]
        xa[s, LANES:, :LANES] = gram[LANES:, LANES:]
        xa[s, :, LANES:] = xr[s]
    factor_all([(zw, ow, s) for s in range(slots)] + [(zl, ol, s) for s in range(slots)])
    for s in range(slots):
        lb_o[s] = ol[s].T
        done = mm(ow[s], xa[s, :LANES, :])
        rb_o[s, :, :LANES] = done[:, LANES:].T
        rest = xa[s, LANES:, :] - mm(done[:, :LANES], done, 0, 0)
        zw[s, :, :LANES] = rest[:, :LANES]
        zw[s, :, LANES:] = eye
        xa[s, LANES:, :] = rest
    factor_all([(zw, ow, s) for s in range(slots)])
    for s in range(slots):
        rb_o[s, :, LANES:] = mm(ow[s], xa[s, LANES:, LANES:]).T
    v_o[...] = second[...]
    ls_o[...] = lnew[...]
    rs_o[...] = rnew[...]
    for s in range(slots):
        m_o[s] = BETA_ONE * m[s] + (1.0 - BETA_ONE) * g[s]
    grad = gvec[...]
    first = BETA_ONE * vf[...] + (1.0 - BETA_ONE) * grad
    moment = BETA_TWO * vs[...] + (1.0 - BETA_TWO) * grad * grad
    step = first / (1.0 - BETA_ONE**STEP) / (jnp.sqrt(moment / (1.0 - BETA_TWO**STEP)) + ADAM_EPS)
    new = vw[...] * (1.0 - TABLE_LEARN * DECAY) - TABLE_LEARN * step
    vf_o[...] = first
    vs_o[...] = moment
    vw_o[...] = new
    ve_o[...] = EMA_RATE * ve[...] + (1.0 - EMA_RATE) * new
    for unit in range(UNITS):
        new = mat[unit] * (1.0 - LEARN * DECAY) - LEARN * back[owners[unit]]
        mat_o[unit] = new
        ema_o[unit] = EMA_RATE * ema[unit] + (1.0 - EMA_RATE) * new


def soap(owners, g, gvec, second, lnew, rnew, xl, xr, back, m, mat, ema, vw, vf, vs, ve):
    slots = g.shape[0]
    f = jax.ShapeDtypeStruct
    vm = pl.BlockSpec(memory_space=pltpu.VMEM)
    outs = [f(x.shape, F32) for x in (mat, ema, m, second, lnew, rnew, xl, xr, vw, vf, vs, ve)]
    return pl.pallas_call(
        functools.partial(soap_kernel, slots),
        out_shape=outs,
        in_specs=[pl.BlockSpec(memory_space=pltpu.SMEM)] + [vm] * 15,
        out_specs=[vm] * 12,
        scratch_shapes=[
            pltpu.VMEM((slots, LANES, 2 * LANES), F32),
            pltpu.VMEM((slots, LANES, LANES), F32),
            pltpu.VMEM((slots, LANES, 2 * LANES), F32),
            pltpu.VMEM((slots, LANES, LANES), F32),
            pltpu.VMEM((slots, 2 * LANES, 3 * LANES), F32),
        ],
        compiler_params=pltpu.CompilerParams(vmem_limit_bytes=56 * 2**20),
        name="soap",
    )(owners, g, gvec, second, lnew, rnew, xl, xr, back, m, mat, ema, vw, vf, vs, ve)


def time_table():
    steps = np.arange(32, dtype=np.float32)
    halfway = TDIM // 2
    freqs = np.exp(-math.log(10000.0) * np.arange(halfway, dtype=np.float32) / (halfway - 1)).astype(np.float32)
    angles = (freqs[:, None] * steps[None, :]).astype(np.float32)
    offset = 0.008
    ratio = (steps + 1.0) / DSTEPS
    upper = np.cos((ratio + offset) / (1.0 + offset) * math.pi / 2) ** 2
    level = upper / math.cos(offset / (1.0 + offset) * math.pi / 2) ** 2
    level = np.clip(np.where(steps < DSTEPS, level, 0.0), 0.0, 1.0)
    levels = np.stack([np.sqrt(level), np.sqrt(1.0 - level)] + [np.zeros(32)] * 6)
    return np.concatenate([np.sin(angles), np.cos(angles), levels]).astype(np.float32)


def dot(a, b, ca=1, cb=0):
    return lax.dot_general(a, b, (((ca,), (cb,)), ((), ())), preferred_element_type=F32)


def mish_parts(v):
    e = jnp.exp(jnp.minimum(v, 20.0))
    n = e * (e + 2.0)
    r = pl.reciprocal(n + 2.0)
    return e, r, n * r


def mish_slope(v, e, r, t):
    return t + v * (4.0 * e * (e + 1.0)) * (r * r)


def gather_parts():
    taps = 2 * KERNEL
    bounds = [3, 3 + taps, UNITS + 3 - (OWNED - 1) * taps]
    while bounds[-1] < UNITS + 3:
        bounds.append(bounds[-1] + taps)
    return [(0, bounds[1])] + list(zip(bounds[1:-1], bounds[2:]))


def net_kernel(trajs, frames, groups, outer, inner, traj, noise, steps, valid, times, gmat, mat, vec, mat_o, vec_o, loss_o,
               other, other_vec, mb, xin, xhat, h, skip, d, dskip, dy, dp, low, xt, s_one, s_two, mean, rstd, xsum, q_one, q_two,
               g_one, g_two, tb, dtb, noisy_t, noise_t, mask_t, dpl, acc, table, sem_c, sem_z, sem_y, sem_s, sem_t):
    dpi = lax.axis_index("dp")
    a, b, c = place(outer, inner)
    piece = mat.shape[1]
    chunks = trajs // TILE
    rows_c = TILE * frames
    rows = trajs * frames
    taps = 2 * KERNEL
    part = 1.0 / (frames * (WIDTH // GROUPS))
    group = gmat[...]
    core_peer = (dpi, spot(inner, a, b, 1 - c))
    in_peers = [(dpi, spot(inner, a, lax.rem(b + i, inner), c)) for i in range(1, inner)]
    out_peers = [(dpi, spot(inner, lax.rem(a + i, outer), b, c)) for i in range(1, outer)]
    greet([core_peer] + in_peers + out_peers)
    waits = []

    def send(src, dst, sems, index, peer):
        copy = pltpu.make_async_remote_copy(
            src_ref=src, dst_ref=dst, send_sem=sems.at[(0,) + index], recv_sem=sems.at[(1,) + index],
            device_id=peer, device_id_type=MESH)
        copy.start()
        waits.append(copy)
        return copy

    spans = [(0, taps), (taps * OWNED, UNITS), (taps, taps * OWNED)]
    first_copies = [send(vec, other_vec, sem_c, (3,), core_peer)]
    for k, (lo, hi) in enumerate(spans):
        first_copies.append(send(mat.at[pl.ds(lo, hi - lo)], other.at[pl.ds(lo, hi - lo)], sem_c, (k,), core_peer))
    parts = gather_parts()
    start_of = [3 if l == 0 else parts[l + 1][0] for l in range(OWNED)]
    time_at = parts[1][0]
    source = {0: 0, 1: taps * OWNED}
    for g in range(2, len(parts)):
        source[g] = taps * (g - 1)
    cols = pl.ds(pl.multiple_of(c * LANES, LANES), LANES)
    state = {}

    def chip_rows(mine, theirs):
        mine_first = jnp.where(c == 0, mine, theirs)
        then = jnp.where(c == 0, theirs, mine)
        return jnp.concatenate([mine_first, then], axis=mine.ndim - 2)

    def build(g):
        lo, hi = parts[g]
        count = hi - lo
        if g == 0:
            count -= 3
            first_copies[0].wait_recv()
            first_copies[1].wait_recv()
            rows_v = chip_rows(vec[...], other_vec[...])
            one, two, three = split3(rows_v)
            mb[0, a, b] = one.astype(mb.dtype)
            mb[1, a, b] = two.astype(mb.dtype)
            mb[2, a, b] = three.astype(mb.dtype)
        elif g == 1:
            first_copies[2].wait_recv()
        elif g == 2:
            first_copies[3].wait_recv()
        at = source[g]
        mb[hi - count : hi, a, b] = chip_rows(mat[at : at + count], other[at : at + count]).astype(BF16).astype(mb.dtype)
        region = mb.at[pl.ds(lo, hi - lo), a, b, :, cols]
        state[g] = [send(region, region, sem_z, (g, k), p) for k, p in enumerate(out_peers)]

    def along(g):
        lo, hi = parts[g]
        for copy in state[g]:
            copy.wait_recv()
        region = mb.at[pl.ds(lo, hi - lo), :, b, :, cols]
        nexts = [send(region, region, sem_y, (g, k), p) for k, p in enumerate(in_peers)]
        sib = []
        for i in range(1, outer):
            region = mb.at[pl.ds(lo, hi - lo), lax.rem(a + i, outer), b, :, cols]
            sib.append(send(region, region, sem_s, (g, i - 1), core_peer))
        state[g] = (nexts, sib)

    def across(g):
        lo, hi = parts[g]
        nexts, sib = state[g]
        for copy in nexts:
            copy.wait_recv()
        for i in range(1, inner):
            region = mb.at[pl.ds(lo, hi - lo), :, lax.rem(b + i, inner), :, cols]
            sib.append(send(region, region, sem_t, (g, i - 1), core_peer))
        state[g] = sib

    def whole(g):
        for copy in state[g]:
            copy.wait_recv()

    def chunk_of(n):
        return pl.ds(pl.multiple_of(n * TILE, TILE), TILE)

    def flat(v):
        return v.reshape(rows_c, WIDTH)

    def wide(v):
        return v.reshape(frames, TILE, WIDTH)

    def row(index):
        return table[index : index + 1, :]

    def gain(l):
        return row(BASE + 3 + OWNED + l), row(BASE + 3 + 2 * OWNED + l)

    def tap(l, k):
        at = start_of[l] + 2 * k
        return mb[at : at + 2].reshape(WIDTH, WIDTH).astype(BF16)

    def lin(j):
        at = time_at + 2 * j
        return mb[at : at + 2].reshape(WIDTH, WIDTH).astype(BF16)

    def group_sum(v):
        return lax.dot_general(v, group, (((1,), (0,)), ((), ())), precision=HIGH, preferred_element_type=F32)

    def loop(body):
        def step(n, carry):
            body(n)
            return carry

        lax.fori_loop(0, chunks, step, 0)

    def pass_one(l, n, x):
        at = chunk_of(n)
        xin[l, KERNEL // 2 : KERNEL // 2 + frames, at, :] = wide(x).astype(BF16)
        p = None
        for k in range(KERNEL):
            term = dot(flat(xin[l, k : k + frames, at, :]), tap(l, k))
            p = term if p is None else p + term
        p = wide(p + row(BASE + 3 + l))
        xhat[l, :, at, :] = p
        total = jnp.sum(p, axis=0)
        s_one[at, :] = total
        off = p - (total * (1.0 / frames))[None]
        s_two[at, :] = jnp.sum(off * off, axis=0)

    def stats(l):
        total = s_one[...]
        centre = group_sum(total) * part
        off = total * (1.0 / frames) - centre
        var = group_sum(s_two[...] + frames * off * off) * part
        scale = lax.rsqrt(var + NORM_EPS)
        mean[...] = centre
        rstd[l] = scale
        xsum[l] = frames * off * scale

    def normed(l, n):
        at = chunk_of(n)
        x = (xhat[l, :, at, :] - mean[at, :][None]) * rstd[l, at, :][None]
        xhat[l, :, at, :] = x
        g, s = gain(l)
        return x, x * g + s

    def pass_a(n, dm, x, v, pieces):
        at = chunk_of(n)
        slope = dm * mish_slope(v, *pieces)
        dy[:, at, :] = slope
        q_one[at, :] = jnp.sum(slope, axis=0)
        q_two[at, :] = jnp.sum(slope * x, axis=0)

    def pass_a_load(l, n, dm):
        x = xhat[l, :, chunk_of(n), :]
        g, s = gain(l)
        v = x * g + s
        pass_a(n, dm, x, v, mish_parts(v))

    def stats_back(l):
        g, s = gain(l)
        one, two = q_one[...], q_two[...]
        vec_o[BASE + 3 + OWNED + l : BASE + 4 + OWNED + l, :] = jnp.sum(two, axis=0, keepdims=True)
        vec_o[BASE + 3 + 2 * OWNED + l : BASE + 4 + 2 * OWNED + l, :] = jnp.sum(one, axis=0, keepdims=True)
        sums = group_sum(jnp.concatenate([one * g, two * g], axis=0)) * part
        first, second = sums[:trajs], sums[trajs:]
        g_one[...] = first
        g_two[...] = second
        dc = rstd[l] * (one * g - frames * first - xsum[l] * second)
        vec_o[BASE + 3 + l : BASE + 4 + l, :] = jnp.sum(dc, axis=0, keepdims=True)

    build(0)
    build(1)
    build(2)
    vec_o[...] = jnp.zeros_like(vec_o)
    edge = jnp.zeros((OWNED, KERNEL // 2, trajs, WIDTH), BF16)
    xin[:, : KERNEL // 2] = edge
    xin[:, KERNEL // 2 + frames :] = edge
    dp[: KERNEL // 2] = edge[0]
    dp[KERNEL // 2 + frames :] = edge[0]
    acc[...] = jnp.zeros_like(acc)
    stepid = lax.broadcasted_iota(jnp.int32, (32, trajs), 0)
    picked = mm(times[...], (stepid == steps[...]).astype(F32))
    emb = picked[:TDIM].astype(BF16)
    keep, add = picked[TDIM : TDIM + 1], picked[TDIM + 1 : TDIM + 2]
    for f in range(frames):
        at = slice(f * trajs, (f + 1) * trajs)
        raw = noise[:, f, :]
        noise_t[:, at] = raw
        noisy_t[:, at] = (keep * traj[:, f, :] + add * raw).astype(BF16)
        mask_t[:, at] = valid[f : f + 1, :].astype(F32)
    along(0)
    build(3)
    along(1)
    across(0)
    along(2)
    build(4)
    across(1)
    whole(0)
    full = [mb[k].reshape(VROWS, WIDTH).astype(F32) for k in range(3)]
    table[...] = (full[0] + full[1]) + full[2]
    low[...] = full[0].astype(BF16)
    w_in, w_head = low[:FEAT, :], low[FEAT : 2 * FEAT, :]
    h[...] = (dot(noisy_t[...], w_in, 0, 0) + row(BASE)).reshape(frames, trajs, WIDTH)

    def enter(n):
        pass_one(0, n, flat(h[:, chunk_of(n), :]))

    loop(enter)
    along(3)
    build(5)
    across(2)
    whole(1)
    pre_time = dot(emb, mb[time_at + 2 * BLOCKS].reshape(TDIM, WIDTH).astype(BF16), 0, 0) + row(BASE + 1)
    time_parts = mish_parts(pre_time)
    temb = (pre_time * time_parts[2]).astype(BF16)
    time_slope = mish_slope(pre_time, *time_parts)
    for j in range(BLOCKS):
        tb[j] = dot(temb, lin(j)) + row(BASE + 3 + 3 * OWNED + j)
    moves = {0: [(along, 4), (build, 6), (across, 3), (whole, 2)], 1: [(along, 5), (across, 4), (whole, 3)],
             2: [(along, 6), (across, 5), (whole, 4)], 3: [(across, 6), (whole, 5)], 4: [(whole, 6)]}
    for l in range(OWNED - 1):
        stats(l)
        for act, g in moves[l]:
            act(g)

        def forward(n, l=l):
            at = chunk_of(n)
            _, v = normed(l, n)
            m = v * mish_parts(v)[2]
            if l % 2 == 0:
                m = m + tb[l // 2, at, :][None]
            else:
                m = h[:, at, :] + m
                if l == 1:
                    skip[:, at, :] = m
                if l == 2 * BLOCKS - 3:
                    m = m + skip[:, at, :]
                h[:, at, :] = m
            pass_one(l + 1, n, flat(m))

        loop(forward)
    stats(OWNED - 1)
    head_bias = table[BASE + 2 : BASE + 3, :]

    def settle(n):
        at = chunk_of(n)
        _, v = normed(OWNED - 1, n)
        dp[KERNEL // 2 : KERNEL // 2 + frames, at, :] = (h[:, at, :] + v * mish_parts(v)[2]).astype(BF16)

    loop(settle)
    top = dp[KERNEL // 2 : KERNEL // 2 + frames].reshape(rows, WIDTH)
    pick = lax.broadcasted_iota(jnp.int32, (FEAT, WIDTH), 0) == lax.broadcasted_iota(jnp.int32, (FEAT, WIDTH), 1)
    bias = jnp.sum(jnp.where(pick, head_bias, 0.0), axis=1, keepdims=True)
    err = dot(w_head, top, 1, 1) + bias - noise_t[...]
    weighted = mask_t[...] * err
    loss = jnp.sum(jnp.sum(weighted * err, axis=0, keepdims=True), axis=1, keepdims=True)
    count = FEAT * jnp.sum(mask_t[...], axis=1, keepdims=True)
    rowid = lax.broadcasted_iota(jnp.int32, (8, LANES), 0)
    loss_o[...] = jnp.where(rowid == 0, loss, jnp.where(rowid == 1, count, 0.0))
    grad = 2.0 * weighted
    g_bias = jnp.sum(grad, axis=1, keepdims=True)
    vec_o[BASE + 2 : BASE + 3, :] = jnp.sum(jnp.where(pick, g_bias, 0.0), axis=0, keepdims=True)
    dpl[...] = grad.astype(BF16)
    vec_o[FEAT : 2 * FEAT, :] = dot(dpl[...], top)
    d[...] = dot(dpl[...], w_head, 0, 0).reshape(frames, trajs, WIDTH)

    def turn(n):
        pass_a_load(OWNED - 1, n, d[:, chunk_of(n), :])

    loop(turn)
    for l in reversed(range(OWNED)):
        stats_back(l)

        def backward(n, l=l):
            g, s = gain(l)
            at = chunk_of(n)
            x = xhat[l, :, at, :]
            back = rstd[l, at, :][None] * (dy[:, at, :] * g - g_one[at, :][None] - x * g_two[at, :][None])
            dp[KERNEL // 2 : KERNEL // 2 + frames, at, :] = back.astype(BF16)
            dx = None
            for k in range(KERNEL):
                shift = KERNEL - 1 - k
                term = dot(flat(dp[shift : shift + frames, at, :]), tap(l, k), 1, 1)
                dx = term if dx is None else dx + term
            dx = wide(dx)
            if l % 2 == 1:
                dtb[l // 2, at, :] = jnp.sum(dx, axis=0)
                pass_a_load(l - 1, n, dx)
            else:
                dx = d[:, at, :] + dx
                if l == OWNED - 2:
                    dskip[:, at, :] = dx
                if l == 2:
                    dx = dx + dskip[:, at, :]
                d[:, at, :] = dx
                if l > 0:
                    pass_a_load(l - 1, n, dx)

        loop(backward)
        xt[...] = xin[l, KERNEL // 2 : KERNEL // 2 + frames].reshape(rows, WIDTH).T
        for k in range(KERNEL):
            shift = KERNEL - 1 - k
            w_grad = dot(xt[...], dp[shift : shift + frames].reshape(rows, WIDTH))
            for half in range(2):
                mat_o[taps * l + 2 * k + half] = w_grad[half * LANES : (half + 1) * LANES].astype(mat_o.dtype)

    d_in = d[...].reshape(rows, WIDTH)
    vec_o[BASE : BASE + 1, :] = jnp.sum(d_in, axis=0, keepdims=True)
    vec_o[:FEAT, :] = dot(noisy_t[...], d_in.astype(BF16))
    d_temb = None
    for j in range(BLOCKS):
        grads = dtb[j]
        vec_o[BASE + 3 + 3 * OWNED + j : BASE + 4 + 3 * OWNED + j, :] = jnp.sum(grads, axis=0, keepdims=True)
        grads = grads.astype(BF16)
        t_grad = dot(temb, grads, 0, 0)
        for half in range(2):
            mat_o[taps * OWNED + 2 * j + half] = t_grad[half * LANES : (half + 1) * LANES].astype(mat_o.dtype)
        term = dot(grads, lin(j), 1, 1)
        d_temb = term if d_temb is None else d_temb + term
    d_pre = d_temb * time_slope
    vec_o[BASE + 1 : BASE + 2, :] = jnp.sum(d_pre, axis=0, keepdims=True)
    mat_o[UNITS] = jnp.zeros((LANES, WIDTH), mat_o.dtype)
    mat_o[UNITS - 1] = dot(emb, d_pre.astype(BF16)).astype(mat_o.dtype)
    for copy in waits:
        copy.wait_send()


def net(traj, noise, steps, valid, mat, vec, groups, shards):
    outer, inner = split_shard(shards)
    feats, frames, trajs = traj.shape
    rows = frames * trajs
    piece = mat.shape[1]
    lane = np.arange(WIDTH) // (WIDTH // GROUPS)
    gmat = jnp.asarray((lane[:, None] == lane[None, :]).astype(np.float32))
    times = jnp.asarray(time_table())
    wire = BF16 if (2 * piece) % TILE == 0 else F32
    vm = pl.BlockSpec(memory_space=pltpu.VMEM)
    f = jax.ShapeDtypeStruct
    big = pltpu.VMEM((frames, trajs, WIDTH), F32)
    small = pltpu.VMEM((trajs, WIDTH), F32)
    padded = frames + KERNEL - 1
    dma = pltpu.SemaphoreType.DMA
    count = len(gather_parts())
    return pl.pallas_call(
        functools.partial(net_kernel, trajs, frames, groups, outer, inner),
        out_shape=[f((UNITS + 1, LANES, WIDTH), BF16), f((VROWS, WIDTH), F32), f((8, LANES), F32)],
        in_specs=[vm] * 8,
        out_specs=[vm] * 3,
        scratch_shapes=[
            pltpu.VMEM((UNITS, piece, WIDTH), F32),
            pltpu.VMEM((piece, WIDTH), F32),
            pltpu.VMEM((UNITS + 3, outer, inner, 2 * piece, WIDTH), wire),
            pltpu.VMEM((OWNED, padded, trajs, WIDTH), BF16),
            pltpu.VMEM((OWNED, frames, trajs, WIDTH), F32),
            big, big, big, big, big,
            pltpu.VMEM((padded, trajs, WIDTH), BF16),
            pltpu.VMEM((VROWS, WIDTH), BF16),
            pltpu.VMEM((WIDTH, rows), BF16),
            small, small, small,
            pltpu.VMEM((OWNED, trajs, WIDTH), F32),
            pltpu.VMEM((OWNED, trajs, WIDTH), F32),
            small, small, small, small,
            pltpu.VMEM((BLOCKS, trajs, WIDTH), F32),
            pltpu.VMEM((BLOCKS, trajs, WIDTH), F32),
            pltpu.VMEM((feats, rows), BF16),
            pltpu.VMEM((feats, rows), F32),
            pltpu.VMEM((1, rows), F32),
            pltpu.VMEM((feats, rows), BF16),
            pltpu.VMEM((16, WIDTH), F32),
            pltpu.VMEM((VROWS, WIDTH), F32),
            dma((2, 4)), dma((2, count, outer - 1)), dma((2, count, max(inner - 1, 1))),
            dma((2, count, outer - 1)), dma((2, count, max(inner - 1, 1))),
        ],
        compiler_params=pltpu.CompilerParams(collective_id=3, has_side_effects=True, vmem_limit_bytes=62 * 2**20),
        name="net",
    )(traj, noise, steps, valid, times, gmat, mat, vec)


def body(
    trajectories,
    noise,
    timesteps,
    valid,
    owners,
    mat_weight,
    mat_ema,
    soap_first,
    soap_second,
    left_stat,
    right_stat,
    left_basis,
    right_basis,
    vec_weight,
    vec_first,
    vec_second,
    vec_ema,
):
    shards = lax.axis_size("shard")
    groups = lax.axis_size("dp")
    slots = soap_first.shape[0]
    mat_grad, vec_grad, scal = net(
        trajectories.transpose(2, 1, 0),
        noise.transpose(2, 1, 0),
        timesteps.reshape(1, -1),
        valid.T,
        mat_weight,
        vec_weight,
        groups,
        shards,
    )
    choose = owners[None, :] == jnp.arange(shards * slots, dtype=jnp.int32)[:, None]
    order = jnp.arange(UNITS, dtype=jnp.int32)[None, :]
    inverse = jnp.min(jnp.where(choose, order, UNITS), axis=1)
    grads, grads_vec, scal, second, lnew, rnew, xl, xr, back = reduce_grads(
        inverse, mat_grad, vec_grad, scal, soap_first, soap_second, left_stat, right_stat, left_basis, right_basis, groups, shards
    )
    results = soap(
        owners, grads, grads_vec, second, lnew, rnew, xl, xr, back,
        soap_first, mat_weight, mat_ema, vec_weight, vec_first, vec_second, vec_ema,
    )
    return (scal[0, 0], scal[1, 0], scal[2, 0]) + tuple(results)


def solution(mesh):
    placed = (
        P(("dp", "shard"), None, None),
        P(("dp", "shard"), None, None),
        P(("dp", "shard")),
        P(("dp", "shard"), None),
        P(),
        P(None, "shard", None),
        P(None, "shard", None),
        P("shard", None, None),
        P("shard", None, None),
        P("shard", None, None),
        P("shard", None, None),
        P("shard", None, None),
        P("shard", None, None),
        P("shard", None),
        P("shard", None),
        P("shard", None),
        P("shard", None),
    )
    return jax.shard_map(
        body,
        mesh=mesh,
        in_specs=placed,
        out_specs=(
            P(),
            P(),
            P(),
            P(None, "shard", None),
            P(None, "shard", None),
            P("shard", None, None),
            P("shard", None, None),
            P("shard", None, None),
            P("shard", None, None),
            P("shard", None, None),
            P("shard", None, None),
            P("shard", None),
            P("shard", None),
            P("shard", None),
            P("shard", None),
        ),
        check_vma=False,
    )
```

```python
import functools
import math

import jax
import jax.numpy as jnp
import numpy as np
from jax import lax
from jax.experimental import pallas as pl
from jax.experimental.pallas import tpu as pltpu
from jax.sharding import PartitionSpec as P

WIDTH = 256
KERNEL = 5
GROUPS = 8
TDIM = 128
FEAT = 23
BLOCKS = 3
DSTEPS = 20
STEP = 10
OWNED = 6
UNITS = 67
VROWS = 128

HIGH = lax.Precision.HIGHEST
BETA_ONE = 0.9
BETA_TWO = 0.95
ADAM_EPS = 1e-08
LEARN = 0.05
TABLE_LEARN = 0.25
DECAY = 0.01
CLIP = 0.05
EMA_RATE = 0.8
NORM_EPS = 1e-05
PANEL = 32
LANES = 128
PAD = 8
CHUNK = 8
TILE = 16
BASE = 2 * FEAT
F32 = jnp.float32
BF16 = jnp.bfloat16
MESH = pl.DeviceIdType.MESH


def mm(a, b, ca=1, cb=0):
    return lax.dot_general(a, b, (((ca,), (cb,)), ((), ())), precision=HIGH, preferred_element_type=F32)

def mm3(a, b, ca=1, cb=0):
    ah = a.astype(BF16)
    al = (a - ah.astype(F32)).astype(BF16)
    bh = b.astype(BF16)
    bl = (b - bh.astype(F32)).astype(BF16)
    d = (((ca,), (cb,)), ((), ()))

    def product(p, q):
        return lax.dot_general(p, q, d, preferred_element_type=F32)

    return product(ah, bh) + (product(ah, bl) + product(al, bh))


def split3(v):
    hi = v.astype(BF16)
    rest = v - hi.astype(F32)
    mid = rest.astype(BF16)
    last = (rest - mid.astype(F32)).astype(BF16)
    return hi, mid, last

def eliminate(held):
    lanes = lax.broadcasted_iota(jnp.int32, (8, LANES), 1)
    sub = lax.broadcasted_iota(jnp.int32, (8, LANES), 0)
    tall = PANEL // 8

    def lane(v, k):
        return jnp.broadcast_to(v[:, k : k + 1], (8, LANES))

    for k in range(0, PANEL, 2):
        top, r = k // 8, k % 8
        for e in held:
            first = jnp.broadcast_to(e[top][r : r + 1, :], (8, LANES))
            second = jnp.broadcast_to(e[top][r + 1 : r + 2, :], (8, LANES))
            corner = lane(first, k + 1)
            one = pl.reciprocal(lane(first, k))
            ratio = corner * one
            two = pl.reciprocal(lane(second, k + 1) - corner * ratio)
            second = second - ratio * first
            by_first = first * one
            by_second = second * two
            for v in range(top, tall):
                left = lane(e[v], k)
                right = lane(e[v], k + 1) - left * ratio
                less = e[v] - left * by_first - right * by_second
                if v == top:
                    less = jnp.where(sub > r + 1, less, jnp.where(sub == r + 1, second, e[v]))
                e[v] = less
    results = []
    for e in held:
        parts = []
        for v in range(tall):
            pivots = jnp.sum(jnp.where(lanes == sub + 8 * v, e[v], 0.0), axis=1, keepdims=True)
            parts.append(e[v] * lax.rsqrt(pivots))
        results.append(jnp.concatenate(parts, axis=0)[:, PANEL : 2 * PANEL])
    return results


def factor_panels(chains, start):
    rows = lax.broadcasted_iota(jnp.int32, (PANEL, LANES), 0)
    lanes = lax.broadcasted_iota(jnp.int32, (PANEL, LANES), 1)
    unit = jnp.where(lanes - PANEL == rows, 1.0, 0.0).astype(F32)
    shift = lax.rem(LANES - start, LANES)
    at = pl.ds(start, PANEL)
    held = []
    for z, out, s in chains:
        block = jnp.where(lanes < PANEL, pltpu.roll(z[s, at, :LANES], shift, 1), unit)
        held.append([block[8 * v : 8 * v + 8] for v in range(PANEL // 8)])
    panels = [mm(inverse, z[s, at, :]) for (z, out, s), inverse in zip(chains, eliminate(held))]
    for (z, out, s), done in zip(chains, panels):
        out[s, at, :] = done[:, LANES:]
    for (z, out, s), done in zip(chains, panels):
        hi, mid, last = split3(done)
        lhs = jnp.concatenate([hi, hi, mid, hi, last, mid], axis=0)[:, :LANES]
        rhs = jnp.concatenate([hi, mid, hi, last, hi, mid], axis=0)
        z[s] = z[s] - lax.dot_general(lhs, rhs, (((0,), (0,)), ((), ())), preferred_element_type=F32)


def factor_all(chains):
    def step(p, carry):
        factor_panels(chains, pl.multiple_of(p * PANEL, PANEL))
        return carry

    lax.fori_loop(0, LANES // PANEL, step, 0)


def split_shard(shards):
    return 4, shards // 8


def place(outer, inner):
    s = lax.axis_index("shard")
    return s // (2 * inner), lax.rem(s // 2, inner), lax.rem(s, 2)


def spot(inner, a, b, c):
    return (a * inner + b) * 2 + c


def greet(peers):
    barrier = pltpu.get_barrier_semaphore()
    for peer in peers:
        pl.semaphore_signal(barrier, inc=1, device_id=peer, device_id_type=MESH)
    pl.semaphore_wait(barrier, len(peers))


def reduce_kernel(groups, outer, inner, slots, shards, inverse, grad, vec, scal, m, v, ls, rs, lb, rb,
                  grad_o, vec_o, scal_o, second_o, lnew_o, rnew_o, xl_o, xr_o, back_o,
                  s_core, r_core, held, r_in_a, sum_a, r_dp_a, r_dp_b, sum_b, r_in_b, ready, r_out, final, sc, turn, norms, sent, got,
                  w_core, w_in, w_dp, w_out, w_sum,
                  sem_core, sem_in_a, sem_dp_a, sem_dp_b, sem_in_b, sem_out, sem_fin, sem_sc, sem_n, sem_u):
    d = lax.axis_index("dp")
    a, b, c = place(outer, inner)
    me = lax.axis_index("shard")
    rows = slots * LANES
    half = rows // 2
    piece = half // groups
    core_peer = (d, spot(inner, a, b, 1 - c))
    in_peers = [(d, spot(inner, a, lax.rem(b + i, inner), c)) for i in range(1, inner)]
    dp_peers = [(lax.rem(d + i, groups), me) for i in range(1, groups)]
    out_peers = [(d, spot(inner, lax.rem(a + i, outer), b, c)) for i in range(1, outer)]
    peers = [(d, lax.rem(me + i, shards)) for i in range(1, shards)]
    greet(peers + dp_peers)
    waits = []

    def send(src, dst, sems, index, peer):
        copy = pltpu.make_async_remote_copy(
            src_ref=src, dst_ref=dst, send_sem=sems.at[(0,) + index], recv_sem=sems.at[(1,) + index],
            device_id=peer, device_id_type=MESH)
        copy.start()
        waits.append(copy)
        return copy

    def load(aa, bb, cc):
        first = spot(inner, aa, bb, cc) * slots
        return jnp.concatenate([grad[inverse[first + s, 0]] for s in range(slots)], axis=0)

    order = [lax.rem(a + i, outer) for i in range(1, outer + 1)]
    core_copies = {}

    def begin(i):
        for j in range(inner):
            at = i * inner + j
            s_core[at] = load(order[i], j, 1 - c)
            core_copies[at] = send(s_core.at[at], r_core.at[at], sem_core, (at,), core_peer)

    begin(0)
    sc[0, c] = scal[...]
    small = [send(sc.at[0, c], sc.at[0, c], sem_sc, (0, 0), core_peer),
             send(vec.at[:, :, 1 - c], w_core, sem_sc, (0, 3), core_peer)]
    begin(1)
    in_a, dp_b, dp_a, in_b, out = {}, {}, {}, {}, {}

    def first_hop(i):
        for j in range(inner):
            at = i * inner + j
            core_copies[at].wait_recv()
            held[at] = (load(order[i], j, c).astype(F32) + r_core[at].astype(F32)).astype(BF16)
        in_a[i] = [send(held.at[i * inner + lax.rem(b + k, inner), pl.ds(0, half)], r_in_a.at[i, k - 1], sem_in_a, (i, k - 1), in_peers[k - 1])
                   for k in range(1, inner)]
        dp_b[i] = [send(held.at[i * inner + j, pl.ds(pl.multiple_of(half + lax.rem(d + k, groups) * piece, TILE), piece)],
                        r_dp_b.at[i, j, k - 1], sem_dp_b, (i, j, k - 1), dp_peers[k - 1])
                   for k in range(1, groups) for j in range(inner)]

    def second_hop(i):
        for copy in in_a[i]:
            copy.wait_recv()
        total = held[i * inner + b, pl.ds(0, half)].astype(F32)
        for k in range(inner - 1):
            total = total + r_in_a[i, k].astype(F32)
        sum_a[i] = total.astype(BF16)
        dp_a[i] = [send(sum_a.at[i, pl.ds(pl.multiple_of(lax.rem(d + k, groups) * piece, TILE), piece)], r_dp_a.at[i, k - 1], sem_dp_a, (i, k - 1), dp_peers[k - 1])
                   for k in range(1, groups)]
        for copy in dp_b[i]:
            copy.wait_recv()
        for j in range(inner):
            total = held[i * inner + j, pl.ds(pl.multiple_of(half + d * piece, TILE), piece)].astype(F32)
            for k in range(groups - 1):
                total = total + r_dp_b[i, j, k].astype(F32)
            sum_b[i * inner + j] = total.astype(BF16)
        in_b[i] = [send(sum_b.at[i * inner + lax.rem(b + k, inner)], r_in_b.at[i, k - 1], sem_in_b, (i, k - 1), in_peers[k - 1])
                   for k in range(1, inner)]

    def third_hop(i):
        for copy in dp_a[i] + in_b[i]:
            copy.wait_recv()
        first = sum_a[i, pl.ds(pl.multiple_of(d * piece, TILE), piece)].astype(F32)
        for k in range(groups - 1):
            first = first + r_dp_a[i, k].astype(F32)
        second = sum_b[i * inner + b].astype(F32)
        for k in range(inner - 1):
            second = second + r_in_b[i, k].astype(F32)
        ready[i, 0:piece] = first.astype(BF16)
        ready[i, piece : 2 * piece] = second.astype(BF16)
        if i < outer - 1:
            out[i] = send(ready.at[i], r_out.at[i], sem_out, (i,), out_peers[i])

    def gathered(level, count):
        for copy in small:
            copy.wait_recv()
        total = sc[level, 0]
        for k in range(1, count):
            total = total + sc[level, k]
        return total

    first_hop(0)
    if outer > 2:
        begin(2)
    first_hop(1)
    total = gathered(0, 2)
    sc[1, b] = total
    w_sum[0] = vec[:, :, c] + w_core[...]
    small = [send(sc.at[1, b], sc.at[1, b], sem_sc, (1, k), p) for k, p in enumerate(in_peers)]
    small += [send(w_sum.at[0, :, lax.rem(b + k, inner)], w_in.at[k - 1], sem_sc, (1, 2 + k), in_peers[k - 1]) for k in range(1, inner)]
    second_hop(0)
    for i in range(2, outer):
        if i + 1 < outer:
            begin(i + 1)
        first_hop(i)
        second_hop(i - 1)
        third_hop(i - 2)
    total = gathered(1, inner)
    sc[2, d] = total
    summed = w_sum[0, :, b]
    for k in range(inner - 1):
        summed = summed + w_in[k]
    w_dp[d] = summed
    small = [send(sc.at[2, d], sc.at[2, d], sem_sc, (2, k), p) for k, p in enumerate(dp_peers)]
    small += [send(w_dp.at[d], w_dp.at[d], sem_sc, (2, 3 + k), p) for k, p in enumerate(dp_peers)]
    second_hop(outer - 1)
    third_hop(outer - 2)
    for s in range(slots):
        second_o[s] = mm3(mm3(lb[s], m[s], 0, 0), rb[s])
    total = gathered(2, groups)
    sc[3, a] = total
    summed = w_dp[0]
    for k in range(1, groups):
        summed = summed + w_dp[k]
    w_sum[1, :, 0] = summed
    small = [send(sc.at[3, a], sc.at[3, a], sem_sc, (3, k), p) for k, p in enumerate(out_peers)]
    small += [send(w_sum.at[1, lax.rem(a + k, outer), 0], w_out.at[k - 1], sem_sc, (3, 2 + k), out_peers[k - 1]) for k in range(1, outer)]
    third_hop(outer - 1)
    total = ready[outer - 1].astype(F32)
    for i in range(outer - 1):
        out[i].wait_recv()
        total = total + r_out[i].astype(F32)
    final[d] = total.astype(BF16)
    last = [send(final.at[d], final.at[d], sem_fin, (k,), p) for k, p in enumerate(dp_peers)]
    counts = gathered(3, outer)
    scale = 1.0 / counts[1:2, 0:1]
    table = w_sum[1, a, 0]
    for k in range(outer - 1):
        table = table + w_out[k]
    table = table * scale
    for copy in last:
        copy.wait_recv()
    parts = [final[k, 0:piece] for k in range(groups)] + [final[k, piece : 2 * piece] for k in range(groups)]
    whole = jnp.concatenate(parts, axis=0).astype(F32) * scale
    squares = jnp.sum(table * table) + jnp.sum(whole * whole)
    norms[me] = jnp.full((8, LANES), squares, F32)
    moves = [send(norms.at[me], norms.at[me], sem_n, (k,), p) for k, p in enumerate(peers)]
    for s in range(slots):
        slot = whole[s * LANES : (s + 1) * LANES]
        grad_o[s] = slot
        turn[s] = mm3(mm3(lb[s], slot, 0, 0), rb[s])
    for copy in moves:
        copy.wait_recv()
    total = norms[0]
    for k in range(1, shards):
        total = total + norms[k]
    norm = jnp.sqrt(total)
    factor = jnp.minimum(1.0, CLIP / (norm + 1e-06))
    rowid = lax.broadcasted_iota(jnp.int32, (8, LANES), 0)
    scal_o[...] = jnp.where(rowid == 2, norm, counts)
    scale = factor[0:1, 0:1]
    vec_o[...] = table * scale
    for s in range(slots):
        turned = turn[s] * scale
        moment = BETA_ONE * second_o[s] + (1.0 - BETA_ONE) * turned
        second = BETA_TWO * v[s] + (1.0 - BETA_TWO) * turned * turned
        second_o[s] = second
        normed = moment / (1.0 - BETA_ONE**STEP) / (jnp.sqrt(second / (1.0 - BETA_TWO**STEP)) + ADAM_EPS)
        turn[s] = mm3(mm3(lb[s], normed), rb[s], 1, 1)
    width = back_o.shape[1]
    used = slots * width
    full = sent.shape[1]
    for t in range(shards):
        parts = [turn[s, t * width : (t + 1) * width, :] for s in range(slots)]
        if full > used:
            parts.append(jnp.zeros((full - used, WIDTH), F32))
        sent[t] = jnp.concatenate(parts, axis=0).astype(BF16)
    got[me] = sent[me]
    moves = [send(sent.at[p[1]], got.at[me], sem_u, (k,), p) for k, p in enumerate(peers)]
    for s in range(slots):
        slot = grad_o[s] * scale
        grad_o[s] = slot
        lnew = BETA_TWO * ls[s] + (1.0 - BETA_TWO) * mm3(slot, slot, 1, 1)
        rnew = BETA_TWO * rs[s] + (1.0 - BETA_TWO) * mm3(slot, slot, 0, 0)
        lnew_o[s] = lnew
        rnew_o[s] = rnew
        xl_o[s] = mm3(lb[s], lnew, 0, 1)
        xr_o[s] = mm3(rb[s], rnew, 0, 1)
    for copy in moves:
        copy.wait_recv()
    for t in range(shards):
        rows_t = got[t].astype(F32)
        for s in range(slots):
            back_o[t * slots + s] = rows_t[s * width : (s + 1) * width]
    for copy in waits:
        copy.wait_send()


def reduce_grads(inverse, grad, vec, scal, m, v, ls, rs, lb, rb, groups, shards):
    outer, inner = split_shard(shards)
    slots = m.shape[0]
    width = LANES // shards
    full = -(-slots * width // TILE) * TILE
    rows = slots * LANES
    half = rows // 2
    piece = half // groups
    f = jax.ShapeDtypeStruct
    vm = pl.BlockSpec(memory_space=pltpu.VMEM)
    sm = pl.BlockSpec(memory_space=pltpu.SMEM)
    both = outer * inner
    table = vec.reshape(outer, inner, 2, width, WIDTH)

    def buf(*shape):
        return pltpu.VMEM(shape + (WIDTH,), BF16)

    def wide(*shape):
        return pltpu.VMEM(shape + (WIDTH,), F32)

    dma = pltpu.SemaphoreType.DMA
    peers_in, peers_dp = max(inner - 1, 1), max(groups - 1, 1)
    outs = [f(m.shape, F32), f((width, WIDTH), F32), f((8, LANES), F32)]
    outs += [f(x.shape, F32) for x in (v, ls, rs, lb, rb)] + [f((shards * slots, width, WIDTH), F32)]
    return pl.pallas_call(
        functools.partial(reduce_kernel, groups, outer, inner, slots, shards),
        out_shape=outs,
        in_specs=[sm] + [vm] * 9,
        out_specs=[vm] * 9,
        scratch_shapes=[
            buf(both, rows), buf(both, rows), buf(both, rows),
            buf(outer, peers_in, half), buf(outer, half), buf(outer, peers_dp, piece),
            buf(outer, inner, peers_dp, piece), buf(both, piece), buf(outer, peers_in, piece),
            buf(outer, 2 * piece), buf(outer - 1, 2 * piece), buf(groups, 2 * piece),
            pltpu.VMEM((4, 4, 8, LANES), F32),
            wide(slots, LANES), pltpu.VMEM((shards, 8, LANES), F32), buf(shards, full), buf(shards, full),
            wide(outer, inner, width), wide(peers_in, outer, width), wide(groups, outer, width), wide(outer - 1, width),
            wide(2, outer, inner, width),
            dma((2, both)), dma((2, outer, peers_in)), dma((2, outer, peers_dp)), dma((2, outer, inner, peers_dp)),
            dma((2, outer, peers_in)), dma((2, outer - 1)), dma((2, peers_dp)), dma((2, 4, 6)),
            dma((2, shards - 1)), dma((2, shards - 1)),
        ],
        compiler_params=pltpu.CompilerParams(collective_id=1, has_side_effects=True, vmem_limit_bytes=36 * 2**20),
        name="reduce",
    )(inverse, grad, table, scal, m, v, ls, rs, lb, rb)


def soap_kernel(slots, owners, scal, g, gvec, second, lnew, rnew, xl, xr, back, m, mat, ema, vw, vf, vs, ve,
                loss_o, count_o, norm_o, mat_o, ema_o, m_o, v_o, ls_o, rs_o, lb_o, rb_o, vw_o, vf_o, vs_o, ve_o, zl, ol, zw, ow, xa):
    loss_o[...] = scal[0:1, 0:1]
    count_o[...] = scal[1:2, 0:1]
    norm_o[...] = scal[2:3, 0:1]
    eye = (lax.broadcasted_iota(jnp.int32, (LANES, LANES), 0) == lax.broadcasted_iota(jnp.int32, (LANES, LANES), 1)).astype(F32)
    for s in range(slots):
        zl[s, :, :LANES] = mm(xl[s], xl[s], 1, 1)
        zl[s, :, LANES:] = xl[s]
        gram = mm(xr[s], xr[s], 1, 1)
        zw[s, :, :LANES] = gram[:LANES, :LANES]
        zw[s, :, LANES:] = eye
        xa[s, :LANES, :LANES] = gram[:LANES, LANES:]
        xa[s, LANES:, :LANES] = gram[LANES:, LANES:]
        xa[s, :, LANES:] = xr[s]
    factor_all([(zw, ow, s) for s in range(slots)] + [(zl, ol, s) for s in range(slots)])
    for s in range(slots):
        lb_o[s] = ol[s].T
        done = mm(ow[s], xa[s, :LANES, :])
        rb_o[s, :, :LANES] = done[:, LANES:].T
        rest = xa[s, LANES:, :] - mm(done[:, :LANES], done, 0, 0)
        zw[s, :, :LANES] = rest[:, :LANES]
        zw[s, :, LANES:] = eye
        xa[s, LANES:, :] = rest
    factor_all([(zw, ow, s) for s in range(slots)])
    for s in range(slots):
        rb_o[s, :, LANES:] = mm(ow[s], xa[s, LANES:, LANES:]).T
    v_o[...] = second[...]
    ls_o[...] = lnew[...]
    rs_o[...] = rnew[...]
    for s in range(slots):
        m_o[s] = BETA_ONE * m[s] + (1.0 - BETA_ONE) * g[s]
    grad = gvec[...]
    first = BETA_ONE * vf[...] + (1.0 - BETA_ONE) * grad
    moment = BETA_TWO * vs[...] + (1.0 - BETA_TWO) * grad * grad
    step = first / (1.0 - BETA_ONE**STEP) / (jnp.sqrt(moment / (1.0 - BETA_TWO**STEP)) + ADAM_EPS)
    new = vw[...] * (1.0 - TABLE_LEARN * DECAY) - TABLE_LEARN * step
    vf_o[...] = first
    vs_o[...] = moment
    vw_o[...] = new
    ve_o[...] = EMA_RATE * ve[...] + (1.0 - EMA_RATE) * new
    for unit in range(UNITS):
        new = mat[unit] * (1.0 - LEARN * DECAY) - LEARN * back[owners[unit]]
        mat_o[unit] = new
        ema_o[unit] = EMA_RATE * ema[unit] + (1.0 - EMA_RATE) * new


def soap(owners, scal, g, gvec, second, lnew, rnew, xl, xr, back, m, mat, ema, vw, vf, vs, ve):
    slots = g.shape[0]
    f = jax.ShapeDtypeStruct
    vm = pl.BlockSpec(memory_space=pltpu.VMEM)
    outs = [f((1, 1), F32)] * 3 + [f(x.shape, F32) for x in (mat, ema, m, second, lnew, rnew, xl, xr, vw, vf, vs, ve)]
    return pl.pallas_call(
        functools.partial(soap_kernel, slots),
        out_shape=outs,
        in_specs=[pl.BlockSpec(memory_space=pltpu.SMEM)] + [vm] * 16,
        out_specs=[vm] * 15,
        scratch_shapes=[
            pltpu.VMEM((slots, LANES, 2 * LANES), F32),
            pltpu.VMEM((slots, LANES, LANES), F32),
            pltpu.VMEM((slots, LANES, 2 * LANES), F32),
            pltpu.VMEM((slots, LANES, LANES), F32),
            pltpu.VMEM((slots, 2 * LANES, 3 * LANES), F32),
        ],
        compiler_params=pltpu.CompilerParams(vmem_limit_bytes=30 * 2**20),
        name="soap",
    )(owners, scal, g, gvec, second, lnew, rnew, xl, xr, back, m, mat, ema, vw, vf, vs, ve)


def time_table():
    steps = np.arange(32, dtype=np.float32)
    halfway = TDIM // 2
    freqs = np.exp(-math.log(10000.0) * np.arange(halfway, dtype=np.float32) / (halfway - 1)).astype(np.float32)
    angles = (freqs[:, None] * steps[None, :]).astype(np.float32)
    offset = 0.008
    ratio = (steps + 1.0) / DSTEPS
    upper = np.cos((ratio + offset) / (1.0 + offset) * math.pi / 2) ** 2
    level = upper / math.cos(offset / (1.0 + offset) * math.pi / 2) ** 2
    level = np.clip(np.where(steps < DSTEPS, level, 0.0), 0.0, 1.0)
    levels = np.stack([np.sqrt(level), np.sqrt(1.0 - level)] + [np.zeros(32)] * 6)
    return np.concatenate([np.sin(angles), np.cos(angles), levels]).astype(np.float32)


def dot(a, b, ca=1, cb=0):
    return lax.dot_general(a, b, (((ca,), (cb,)), ((), ())), preferred_element_type=F32)


def mish_parts(v):
    e = jnp.exp(jnp.minimum(v, 20.0))
    n = e * (e + 2.0)
    r = pl.reciprocal(n + 2.0)
    return e, r, n * r


def mish_slope(v, e, r, t):
    return t + v * (4.0 * e * (e + 1.0)) * (r * r)


def gather_parts():
    taps = 2 * KERNEL
    bounds = [3, 3 + taps, UNITS + 3 - (OWNED - 1) * taps]
    while bounds[-1] < UNITS + 3:
        bounds.append(bounds[-1] + taps)
    return [(0, bounds[1])] + list(zip(bounds[1:-1], bounds[2:]))


def net_kernel(trajs, frames, groups, outer, inner, traj, noise, steps, valid, times, gmat, mat, vec, owners, mat_o, vec_o, loss_o, inverse_o,
               other, other_vec, stage, mb, xin, xhat, h, skip, d, dskip, dy, dp, low, xt, s_one, s_two, mean, rstd, xsum, q_one, q_two,
               g_one, g_two, tb, dtb, noisy_t, noise_t, mask_t, dpl, acc, table, sem_c, sem_z, sem_y, sem_s, sem_x):
    dpi = lax.axis_index("dp")
    a, b, c = place(outer, inner)
    piece = mat.shape[1]
    chunks = trajs // TILE
    rows_c = TILE * frames
    rows = trajs * frames
    taps = 2 * KERNEL
    part = 1.0 / (frames * (WIDTH // GROUPS))
    group = gmat[...]
    core_peer = (dpi, spot(inner, a, b, 1 - c))
    in_peers = [(dpi, spot(inner, a, lax.rem(b + i, inner), c)) for i in range(1, inner)]
    out_peers = [(dpi, spot(inner, lax.rem(a + i, outer), b, c)) for i in range(1, outer)]
    odd = lax.rem(dpi, 2)
    twin_peer = (dpi + 1 - 2 * odd, spot(inner, a, b, c))
    greet([core_peer, twin_peer] + in_peers + out_peers)
    waits = []

    def send(src, dst, sems, index, peer):
        copy = pltpu.make_async_remote_copy(
            src_ref=src, dst_ref=dst, send_sem=sems.at[(0,) + index], recv_sem=sems.at[(1,) + index],
            device_id=peer, device_id_type=MESH)
        copy.start()
        waits.append(copy)
        return copy

    spans = [(0, taps), (taps * OWNED, UNITS), (taps, taps * OWNED)]
    first_copies = [send(vec, other_vec, sem_c, (3,), core_peer)]
    for k, (lo, hi) in enumerate(spans):
        first_copies.append(send(mat.at[pl.ds(lo, hi - lo)], other.at[pl.ds(lo, hi - lo)], sem_c, (k,), core_peer))
    parts = gather_parts()
    start_of = [3 if l == 0 else parts[l + 1][0] for l in range(OWNED)]
    time_at = parts[1][0]
    shares = [(lo, hi - lo, (hi - lo) * 3 // 10) for lo, hi in parts]
    source = {0: 0, 1: taps * OWNED}
    for g in range(2, len(parts)):
        source[g] = taps * (g - 1)
    cols = pl.ds(pl.multiple_of(c * LANES, LANES), LANES)
    state = {}

    def chip_rows(mine, theirs):
        upper = jnp.where(c == 0, mine, theirs)
        lower = jnp.where(c == 0, theirs, mine)
        return jnp.concatenate([upper, lower], axis=mine.ndim - 2)

    def region(g, kind, at_a, at_b):
        lo, count, side = shares[g]
        both = count - side
        if kind == "own":
            start, size = lo + odd * side, both
        elif kind == "lend":
            start, size = lo + odd * both, side
        else:
            start, size = lo + (1 - odd) * both, side
        return mb.at[pl.ds(start, size), at_a, at_b, :, cols]

    def build(g):
        lo, count, side = shares[g]
        hi = lo + count
        if g == 0:
            first_copies[0].wait_recv()
            first_copies[1].wait_recv()
            rows_v = chip_rows(vec[...], other_vec[...])
            for k, value in enumerate(split3(rows_v)):
                stage[k] = value.astype(mb.dtype)
            count -= 3
        elif g == 1:
            first_copies[2].wait_recv()
        elif g == 2:
            first_copies[3].wait_recv()
        at = source[g]
        stage[hi - count : hi] = chip_rows(mat[at : at + count], other[at : at + count]).astype(BF16).astype(mb.dtype)
        both = hi - lo - side
        mine = region(g, "own", a, b)
        mine[...] = stage[pl.ds(lo + odd * side, both), :, cols]
        state[g] = [send(mine, mine, sem_z, (g, k), p) for k, p in enumerate(out_peers)]

    def along(g):
        for copy in state[g]:
            copy.wait_recv()
        column = region(g, "own", slice(None), b)
        nexts = [send(column, column, sem_y, (g, k), p) for k, p in enumerate(in_peers)]
        state[g] = (nexts, [send(column, column, sem_s, (g, 0), core_peer)])

    def across(g):
        nexts, sib = state[g]
        for copy in nexts:
            copy.wait_recv()
        lent = region(g, "lend", slice(None), slice(None))
        twin = [send(lent, lent, sem_x, (g,), twin_peer)]
        for i in range(1, inner):
            column = region(g, "own", slice(None), lax.rem(b + i, inner))
            sib.append(send(column, column, sem_s, (g, i), core_peer))
        state[g] = (twin, sib)

    def beside(g):
        twin, sib = state[g]
        for copy in twin:
            copy.wait_recv()
        lent = region(g, "borrow", slice(None), slice(None))
        sib.append(send(lent, lent, sem_s, (g, inner), core_peer))
        state[g] = sib

    def whole(g):
        for copy in state[g]:
            copy.wait_recv()

    def chunk_of(n):
        return slice(n * TILE, (n + 1) * TILE)

    def flat(v):
        return v.reshape(rows_c, WIDTH)

    def wide(v):
        return v.reshape(frames, TILE, WIDTH)

    def row(index):
        return table[index : index + 1, :]

    def gain(l):
        return row(BASE + 3 + OWNED + l), row(BASE + 3 + 2 * OWNED + l)

    def tap(l, k):
        at = start_of[l] + 2 * k
        return mb[at : at + 2].reshape(WIDTH, WIDTH).astype(BF16)

    def lin(j):
        at = time_at + 2 * j
        return mb[at : at + 2].reshape(WIDTH, WIDTH).astype(BF16)

    def group_sum(v):
        return lax.dot_general(v, group, (((1,), (0,)), ((), ())), precision=HIGH, preferred_element_type=F32)

    def loop(body, moves=()):
        for n in range(max(chunks, len(moves))):
            if n < len(moves):
                for act, g in moves[n]:
                    act(g)
            if n < chunks:
                body(n)

    def pass_one(l, n, x):
        at = chunk_of(n)
        xin[l, KERNEL // 2 : KERNEL // 2 + frames, at, :] = wide(x).astype(BF16)
        p = None
        for k in range(KERNEL):
            term = dot(flat(xin[l, k : k + frames, at, :]), tap(l, k))
            p = term if p is None else p + term
        p = wide(p + row(BASE + 3 + l))
        xhat[l, :, at, :] = p
        total = jnp.sum(p, axis=0)
        s_one[at, :] = total
        off = p - (total * (1.0 / frames))[None]
        s_two[at, :] = jnp.sum(off * off, axis=0)

    def stats(l):
        total = s_one[...]
        centre = group_sum(total) * part
        off = total * (1.0 / frames) - centre
        var = group_sum(s_two[...] + frames * off * off) * part
        scale = lax.rsqrt(var + NORM_EPS)
        mean[...] = centre
        rstd[l] = scale
        xsum[l] = frames * off * scale

    def normed(l, n):
        at = chunk_of(n)
        x = (xhat[l, :, at, :] - mean[at, :][None]) * rstd[l, at, :][None]
        xhat[l, :, at, :] = x
        g, s = gain(l)
        return x, x * g + s

    def pass_a(n, dm, x, v, pieces):
        at = chunk_of(n)
        slope = dm * mish_slope(v, *pieces)
        dy[:, at, :] = slope
        q_one[at, :] = jnp.sum(slope, axis=0)
        q_two[at, :] = jnp.sum(slope * x, axis=0)

    def pass_a_load(l, n, dm):
        x = xhat[l, :, chunk_of(n), :]
        g, s = gain(l)
        v = x * g + s
        pass_a(n, dm, x, v, mish_parts(v))

    def stats_back(l):
        g, s = gain(l)
        one, two = q_one[...], q_two[...]
        vec_o[BASE + 3 + OWNED + l : BASE + 4 + OWNED + l, :] = jnp.sum(two, axis=0, keepdims=True)
        vec_o[BASE + 3 + 2 * OWNED + l : BASE + 4 + 2 * OWNED + l, :] = jnp.sum(one, axis=0, keepdims=True)
        sums = group_sum(jnp.concatenate([one * g, two * g], axis=0)) * part
        first, second = sums[:trajs], sums[trajs:]
        g_one[...] = first
        g_two[...] = second
        dc = rstd[l] * (one * g - frames * first - xsum[l] * second)
        vec_o[BASE + 3 + l : BASE + 4 + l, :] = jnp.sum(dc, axis=0, keepdims=True)

    build(0)
    build(1)
    build(2)
    vec_o[...] = jnp.zeros_like(vec_o)
    edge = jnp.zeros((OWNED, KERNEL // 2, trajs, WIDTH), BF16)
    xin[:, : KERNEL // 2] = edge
    xin[:, KERNEL // 2 + frames :] = edge
    dp[: KERNEL // 2] = edge[0]
    dp[KERNEL // 2 + frames :] = edge[0]
    acc[...] = jnp.zeros_like(acc)
    total = inverse_o.shape[0]
    slot = lax.broadcasted_iota(jnp.int32, (total, UNITS), 0)
    unit = lax.broadcasted_iota(jnp.int32, (total, UNITS), 1).astype(F32)
    inverse_o[...] = jnp.min(jnp.where(slot == owners[...], unit, float(UNITS)), axis=1, keepdims=True).astype(jnp.int32)
    stepid = lax.broadcasted_iota(jnp.int32, (32, trajs), 0)
    picked = mm(times[...], (stepid == steps[...]).astype(F32))
    emb = picked[:TDIM].astype(BF16)
    keep, add = picked[TDIM : TDIM + 1], picked[TDIM + 1 : TDIM + 2]
    for f in range(frames):
        at = slice(f * trajs, (f + 1) * trajs)
        raw = noise[:, f, :]
        noise_t[:, at] = raw
        noisy_t[:, at] = (keep * traj[:, f, :] + add * raw).astype(BF16)
        mask_t[:, at] = valid[f : f + 1, :].astype(F32)
    along(0)
    build(3)
    along(1)
    build(4)
    across(0)
    along(2)
    build(5)
    across(1)
    along(3)
    build(6)
    beside(0)
    across(2)
    along(4)
    beside(1)
    whole(0)
    full = [mb[k].reshape(VROWS, WIDTH).astype(F32) for k in range(3)]
    table[...] = (full[0] + full[1]) + full[2]
    low[...] = full[0].astype(BF16)
    w_in, w_head = low[:FEAT, :], low[FEAT : 2 * FEAT, :]
    h[...] = (dot(noisy_t[...], w_in, 0, 0) + row(BASE)).reshape(frames, trajs, WIDTH)

    def enter(n):
        pass_one(0, n, flat(h[:, chunk_of(n), :]))

    loop(enter, [[], [(across, 3)], [(along, 5)], [(beside, 2)]])
    across(4)
    whole(1)
    pre_time = dot(emb, mb[time_at + 2 * BLOCKS].reshape(TDIM, WIDTH).astype(BF16), 0, 0) + row(BASE + 1)
    time_parts = mish_parts(pre_time)
    temb = (pre_time * time_parts[2]).astype(BF16)
    time_slope = mish_slope(pre_time, *time_parts)
    for j in range(BLOCKS):
        tb[j] = dot(temb, lin(j)) + row(BASE + 3 + 3 * OWNED + j)
    moves = [[[], [(along, 6), (beside, 3)], [(across, 5)], [(beside, 4)]], [[(across, 6)], [], [(beside, 5)], []], [[], [(beside, 6)]], [], []]
    for l in range(OWNED - 1):
        stats(l)
        whole(l + 2)

        def forward(n, l=l):
            at = chunk_of(n)
            _, v = normed(l, n)
            m = v * mish_parts(v)[2]
            if l % 2 == 0:
                m = m + tb[l // 2, at, :][None]
            else:
                m = h[:, at, :] + m
                if l == 1:
                    skip[:, at, :] = m
                if l == 2 * BLOCKS - 3:
                    m = m + skip[:, at, :]
                h[:, at, :] = m
            pass_one(l + 1, n, flat(m))

        loop(forward, moves[l])
    stats(OWNED - 1)
    head_bias = table[BASE + 2 : BASE + 3, :]

    def settle(n):
        at = chunk_of(n)
        _, v = normed(OWNED - 1, n)
        dp[KERNEL // 2 : KERNEL // 2 + frames, at, :] = (h[:, at, :] + v * mish_parts(v)[2]).astype(BF16)

    loop(settle)
    top = dp[KERNEL // 2 : KERNEL // 2 + frames].reshape(rows, WIDTH)
    pick = lax.broadcasted_iota(jnp.int32, (FEAT, WIDTH), 0) == lax.broadcasted_iota(jnp.int32, (FEAT, WIDTH), 1)
    bias = jnp.sum(jnp.where(pick, head_bias, 0.0), axis=1, keepdims=True)
    err = dot(w_head, top, 1, 1) + bias - noise_t[...]
    weighted = mask_t[...] * err
    loss = jnp.sum(jnp.sum(weighted * err, axis=0, keepdims=True), axis=1, keepdims=True)
    count = FEAT * jnp.sum(mask_t[...], axis=1, keepdims=True)
    rowid = lax.broadcasted_iota(jnp.int32, (8, LANES), 0)
    loss_o[...] = jnp.where(rowid == 0, loss, jnp.where(rowid == 1, count, 0.0))
    grad = 2.0 * weighted
    g_bias = jnp.sum(grad, axis=1, keepdims=True)
    vec_o[BASE + 2 : BASE + 3, :] = jnp.sum(jnp.where(pick, g_bias, 0.0), axis=0, keepdims=True)
    dpl[...] = grad.astype(BF16)
    vec_o[FEAT : 2 * FEAT, :] = dot(dpl[...], top)
    d[...] = dot(dpl[...], w_head, 0, 0).reshape(frames, trajs, WIDTH)

    def turn(n):
        pass_a_load(OWNED - 1, n, d[:, chunk_of(n), :])

    loop(turn)
    for l in reversed(range(OWNED)):
        stats_back(l)

        def backward(n, l=l):
            g, s = gain(l)
            at = chunk_of(n)
            x = xhat[l, :, at, :]
            back = rstd[l, at, :][None] * (dy[:, at, :] * g - g_one[at, :][None] - x * g_two[at, :][None])
            dp[KERNEL // 2 : KERNEL // 2 + frames, at, :] = back.astype(BF16)
            dx = None
            for k in range(KERNEL):
                shift = KERNEL - 1 - k
                term = dot(flat(dp[shift : shift + frames, at, :]), tap(l, k), 1, 1)
                dx = term if dx is None else dx + term
            dx = wide(dx)
            if l % 2 == 1:
                dtb[l // 2, at, :] = jnp.sum(dx, axis=0)
                pass_a_load(l - 1, n, dx)
            else:
                dx = d[:, at, :] + dx
                if l == OWNED - 2:
                    dskip[:, at, :] = dx
                if l == 2:
                    dx = dx + dskip[:, at, :]
                d[:, at, :] = dx
                if l > 0:
                    pass_a_load(l - 1, n, dx)

        loop(backward)
        xt[...] = xin[l, KERNEL // 2 : KERNEL // 2 + frames].reshape(rows, WIDTH).T
        for k in range(KERNEL):
            shift = KERNEL - 1 - k
            w_grad = dot(xt[...], dp[shift : shift + frames].reshape(rows, WIDTH))
            for half in range(2):
                mat_o[taps * l + 2 * k + half] = w_grad[half * LANES : (half + 1) * LANES].astype(mat_o.dtype)

    d_in = d[...].reshape(rows, WIDTH)
    vec_o[BASE : BASE + 1, :] = jnp.sum(d_in, axis=0, keepdims=True)
    vec_o[:FEAT, :] = dot(noisy_t[...], d_in.astype(BF16))
    d_temb = None
    for j in range(BLOCKS):
        grads = dtb[j]
        vec_o[BASE + 3 + 3 * OWNED + j : BASE + 4 + 3 * OWNED + j, :] = jnp.sum(grads, axis=0, keepdims=True)
        grads = grads.astype(BF16)
        t_grad = dot(temb, grads, 0, 0)
        for half in range(2):
            mat_o[taps * OWNED + 2 * j + half] = t_grad[half * LANES : (half + 1) * LANES].astype(mat_o.dtype)
        term = dot(grads, lin(j), 1, 1)
        d_temb = term if d_temb is None else d_temb + term
    d_pre = d_temb * time_slope
    vec_o[BASE + 1 : BASE + 2, :] = jnp.sum(d_pre, axis=0, keepdims=True)
    mat_o[UNITS] = jnp.zeros((LANES, WIDTH), mat_o.dtype)
    mat_o[UNITS - 1] = dot(emb, d_pre.astype(BF16)).astype(mat_o.dtype)
    for copy in waits:
        copy.wait_send()


def net(traj, noise, steps, valid, mat, vec, owners, total, groups, shards):
    outer, inner = split_shard(shards)
    feats, frames, trajs = traj.shape
    rows = frames * trajs
    piece = mat.shape[1]
    lane = np.arange(WIDTH) // (WIDTH // GROUPS)
    gmat = jnp.asarray((lane[:, None] == lane[None, :]).astype(np.float32))
    times = jnp.asarray(time_table())
    wire = BF16 if (2 * piece) % TILE == 0 else F32
    vm = pl.BlockSpec(memory_space=pltpu.VMEM)
    f = jax.ShapeDtypeStruct
    big = pltpu.VMEM((frames, trajs, WIDTH), F32)
    small = pltpu.VMEM((trajs, WIDTH), F32)
    padded = frames + KERNEL - 1
    dma = pltpu.SemaphoreType.DMA
    count = len(gather_parts())
    return pl.pallas_call(
        functools.partial(net_kernel, trajs, frames, groups, outer, inner),
        out_shape=[f((UNITS + 1, LANES, WIDTH), BF16), f((VROWS, WIDTH), F32), f((8, LANES), F32), f((total, 1), jnp.int32)],
        in_specs=[vm] * 9,
        out_specs=[vm] * 4,
        scratch_shapes=[
            pltpu.VMEM((UNITS, piece, WIDTH), F32),
            pltpu.VMEM((piece, WIDTH), F32),
            pltpu.VMEM((UNITS + 3, 2 * piece, WIDTH), wire),
            pltpu.VMEM((UNITS + 3, outer, inner, 2 * piece, WIDTH), wire),
            pltpu.VMEM((OWNED, padded, trajs, WIDTH), BF16),
            pltpu.VMEM((OWNED, frames, trajs, WIDTH), F32),
            big, big, big, big, big,
            pltpu.VMEM((padded, trajs, WIDTH), BF16),
            pltpu.VMEM((VROWS, WIDTH), BF16),
            pltpu.VMEM((WIDTH, rows), BF16),
            small, small, small,
            pltpu.VMEM((OWNED, trajs, WIDTH), F32),
            pltpu.VMEM((OWNED, trajs, WIDTH), F32),
            small, small, small, small,
            pltpu.VMEM((BLOCKS, trajs, WIDTH), F32),
            pltpu.VMEM((BLOCKS, trajs, WIDTH), F32),
            pltpu.VMEM((feats, rows), BF16),
            pltpu.VMEM((feats, rows), F32),
            pltpu.VMEM((1, rows), F32),
            pltpu.VMEM((feats, rows), BF16),
            pltpu.VMEM((16, WIDTH), F32),
            pltpu.VMEM((VROWS, WIDTH), F32),
            dma((2, 4)), dma((2, count, outer - 1)), dma((2, count, max(inner - 1, 1))),
            dma((2, count, inner + 1)), dma((2, count)),
        ],
        compiler_params=pltpu.CompilerParams(collective_id=3, has_side_effects=True, vmem_limit_bytes=54 * 2**20),
        name="net",
    )(traj, noise, steps, valid, times, gmat, mat, vec, owners)


def body(
    trajectories,
    noise,
    timesteps,
    valid,
    owners,
    mat_weight,
    mat_ema,
    soap_first,
    soap_second,
    left_stat,
    right_stat,
    left_basis,
    right_basis,
    vec_weight,
    vec_first,
    vec_second,
    vec_ema,
):
    shards = lax.axis_size("shard")
    groups = lax.axis_size("dp")
    slots = soap_first.shape[0]
    mat_grad, vec_grad, scal, inverse = net(
        trajectories.transpose(2, 1, 0),
        noise.transpose(2, 1, 0),
        timesteps.reshape(1, -1),
        valid.T,
        mat_weight,
        vec_weight,
        owners.reshape(1, -1),
        shards * slots,
        groups,
        shards,
    )
    grads, grads_vec, scal, second, lnew, rnew, xl, xr, back = reduce_grads(
        inverse, mat_grad, vec_grad, scal, soap_first, soap_second, left_stat, right_stat, left_basis, right_basis, groups, shards
    )
    results = soap(
        owners, scal, grads, grads_vec, second, lnew, rnew, xl, xr, back,
        soap_first, mat_weight, mat_ema, vec_weight, vec_first, vec_second, vec_ema,
    )
    return tuple(x.reshape(()) for x in results[:3]) + tuple(results[3:])


def solution(mesh):
    placed = (
        P(("dp", "shard"), None, None),
        P(("dp", "shard"), None, None),
        P(("dp", "shard")),
        P(("dp", "shard"), None),
        P(),
        P(None, "shard", None),
        P(None, "shard", None),
        P("shard", None, None),
        P("shard", None, None),
        P("shard", None, None),
        P("shard", None, None),
        P("shard", None, None),
        P("shard", None, None),
        P("shard", None),
        P("shard", None),
        P("shard", None),
        P("shard", None),
    )
    return jax.shard_map(
        body,
        mesh=mesh,
        in_specs=placed,
        out_specs=(
            P(),
            P(),
            P(),
            P(None, "shard", None),
            P(None, "shard", None),
            P("shard", None, None),
            P("shard", None, None),
            P("shard", None, None),
            P("shard", None, None),
            P("shard", None, None),
            P("shard", None, None),
            P("shard", None),
            P("shard", None),
            P("shard", None),
            P("shard", None),
        ),
        check_vma=False,
    )
```

```python
import functools
import math

import jax
import jax.numpy as jnp
import numpy as np
from jax import lax
from jax.experimental import pallas as pl
from jax.experimental.pallas import tpu as pltpu
from jax.sharding import PartitionSpec as P

WIDTH = 256
KERNEL = 5
GROUPS = 8
TDIM = 128
FEAT = 23
BLOCKS = 3
DSTEPS = 20
STEP = 10
OWNED = 6
UNITS = 67
VROWS = 128

HIGH = lax.Precision.HIGHEST
BETA_ONE = 0.9
BETA_TWO = 0.95
ADAM_EPS = 1e-08
LEARN = 0.05
TABLE_LEARN = 0.25
DECAY = 0.01
CLIP = 0.05
EMA_RATE = 0.8
NORM_EPS = 1e-05
PANEL = 32
LANES = 128
PAD = 8
CHUNK = 8
TILE = 16
BASE = 2 * FEAT
F32 = jnp.float32
BF16 = jnp.bfloat16
MESH = pl.DeviceIdType.MESH


def mm(a, b, ca=1, cb=0):
    return lax.dot_general(a, b, (((ca,), (cb,)), ((), ())), precision=HIGH, preferred_element_type=F32)

def mm3(a, b, ca=1, cb=0):
    ah = a.astype(BF16)
    al = (a - ah.astype(F32)).astype(BF16)
    bh = b.astype(BF16)
    bl = (b - bh.astype(F32)).astype(BF16)
    d = (((ca,), (cb,)), ((), ()))

    def product(p, q):
        return lax.dot_general(p, q, d, preferred_element_type=F32)

    return product(ah, bh) + (product(ah, bl) + product(al, bh))


def split3(v):
    hi = v.astype(BF16)
    rest = v - hi.astype(F32)
    mid = rest.astype(BF16)
    last = (rest - mid.astype(F32)).astype(BF16)
    return hi, mid, last

def eliminate(held):
    lanes = lax.broadcasted_iota(jnp.int32, (8, LANES), 1)
    sub = lax.broadcasted_iota(jnp.int32, (8, LANES), 0)
    tall = PANEL // 8

    def lane(v, k):
        return jnp.broadcast_to(v[:, k : k + 1], (8, LANES))

    def combine(x0, x1, x2, x3, l10, l20, l30, l21, l31, l32):
        x1 = x1 - l10 * x0
        x2 = (x2 - l20 * x0) - l21 * x1
        x3 = ((x3 - l30 * x0) - l31 * x1) - l32 * x2
        return x0, x1, x2, x3

    for k in range(0, PANEL, 4):
        top, r = k // 8, k % 8
        for e in held:
            rows = [jnp.broadcast_to(e[top][r + i : r + i + 1, :], (8, LANES)) for i in range(4)]
            p = {(i, j): lane(rows[i], k + j) for i in range(4) for j in range(i, 4)}
            d0 = pl.reciprocal(p[0, 0])
            l10, l20, l30 = p[0, 1] * d0, p[0, 2] * d0, p[0, 3] * d0
            d1 = pl.reciprocal(p[1, 1] - p[0, 1] * l10)
            s12, s13 = p[1, 2] - p[0, 2] * l10, p[1, 3] - p[0, 3] * l10
            l21, l31 = s12 * d1, s13 * d1
            d2 = pl.reciprocal((p[2, 2] - p[0, 2] * l20) - s12 * l21)
            t23 = (p[2, 3] - p[0, 3] * l20) - s13 * l21
            l32 = t23 * d2
            d3 = pl.reciprocal(((p[3, 3] - p[0, 3] * l30) - s13 * l31) - t23 * l32)
            lower = (l10, l20, l30, l21, l31, l32)
            rows = combine(*rows, *lower)
            by = [x * y for x, y in zip(rows, (d0, d1, d2, d3))]
            for v in range(top, tall):
                columns = combine(*[lane(e[v], k + j) for j in range(4)], *lower)
                less = e[v]
                for x, y in zip(columns, by):
                    less = less - x * y
                if v == top:
                    kept = jnp.where(sub == r + 1, rows[1], e[v])
                    kept = jnp.where(sub == r + 2, rows[2], kept)
                    kept = jnp.where(sub == r + 3, rows[3], kept)
                    less = jnp.where(sub > r + 3, less, kept) if r == 0 else kept
                e[v] = less
    results = []
    for e in held:
        parts = []
        for v in range(tall):
            pivots = jnp.sum(jnp.where(lanes == sub + 8 * v, e[v], 0.0), axis=1, keepdims=True)
            parts.append(e[v] * lax.rsqrt(pivots))
        results.append(jnp.concatenate(parts, axis=0)[:, PANEL : 2 * PANEL])
    return results


def factor_panels(chains, start):
    rows = lax.broadcasted_iota(jnp.int32, (PANEL, LANES), 0)
    lanes = lax.broadcasted_iota(jnp.int32, (PANEL, LANES), 1)
    unit = jnp.where(lanes - PANEL == rows, 1.0, 0.0).astype(F32)
    shift = lax.rem(LANES - start, LANES)
    at = pl.ds(start, PANEL)
    held = []
    for z, out, s in chains:
        block = jnp.where(lanes < PANEL, pltpu.roll(z[s, at, :LANES], shift, 1), unit)
        held.append([block[8 * v : 8 * v + 8] for v in range(PANEL // 8)])
    panels = [mm(inverse, z[s, at, :]) for (z, out, s), inverse in zip(chains, eliminate(held))]
    for (z, out, s), done in zip(chains, panels):
        out[s, at, :] = done[:, LANES:]
    for (z, out, s), done in zip(chains, panels):
        hi, mid, last = split3(done)
        lhs = jnp.concatenate([hi, hi, mid, hi, last, mid], axis=0)[:, :LANES]
        rhs = jnp.concatenate([hi, mid, hi, last, hi, mid], axis=0)
        z[s] = z[s] - lax.dot_general(lhs, rhs, (((0,), (0,)), ((), ())), preferred_element_type=F32)


def factor_all(chains):
    def step(p, carry):
        factor_panels(chains, pl.multiple_of(p * PANEL, PANEL))
        return carry

    lax.fori_loop(0, LANES // PANEL, step, 0)


def split_shard(shards):
    return 4, shards // 8


def place(outer, inner):
    s = lax.axis_index("shard")
    return s // (2 * inner), lax.rem(s // 2, inner), lax.rem(s, 2)


def spot(inner, a, b, c):
    return (a * inner + b) * 2 + c


def greet(peers):
    barrier = pltpu.get_barrier_semaphore()
    for peer in peers:
        pl.semaphore_signal(barrier, inc=1, device_id=peer, device_id_type=MESH)
    pl.semaphore_wait(barrier, len(peers))


def reduce_kernel(groups, outer, inner, slots, shards, inverse, grad, vec, scal, m_h, v_h, ls_h, rs_h, lb_h, rb_h,
                  grad_o, vec_o, scal_o, second_o, lnew_o, rnew_o, xl_o, xr_o, back_o,
                  held, r_in_a, sum_a, r_dp_a, r_dp_b, sum_b, r_in_b, ready, r_out, final, landed, sc, turn, norms, sent, got,
                  w_core, w_in, w_dp, w_out, w_sum, m, v, ls, rs, lb, rb,
                  sem_in_a, sem_dp_a, sem_dp_b, sem_in_b, sem_out, sem_fin, sem_sc, sem_n, sem_u, sem_h):
    d = lax.axis_index("dp")
    a, b, c = place(outer, inner)
    me = lax.axis_index("shard")
    rows = slots * LANES
    half = rows // 2
    piece = half // groups
    core_peer = (d, spot(inner, a, b, 1 - c))
    in_peers = [(d, spot(inner, a, lax.rem(b + i, inner), c)) for i in range(1, inner)]
    dp_peers = [(lax.rem(d + i, groups), me) for i in range(1, groups)]
    out_peers = [(d, spot(inner, lax.rem(a + i, outer), b, c)) for i in range(1, outer)]
    peers = [(d, lax.rem(me + i, shards)) for i in range(1, shards)]
    far = [(lax.rem(d + k, groups), lax.rem(me + i, shards)) for k in range(1, groups) for i in range(shards)]
    pulls = [pltpu.make_async_copy(src, dst, sem_h.at[k])
             for k, (src, dst) in enumerate(((lb_h, lb), (rb_h, rb), (m_h, m), (v_h, v), (ls_h, ls), (rs_h, rs)))]
    for copy in pulls:
        copy.start()
    greet(peers + far)
    waits = []

    def send(src, dst, sems, index, peer):
        copy = pltpu.make_async_remote_copy(
            src_ref=src, dst_ref=dst, send_sem=sems.at[(0,) + index], recv_sem=sems.at[(1,) + index],
            device_id=peer, device_id_type=MESH)
        copy.start()
        waits.append(copy)
        return copy

    def load(aa, bb):
        first = spot(inner, aa, bb, 0) * slots
        return jnp.concatenate([grad[inverse[first + s, 0]] for s in range(2 * slots)], axis=0)

    order = [lax.rem(a + i, outer) for i in range(1, outer + 1)]
    sc[0, c] = scal[...]
    small = [send(sc.at[0, c], sc.at[0, c], sem_sc, (0, 0), core_peer),
             send(vec.at[:, :, 1 - c], w_core, sem_sc, (0, 3), core_peer)]
    in_a, dp_b, dp_a, in_b, out = {}, {}, {}, {}, {}

    def first_hop(i):
        for j in range(inner):
            at = i * inner + j
            held[at] = load(order[i], j)
        in_a[i] = [send(held.at[i * inner + lax.rem(b + k, inner), pl.ds(0, half)], r_in_a.at[i, k - 1], sem_in_a, (i, k - 1), in_peers[k - 1])
                   for k in range(1, inner)]
        dp_b[i] = [send(held.at[i * inner + j, pl.ds(pl.multiple_of(half + lax.rem(d + k, groups) * piece, TILE), piece)],
                        r_dp_b.at[i, j, k - 1], sem_dp_b, (i, j, k - 1), dp_peers[k - 1])
                   for k in range(1, groups) for j in range(inner)]

    def second_hop(i):
        for copy in in_a[i]:
            copy.wait_recv()
        total = held[i * inner + b, pl.ds(0, half)].astype(F32)
        for k in range(inner - 1):
            total = total + r_in_a[i, k].astype(F32)
        sum_a[i] = total.astype(BF16)
        dp_a[i] = [send(sum_a.at[i, pl.ds(pl.multiple_of(lax.rem(d + k, groups) * piece, TILE), piece)], r_dp_a.at[i, k - 1], sem_dp_a, (i, k - 1), dp_peers[k - 1])
                   for k in range(1, groups)]
        for copy in dp_b[i]:
            copy.wait_recv()
        for j in range(inner):
            total = held[i * inner + j, pl.ds(pl.multiple_of(half + d * piece, TILE), piece)].astype(F32)
            for k in range(groups - 1):
                total = total + r_dp_b[i, j, k].astype(F32)
            sum_b[i * inner + j] = total.astype(BF16)
        in_b[i] = [send(sum_b.at[i * inner + lax.rem(b + k, inner)], r_in_b.at[i, k - 1], sem_in_b, (i, k - 1), in_peers[k - 1])
                   for k in range(1, inner)]

    def third_hop(i):
        for copy in dp_a[i] + in_b[i]:
            copy.wait_recv()
        first = sum_a[i, pl.ds(pl.multiple_of(d * piece, TILE), piece)].astype(F32)
        for k in range(groups - 1):
            first = first + r_dp_a[i, k].astype(F32)
        second = sum_b[i * inner + b].astype(F32)
        for k in range(inner - 1):
            second = second + r_in_b[i, k].astype(F32)
        ready[i, 0:piece] = first.astype(BF16)
        ready[i, piece : 2 * piece] = second.astype(BF16)
        if i < outer - 1:
            out[i] = send(ready.at[i], r_out.at[i], sem_out, (i,), out_peers[i])

    def gathered(level, count):
        for copy in small:
            copy.wait_recv()
        total = sc[level, 0]
        for k in range(1, count):
            total = total + sc[level, k]
        return total

    first_hop(0)
    first_hop(1)
    total = gathered(0, 2)
    sc[1, b] = total
    w_sum[0] = vec[:, :, c] + w_core[...]
    small = [send(sc.at[1, b], sc.at[1, b], sem_sc, (1, k), p) for k, p in enumerate(in_peers)]
    small += [send(w_sum.at[0, :, lax.rem(b + k, inner)], w_in.at[k - 1], sem_sc, (1, 2 + k), in_peers[k - 1]) for k in range(1, inner)]
    second_hop(0)
    for i in range(2, outer):
        first_hop(i)
        second_hop(i - 1)
        third_hop(i - 2)
    total = gathered(1, inner)
    sc[2, d] = total
    summed = w_sum[0, :, b]
    for k in range(inner - 1):
        summed = summed + w_in[k]
    w_dp[d] = summed
    small = [send(sc.at[2, d], sc.at[2, d], sem_sc, (2, k), p) for k, p in enumerate(dp_peers)]
    small += [send(w_dp.at[d], w_dp.at[d], sem_sc, (2, 3 + k), p) for k, p in enumerate(dp_peers)]
    second_hop(outer - 1)
    third_hop(outer - 2)
    for copy in pulls:
        copy.wait()
    for s in range(slots):
        second_o[s] = mm3(mm3(lb[s], m[s], 0, 0), rb[s])
    total = gathered(2, groups)
    sc[3, a] = total
    summed = w_dp[0]
    for k in range(1, groups):
        summed = summed + w_dp[k]
    w_sum[1, :, 0] = summed
    small = [send(sc.at[3, a], sc.at[3, a], sem_sc, (3, k), p) for k, p in enumerate(out_peers)]
    small += [send(w_sum.at[1, lax.rem(a + k, outer), 0], w_out.at[k - 1], sem_sc, (3, 2 + k), out_peers[k - 1]) for k in range(1, outer)]
    third_hop(outer - 1)
    total = ready[outer - 1].astype(F32)
    for i in range(outer - 1):
        out[i].wait_recv()
        total = total + r_out[i].astype(F32)
    mine = total.astype(BF16)
    final[0] = mine[:piece]
    final[1] = mine[piece:]
    near = [(k, flip) for k in range(groups) for flip in range(2) if k or flip]
    last = []
    for n, (k, flip) in enumerate(near):
        core = lax.rem(c + flip, 2)
        target = (lax.rem(d + k, groups), spot(inner, a, b, core))
        last.append(send(final.at[core], landed.at[c, d], sem_fin, (n,), target))
    landed[c, d] = final[c]
    counts = gathered(3, outer)
    scale = 1.0 / counts[1:2, 0:1]
    table = w_sum[1, a, 0]
    for k in range(outer - 1):
        table = table + w_out[k]
    table = table * scale
    total = mine.astype(F32) * scale
    squares = jnp.sum(total * total) + jnp.where(d == 0, jnp.sum(table * table), 0.0)
    place_n = d * shards + me
    norms[place_n] = jnp.full((8, LANES), squares, F32)
    moves = [send(norms.at[place_n], norms.at[place_n], sem_n, (k,), p) for k, p in enumerate(peers + far)]
    for copy in last:
        copy.wait_recv()
    halves = [jnp.concatenate([landed[q, k] for k in range(groups)], axis=0).astype(F32) * scale for q in range(2)]
    quarter = LANES // 2
    for s in range(slots):
        slot = jnp.concatenate([halves[q][s * quarter : (s + 1) * quarter] for q in range(2)], axis=0)
        grad_o[s] = slot
        turn[s] = mm3(mm3(lb[s], slot, 0, 0), rb[s])
    for copy in moves:
        copy.wait_recv()
    total = norms[0]
    for k in range(1, groups * shards):
        total = total + norms[k]
    norm = jnp.sqrt(total)
    factor = jnp.minimum(1.0, CLIP / (norm + 1e-06))
    rowid = lax.broadcasted_iota(jnp.int32, (8, LANES), 0)
    scal_o[...] = jnp.where(rowid == 2, norm, counts)
    scale = factor[0:1, 0:1]
    vec_o[...] = table * scale
    for s in range(slots):
        turned = turn[s] * scale
        moment = BETA_ONE * second_o[s] + (1.0 - BETA_ONE) * turned
        second = BETA_TWO * v[s] + (1.0 - BETA_TWO) * turned * turned
        second_o[s] = second
        normed = moment / (1.0 - BETA_ONE**STEP) / (jnp.sqrt(second / (1.0 - BETA_TWO**STEP)) + ADAM_EPS)
        turn[s] = mm3(mm3(lb[s], normed), rb[s], 1, 1)
    width = back_o.shape[1]
    used = slots * width
    full = sent.shape[1]
    for t in range(shards):
        parts = [turn[s, t * width : (t + 1) * width, :] for s in range(slots)]
        if full > used:
            parts.append(jnp.zeros((full - used, WIDTH), F32))
        sent[t] = jnp.concatenate(parts, axis=0).astype(BF16)
    got[me] = sent[me]
    moves = [send(sent.at[p[1]], got.at[me], sem_u, (k,), p) for k, p in enumerate(peers)]
    for s in range(slots):
        slot = grad_o[s] * scale
        grad_o[s] = slot
        lnew = BETA_TWO * ls[s] + (1.0 - BETA_TWO) * mm3(slot, slot, 1, 1)
        rnew = BETA_TWO * rs[s] + (1.0 - BETA_TWO) * mm3(slot, slot, 0, 0)
        lnew_o[s] = lnew
        rnew_o[s] = rnew
        xl_o[s] = mm3(lb[s], lnew, 0, 1)
        xr_o[s] = mm3(rb[s], rnew, 0, 1)
    for copy in moves:
        copy.wait_recv()
    for t in range(shards):
        rows_t = got[t].astype(F32)
        for s in range(slots):
            back_o[t * slots + s] = rows_t[s * width : (s + 1) * width]
    for copy in waits:
        copy.wait_send()


def reduce_grads(inverse, grad, vec, scal, m, v, ls, rs, lb, rb, groups, shards):
    outer, inner = split_shard(shards)
    slots = m.shape[0]
    width = LANES // shards
    full = -(-slots * width // TILE) * TILE
    rows = slots * LANES
    half = rows // 2
    piece = half // groups
    f = jax.ShapeDtypeStruct
    vm = pl.BlockSpec(memory_space=pltpu.VMEM)
    sm = pl.BlockSpec(memory_space=pltpu.SMEM)
    both = outer * inner
    table = vec.reshape(outer, inner, 2, width, WIDTH)

    def buf(*shape):
        return pltpu.VMEM(shape + (WIDTH,), BF16)

    def wide(*shape):
        return pltpu.VMEM(shape + (WIDTH,), F32)

    dma = pltpu.SemaphoreType.DMA
    peers_in, peers_dp = max(inner - 1, 1), max(groups - 1, 1)
    outs = [f(m.shape, F32), f((width, WIDTH), F32), f((8, LANES), F32)]
    outs += [f(x.shape, F32) for x in (v, ls, rs, lb, rb)] + [f((shards * slots, width, WIDTH), F32)]
    return pl.pallas_call(
        functools.partial(reduce_kernel, groups, outer, inner, slots, shards),
        out_shape=outs,
        in_specs=[sm] + [vm] * 3 + [pl.BlockSpec(memory_space=pltpu.HBM)] * 6,
        out_specs=[vm] * 9,
        scratch_shapes=[
            buf(both, rows),
            buf(outer, peers_in, half), buf(outer, half), buf(outer, peers_dp, piece),
            buf(outer, inner, peers_dp, piece), buf(both, piece), buf(outer, peers_in, piece),
            buf(outer, 2 * piece), buf(outer - 1, 2 * piece), buf(2, piece), buf(2, groups, piece),
            pltpu.VMEM((4, 4, 8, LANES), F32),
            wide(slots, LANES), pltpu.VMEM((groups * shards, 8, LANES), F32), buf(shards, full), buf(shards, full),
            wide(outer, inner, width), wide(peers_in, outer, width), wide(groups, outer, width), wide(outer - 1, width),
            wide(2, outer, inner, width),
            *[pltpu.VMEM(x.shape, F32) for x in (m, v, ls, rs, lb, rb)],
            dma((2, outer, peers_in)), dma((2, outer, peers_dp)), dma((2, outer, inner, peers_dp)),
            dma((2, outer, peers_in)), dma((2, outer - 1)), dma((2, 2 * groups - 1)), dma((2, 4, 6)),
            dma((2, groups * shards - 1)), dma((2, shards - 1)), dma((6,)),
        ],
        compiler_params=pltpu.CompilerParams(collective_id=1, has_side_effects=True, vmem_limit_bytes=36 * 2**20),
        name="reduce",
    )(inverse, grad, table, scal, m, v, ls, rs, lb, rb)


def soap_kernel(slots, owners, scal, g, gvec, second, lnew, rnew, xl, xr, back, m, mat, ema, vw, vf, vs, ve,
                loss_o, count_o, norm_o, mat_h, ema_h, m_h, v_h, ls_h, rs_h, lb_o, rb_o, vw_o, vf_o, vs_o, ve_o, zl, ol, zw, ow, xa, mat_o, ema_o, m_o, sem):
    outs = [pltpu.make_async_copy(src, dst, sem.at[k])
            for k, (src, dst) in enumerate(((second, v_h), (lnew, ls_h), (rnew, rs_h), (mat_o, mat_h), (ema_o, ema_h), (m_o, m_h)))]
    for copy in outs[:3]:
        copy.start()
    loss_o[...] = scal[0:1, 0:1]
    count_o[...] = scal[1:2, 0:1]
    norm_o[...] = scal[2:3, 0:1]
    eye = (lax.broadcasted_iota(jnp.int32, (LANES, LANES), 0) == lax.broadcasted_iota(jnp.int32, (LANES, LANES), 1)).astype(F32)
    for s in range(slots):
        zl[s, :, :LANES] = mm(xl[s], xl[s], 1, 1)
        zl[s, :, LANES:] = xl[s]
        gram = mm(xr[s], xr[s], 1, 1)
        zw[s, :, :LANES] = gram[:LANES, :LANES]
        zw[s, :, LANES:] = eye
        xa[s, :LANES, :LANES] = gram[:LANES, LANES:]
        xa[s, LANES:, :LANES] = gram[LANES:, LANES:]
        xa[s, :, LANES:] = xr[s]
    for s in range(slots):
        m_o[s] = BETA_ONE * m[s] + (1.0 - BETA_ONE) * g[s]
    for unit in range(UNITS):
        new = mat[unit] * (1.0 - LEARN * DECAY) - LEARN * back[owners[unit]]
        mat_o[unit] = new
        ema_o[unit] = EMA_RATE * ema[unit] + (1.0 - EMA_RATE) * new
    for copy in outs[3:]:
        copy.start()
    factor_all([(zw, ow, s) for s in range(slots)] + [(zl, ol, s) for s in range(slots)])
    for s in range(slots):
        lb_o[s] = ol[s].T
        done = mm(ow[s], xa[s, :LANES, :])
        rb_o[s, :, :LANES] = done[:, LANES:].T
        rest = xa[s, LANES:, :] - mm(done[:, :LANES], done, 0, 0)
        zw[s, :, :LANES] = rest[:, :LANES]
        zw[s, :, LANES:] = eye
        xa[s, LANES:, :] = rest
    factor_all([(zw, ow, s) for s in range(slots)])
    for s in range(slots):
        rb_o[s, :, LANES:] = mm(ow[s], xa[s, LANES:, LANES:]).T
    grad = gvec[...]
    first = BETA_ONE * vf[...] + (1.0 - BETA_ONE) * grad
    moment = BETA_TWO * vs[...] + (1.0 - BETA_TWO) * grad * grad
    step = first / (1.0 - BETA_ONE**STEP) / (jnp.sqrt(moment / (1.0 - BETA_TWO**STEP)) + ADAM_EPS)
    new = vw[...] * (1.0 - TABLE_LEARN * DECAY) - TABLE_LEARN * step
    vf_o[...] = first
    vs_o[...] = moment
    vw_o[...] = new
    ve_o[...] = EMA_RATE * ve[...] + (1.0 - EMA_RATE) * new
    for copy in outs:
        copy.wait()


def soap(owners, scal, g, gvec, second, lnew, rnew, xl, xr, back, m, mat, ema, vw, vf, vs, ve):
    slots = g.shape[0]
    f = jax.ShapeDtypeStruct
    vm = pl.BlockSpec(memory_space=pltpu.VMEM)
    outs = [f((1, 1), F32)] * 3 + [f(x.shape, F32) for x in (mat, ema, m, second, lnew, rnew, xl, xr, vw, vf, vs, ve)]
    return pl.pallas_call(
        functools.partial(soap_kernel, slots),
        out_shape=outs,
        in_specs=[pl.BlockSpec(memory_space=pltpu.SMEM)] + [vm] * 16,
        out_specs=[vm] * 3 + [pl.BlockSpec(memory_space=pltpu.HBM)] * 6 + [vm] * 6,
        scratch_shapes=[
            pltpu.VMEM((slots, LANES, 2 * LANES), F32),
            pltpu.VMEM((slots, LANES, LANES), F32),
            pltpu.VMEM((slots, LANES, 2 * LANES), F32),
            pltpu.VMEM((slots, LANES, LANES), F32),
            pltpu.VMEM((slots, 2 * LANES, 3 * LANES), F32),
            pltpu.VMEM(mat.shape, F32),
            pltpu.VMEM(mat.shape, F32),
            pltpu.VMEM(m.shape, F32),
            pltpu.SemaphoreType.DMA((6,)),
        ],
        compiler_params=pltpu.CompilerParams(vmem_limit_bytes=30 * 2**20),
        name="soap",
    )(owners, scal, g, gvec, second, lnew, rnew, xl, xr, back, m, mat, ema, vw, vf, vs, ve)


def time_table():
    steps = np.arange(32, dtype=np.float32)
    halfway = TDIM // 2
    freqs = np.exp(-math.log(10000.0) * np.arange(halfway, dtype=np.float32) / (halfway - 1)).astype(np.float32)
    angles = (freqs[:, None] * steps[None, :]).astype(np.float32)
    offset = 0.008
    ratio = (steps + 1.0) / DSTEPS
    upper = np.cos((ratio + offset) / (1.0 + offset) * math.pi / 2) ** 2
    level = upper / math.cos(offset / (1.0 + offset) * math.pi / 2) ** 2
    level = np.clip(np.where(steps < DSTEPS, level, 0.0), 0.0, 1.0)
    levels = np.stack([np.sqrt(level), np.sqrt(1.0 - level)] + [np.zeros(32)] * 6)
    return np.concatenate([np.sin(angles), np.cos(angles), levels]).astype(np.float32)


def dot(a, b, ca=1, cb=0):
    return lax.dot_general(a, b, (((ca,), (cb,)), ((), ())), preferred_element_type=F32)


def mish_parts(v):
    e = jnp.exp(jnp.minimum(v, 20.0))
    n = e * (e + 2.0)
    r = pl.reciprocal(n + 2.0)
    return e, r, n * r


def mish_slope(v, e, r, t):
    return t + v * (4.0 * e * (e + 1.0)) * (r * r)


def gather_parts():
    taps = 2 * KERNEL
    bounds = [3, 3 + taps, UNITS + 3 - (OWNED - 1) * taps]
    while bounds[-1] < UNITS + 3:
        bounds.append(bounds[-1] + taps)
    return [(0, bounds[1])] + list(zip(bounds[1:-1], bounds[2:]))


def net_kernel(trajs, frames, groups, outer, inner, traj, noise, steps, valid, times, gmat, mat, vec, owners, mat_o, vec_o, loss_o, inverse_o,
               other, other_vec, shares_g, theirs, stage, mb, xin, xhat, h, skip, d, dskip, dy, dp, low, xt, s_one, s_two, mean, rstd, xsum, q_one, q_two,
               g_one, g_two, tb, dtb, noisy_t, noise_t, mask_t, dpl, acc, table, sem_c, sem_z, sem_y, sem_s, sem_x, sem_g):
    dpi = lax.axis_index("dp")
    a, b, c = place(outer, inner)
    piece = mat.shape[1]
    chunks = trajs // TILE
    rows_c = TILE * frames
    rows = trajs * frames
    taps = 2 * KERNEL
    part = 1.0 / (frames * (WIDTH // GROUPS))
    group = gmat[...]
    core_peer = (dpi, spot(inner, a, b, 1 - c))
    in_peers = [(dpi, spot(inner, a, lax.rem(b + i, inner), c)) for i in range(1, inner)]
    out_peers = [(dpi, spot(inner, lax.rem(a + i, outer), b, c)) for i in range(1, outer)]
    odd = lax.rem(dpi, 2)
    twin_peer = (dpi + 1 - 2 * odd, spot(inner, a, b, c))
    greet([core_peer, twin_peer] + in_peers + out_peers)
    waits = []

    def send(src, dst, sems, index, peer):
        copy = pltpu.make_async_remote_copy(
            src_ref=src, dst_ref=dst, send_sem=sems.at[(0,) + index], recv_sem=sems.at[(1,) + index],
            device_id=peer, device_id_type=MESH)
        copy.start()
        waits.append(copy)
        return copy

    spans = [(0, taps), (taps * OWNED, UNITS), (taps, taps * OWNED)]
    first_copies = [send(vec, other_vec, sem_c, (3,), core_peer)]
    for k, (lo, hi) in enumerate(spans):
        first_copies.append(send(mat.at[pl.ds(lo, hi - lo)], other.at[pl.ds(lo, hi - lo)], sem_c, (k,), core_peer))
    parts = gather_parts()
    start_of = [3 if l == 0 else parts[l + 1][0] for l in range(OWNED)]
    time_at = parts[1][0]
    shares = [(lo, hi - lo, (hi - lo) * 3 // 10) for lo, hi in parts]
    source = {0: 0, 1: taps * OWNED}
    for g in range(2, len(parts)):
        source[g] = taps * (g - 1)
    cols = pl.ds(pl.multiple_of(c * LANES, LANES), LANES)
    state = {}

    def chip_rows(mine, theirs):
        upper = jnp.where(c == 0, mine, theirs)
        lower = jnp.where(c == 0, theirs, mine)
        return jnp.concatenate([upper, lower], axis=mine.ndim - 2)

    def region(g, kind, at_a, at_b):
        lo, count, side = shares[g]
        both = count - side
        if kind == "own":
            start, size = lo + odd * side, both
        elif kind == "lend":
            start, size = lo + odd * both, side
        else:
            start, size = lo + (1 - odd) * both, side
        return mb.at[pl.ds(start, size), at_a, at_b, :, cols]

    def build(g):
        lo, count, side = shares[g]
        hi = lo + count
        if g == 0:
            first_copies[0].wait_recv()
            first_copies[1].wait_recv()
            rows_v = chip_rows(vec[...], other_vec[...])
            for k, value in enumerate(split3(rows_v)):
                stage[k] = value.astype(mb.dtype)
            count -= 3
        elif g == 1:
            first_copies[2].wait_recv()
        elif g == 2:
            first_copies[3].wait_recv()
        at = source[g]
        stage[hi - count : hi] = chip_rows(mat[at : at + count], other[at : at + count]).astype(BF16).astype(mb.dtype)
        both = hi - lo - side
        mine = region(g, "own", a, b)
        mine[...] = stage[pl.ds(lo + odd * side, both), :, cols]
        state[g] = [send(mine, mine, sem_z, (g, k), p) for k, p in enumerate(out_peers)]

    def along(g):
        for copy in state[g]:
            copy.wait_recv()
        column = region(g, "own", slice(None), b)
        nexts = [send(column, column, sem_y, (g, k), p) for k, p in enumerate(in_peers)]
        state[g] = (nexts, [send(column, column, sem_s, (g, 0), core_peer)])

    def across(g):
        nexts, sib = state[g]
        for copy in nexts:
            copy.wait_recv()
        lent = region(g, "lend", slice(None), slice(None))
        twin = [send(lent, lent, sem_x, (g,), twin_peer)]
        for i in range(1, inner):
            column = region(g, "own", slice(None), lax.rem(b + i, inner))
            sib.append(send(column, column, sem_s, (g, i), core_peer))
        state[g] = (twin, sib)

    def beside(g):
        twin, sib = state[g]
        for copy in twin:
            copy.wait_recv()
        lent = region(g, "borrow", slice(None), slice(None))
        sib.append(send(lent, lent, sem_s, (g, inner), core_peer))
        state[g] = sib

    def whole(g):
        for copy in state[g]:
            copy.wait_recv()

    def chunk_of(n):
        return slice(n * TILE, (n + 1) * TILE)

    def flat(v):
        return v.reshape(rows_c, WIDTH)

    def wide(v):
        return v.reshape(frames, TILE, WIDTH)

    def row(index):
        return table[index : index + 1, :]

    def gain(l):
        return row(BASE + 3 + OWNED + l), row(BASE + 3 + 2 * OWNED + l)

    def tap(l, k):
        at = start_of[l] + 2 * k
        return mb[at : at + 2].reshape(WIDTH, WIDTH).astype(BF16)

    def lin(j):
        at = time_at + 2 * j
        return mb[at : at + 2].reshape(WIDTH, WIDTH).astype(BF16)

    def group_sum(v):
        return lax.dot_general(v, group, (((1,), (0,)), ((), ())), precision=HIGH, preferred_element_type=F32)

    def loop(body, moves=()):
        for n in range(max(chunks, len(moves))):
            if n < len(moves):
                for act, g in moves[n]:
                    act(g)
            if n < chunks:
                body(n)

    def pass_one(l, n, x):
        at = chunk_of(n)
        xin[l, KERNEL // 2 : KERNEL // 2 + frames, at, :] = wide(x).astype(BF16)
        p = None
        for k in range(KERNEL):
            term = dot(flat(xin[l, k : k + frames, at, :]), tap(l, k))
            p = term if p is None else p + term
        p = wide(p + row(BASE + 3 + l))
        xhat[l, :, at, :] = p
        total = jnp.sum(p, axis=0)
        s_one[at, :] = total
        off = p - (total * (1.0 / frames))[None]
        s_two[at, :] = jnp.sum(off * off, axis=0)

    def stats(l):
        total = s_one[...]
        centre = group_sum(total) * part
        off = total * (1.0 / frames) - centre
        var = group_sum(s_two[...] + frames * off * off) * part
        scale = lax.rsqrt(var + NORM_EPS)
        mean[...] = centre
        rstd[l] = scale
        xsum[l] = frames * off * scale

    def normed(l, n):
        at = chunk_of(n)
        x = (xhat[l, :, at, :] - mean[at, :][None]) * rstd[l, at, :][None]
        xhat[l, :, at, :] = x
        g, s = gain(l)
        return x, x * g + s

    def pass_a(n, dm, x, v, pieces):
        at = chunk_of(n)
        slope = dm * mish_slope(v, *pieces)
        dy[:, at, :] = slope
        q_one[at, :] = jnp.sum(slope, axis=0)
        q_two[at, :] = jnp.sum(slope * x, axis=0)

    def pass_a_load(l, n, dm):
        x = xhat[l, :, chunk_of(n), :]
        g, s = gain(l)
        v = x * g + s
        pass_a(n, dm, x, v, mish_parts(v))

    def stats_back(l):
        g, s = gain(l)
        one, two = q_one[...], q_two[...]
        vec_o[BASE + 3 + OWNED + l : BASE + 4 + OWNED + l, :] = jnp.sum(two, axis=0, keepdims=True)
        vec_o[BASE + 3 + 2 * OWNED + l : BASE + 4 + 2 * OWNED + l, :] = jnp.sum(one, axis=0, keepdims=True)
        sums = group_sum(jnp.concatenate([one * g, two * g], axis=0)) * part
        first, second = sums[:trajs], sums[trajs:]
        g_one[...] = first
        g_two[...] = second
        dc = rstd[l] * (one * g - frames * first - xsum[l] * second)
        vec_o[BASE + 3 + l : BASE + 4 + l, :] = jnp.sum(dc, axis=0, keepdims=True)

    half_rows = LANES // 2
    trades = {}

    def put(block, value):
        for side in range(2):
            shares_g[side, block] = value[side * half_rows : (side + 1) * half_rows].astype(BF16)

    def trade(group, lo, hi):
        span = pl.ds(lo, hi - lo)
        trades[group] = send(shares_g.at[1 - c, span], theirs.at[span], sem_g, (group,), core_peer)

    def merge(group, lo, hi):
        trades[group].wait_recv()
        mat_o[lo:hi] = (shares_g[c, lo:hi].astype(F32) + theirs[lo:hi].astype(F32)).astype(BF16)

    build(0)
    build(1)
    build(2)
    vec_o[...] = jnp.zeros_like(vec_o)
    edge = jnp.zeros((OWNED, KERNEL // 2, trajs, WIDTH), BF16)
    xin[:, : KERNEL // 2] = edge
    xin[:, KERNEL // 2 + frames :] = edge
    dp[: KERNEL // 2] = edge[0]
    dp[KERNEL // 2 + frames :] = edge[0]
    acc[...] = jnp.zeros_like(acc)
    total = inverse_o.shape[0]
    slot = lax.broadcasted_iota(jnp.int32, (total, UNITS), 0)
    unit = lax.broadcasted_iota(jnp.int32, (total, UNITS), 1).astype(F32)
    inverse_o[...] = jnp.min(jnp.where(slot == owners[...], unit, float(UNITS)), axis=1, keepdims=True).astype(jnp.int32)
    stepid = lax.broadcasted_iota(jnp.int32, (32, trajs), 0)
    picked = mm(times[...], (stepid == steps[...]).astype(F32))
    emb = picked[:TDIM].astype(BF16)
    keep, add = picked[TDIM : TDIM + 1], picked[TDIM + 1 : TDIM + 2]
    for f in range(frames):
        at = slice(f * trajs, (f + 1) * trajs)
        raw = noise[:, f, :]
        noise_t[:, at] = raw
        noisy_t[:, at] = (keep * traj[:, f, :] + add * raw).astype(BF16)
        mask_t[:, at] = valid[f : f + 1, :].astype(F32)
    along(0)
    build(3)
    along(1)
    build(4)
    across(0)
    along(2)
    build(5)
    across(1)
    along(3)
    build(6)
    beside(0)
    across(2)
    along(4)
    beside(1)
    whole(0)
    full = [mb[k].reshape(VROWS, WIDTH).astype(F32) for k in range(3)]
    table[...] = (full[0] + full[1]) + full[2]
    low[...] = full[0].astype(BF16)
    w_in, w_head = low[:FEAT, :], low[FEAT : 2 * FEAT, :]
    h[...] = (dot(noisy_t[...], w_in, 0, 0) + row(BASE)).reshape(frames, trajs, WIDTH)

    def enter(n):
        pass_one(0, n, flat(h[:, chunk_of(n), :]))

    loop(enter, [[], [(across, 3)], [(along, 5)], [(beside, 2)]])
    across(4)
    whole(1)
    pre_time = dot(emb, mb[time_at + 2 * BLOCKS].reshape(TDIM, WIDTH).astype(BF16), 0, 0) + row(BASE + 1)
    time_parts = mish_parts(pre_time)
    temb = (pre_time * time_parts[2]).astype(BF16)
    time_slope = mish_slope(pre_time, *time_parts)
    for j in range(BLOCKS):
        tb[j] = dot(temb, lin(j)) + row(BASE + 3 + 3 * OWNED + j)
    moves = [[[], [(along, 6), (beside, 3)], [(across, 5)], [(beside, 4)]], [[(across, 6)], [], [(beside, 5)], []], [[], [(beside, 6)]], [], []]
    for l in range(OWNED - 1):
        stats(l)
        whole(l + 2)

        def forward(n, l=l):
            at = chunk_of(n)
            _, v = normed(l, n)
            m = v * mish_parts(v)[2]
            if l % 2 == 0:
                m = m + tb[l // 2, at, :][None]
            else:
                m = h[:, at, :] + m
                if l == 1:
                    skip[:, at, :] = m
                if l == 2 * BLOCKS - 3:
                    m = m + skip[:, at, :]
                h[:, at, :] = m
            pass_one(l + 1, n, flat(m))

        loop(forward, moves[l])
    stats(OWNED - 1)
    head_bias = table[BASE + 2 : BASE + 3, :]

    def settle(n):
        at = chunk_of(n)
        _, v = normed(OWNED - 1, n)
        dp[KERNEL // 2 : KERNEL // 2 + frames, at, :] = (h[:, at, :] + v * mish_parts(v)[2]).astype(BF16)

    loop(settle)
    top = dp[KERNEL // 2 : KERNEL // 2 + frames].reshape(rows, WIDTH)
    pick = lax.broadcasted_iota(jnp.int32, (FEAT, WIDTH), 0) == lax.broadcasted_iota(jnp.int32, (FEAT, WIDTH), 1)
    bias = jnp.sum(jnp.where(pick, head_bias, 0.0), axis=1, keepdims=True)
    err = dot(w_head, top, 1, 1) + bias - noise_t[...]
    weighted = mask_t[...] * err
    loss = jnp.sum(jnp.sum(weighted * err, axis=0, keepdims=True), axis=1, keepdims=True)
    count = FEAT * jnp.sum(mask_t[...], axis=1, keepdims=True)
    rowid = lax.broadcasted_iota(jnp.int32, (8, LANES), 0)
    loss_o[...] = jnp.where(rowid == 0, loss, jnp.where(rowid == 1, count, 0.0))
    grad = 2.0 * weighted
    g_bias = jnp.sum(grad, axis=1, keepdims=True)
    vec_o[BASE + 2 : BASE + 3, :] = jnp.sum(jnp.where(pick, g_bias, 0.0), axis=0, keepdims=True)
    dpl[...] = grad.astype(BF16)
    vec_o[FEAT : 2 * FEAT, :] = dot(dpl[...], top)
    d[...] = dot(dpl[...], w_head, 0, 0).reshape(frames, trajs, WIDTH)

    def turn(n):
        pass_a_load(OWNED - 1, n, d[:, chunk_of(n), :])

    loop(turn)
    def finish():
        d_in = d[...].reshape(rows, WIDTH)
        vec_o[BASE : BASE + 1, :] = jnp.sum(d_in, axis=0, keepdims=True)
        vec_o[:FEAT, :] = dot(noisy_t[...], d_in.astype(BF16))
        d_temb = None
        for j in range(BLOCKS):
            grads = dtb[j]
            vec_o[BASE + 3 + 3 * OWNED + j : BASE + 4 + 3 * OWNED + j, :] = jnp.sum(grads, axis=0, keepdims=True)
            grads = grads.astype(BF16)
            t_grad = dot(temb, grads, 0, 0)
            for half in range(2):
                put(taps * OWNED + 2 * j + half, t_grad[half * LANES : (half + 1) * LANES])
            term = dot(grads, lin(j), 1, 1)
            d_temb = term if d_temb is None else d_temb + term
        d_pre = d_temb * time_slope
        vec_o[BASE + 1 : BASE + 2, :] = jnp.sum(d_pre, axis=0, keepdims=True)
        put(UNITS - 1, dot(emb, d_pre.astype(BF16)))
        trade(OWNED, taps * OWNED, UNITS)

    for l in reversed(range(OWNED)):
        stats_back(l)

        def backward(n, l=l):
            g, s = gain(l)
            at = chunk_of(n)
            x = xhat[l, :, at, :]
            back = rstd[l, at, :][None] * (dy[:, at, :] * g - g_one[at, :][None] - x * g_two[at, :][None])
            dp[KERNEL // 2 : KERNEL // 2 + frames, at, :] = back.astype(BF16)
            dx = None
            for k in range(KERNEL):
                shift = KERNEL - 1 - k
                term = dot(flat(dp[shift : shift + frames, at, :]), tap(l, k), 1, 1)
                dx = term if dx is None else dx + term
            dx = wide(dx)
            if l % 2 == 1:
                dtb[l // 2, at, :] = jnp.sum(dx, axis=0)
                pass_a_load(l - 1, n, dx)
            else:
                dx = d[:, at, :] + dx
                if l == OWNED - 2:
                    dskip[:, at, :] = dx
                if l == 2:
                    dx = dx + dskip[:, at, :]
                d[:, at, :] = dx
                if l > 0:
                    pass_a_load(l - 1, n, dx)

        loop(backward)
        if l == 0:
            finish()
        xt[...] = xin[l, KERNEL // 2 : KERNEL // 2 + frames].reshape(rows, WIDTH).T
        for k in range(KERNEL):
            shift = KERNEL - 1 - k
            w_grad = dot(xt[...], dp[shift : shift + frames].reshape(rows, WIDTH))
            for half in range(2):
                put(taps * l + 2 * k + half, w_grad[half * LANES : (half + 1) * LANES])
        trade(l, taps * l, taps * (l + 1))

    mat_o[UNITS] = jnp.zeros((half_rows, WIDTH), BF16)
    for l in reversed(range(1, OWNED)):
        merge(l, taps * l, taps * (l + 1))
    merge(OWNED, taps * OWNED, UNITS)
    merge(0, 0, taps)
    for copy in waits:
        copy.wait_send()


def net(traj, noise, steps, valid, mat, vec, owners, total, groups, shards):
    outer, inner = split_shard(shards)
    feats, frames, trajs = traj.shape
    rows = frames * trajs
    piece = mat.shape[1]
    lane = np.arange(WIDTH) // (WIDTH // GROUPS)
    gmat = jnp.asarray((lane[:, None] == lane[None, :]).astype(np.float32))
    times = jnp.asarray(time_table())
    wire = BF16 if (2 * piece) % TILE == 0 else F32
    vm = pl.BlockSpec(memory_space=pltpu.VMEM)
    f = jax.ShapeDtypeStruct
    big = pltpu.VMEM((frames, trajs, WIDTH), F32)
    small = pltpu.VMEM((trajs, WIDTH), F32)
    padded = frames + KERNEL - 1
    dma = pltpu.SemaphoreType.DMA
    count = len(gather_parts())
    return pl.pallas_call(
        functools.partial(net_kernel, trajs, frames, groups, outer, inner),
        out_shape=[f((UNITS + 1, LANES // 2, WIDTH), BF16), f((VROWS, WIDTH), F32), f((8, LANES), F32), f((total, 1), jnp.int32)],
        in_specs=[vm] * 9,
        out_specs=[vm] * 4,
        scratch_shapes=[
            pltpu.VMEM((UNITS, piece, WIDTH), F32),
            pltpu.VMEM((piece, WIDTH), F32),
            pltpu.VMEM((2, UNITS, LANES // 2, WIDTH), BF16),
            pltpu.VMEM((UNITS, LANES // 2, WIDTH), BF16),
            pltpu.VMEM((UNITS + 3, 2 * piece, WIDTH), wire),
            pltpu.VMEM((UNITS + 3, outer, inner, 2 * piece, WIDTH), wire),
            pltpu.VMEM((OWNED, padded, trajs, WIDTH), BF16),
            pltpu.VMEM((OWNED, frames, trajs, WIDTH), F32),
            big, big, big, big, big,
            pltpu.VMEM((padded, trajs, WIDTH), BF16),
            pltpu.VMEM((VROWS, WIDTH), BF16),
            pltpu.VMEM((WIDTH, rows), BF16),
            small, small, small,
            pltpu.VMEM((OWNED, trajs, WIDTH), F32),
            pltpu.VMEM((OWNED, trajs, WIDTH), F32),
            small, small, small, small,
            pltpu.VMEM((BLOCKS, trajs, WIDTH), F32),
            pltpu.VMEM((BLOCKS, trajs, WIDTH), F32),
            pltpu.VMEM((feats, rows), BF16),
            pltpu.VMEM((feats, rows), F32),
            pltpu.VMEM((1, rows), F32),
            pltpu.VMEM((feats, rows), BF16),
            pltpu.VMEM((16, WIDTH), F32),
            pltpu.VMEM((VROWS, WIDTH), F32),
            dma((2, 4)), dma((2, count, outer - 1)), dma((2, count, max(inner - 1, 1))),
            dma((2, count, inner + 1)), dma((2, count)), dma((2, OWNED + 1)),
        ],
        compiler_params=pltpu.CompilerParams(collective_id=3, has_side_effects=True, vmem_limit_bytes=50 * 2**20),
        name="net",
    )(traj, noise, steps, valid, times, gmat, mat, vec, owners)


def body(
    trajectories,
    noise,
    timesteps,
    valid,
    owners,
    mat_weight,
    mat_ema,
    soap_first,
    soap_second,
    left_stat,
    right_stat,
    left_basis,
    right_basis,
    vec_weight,
    vec_first,
    vec_second,
    vec_ema,
):
    shards = lax.axis_size("shard")
    groups = lax.axis_size("dp")
    slots = soap_first.shape[0]
    mat_grad, vec_grad, scal, inverse = net(
        trajectories.transpose(2, 1, 0),
        noise.transpose(2, 1, 0),
        timesteps.reshape(1, -1),
        valid.T,
        mat_weight,
        vec_weight,
        owners.reshape(1, -1),
        shards * slots,
        groups,
        shards,
    )
    grads, grads_vec, scal, second, lnew, rnew, xl, xr, back = reduce_grads(
        inverse, mat_grad, vec_grad, scal, soap_first, soap_second, left_stat, right_stat, left_basis, right_basis, groups, shards
    )
    results = soap(
        owners, scal, grads, grads_vec, second, lnew, rnew, xl, xr, back,
        soap_first, mat_weight, mat_ema, vec_weight, vec_first, vec_second, vec_ema,
    )
    return tuple(x.reshape(()) for x in results[:3]) + tuple(results[3:])


def solution(mesh):
    placed = (
        P(("dp", "shard"), None, None),
        P(("dp", "shard"), None, None),
        P(("dp", "shard")),
        P(("dp", "shard"), None),
        P(),
        P(None, "shard", None),
        P(None, "shard", None),
        P("shard", None, None),
        P("shard", None, None),
        P("shard", None, None),
        P("shard", None, None),
        P("shard", None, None),
        P("shard", None, None),
        P("shard", None),
        P("shard", None),
        P("shard", None),
        P("shard", None),
    )
    return jax.shard_map(
        body,
        mesh=mesh,
        in_specs=placed,
        out_specs=(
            P(),
            P(),
            P(),
            P(None, "shard", None),
            P(None, "shard", None),
            P("shard", None, None),
            P("shard", None, None),
            P("shard", None, None),
            P("shard", None, None),
            P("shard", None, None),
            P("shard", None, None),
            P("shard", None),
            P("shard", None),
            P("shard", None),
            P("shard", None),
        ),
        check_vma=False,
    )
```

```python
import functools
import math

import jax
import jax.numpy as jnp
import numpy as np
from jax import lax
from jax.experimental import pallas as pl
from jax.experimental.pallas import tpu as pltpu
from jax.sharding import PartitionSpec as P

WIDTH = 256
KERNEL = 5
GROUPS = 8
TDIM = 128
FEAT = 23
BLOCKS = 3
DSTEPS = 20
STEP = 10
OWNED = 6
UNITS = 67
VROWS = 128

HIGH = lax.Precision.HIGHEST
BETA_ONE = 0.9
BETA_TWO = 0.95
ADAM_EPS = 1e-08
LEARN = 0.05
TABLE_LEARN = 0.25
DECAY = 0.01
CLIP = 0.05
EMA_RATE = 0.8
NORM_EPS = 1e-05
PANEL = 32
LANES = 128
PAD = 8
CHUNK = 8
TILE = 16
BASE = 2 * FEAT
F32 = jnp.float32
BF16 = jnp.bfloat16
MESH = pl.DeviceIdType.MESH


def mm(a, b, ca=1, cb=0):
    return lax.dot_general(a, b, (((ca,), (cb,)), ((), ())), precision=HIGH, preferred_element_type=F32)

def mm3(a, b, ca=1, cb=0):
    ah = a.astype(BF16)
    al = (a - ah.astype(F32)).astype(BF16)
    bh = b.astype(BF16)
    bl = (b - bh.astype(F32)).astype(BF16)
    d = (((ca,), (cb,)), ((), ()))

    def product(p, q):
        return lax.dot_general(p, q, d, preferred_element_type=F32)

    return product(ah, bh) + (product(ah, bl) + product(al, bh))


def split3(v):
    hi = v.astype(BF16)
    rest = v - hi.astype(F32)
    mid = rest.astype(BF16)
    last = (rest - mid.astype(F32)).astype(BF16)
    return hi, mid, last

def eliminate(held):
    lanes = lax.broadcasted_iota(jnp.int32, (8, LANES), 1)
    sub = lax.broadcasted_iota(jnp.int32, (8, LANES), 0)
    tall = PANEL // 8

    def lane(v, k):
        return jnp.broadcast_to(v[:, k : k + 1], (8, LANES))

    def combine(x0, x1, x2, x3, l10, l20, l30, l21, l31, l32):
        x1 = x1 - l10 * x0
        x2 = (x2 - l20 * x0) - l21 * x1
        x3 = ((x3 - l30 * x0) - l31 * x1) - l32 * x2
        return x0, x1, x2, x3

    for k in range(0, PANEL, 4):
        top, r = k // 8, k % 8
        for e in held:
            rows = [jnp.broadcast_to(e[top][r + i : r + i + 1, :], (8, LANES)) for i in range(4)]
            p = {(i, j): lane(rows[i], k + j) for i in range(4) for j in range(i, 4)}
            d0 = pl.reciprocal(p[0, 0])
            l10, l20, l30 = p[0, 1] * d0, p[0, 2] * d0, p[0, 3] * d0
            d1 = pl.reciprocal(p[1, 1] - p[0, 1] * l10)
            s12, s13 = p[1, 2] - p[0, 2] * l10, p[1, 3] - p[0, 3] * l10
            l21, l31 = s12 * d1, s13 * d1
            d2 = pl.reciprocal((p[2, 2] - p[0, 2] * l20) - s12 * l21)
            t23 = (p[2, 3] - p[0, 3] * l20) - s13 * l21
            l32 = t23 * d2
            d3 = pl.reciprocal(((p[3, 3] - p[0, 3] * l30) - s13 * l31) - t23 * l32)
            lower = (l10, l20, l30, l21, l31, l32)
            rows = combine(*rows, *lower)
            by = [x * y for x, y in zip(rows, (d0, d1, d2, d3))]
            for v in range(top, tall):
                columns = combine(*[lane(e[v], k + j) for j in range(4)], *lower)
                less = e[v]
                for x, y in zip(columns, by):
                    less = less - x * y
                if v == top:
                    kept = jnp.where(sub == r + 1, rows[1], e[v])
                    kept = jnp.where(sub == r + 2, rows[2], kept)
                    kept = jnp.where(sub == r + 3, rows[3], kept)
                    less = jnp.where(sub > r + 3, less, kept) if r == 0 else kept
                e[v] = less
    results = []
    for e in held:
        parts = []
        for v in range(tall):
            pivots = jnp.sum(jnp.where(lanes == sub + 8 * v, e[v], 0.0), axis=1, keepdims=True)
            parts.append(e[v] * lax.rsqrt(pivots))
        results.append(jnp.concatenate(parts, axis=0)[:, PANEL : 2 * PANEL])
    return results


def factor_panels(chains, start):
    rows = lax.broadcasted_iota(jnp.int32, (PANEL, LANES), 0)
    lanes = lax.broadcasted_iota(jnp.int32, (PANEL, LANES), 1)
    unit = jnp.where(lanes - PANEL == rows, 1.0, 0.0).astype(F32)
    shift = lax.rem(LANES - start, LANES)
    at = pl.ds(start, PANEL)
    held = []
    for z, out, s in chains:
        block = jnp.where(lanes < PANEL, pltpu.roll(z[s, at, :LANES], shift, 1), unit)
        held.append([block[8 * v : 8 * v + 8] for v in range(PANEL // 8)])
    panels = [mm(inverse, z[s, at, :]) for (z, out, s), inverse in zip(chains, eliminate(held))]
    for (z, out, s), done in zip(chains, panels):
        out[s, at, :] = done[:, LANES:]
    for (z, out, s), done in zip(chains, panels):
        hi, mid, last = split3(done)
        lhs = jnp.concatenate([hi, hi, mid, hi, last, mid], axis=0)[:, :LANES]
        rhs = jnp.concatenate([hi, mid, hi, last, hi, mid], axis=0)
        z[s] = z[s] - lax.dot_general(lhs, rhs, (((0,), (0,)), ((), ())), preferred_element_type=F32)


def factor_all(chains):
    def step(p, carry):
        factor_panels(chains, pl.multiple_of(p * PANEL, PANEL))
        return carry

    lax.fori_loop(0, LANES // PANEL, step, 0)


def split_shard(shards):
    return 4, shards // 8


def place(outer, inner):
    s = lax.axis_index("shard")
    return s // (2 * inner), lax.rem(s // 2, inner), lax.rem(s, 2)


def spot(inner, a, b, c):
    return (a * inner + b) * 2 + c


def greet(peers):
    barrier = pltpu.get_barrier_semaphore()
    for peer in peers:
        pl.semaphore_signal(barrier, inc=1, device_id=peer, device_id_type=MESH)
    pl.semaphore_wait(barrier, len(peers))


def reduce_kernel(groups, outer, inner, slots, shards, inverse, grad, vec, scal, m_h, v_h, ls_h, rs_h, lb_h, rb_h,
                  grad_h, vec_o, scal_o, second_h, lnew_h, rnew_h, xl_h, xr_h, back_h,
                  held, r_in_a, sum_a, r_dp_a, r_dp_b, sum_b, r_in_b, ready, r_out, final, landed, sc, turn, norms, sent, got,
                  w_core, w_in, w_dp, w_out, w_sum, m, v, ls, rs, lb, rb,
                  grad_o, second_o, lnew_o, rnew_o, xl_o, xr_o, back_o,
                  sem_in_a, sem_dp_a, sem_dp_b, sem_in_b, sem_out, sem_fin, sem_sc, sem_n, sem_u, sem_h, sem_p):
    d = lax.axis_index("dp")
    a, b, c = place(outer, inner)
    me = lax.axis_index("shard")
    rows = slots * LANES
    half = rows // 2
    piece = half // groups
    core_peer = (d, spot(inner, a, b, 1 - c))
    in_peers = [(d, spot(inner, a, lax.rem(b + i, inner), c)) for i in range(1, inner)]
    dp_peers = [(lax.rem(d + i, groups), me) for i in range(1, groups)]
    out_peers = [(d, spot(inner, lax.rem(a + i, outer), b, c)) for i in range(1, outer)]
    peers = [(d, lax.rem(me + i, shards)) for i in range(1, shards)]
    far = [(lax.rem(d + k, groups), lax.rem(me + i, shards)) for k in range(1, groups) for i in range(shards)]
    pulls = [pltpu.make_async_copy(src, dst, sem_h.at[k])
             for k, (src, dst) in enumerate(((lb_h, lb), (rb_h, rb), (m_h, m), (v_h, v), (ls_h, ls), (rs_h, rs)))]
    pushes = [pltpu.make_async_copy(src, dst, sem_p.at[k])
              for k, (src, dst) in enumerate(((second_o, second_h), (grad_o, grad_h), (lnew_o, lnew_h), (rnew_o, rnew_h),
                                              (xl_o, xl_h), (xr_o, xr_h), (back_o, back_h)))]
    for copy in pulls:
        copy.start()
    greet(peers + far)
    waits = []

    def send(src, dst, sems, index, peer):
        copy = pltpu.make_async_remote_copy(
            src_ref=src, dst_ref=dst, send_sem=sems.at[(0,) + index], recv_sem=sems.at[(1,) + index],
            device_id=peer, device_id_type=MESH)
        copy.start()
        waits.append(copy)
        return copy

    def load(aa, bb):
        first = spot(inner, aa, bb, 0) * slots
        return jnp.concatenate([grad[inverse[first + s, 0]] for s in range(2 * slots)], axis=0)

    order = [lax.rem(a + i, outer) for i in range(1, outer + 1)]
    sc[0, c] = scal[...]
    small = [send(sc.at[0, c], sc.at[0, c], sem_sc, (0, 0), core_peer),
             send(vec.at[:, :, 1 - c], w_core, sem_sc, (0, 3), core_peer)]
    in_a, dp_b, dp_a, in_b, out = {}, {}, {}, {}, {}

    def first_hop(i):
        for j in range(inner):
            at = i * inner + j
            held[at] = load(order[i], j)
        in_a[i] = [send(held.at[i * inner + lax.rem(b + k, inner), pl.ds(0, half)], r_in_a.at[i, k - 1], sem_in_a, (i, k - 1), in_peers[k - 1])
                   for k in range(1, inner)]
        dp_b[i] = [send(held.at[i * inner + j, pl.ds(pl.multiple_of(half + lax.rem(d + k, groups) * piece, TILE), piece)],
                        r_dp_b.at[i, j, k - 1], sem_dp_b, (i, j, k - 1), dp_peers[k - 1])
                   for k in range(1, groups) for j in range(inner)]

    def second_hop(i):
        for copy in in_a[i]:
            copy.wait_recv()
        total = held[i * inner + b, pl.ds(0, half)].astype(F32)
        for k in range(inner - 1):
            total = total + r_in_a[i, k].astype(F32)
        sum_a[i] = total.astype(BF16)
        dp_a[i] = [send(sum_a.at[i, pl.ds(pl.multiple_of(lax.rem(d + k, groups) * piece, TILE), piece)], r_dp_a.at[i, k - 1], sem_dp_a, (i, k - 1), dp_peers[k - 1])
                   for k in range(1, groups)]
        for copy in dp_b[i]:
            copy.wait_recv()
        for j in range(inner):
            total = held[i * inner + j, pl.ds(pl.multiple_of(half + d * piece, TILE), piece)].astype(F32)
            for k in range(groups - 1):
                total = total + r_dp_b[i, j, k].astype(F32)
            sum_b[i * inner + j] = total.astype(BF16)
        in_b[i] = [send(sum_b.at[i * inner + lax.rem(b + k, inner)], r_in_b.at[i, k - 1], sem_in_b, (i, k - 1), in_peers[k - 1])
                   for k in range(1, inner)]

    def third_hop(i):
        for copy in dp_a[i] + in_b[i]:
            copy.wait_recv()
        first = sum_a[i, pl.ds(pl.multiple_of(d * piece, TILE), piece)].astype(F32)
        for k in range(groups - 1):
            first = first + r_dp_a[i, k].astype(F32)
        second = sum_b[i * inner + b].astype(F32)
        for k in range(inner - 1):
            second = second + r_in_b[i, k].astype(F32)
        ready[i, 0:piece] = first.astype(BF16)
        ready[i, piece : 2 * piece] = second.astype(BF16)
        if i < outer - 1:
            out[i] = send(ready.at[i], r_out.at[i], sem_out, (i,), out_peers[i])

    def gathered(level, count):
        for copy in small:
            copy.wait_recv()
        total = sc[level, 0]
        for k in range(1, count):
            total = total + sc[level, k]
        return total

    first_hop(0)
    first_hop(1)
    total = gathered(0, 2)
    sc[1, b] = total
    w_sum[0] = vec[:, :, c] + w_core[...]
    small = [send(sc.at[1, b], sc.at[1, b], sem_sc, (1, k), p) for k, p in enumerate(in_peers)]
    small += [send(w_sum.at[0, :, lax.rem(b + k, inner)], w_in.at[k - 1], sem_sc, (1, 2 + k), in_peers[k - 1]) for k in range(1, inner)]
    second_hop(0)
    for i in range(2, outer):
        first_hop(i)
        second_hop(i - 1)
        third_hop(i - 2)
    total = gathered(1, inner)
    sc[2, d] = total
    summed = w_sum[0, :, b]
    for k in range(inner - 1):
        summed = summed + w_in[k]
    w_dp[d] = summed
    small = [send(sc.at[2, d], sc.at[2, d], sem_sc, (2, k), p) for k, p in enumerate(dp_peers)]
    small += [send(w_dp.at[d], w_dp.at[d], sem_sc, (2, 3 + k), p) for k, p in enumerate(dp_peers)]
    second_hop(outer - 1)
    third_hop(outer - 2)
    for copy in pulls:
        copy.wait()
    for s in range(slots):
        second_o[s] = mm3(mm3(lb[s], m[s], 0, 0), rb[s])
    total = gathered(2, groups)
    sc[3, a] = total
    summed = w_dp[0]
    for k in range(1, groups):
        summed = summed + w_dp[k]
    w_sum[1, :, 0] = summed
    small = [send(sc.at[3, a], sc.at[3, a], sem_sc, (3, k), p) for k, p in enumerate(out_peers)]
    small += [send(w_sum.at[1, lax.rem(a + k, outer), 0], w_out.at[k - 1], sem_sc, (3, 2 + k), out_peers[k - 1]) for k in range(1, outer)]
    third_hop(outer - 1)
    total = ready[outer - 1].astype(F32)
    for i in range(outer - 1):
        out[i].wait_recv()
        total = total + r_out[i].astype(F32)
    mine = total.astype(BF16)
    final[0] = mine[:piece]
    final[1] = mine[piece:]
    near = [(k, flip) for k in range(groups) for flip in range(2) if k or flip]
    last = []
    for n, (k, flip) in enumerate(near):
        core = lax.rem(c + flip, 2)
        target = (lax.rem(d + k, groups), spot(inner, a, b, core))
        last.append(send(final.at[core], landed.at[c, d], sem_fin, (n,), target))
    landed[c, d] = final[c]
    counts = gathered(3, outer)
    scale = 1.0 / counts[1:2, 0:1]
    table = w_sum[1, a, 0]
    for k in range(outer - 1):
        table = table + w_out[k]
    table = table * scale
    total = mine.astype(F32) * scale
    squares = jnp.sum(total * total) + jnp.where(d == 0, jnp.sum(table * table), 0.0)
    place_n = d * shards + me
    norms[place_n] = jnp.full((8, LANES), squares, F32)
    moves = [send(norms.at[place_n], norms.at[place_n], sem_n, (k,), p) for k, p in enumerate(peers + far)]
    for copy in last:
        copy.wait_recv()
    halves = [jnp.concatenate([landed[q, k] for k in range(groups)], axis=0).astype(F32) * scale for q in range(2)]
    quarter = LANES // 2
    for s in range(slots):
        slot = jnp.concatenate([halves[q][s * quarter : (s + 1) * quarter] for q in range(2)], axis=0)
        grad_o[s] = slot
        turn[s] = mm3(mm3(lb[s], slot, 0, 0), rb[s])
    for copy in moves:
        copy.wait_recv()
    total = norms[0]
    for k in range(1, groups * shards):
        total = total + norms[k]
    norm = jnp.sqrt(total)
    factor = jnp.minimum(1.0, CLIP / (norm + 1e-06))
    rowid = lax.broadcasted_iota(jnp.int32, (8, LANES), 0)
    scal_o[...] = jnp.where(rowid == 2, norm, counts)
    scale = factor[0:1, 0:1]
    vec_o[...] = table * scale
    for s in range(slots):
        turned = turn[s] * scale
        moment = BETA_ONE * second_o[s] + (1.0 - BETA_ONE) * turned
        second = BETA_TWO * v[s] + (1.0 - BETA_TWO) * turned * turned
        second_o[s] = second
        normed = moment / (1.0 - BETA_ONE**STEP) / (jnp.sqrt(second / (1.0 - BETA_TWO**STEP)) + ADAM_EPS)
        turn[s] = mm3(mm3(lb[s], normed), rb[s], 1, 1)
    width = back_o.shape[1]
    used = slots * width
    full = sent.shape[1]
    for t in range(shards):
        parts = [turn[s, t * width : (t + 1) * width, :] for s in range(slots)]
        if full > used:
            parts.append(jnp.zeros((full - used, WIDTH), F32))
        sent[t] = jnp.concatenate(parts, axis=0).astype(BF16)
    got[me] = sent[me]
    moves = [send(sent.at[p[1]], got.at[me], sem_u, (k,), p) for k, p in enumerate(peers)]
    pushes[0].start()
    for s in range(slots):
        slot = grad_o[s] * scale
        grad_o[s] = slot
        lnew = BETA_TWO * ls[s] + (1.0 - BETA_TWO) * mm3(slot, slot, 1, 1)
        rnew = BETA_TWO * rs[s] + (1.0 - BETA_TWO) * mm3(slot, slot, 0, 0)
        lnew_o[s] = lnew
        rnew_o[s] = rnew
        xl_o[s] = mm3(lb[s], lnew, 0, 1)
        xr_o[s] = mm3(rb[s], rnew, 0, 1)
    for copy in pushes[1:6]:
        copy.start()
    for copy in moves:
        copy.wait_recv()
    for t in range(shards):
        rows_t = got[t].astype(F32)
        for s in range(slots):
            back_o[t * slots + s] = rows_t[s * width : (s + 1) * width]
    pushes[6].start()
    for copy in waits:
        copy.wait_send()
    for copy in pushes:
        copy.wait()


def reduce_grads(inverse, grad, vec, scal, m, v, ls, rs, lb, rb, groups, shards):
    outer, inner = split_shard(shards)
    slots = m.shape[0]
    width = LANES // shards
    full = -(-slots * width // TILE) * TILE
    rows = slots * LANES
    half = rows // 2
    piece = half // groups
    f = jax.ShapeDtypeStruct
    hb = pl.BlockSpec(memory_space=pltpu.HBM)
    vm = pl.BlockSpec(memory_space=pltpu.VMEM)
    sm = pl.BlockSpec(memory_space=pltpu.SMEM)
    both = outer * inner
    table = vec.reshape(outer, inner, 2, width, WIDTH)

    def buf(*shape):
        return pltpu.VMEM(shape + (WIDTH,), BF16)

    def wide(*shape):
        return pltpu.VMEM(shape + (WIDTH,), F32)

    dma = pltpu.SemaphoreType.DMA
    peers_in, peers_dp = max(inner - 1, 1), max(groups - 1, 1)
    outs = [f(m.shape, F32), f((width, WIDTH), F32), f((8, LANES), F32)]
    outs += [f(x.shape, F32) for x in (v, ls, rs, lb, rb)] + [f((shards * slots, width, WIDTH), F32)]
    return pl.pallas_call(
        functools.partial(reduce_kernel, groups, outer, inner, slots, shards),
        out_shape=outs,
        in_specs=[sm] + [vm] * 3 + [hb] * 6,
        out_specs=[hb, vm, vm] + [hb] * 6,
        scratch_shapes=[
            buf(both, rows),
            buf(outer, peers_in, half), buf(outer, half), buf(outer, peers_dp, piece),
            buf(outer, inner, peers_dp, piece), buf(both, piece), buf(outer, peers_in, piece),
            buf(outer, 2 * piece), buf(outer - 1, 2 * piece), buf(2, piece), buf(2, groups, piece),
            pltpu.VMEM((4, 4, 8, LANES), F32),
            wide(slots, LANES), pltpu.VMEM((groups * shards, 8, LANES), F32), buf(shards, full), buf(shards, full),
            wide(outer, inner, width), wide(peers_in, outer, width), wide(groups, outer, width), wide(outer - 1, width),
            wide(2, outer, inner, width),
            *[pltpu.VMEM(x.shape, F32) for x in (m, v, ls, rs, lb, rb)],
            *[pltpu.VMEM(x.shape, F32) for x in (m, v, ls, rs, lb, rb)],
            pltpu.VMEM((shards * slots, width, WIDTH), F32),
            dma((2, outer, peers_in)), dma((2, outer, peers_dp)), dma((2, outer, inner, peers_dp)),
            dma((2, outer, peers_in)), dma((2, outer - 1)), dma((2, 2 * groups - 1)), dma((2, 4, 6)),
            dma((2, groups * shards - 1)), dma((2, shards - 1)), dma((6,)), dma((7,)),
        ],
        compiler_params=pltpu.CompilerParams(collective_id=1, has_side_effects=True, vmem_limit_bytes=62 * 2**20),
        name="reduce",
    )(inverse, grad, table, scal, m, v, ls, rs, lb, rb)


def soap_kernel(slots, owners, scal, g_h, gvec, second_i, lnew_i, rnew_i, xl, xr, back_h, m_i, mat_i, ema_i, vw, vf, vs, ve,
                loss_o, count_o, norm_o, mat_h, ema_h, m_h, v_h, ls_h, rs_h, lb_o, rb_o, vw_o, vf_o, vs_o, ve_o, zl, ol, zw, ow, xa, mat_o, ema_o, m_o, g, m, back, mat, ema, second, lnew, rnew, sem, sem_in):
    pulls = [pltpu.make_async_copy(src, dst, sem_in.at[k])
             for k, (src, dst) in enumerate(((second_i, second), (lnew_i, lnew), (rnew_i, rnew), (g_h, g), (m_i, m), (back_h, back), (mat_i, mat), (ema_i, ema)))]
    for copy in pulls:
        copy.start()
    outs = [pltpu.make_async_copy(src, dst, sem.at[k])
            for k, (src, dst) in enumerate(((second, v_h), (lnew, ls_h), (rnew, rs_h), (mat_o, mat_h), (ema_o, ema_h), (m_o, m_h)))]
    loss_o[...] = scal[0:1, 0:1]
    count_o[...] = scal[1:2, 0:1]
    norm_o[...] = scal[2:3, 0:1]
    eye = (lax.broadcasted_iota(jnp.int32, (LANES, LANES), 0) == lax.broadcasted_iota(jnp.int32, (LANES, LANES), 1)).astype(F32)
    for s in range(slots):
        zl[s, :, :LANES] = mm(xl[s], xl[s], 1, 1)
        zl[s, :, LANES:] = xl[s]
        gram = mm(xr[s], xr[s], 1, 1)
        zw[s, :, :LANES] = gram[:LANES, :LANES]
        zw[s, :, LANES:] = eye
        xa[s, :LANES, :LANES] = gram[:LANES, LANES:]
        xa[s, LANES:, :LANES] = gram[LANES:, LANES:]
        xa[s, :, LANES:] = xr[s]
    factor_all([(zw, ow, s) for s in range(slots)] + [(zl, ol, s) for s in range(slots)])
    for s in range(slots):
        lb_o[s] = ol[s].T
        done = mm(ow[s], xa[s, :LANES, :])
        rb_o[s, :, :LANES] = done[:, LANES:].T
        rest = xa[s, LANES:, :] - mm(done[:, :LANES], done, 0, 0)
        zw[s, :, :LANES] = rest[:, :LANES]
        zw[s, :, LANES:] = eye
        xa[s, LANES:, :] = rest
    for copy in pulls:
        copy.wait()
    for copy in outs[:3]:
        copy.start()
    for s in range(slots):
        m_o[s] = BETA_ONE * m[s] + (1.0 - BETA_ONE) * g[s]
    for unit in range(UNITS):
        new = mat[unit] * (1.0 - LEARN * DECAY) - LEARN * back[owners[unit]]
        mat_o[unit] = new
        ema_o[unit] = EMA_RATE * ema[unit] + (1.0 - EMA_RATE) * new
    for copy in outs[3:]:
        copy.start()
    factor_all([(zw, ow, s) for s in range(slots)])
    for s in range(slots):
        rb_o[s, :, LANES:] = mm(ow[s], xa[s, LANES:, LANES:]).T
    grad = gvec[...]
    first = BETA_ONE * vf[...] + (1.0 - BETA_ONE) * grad
    moment = BETA_TWO * vs[...] + (1.0 - BETA_TWO) * grad * grad
    step = first / (1.0 - BETA_ONE**STEP) / (jnp.sqrt(moment / (1.0 - BETA_TWO**STEP)) + ADAM_EPS)
    new = vw[...] * (1.0 - TABLE_LEARN * DECAY) - TABLE_LEARN * step
    vf_o[...] = first
    vs_o[...] = moment
    vw_o[...] = new
    ve_o[...] = EMA_RATE * ve[...] + (1.0 - EMA_RATE) * new
    for copy in outs:
        copy.wait()


def soap(owners, scal, g, gvec, second, lnew, rnew, xl, xr, back, m, mat, ema, vw, vf, vs, ve):
    slots = g.shape[0]
    f = jax.ShapeDtypeStruct
    hb = pl.BlockSpec(memory_space=pltpu.HBM)
    vm = pl.BlockSpec(memory_space=pltpu.VMEM)
    outs = [f((1, 1), F32)] * 3 + [f(x.shape, F32) for x in (mat, ema, m, second, lnew, rnew, xl, xr, vw, vf, vs, ve)]
    return pl.pallas_call(
        functools.partial(soap_kernel, slots),
        out_shape=outs,
        in_specs=[pl.BlockSpec(memory_space=pltpu.SMEM), vm, hb, vm, hb, hb, hb, vm, vm, hb, hb, hb, hb, vm, vm, vm, vm],
        out_specs=[vm] * 3 + [hb] * 6 + [vm] * 6,
        scratch_shapes=[
            pltpu.VMEM((slots, LANES, 2 * LANES), F32),
            pltpu.VMEM((slots, LANES, LANES), F32),
            pltpu.VMEM((slots, LANES, 2 * LANES), F32),
            pltpu.VMEM((slots, LANES, LANES), F32),
            pltpu.VMEM((slots, 2 * LANES, 3 * LANES), F32),
            pltpu.VMEM(mat.shape, F32),
            pltpu.VMEM(mat.shape, F32),
            pltpu.VMEM(m.shape, F32),
            *[pltpu.VMEM(x.shape, F32) for x in (g, m, back, mat, ema, second, lnew, rnew)],
            pltpu.SemaphoreType.DMA((6,)),
            pltpu.SemaphoreType.DMA((8,)),
        ],
        compiler_params=pltpu.CompilerParams(vmem_limit_bytes=62 * 2**20),
        name="soap",
    )(owners, scal, g, gvec, second, lnew, rnew, xl, xr, back, m, mat, ema, vw, vf, vs, ve)


def time_table():
    steps = np.arange(32, dtype=np.float32)
    halfway = TDIM // 2
    freqs = np.exp(-math.log(10000.0) * np.arange(halfway, dtype=np.float32) / (halfway - 1)).astype(np.float32)
    angles = (freqs[:, None] * steps[None, :]).astype(np.float32)
    offset = 0.008
    ratio = (steps + 1.0) / DSTEPS
    upper = np.cos((ratio + offset) / (1.0 + offset) * math.pi / 2) ** 2
    level = upper / math.cos(offset / (1.0 + offset) * math.pi / 2) ** 2
    level = np.clip(np.where(steps < DSTEPS, level, 0.0), 0.0, 1.0)
    levels = np.stack([np.sqrt(level), np.sqrt(1.0 - level)] + [np.zeros(32)] * 6)
    return np.concatenate([np.sin(angles), np.cos(angles), levels]).astype(np.float32)


def dot(a, b, ca=1, cb=0):
    return lax.dot_general(a, b, (((ca,), (cb,)), ((), ())), preferred_element_type=F32)


def mish_parts(v):
    e = jnp.exp(jnp.minimum(v, 20.0))
    n = e * (e + 2.0)
    r = pl.reciprocal(n + 2.0)
    return e, r, n * r


def mish_slope(v, e, r, t):
    return t + v * (4.0 * e * (e + 1.0)) * (r * r)


def gather_parts():
    taps = 2 * KERNEL
    bounds = [3, 3 + taps, UNITS + 3 - (OWNED - 1) * taps]
    while bounds[-1] < UNITS + 3:
        bounds.append(bounds[-1] + taps)
    return [(0, bounds[1])] + list(zip(bounds[1:-1], bounds[2:]))


def net_kernel(trajs, frames, groups, outer, inner, traj, noise, steps, valid, times, gmat, mat, vec, owners, mat_o, vec_o, loss_o, inverse_o,
               other, other_vec, shares_g, theirs, stage, mb, xin, xhat, h, skip, d, dskip, dy, dp, low, xt, s_one, s_two, mean, rstd, xsum, q_one, q_two,
               g_one, g_two, tb, dtb, noisy_t, noise_t, mask_t, dpl, acc, table, sem_c, sem_z, sem_y, sem_s, sem_x, sem_g):
    dpi = lax.axis_index("dp")
    a, b, c = place(outer, inner)
    piece = mat.shape[1]
    chunks = trajs // TILE
    rows_c = TILE * frames
    rows = trajs * frames
    taps = 2 * KERNEL
    part = 1.0 / (frames * (WIDTH // GROUPS))
    group = gmat[...]
    core_peer = (dpi, spot(inner, a, b, 1 - c))
    in_peers = [(dpi, spot(inner, a, lax.rem(b + i, inner), c)) for i in range(1, inner)]
    out_peers = [(dpi, spot(inner, lax.rem(a + i, outer), b, c)) for i in range(1, outer)]
    odd = lax.rem(dpi, 2)
    twin_peer = (dpi + 1 - 2 * odd, spot(inner, a, b, c))
    greet([core_peer, twin_peer] + in_peers + out_peers)
    waits = []

    def send(src, dst, sems, index, peer):
        copy = pltpu.make_async_remote_copy(
            src_ref=src, dst_ref=dst, send_sem=sems.at[(0,) + index], recv_sem=sems.at[(1,) + index],
            device_id=peer, device_id_type=MESH)
        copy.start()
        waits.append(copy)
        return copy

    spans = [(0, taps), (taps * OWNED, UNITS), (taps, taps * OWNED)]
    first_copies = [send(vec, other_vec, sem_c, (3,), core_peer)]
    for k, (lo, hi) in enumerate(spans):
        first_copies.append(send(mat.at[pl.ds(lo, hi - lo)], other.at[pl.ds(lo, hi - lo)], sem_c, (k,), core_peer))
    parts = gather_parts()
    start_of = [3 if l == 0 else parts[l + 1][0] for l in range(OWNED)]
    time_at = parts[1][0]
    shares = [(lo, hi - lo, (hi - lo) * 3 // 10) for lo, hi in parts]
    source = {0: 0, 1: taps * OWNED}
    for g in range(2, len(parts)):
        source[g] = taps * (g - 1)
    cols = pl.ds(pl.multiple_of(c * LANES, LANES), LANES)
    state = {}

    def chip_rows(mine, theirs):
        upper = jnp.where(c == 0, mine, theirs)
        lower = jnp.where(c == 0, theirs, mine)
        return jnp.concatenate([upper, lower], axis=mine.ndim - 2)

    def region(g, kind, at_a, at_b):
        lo, count, side = shares[g]
        both = count - side
        if kind == "own":
            start, size = lo + odd * side, both
        elif kind == "lend":
            start, size = lo + odd * both, side
        else:
            start, size = lo + (1 - odd) * both, side
        return mb.at[pl.ds(start, size), at_a, at_b, :, cols]

    def build(g):
        lo, count, side = shares[g]
        hi = lo + count
        if g == 0:
            first_copies[0].wait_recv()
            first_copies[1].wait_recv()
            rows_v = chip_rows(vec[...], other_vec[...])
            for k, value in enumerate(split3(rows_v)):
                stage[k] = value.astype(mb.dtype)
            count -= 3
        elif g == 1:
            first_copies[2].wait_recv()
        elif g == 2:
            first_copies[3].wait_recv()
        at = source[g]
        stage[hi - count : hi] = chip_rows(mat[at : at + count], other[at : at + count]).astype(BF16).astype(mb.dtype)
        both = hi - lo - side
        mine = region(g, "own", a, b)
        mine[...] = stage[pl.ds(lo + odd * side, both), :, cols]
        state[g] = [send(mine, mine, sem_z, (g, k), p) for k, p in enumerate(out_peers)]

    def along(g):
        for copy in state[g]:
            copy.wait_recv()
        column = region(g, "own", slice(None), b)
        nexts = [send(column, column, sem_y, (g, k), p) for k, p in enumerate(in_peers)]
        state[g] = (nexts, [send(column, column, sem_s, (g, 0), core_peer)])

    def across(g):
        nexts, sib = state[g]
        for copy in nexts:
            copy.wait_recv()
        lent = region(g, "lend", slice(None), slice(None))
        twin = [send(lent, lent, sem_x, (g,), twin_peer)]
        for i in range(1, inner):
            column = region(g, "own", slice(None), lax.rem(b + i, inner))
            sib.append(send(column, column, sem_s, (g, i), core_peer))
        state[g] = (twin, sib)

    def beside(g):
        twin, sib = state[g]
        for copy in twin:
            copy.wait_recv()
        lent = region(g, "borrow", slice(None), slice(None))
        sib.append(send(lent, lent, sem_s, (g, inner), core_peer))
        state[g] = sib

    def whole(g):
        for copy in state[g]:
            copy.wait_recv()

    def chunk_of(n):
        return slice(n * TILE, (n + 1) * TILE)

    def flat(v):
        return v.reshape(rows_c, WIDTH)

    def wide(v):
        return v.reshape(frames, TILE, WIDTH)

    def row(index):
        return table[index : index + 1, :]

    def gain(l):
        return row(BASE + 3 + OWNED + l), row(BASE + 3 + 2 * OWNED + l)

    def tap(l, k):
        at = start_of[l] + 2 * k
        return mb[at : at + 2].reshape(WIDTH, WIDTH).astype(BF16)

    def lin(j):
        at = time_at + 2 * j
        return mb[at : at + 2].reshape(WIDTH, WIDTH).astype(BF16)

    def group_sum(v):
        return lax.dot_general(v, group, (((1,), (0,)), ((), ())), precision=HIGH, preferred_element_type=F32)

    def loop(body, moves=()):
        for n in range(max(chunks, len(moves))):
            if n < len(moves):
                for act, g in moves[n]:
                    act(g)
            if n < chunks:
                body(n)

    def pass_one(l, n, x):
        at = chunk_of(n)
        xin[l, KERNEL // 2 : KERNEL // 2 + frames, at, :] = wide(x).astype(BF16)
        p = None
        for k in range(KERNEL):
            term = dot(flat(xin[l, k : k + frames, at, :]), tap(l, k))
            p = term if p is None else p + term
        p = wide(p + row(BASE + 3 + l))
        xhat[l, :, at, :] = p
        total = jnp.sum(p, axis=0)
        s_one[at, :] = total
        off = p - (total * (1.0 / frames))[None]
        s_two[at, :] = jnp.sum(off * off, axis=0)

    def stats(l):
        total = s_one[...]
        centre = group_sum(total) * part
        off = total * (1.0 / frames) - centre
        var = group_sum(s_two[...] + frames * off * off) * part
        scale = lax.rsqrt(var + NORM_EPS)
        mean[...] = centre
        rstd[l] = scale
        xsum[l] = frames * off * scale

    def normed(l, n):
        at = chunk_of(n)
        x = (xhat[l, :, at, :] - mean[at, :][None]) * rstd[l, at, :][None]
        xhat[l, :, at, :] = x
        g, s = gain(l)
        return x, x * g + s

    def pass_a(n, dm, x, v, pieces):
        at = chunk_of(n)
        slope = dm * mish_slope(v, *pieces)
        dy[:, at, :] = slope
        q_one[at, :] = jnp.sum(slope, axis=0)
        q_two[at, :] = jnp.sum(slope * x, axis=0)

    def pass_a_load(l, n, dm):
        x = xhat[l, :, chunk_of(n), :]
        g, s = gain(l)
        v = x * g + s
        pass_a(n, dm, x, v, mish_parts(v))

    def stats_back(l):
        g, s = gain(l)
        one, two = q_one[...], q_two[...]
        vec_o[BASE + 3 + OWNED + l : BASE + 4 + OWNED + l, :] = jnp.sum(two, axis=0, keepdims=True)
        vec_o[BASE + 3 + 2 * OWNED + l : BASE + 4 + 2 * OWNED + l, :] = jnp.sum(one, axis=0, keepdims=True)
        sums = group_sum(jnp.concatenate([one * g, two * g], axis=0)) * part
        first, second = sums[:trajs], sums[trajs:]
        g_one[...] = first
        g_two[...] = second
        dc = rstd[l] * (one * g - frames * first - xsum[l] * second)
        vec_o[BASE + 3 + l : BASE + 4 + l, :] = jnp.sum(dc, axis=0, keepdims=True)

    half_rows = LANES // 2
    trades = {}

    def put(block, value):
        for side in range(2):
            shares_g[side, block] = value[side * half_rows : (side + 1) * half_rows].astype(BF16)

    def trade(group, lo, hi):
        span = pl.ds(lo, hi - lo)
        trades[group] = send(shares_g.at[1 - c, span], theirs.at[span], sem_g, (group,), core_peer)

    def merge(group, lo, hi):
        trades[group].wait_recv()
        mat_o[lo:hi] = (shares_g[c, lo:hi].astype(F32) + theirs[lo:hi].astype(F32)).astype(BF16)

    build(0)
    build(1)
    build(2)
    vec_o[...] = jnp.zeros_like(vec_o)
    edge = jnp.zeros((OWNED, KERNEL // 2, trajs, WIDTH), BF16)
    xin[:, : KERNEL // 2] = edge
    xin[:, KERNEL // 2 + frames :] = edge
    dp[: KERNEL // 2] = edge[0]
    dp[KERNEL // 2 + frames :] = edge[0]
    acc[...] = jnp.zeros_like(acc)
    total = inverse_o.shape[0]
    slot = lax.broadcasted_iota(jnp.int32, (total, UNITS), 0)
    unit = lax.broadcasted_iota(jnp.int32, (total, UNITS), 1).astype(F32)
    inverse_o[...] = jnp.min(jnp.where(slot == owners[...], unit, float(UNITS)), axis=1, keepdims=True).astype(jnp.int32)
    stepid = lax.broadcasted_iota(jnp.int32, (32, trajs), 0)
    picked = mm(times[...], (stepid == steps[...]).astype(F32))
    emb = picked[:TDIM].astype(BF16)
    keep, add = picked[TDIM : TDIM + 1], picked[TDIM + 1 : TDIM + 2]
    for f in range(frames):
        at = slice(f * trajs, (f + 1) * trajs)
        raw = noise[:, f, :]
        noise_t[:, at] = raw
        noisy_t[:, at] = (keep * traj[:, f, :] + add * raw).astype(BF16)
        mask_t[:, at] = valid[f : f + 1, :].astype(F32)
    along(0)
    build(3)
    along(1)
    build(4)
    across(0)
    along(2)
    build(5)
    across(1)
    along(3)
    build(6)
    beside(0)
    across(2)
    along(4)
    beside(1)
    whole(0)
    full = [mb[k].reshape(VROWS, WIDTH).astype(F32) for k in range(3)]
    table[...] = (full[0] + full[1]) + full[2]
    low[...] = full[0].astype(BF16)
    w_in, w_head = low[:FEAT, :], low[FEAT : 2 * FEAT, :]
    h[...] = (dot(noisy_t[...], w_in, 0, 0) + row(BASE)).reshape(frames, trajs, WIDTH)

    def enter(n):
        pass_one(0, n, flat(h[:, chunk_of(n), :]))

    loop(enter, [[], [(across, 3)], [(along, 5)], [(beside, 2)]])
    across(4)
    whole(1)
    pre_time = dot(emb, mb[time_at + 2 * BLOCKS].reshape(TDIM, WIDTH).astype(BF16), 0, 0) + row(BASE + 1)
    time_parts = mish_parts(pre_time)
    temb = (pre_time * time_parts[2]).astype(BF16)
    time_slope = mish_slope(pre_time, *time_parts)
    for j in range(BLOCKS):
        tb[j] = dot(temb, lin(j)) + row(BASE + 3 + 3 * OWNED + j)
    moves = [[[], [(along, 6), (beside, 3)], [(across, 5)], [(beside, 4)]], [[(across, 6)], [], [(beside, 5)], []], [[], [(beside, 6)]], [], []]
    for l in range(OWNED - 1):
        stats(l)
        whole(l + 2)

        def forward(n, l=l):
            at = chunk_of(n)
            _, v = normed(l, n)
            m = v * mish_parts(v)[2]
            if l % 2 == 0:
                m = m + tb[l // 2, at, :][None]
            else:
                m = h[:, at, :] + m
                if l == 1:
                    skip[:, at, :] = m
                if l == 2 * BLOCKS - 3:
                    m = m + skip[:, at, :]
                h[:, at, :] = m
            pass_one(l + 1, n, flat(m))

        loop(forward, moves[l])
    stats(OWNED - 1)
    head_bias = table[BASE + 2 : BASE + 3, :]

    def settle(n):
        at = chunk_of(n)
        _, v = normed(OWNED - 1, n)
        dp[KERNEL // 2 : KERNEL // 2 + frames, at, :] = (h[:, at, :] + v * mish_parts(v)[2]).astype(BF16)

    loop(settle)
    top = dp[KERNEL // 2 : KERNEL // 2 + frames].reshape(rows, WIDTH)
    pick = lax.broadcasted_iota(jnp.int32, (FEAT, WIDTH), 0) == lax.broadcasted_iota(jnp.int32, (FEAT, WIDTH), 1)
    bias = jnp.sum(jnp.where(pick, head_bias, 0.0), axis=1, keepdims=True)
    err = dot(w_head, top, 1, 1) + bias - noise_t[...]
    weighted = mask_t[...] * err
    loss = jnp.sum(jnp.sum(weighted * err, axis=0, keepdims=True), axis=1, keepdims=True)
    count = FEAT * jnp.sum(mask_t[...], axis=1, keepdims=True)
    rowid = lax.broadcasted_iota(jnp.int32, (8, LANES), 0)
    loss_o[...] = jnp.where(rowid == 0, loss, jnp.where(rowid == 1, count, 0.0))
    grad = 2.0 * weighted
    g_bias = jnp.sum(grad, axis=1, keepdims=True)
    vec_o[BASE + 2 : BASE + 3, :] = jnp.sum(jnp.where(pick, g_bias, 0.0), axis=0, keepdims=True)
    dpl[...] = grad.astype(BF16)
    vec_o[FEAT : 2 * FEAT, :] = dot(dpl[...], top)
    d[...] = dot(dpl[...], w_head, 0, 0).reshape(frames, trajs, WIDTH)

    def turn(n):
        pass_a_load(OWNED - 1, n, d[:, chunk_of(n), :])

    loop(turn)
    def finish():
        d_in = d[...].reshape(rows, WIDTH)
        vec_o[BASE : BASE + 1, :] = jnp.sum(d_in, axis=0, keepdims=True)
        vec_o[:FEAT, :] = dot(noisy_t[...], d_in.astype(BF16))
        d_temb = None
        for j in range(BLOCKS):
            grads = dtb[j]
            vec_o[BASE + 3 + 3 * OWNED + j : BASE + 4 + 3 * OWNED + j, :] = jnp.sum(grads, axis=0, keepdims=True)
            grads = grads.astype(BF16)
            t_grad = dot(temb, grads, 0, 0)
            for half in range(2):
                put(taps * OWNED + 2 * j + half, t_grad[half * LANES : (half + 1) * LANES])
            term = dot(grads, lin(j), 1, 1)
            d_temb = term if d_temb is None else d_temb + term
        d_pre = d_temb * time_slope
        vec_o[BASE + 1 : BASE + 2, :] = jnp.sum(d_pre, axis=0, keepdims=True)
        put(UNITS - 1, dot(emb, d_pre.astype(BF16)))
        trade(OWNED, taps * OWNED, UNITS)

    for l in reversed(range(OWNED)):
        stats_back(l)

        def backward(n, l=l):
            g, s = gain(l)
            at = chunk_of(n)
            x = xhat[l, :, at, :]
            back = rstd[l, at, :][None] * (dy[:, at, :] * g - g_one[at, :][None] - x * g_two[at, :][None])
            dp[KERNEL // 2 : KERNEL // 2 + frames, at, :] = back.astype(BF16)
            dx = None
            for k in range(KERNEL):
                shift = KERNEL - 1 - k
                term = dot(flat(dp[shift : shift + frames, at, :]), tap(l, k), 1, 1)
                dx = term if dx is None else dx + term
            dx = wide(dx)
            if l % 2 == 1:
                dtb[l // 2, at, :] = jnp.sum(dx, axis=0)
                pass_a_load(l - 1, n, dx)
            else:
                dx = d[:, at, :] + dx
                if l == OWNED - 2:
                    dskip[:, at, :] = dx
                if l == 2:
                    dx = dx + dskip[:, at, :]
                d[:, at, :] = dx
                if l > 0:
                    pass_a_load(l - 1, n, dx)

        loop(backward)
        if l == 0:
            finish()
        xt[...] = xin[l, KERNEL // 2 : KERNEL // 2 + frames].reshape(rows, WIDTH).T
        for k in range(KERNEL):
            shift = KERNEL - 1 - k
            w_grad = dot(xt[...], dp[shift : shift + frames].reshape(rows, WIDTH))
            for half in range(2):
                put(taps * l + 2 * k + half, w_grad[half * LANES : (half + 1) * LANES])
        trade(l, taps * l, taps * (l + 1))

    mat_o[UNITS] = jnp.zeros((half_rows, WIDTH), BF16)
    for l in reversed(range(1, OWNED)):
        merge(l, taps * l, taps * (l + 1))
    merge(OWNED, taps * OWNED, UNITS)
    merge(0, 0, taps)
    for copy in waits:
        copy.wait_send()


def net(traj, noise, steps, valid, mat, vec, owners, total, groups, shards):
    outer, inner = split_shard(shards)
    feats, frames, trajs = traj.shape
    rows = frames * trajs
    piece = mat.shape[1]
    lane = np.arange(WIDTH) // (WIDTH // GROUPS)
    gmat = jnp.asarray((lane[:, None] == lane[None, :]).astype(np.float32))
    times = jnp.asarray(time_table())
    wire = BF16 if (2 * piece) % TILE == 0 else F32
    vm = pl.BlockSpec(memory_space=pltpu.VMEM)
    f = jax.ShapeDtypeStruct
    big = pltpu.VMEM((frames, trajs, WIDTH), F32)
    small = pltpu.VMEM((trajs, WIDTH), F32)
    padded = frames + KERNEL - 1
    dma = pltpu.SemaphoreType.DMA
    count = len(gather_parts())
    return pl.pallas_call(
        functools.partial(net_kernel, trajs, frames, groups, outer, inner),
        out_shape=[f((UNITS + 1, LANES // 2, WIDTH), BF16), f((VROWS, WIDTH), F32), f((8, LANES), F32), f((total, 1), jnp.int32)],
        in_specs=[vm] * 9,
        out_specs=[vm] * 4,
        scratch_shapes=[
            pltpu.VMEM((UNITS, piece, WIDTH), F32),
            pltpu.VMEM((piece, WIDTH), F32),
            pltpu.VMEM((2, UNITS, LANES // 2, WIDTH), BF16),
            pltpu.VMEM((UNITS, LANES // 2, WIDTH), BF16),
            pltpu.VMEM((UNITS + 3, 2 * piece, WIDTH), wire),
            pltpu.VMEM((UNITS + 3, outer, inner, 2 * piece, WIDTH), wire),
            pltpu.VMEM((OWNED, padded, trajs, WIDTH), BF16),
            pltpu.VMEM((OWNED, frames, trajs, WIDTH), F32),
            big, big, big, big, big,
            pltpu.VMEM((padded, trajs, WIDTH), BF16),
            pltpu.VMEM((VROWS, WIDTH), BF16),
            pltpu.VMEM((WIDTH, rows), BF16),
            small, small, small,
            pltpu.VMEM((OWNED, trajs, WIDTH), F32),
            pltpu.VMEM((OWNED, trajs, WIDTH), F32),
            small, small, small, small,
            pltpu.VMEM((BLOCKS, trajs, WIDTH), F32),
            pltpu.VMEM((BLOCKS, trajs, WIDTH), F32),
            pltpu.VMEM((feats, rows), BF16),
            pltpu.VMEM((feats, rows), F32),
            pltpu.VMEM((1, rows), F32),
            pltpu.VMEM((feats, rows), BF16),
            pltpu.VMEM((16, WIDTH), F32),
            pltpu.VMEM((VROWS, WIDTH), F32),
            dma((2, 4)), dma((2, count, outer - 1)), dma((2, count, max(inner - 1, 1))),
            dma((2, count, inner + 1)), dma((2, count)), dma((2, OWNED + 1)),
        ],
        compiler_params=pltpu.CompilerParams(collective_id=3, has_side_effects=True, vmem_limit_bytes=62 * 2**20),
        name="net",
    )(traj, noise, steps, valid, times, gmat, mat, vec, owners)


def body(
    trajectories,
    noise,
    timesteps,
    valid,
    owners,
    mat_weight,
    mat_ema,
    soap_first,
    soap_second,
    left_stat,
    right_stat,
    left_basis,
    right_basis,
    vec_weight,
    vec_first,
    vec_second,
    vec_ema,
):
    shards = lax.axis_size("shard")
    groups = lax.axis_size("dp")
    slots = soap_first.shape[0]
    mat_grad, vec_grad, scal, inverse = net(
        trajectories.transpose(2, 1, 0),
        noise.transpose(2, 1, 0),
        timesteps.reshape(1, -1),
        valid.T,
        mat_weight,
        vec_weight,
        owners.reshape(1, -1),
        shards * slots,
        groups,
        shards,
    )
    grads, grads_vec, scal, second, lnew, rnew, xl, xr, back = reduce_grads(
        inverse, mat_grad, vec_grad, scal, soap_first, soap_second, left_stat, right_stat, left_basis, right_basis, groups, shards
    )
    results = soap(
        owners, scal, grads, grads_vec, second, lnew, rnew, xl, xr, back,
        soap_first, mat_weight, mat_ema, vec_weight, vec_first, vec_second, vec_ema,
    )
    return tuple(x.reshape(()) for x in results[:3]) + tuple(results[3:])


def solution(mesh):
    placed = (
        P(("dp", "shard"), None, None),
        P(("dp", "shard"), None, None),
        P(("dp", "shard")),
        P(("dp", "shard"), None),
        P(),
        P(None, "shard", None),
        P(None, "shard", None),
        P("shard", None, None),
        P("shard", None, None),
        P("shard", None, None),
        P("shard", None, None),
        P("shard", None, None),
        P("shard", None, None),
        P("shard", None),
        P("shard", None),
        P("shard", None),
        P("shard", None),
    )
    return jax.shard_map(
        body,
        mesh=mesh,
        in_specs=placed,
        out_specs=(
            P(),
            P(),
            P(),
            P(None, "shard", None),
            P(None, "shard", None),
            P("shard", None, None),
            P("shard", None, None),
            P("shard", None, None),
            P("shard", None, None),
            P("shard", None, None),
            P("shard", None, None),
            P("shard", None),
            P("shard", None),
            P("shard", None),
            P("shard", None),
        ),
        check_vma=False,
    )
```

```python
import functools
import math

import jax
import jax.numpy as jnp
import numpy as np
from jax import lax
from jax.experimental import pallas as pl
from jax.experimental.pallas import tpu as pltpu
from jax.sharding import PartitionSpec as P

WIDTH = 256
KERNEL = 5
GROUPS = 8
TDIM = 128
FEAT = 23
BLOCKS = 3
DSTEPS = 20
STEP = 10
OWNED = 6
UNITS = 67
VROWS = 128

HIGH = lax.Precision.HIGHEST
BETA_ONE = 0.9
BETA_TWO = 0.95
ADAM_EPS = 1e-08
LEARN = 0.05
TABLE_LEARN = 0.25
DECAY = 0.01
CLIP = 0.05
EMA_RATE = 0.8
NORM_EPS = 1e-05
PANEL = 32
LANES = 128
PAD = 8
CHUNK = 8
TILE = 16
BASE = 2 * FEAT
F32 = jnp.float32
BF16 = jnp.bfloat16
MESH = pl.DeviceIdType.MESH


def mm(a, b, ca=1, cb=0):
    return lax.dot_general(a, b, (((ca,), (cb,)), ((), ())), precision=HIGH, preferred_element_type=F32)

def mm3(a, b, ca=1, cb=0):
    ah = a.astype(BF16)
    al = (a - ah.astype(F32)).astype(BF16)
    bh = b.astype(BF16)
    bl = (b - bh.astype(F32)).astype(BF16)
    d = (((ca,), (cb,)), ((), ()))

    def product(p, q):
        return lax.dot_general(p, q, d, preferred_element_type=F32)

    return product(ah, bh) + (product(ah, bl) + product(al, bh))


def split3(v):
    hi = v.astype(BF16)
    rest = v - hi.astype(F32)
    mid = rest.astype(BF16)
    last = (rest - mid.astype(F32)).astype(BF16)
    return hi, mid, last

def eliminate(held):
    lanes = lax.broadcasted_iota(jnp.int32, (8, LANES), 1)
    sub = lax.broadcasted_iota(jnp.int32, (8, LANES), 0)
    tall = PANEL // 8

    def lane(v, k):
        return jnp.broadcast_to(v[:, k : k + 1], (8, LANES))

    def combine(x0, x1, x2, x3, l10, l20, l30, l21, l31, l32):
        x1 = x1 - l10 * x0
        x2 = (x2 - l20 * x0) - l21 * x1
        x3 = ((x3 - l30 * x0) - l31 * x1) - l32 * x2
        return x0, x1, x2, x3

    for k in range(0, PANEL, 4):
        top, r = k // 8, k % 8
        for e in held:
            rows = [jnp.broadcast_to(e[top][r + i : r + i + 1, :], (8, LANES)) for i in range(4)]
            p = {(i, j): lane(rows[i], k + j) for i in range(4) for j in range(i, 4)}
            d0 = pl.reciprocal(p[0, 0])
            l10, l20, l30 = p[0, 1] * d0, p[0, 2] * d0, p[0, 3] * d0
            d1 = pl.reciprocal(p[1, 1] - p[0, 1] * l10)
            s12, s13 = p[1, 2] - p[0, 2] * l10, p[1, 3] - p[0, 3] * l10
            l21, l31 = s12 * d1, s13 * d1
            d2 = pl.reciprocal((p[2, 2] - p[0, 2] * l20) - s12 * l21)
            t23 = (p[2, 3] - p[0, 3] * l20) - s13 * l21
            l32 = t23 * d2
            d3 = pl.reciprocal(((p[3, 3] - p[0, 3] * l30) - s13 * l31) - t23 * l32)
            lower = (l10, l20, l30, l21, l31, l32)
            rows = combine(*rows, *lower)
            by = [x * y for x, y in zip(rows, (d0, d1, d2, d3))]
            for v in range(top, tall):
                columns = combine(*[lane(e[v], k + j) for j in range(4)], *lower)
                less = e[v]
                for x, y in zip(columns, by):
                    less = less - x * y
                if v == top:
                    kept = jnp.where(sub == r + 1, rows[1], e[v])
                    kept = jnp.where(sub == r + 2, rows[2], kept)
                    kept = jnp.where(sub == r + 3, rows[3], kept)
                    less = jnp.where(sub > r + 3, less, kept) if r == 0 else kept
                e[v] = less
    results = []
    for e in held:
        parts = []
        for v in range(tall):
            pivots = jnp.sum(jnp.where(lanes == sub + 8 * v, e[v], 0.0), axis=1, keepdims=True)
            parts.append(e[v] * lax.rsqrt(pivots))
        results.append(jnp.concatenate(parts, axis=0)[:, PANEL : 2 * PANEL])
    return results


def factor_panels(chains, start):
    rows = lax.broadcasted_iota(jnp.int32, (PANEL, LANES), 0)
    lanes = lax.broadcasted_iota(jnp.int32, (PANEL, LANES), 1)
    unit = jnp.where(lanes - PANEL == rows, 1.0, 0.0).astype(F32)
    shift = lax.rem(LANES - start, LANES)
    at = pl.ds(start, PANEL)
    held = []
    for z, out, s in chains:
        block = jnp.where(lanes < PANEL, pltpu.roll(z[s, at, :LANES], shift, 1), unit)
        held.append([block[8 * v : 8 * v + 8] for v in range(PANEL // 8)])
    panels = [mm(inverse, z[s, at, :]) for (z, out, s), inverse in zip(chains, eliminate(held))]
    for (z, out, s), done in zip(chains, panels):
        out[s, at, :] = done[:, LANES:]
    for (z, out, s), done in zip(chains, panels):
        hi, mid, last = split3(done)
        lhs = jnp.concatenate([hi, hi, mid, hi, last, mid], axis=0)[:, :LANES]
        rhs = jnp.concatenate([hi, mid, hi, last, hi, mid], axis=0)
        z[s] = z[s] - lax.dot_general(lhs, rhs, (((0,), (0,)), ((), ())), preferred_element_type=F32)


def factor_all(chains):
    def step(p, carry):
        factor_panels(chains, pl.multiple_of(p * PANEL, PANEL))
        return carry

    lax.fori_loop(0, LANES // PANEL, step, 0)


def split_shard(shards):
    return 4, shards // 8


def place(outer, inner):
    s = lax.axis_index("shard")
    return s // (2 * inner), lax.rem(s // 2, inner), lax.rem(s, 2)


def spot(inner, a, b, c):
    return (a * inner + b) * 2 + c


def greet(peers):
    barrier = pltpu.get_barrier_semaphore()
    for peer in peers:
        pl.semaphore_signal(barrier, inc=1, device_id=peer, device_id_type=MESH)
    pl.semaphore_wait(barrier, len(peers))


def reduce_kernel(groups, outer, inner, slots, shards, inverse, grad, vec, scal, m_h, v_h, ls_h, rs_h, lb_h, rb_h,
                  grad_h, vec_o, scal_o, second_h, lnew_h, rnew_h, xl_h, xr_h, back_h,
                  held, r_in_a, sum_a, r_dp_a, r_dp_b, sum_b, r_in_b, ready, r_out, final, landed, sc, turn, norms, sent, got,
                  w_core, w_in, w_dp, w_out, w_sum, m, v, ls, rs, lb, rb,
                  grad_o, second_o, lnew_o, rnew_o, xl_o, xr_o, back_o,
                  sem_in_a, sem_dp_a, sem_dp_b, sem_in_b, sem_out, sem_fin, sem_sc, sem_n, sem_u, sem_h, sem_p):
    d = lax.axis_index("dp")
    a, b, c = place(outer, inner)
    me = lax.axis_index("shard")
    rows = slots * LANES
    half = rows // 2
    piece = half // groups
    core_peer = (d, spot(inner, a, b, 1 - c))
    in_peers = [(d, spot(inner, a, lax.rem(b + i, inner), c)) for i in range(1, inner)]
    dp_peers = [(lax.rem(d + i, groups), me) for i in range(1, groups)]
    out_peers = [(d, spot(inner, lax.rem(a + i, outer), b, c)) for i in range(1, outer)]
    peers = [(d, lax.rem(me + i, shards)) for i in range(1, shards)]
    far = [(lax.rem(d + k, groups), lax.rem(me + i, shards)) for k in range(1, groups) for i in range(shards)]
    pulls = [pltpu.make_async_copy(src, dst, sem_h.at[k])
             for k, (src, dst) in enumerate(((lb_h, lb), (rb_h, rb), (m_h, m), (v_h, v), (ls_h, ls), (rs_h, rs)))]
    pushes = [pltpu.make_async_copy(src, dst, sem_p.at[k])
              for k, (src, dst) in enumerate(((second_o, second_h), (grad_o, grad_h), (lnew_o, lnew_h), (rnew_o, rnew_h),
                                              (xl_o, xl_h), (xr_o, xr_h), (back_o, back_h)))]
    for copy in pulls:
        copy.start()
    greet(peers + far)
    waits = []

    def send(src, dst, sems, index, peer):
        copy = pltpu.make_async_remote_copy(
            src_ref=src, dst_ref=dst, send_sem=sems.at[(0,) + index], recv_sem=sems.at[(1,) + index],
            device_id=peer, device_id_type=MESH)
        copy.start()
        waits.append(copy)
        return copy

    def load(aa, bb):
        first = spot(inner, aa, bb, 0) * slots
        return jnp.concatenate([grad[inverse[first + s, 0]] for s in range(2 * slots)], axis=0)

    order = [lax.rem(a + i, outer) for i in range(1, outer + 1)]
    sc[0, c] = scal[...]
    small = [send(sc.at[0, c], sc.at[0, c], sem_sc, (0, 0), core_peer),
             send(vec.at[:, :, 1 - c], w_core, sem_sc, (0, 3), core_peer)]
    in_a, dp_b, dp_a, in_b, out = {}, {}, {}, {}, {}

    def first_hop(i):
        for j in range(inner):
            at = i * inner + j
            held[at] = load(order[i], j)
        in_a[i] = [send(held.at[i * inner + lax.rem(b + k, inner), pl.ds(0, half)], r_in_a.at[i, k - 1], sem_in_a, (i, k - 1), in_peers[k - 1])
                   for k in range(1, inner)]
        dp_b[i] = [send(held.at[i * inner + j, pl.ds(pl.multiple_of(half + lax.rem(d + k, groups) * piece, TILE), piece)],
                        r_dp_b.at[i, j, k - 1], sem_dp_b, (i, j, k - 1), dp_peers[k - 1])
                   for k in range(1, groups) for j in range(inner)]

    def second_hop(i):
        for copy in in_a[i]:
            copy.wait_recv()
        total = held[i * inner + b, pl.ds(0, half)].astype(F32)
        for k in range(inner - 1):
            total = total + r_in_a[i, k].astype(F32)
        sum_a[i] = total.astype(BF16)
        dp_a[i] = [send(sum_a.at[i, pl.ds(pl.multiple_of(lax.rem(d + k, groups) * piece, TILE), piece)], r_dp_a.at[i, k - 1], sem_dp_a, (i, k - 1), dp_peers[k - 1])
                   for k in range(1, groups)]
        for copy in dp_b[i]:
            copy.wait_recv()
        for j in range(inner):
            total = held[i * inner + j, pl.ds(pl.multiple_of(half + d * piece, TILE), piece)].astype(F32)
            for k in range(groups - 1):
                total = total + r_dp_b[i, j, k].astype(F32)
            sum_b[i * inner + j] = total.astype(BF16)
        in_b[i] = [send(sum_b.at[i * inner + lax.rem(b + k, inner)], r_in_b.at[i, k - 1], sem_in_b, (i, k - 1), in_peers[k - 1])
                   for k in range(1, inner)]

    def third_hop(i):
        for copy in dp_a[i] + in_b[i]:
            copy.wait_recv()
        first = sum_a[i, pl.ds(pl.multiple_of(d * piece, TILE), piece)].astype(F32)
        for k in range(groups - 1):
            first = first + r_dp_a[i, k].astype(F32)
        second = sum_b[i * inner + b].astype(F32)
        for k in range(inner - 1):
            second = second + r_in_b[i, k].astype(F32)
        ready[i, 0:piece] = first.astype(BF16)
        ready[i, piece : 2 * piece] = second.astype(BF16)
        if i < outer - 1:
            out[i] = send(ready.at[i], r_out.at[i], sem_out, (i,), out_peers[i])

    def gathered(level, count):
        for copy in small:
            copy.wait_recv()
        total = sc[level, 0]
        for k in range(1, count):
            total = total + sc[level, k]
        return total

    first_hop(0)
    first_hop(1)
    total = gathered(0, 2)
    sc[1, b] = total
    w_sum[0] = vec[:, :, c] + w_core[...]
    small = [send(sc.at[1, b], sc.at[1, b], sem_sc, (1, k), p) for k, p in enumerate(in_peers)]
    small += [send(w_sum.at[0, :, lax.rem(b + k, inner)], w_in.at[k - 1], sem_sc, (1, 2 + k), in_peers[k - 1]) for k in range(1, inner)]
    second_hop(0)
    for i in range(2, outer):
        first_hop(i)
        second_hop(i - 1)
        third_hop(i - 2)
    total = gathered(1, inner)
    sc[2, d] = total
    summed = w_sum[0, :, b]
    for k in range(inner - 1):
        summed = summed + w_in[k]
    w_dp[d] = summed
    small = [send(sc.at[2, d], sc.at[2, d], sem_sc, (2, k), p) for k, p in enumerate(dp_peers)]
    small += [send(w_dp.at[d], w_dp.at[d], sem_sc, (2, 3 + k), p) for k, p in enumerate(dp_peers)]
    second_hop(outer - 1)
    third_hop(outer - 2)
    for copy in pulls:
        copy.wait()
    for s in range(slots):
        second_o[s] = mm3(mm3(lb[s], m[s], 0, 0), rb[s])
    total = gathered(2, groups)
    sc[3, a] = total
    summed = w_dp[0]
    for k in range(1, groups):
        summed = summed + w_dp[k]
    w_sum[1, :, 0] = summed
    small = [send(sc.at[3, a], sc.at[3, a], sem_sc, (3, k), p) for k, p in enumerate(out_peers)]
    small += [send(w_sum.at[1, lax.rem(a + k, outer), 0], w_out.at[k - 1], sem_sc, (3, 2 + k), out_peers[k - 1]) for k in range(1, outer)]
    third_hop(outer - 1)
    total = ready[outer - 1].astype(F32)
    for i in range(outer - 1):
        out[i].wait_recv()
        total = total + r_out[i].astype(F32)
    mine = total.astype(BF16)
    final[0] = mine[:piece]
    final[1] = mine[piece:]
    near = [(k, flip) for k in range(groups) for flip in range(2) if k or flip]
    last = []
    for n, (k, flip) in enumerate(near):
        core = lax.rem(c + flip, 2)
        target = (lax.rem(d + k, groups), spot(inner, a, b, core))
        last.append(send(final.at[core], landed.at[c, d], sem_fin, (n,), target))
    landed[c, d] = final[c]
    counts = gathered(3, outer)
    scale = 1.0 / counts[1:2, 0:1]
    table = w_sum[1, a, 0]
    for k in range(outer - 1):
        table = table + w_out[k]
    table = table * scale
    total = mine.astype(F32) * scale
    squares = jnp.sum(total * total) + jnp.where(d == 0, jnp.sum(table * table), 0.0)
    place_n = d * shards + me
    norms[place_n] = jnp.full((8, LANES), squares, F32)
    moves = [send(norms.at[place_n], norms.at[place_n], sem_n, (k,), p) for k, p in enumerate(peers + far)]
    for copy in last:
        copy.wait_recv()
    halves = [jnp.concatenate([landed[q, k] for k in range(groups)], axis=0).astype(F32) * scale for q in range(2)]
    quarter = LANES // 2
    for s in range(slots):
        slot = jnp.concatenate([halves[q][s * quarter : (s + 1) * quarter] for q in range(2)], axis=0)
        grad_o[s] = slot
        turn[s] = mm3(mm3(lb[s], slot, 0, 0), rb[s])
    for copy in moves:
        copy.wait_recv()
    total = norms[0]
    for k in range(1, groups * shards):
        total = total + norms[k]
    norm = jnp.sqrt(total)
    factor = jnp.minimum(1.0, CLIP / (norm + 1e-06))
    rowid = lax.broadcasted_iota(jnp.int32, (8, LANES), 0)
    scal_o[...] = jnp.where(rowid == 2, norm, counts)
    scale = factor[0:1, 0:1]
    vec_o[...] = table * scale
    for s in range(slots):
        turned = turn[s] * scale
        moment = BETA_ONE * second_o[s] + (1.0 - BETA_ONE) * turned
        second = BETA_TWO * v[s] + (1.0 - BETA_TWO) * turned * turned
        second_o[s] = second
        normed = moment / (1.0 - BETA_ONE**STEP) / (jnp.sqrt(second / (1.0 - BETA_TWO**STEP)) + ADAM_EPS)
        turn[s] = mm3(mm3(lb[s], normed), rb[s], 1, 1)
    width = back_o.shape[1]
    used = slots * width
    full = sent.shape[1]
    for t in range(shards):
        parts = [turn[s, t * width : (t + 1) * width, :] for s in range(slots)]
        if full > used:
            parts.append(jnp.zeros((full - used, WIDTH), F32))
        sent[t] = jnp.concatenate(parts, axis=0).astype(BF16)
    got[me] = sent[me]
    moves = [send(sent.at[p[1]], got.at[me], sem_u, (k,), p) for k, p in enumerate(peers)]
    pushes[0].start()
    for s in range(slots):
        slot = grad_o[s] * scale
        grad_o[s] = slot
        lnew = BETA_TWO * ls[s] + (1.0 - BETA_TWO) * mm3(slot, slot, 1, 1)
        rnew = BETA_TWO * rs[s] + (1.0 - BETA_TWO) * mm3(slot, slot, 0, 0)
        lnew_o[s] = lnew
        rnew_o[s] = rnew
        xl_o[s] = mm3(lb[s], lnew, 0, 1)
        xr_o[s] = mm3(rb[s], rnew, 0, 1)
    for copy in pushes[1:6]:
        copy.start()
    for copy in moves:
        copy.wait_recv()
    for t in range(shards):
        rows_t = got[t].astype(F32)
        for s in range(slots):
            back_o[t * slots + s] = rows_t[s * width : (s + 1) * width]
    pushes[6].start()
    for copy in waits:
        copy.wait_send()
    for copy in pushes:
        copy.wait()


def reduce_grads(inverse, grad, vec, scal, m, v, ls, rs, lb, rb, groups, shards):
    outer, inner = split_shard(shards)
    slots = m.shape[0]
    width = LANES // shards
    full = -(-slots * width // TILE) * TILE
    rows = slots * LANES
    half = rows // 2
    piece = half // groups
    f = jax.ShapeDtypeStruct
    hb = pl.BlockSpec(memory_space=pltpu.HBM)
    vm = pl.BlockSpec(memory_space=pltpu.VMEM)
    sm = pl.BlockSpec(memory_space=pltpu.SMEM)
    both = outer * inner
    table = vec.reshape(outer, inner, 2, width, WIDTH)

    def buf(*shape):
        return pltpu.VMEM(shape + (WIDTH,), BF16)

    def wide(*shape):
        return pltpu.VMEM(shape + (WIDTH,), F32)

    dma = pltpu.SemaphoreType.DMA
    peers_in, peers_dp = max(inner - 1, 1), max(groups - 1, 1)
    outs = [f(m.shape, F32), f((width, WIDTH), F32), f((8, LANES), F32)]
    outs += [f(x.shape, F32) for x in (v, ls, rs, lb, rb)] + [f((shards * slots, width, WIDTH), F32)]
    return pl.pallas_call(
        functools.partial(reduce_kernel, groups, outer, inner, slots, shards),
        out_shape=outs,
        in_specs=[sm] + [vm] * 3 + [hb] * 6,
        out_specs=[hb, vm, vm] + [hb] * 6,
        scratch_shapes=[
            buf(both, rows),
            buf(outer, peers_in, half), buf(outer, half), buf(outer, peers_dp, piece),
            buf(outer, inner, peers_dp, piece), buf(both, piece), buf(outer, peers_in, piece),
            buf(outer, 2 * piece), buf(outer - 1, 2 * piece), buf(2, piece), buf(2, groups, piece),
            pltpu.VMEM((4, 4, 8, LANES), F32),
            wide(slots, LANES), pltpu.VMEM((groups * shards, 8, LANES), F32), buf(shards, full), buf(shards, full),
            wide(outer, inner, width), wide(peers_in, outer, width), wide(groups, outer, width), wide(outer - 1, width),
            wide(2, outer, inner, width),
            *[pltpu.VMEM(x.shape, F32) for x in (m, v, ls, rs, lb, rb)],
            *[pltpu.VMEM(x.shape, F32) for x in (m, v, ls, rs, lb, rb)],
            pltpu.VMEM((shards * slots, width, WIDTH), F32),
            dma((2, outer, peers_in)), dma((2, outer, peers_dp)), dma((2, outer, inner, peers_dp)),
            dma((2, outer, peers_in)), dma((2, outer - 1)), dma((2, 2 * groups - 1)), dma((2, 4, 6)),
            dma((2, groups * shards - 1)), dma((2, shards - 1)), dma((6,)), dma((7,)),
        ],
        compiler_params=pltpu.CompilerParams(collective_id=1, has_side_effects=True, vmem_limit_bytes=62 * 2**20),
        name="reduce",
    )(inverse, grad, table, scal, m, v, ls, rs, lb, rb)


def soap_kernel(slots, owners, scal, g_h, gvec, second_i, lnew_i, rnew_i, xl, xr, back_h, m_i, mat_i, ema_i, vw, vf, vs, ve,
                loss_o, count_o, norm_o, mat_h, ema_h, m_h, v_h, ls_h, rs_h, lb_o, rb_o, vw_o, vf_o, vs_o, ve_o, zl, ol, zw, ow, xa, mat_o, ema_o, m_o, g, m, back, mat, ema, second, lnew, rnew, sem, sem_in):
    pulls = [pltpu.make_async_copy(src, dst, sem_in.at[k])
             for k, (src, dst) in enumerate(((second_i, second), (lnew_i, lnew), (rnew_i, rnew), (g_h, g), (m_i, m), (back_h, back), (mat_i, mat), (ema_i, ema)))]
    for copy in pulls:
        copy.start()
    outs = [pltpu.make_async_copy(src, dst, sem.at[k])
            for k, (src, dst) in enumerate(((second, v_h), (lnew, ls_h), (rnew, rs_h), (mat_o, mat_h), (ema_o, ema_h), (m_o, m_h)))]
    loss_o[...] = scal[0:1, 0:1]
    count_o[...] = scal[1:2, 0:1]
    norm_o[...] = scal[2:3, 0:1]
    eye = (lax.broadcasted_iota(jnp.int32, (LANES, LANES), 0) == lax.broadcasted_iota(jnp.int32, (LANES, LANES), 1)).astype(F32)
    for s in range(slots):
        zl[s, :, :LANES] = mm(xl[s], xl[s], 1, 1)
        zl[s, :, LANES:] = xl[s]
        gram = mm(xr[s], xr[s], 1, 1)
        zw[s, :, :LANES] = gram[:LANES, :LANES]
        zw[s, :, LANES:] = eye
        xa[s, :LANES, :LANES] = gram[:LANES, LANES:]
        xa[s, LANES:, :LANES] = gram[LANES:, LANES:]
        xa[s, :, LANES:] = xr[s]
    factor_all([(zw, ow, s) for s in range(slots)] + [(zl, ol, s) for s in range(slots)])
    for s in range(slots):
        lb_o[s] = ol[s].T
        done = mm(ow[s], xa[s, :LANES, :])
        rb_o[s, :, :LANES] = done[:, LANES:].T
        rest = xa[s, LANES:, :] - mm(done[:, :LANES], done, 0, 0)
        zw[s, :, :LANES] = rest[:, :LANES]
        zw[s, :, LANES:] = eye
        xa[s, LANES:, :] = rest
    for copy in pulls:
        copy.wait()
    for copy in outs[:3]:
        copy.start()
    for s in range(slots):
        m_o[s] = BETA_ONE * m[s] + (1.0 - BETA_ONE) * g[s]
    for unit in range(UNITS):
        new = mat[unit] * (1.0 - LEARN * DECAY) - LEARN * back[owners[unit]]
        mat_o[unit] = new
        ema_o[unit] = EMA_RATE * ema[unit] + (1.0 - EMA_RATE) * new
    for copy in outs[3:]:
        copy.start()
    factor_all([(zw, ow, s) for s in range(slots)])
    for s in range(slots):
        rb_o[s, :, LANES:] = mm(ow[s], xa[s, LANES:, LANES:]).T
    grad = gvec[...]
    first = BETA_ONE * vf[...] + (1.0 - BETA_ONE) * grad
    moment = BETA_TWO * vs[...] + (1.0 - BETA_TWO) * grad * grad
    step = first / (1.0 - BETA_ONE**STEP) / (jnp.sqrt(moment / (1.0 - BETA_TWO**STEP)) + ADAM_EPS)
    new = vw[...] * (1.0 - TABLE_LEARN * DECAY) - TABLE_LEARN * step
    vf_o[...] = first
    vs_o[...] = moment
    vw_o[...] = new
    ve_o[...] = EMA_RATE * ve[...] + (1.0 - EMA_RATE) * new
    for copy in outs:
        copy.wait()


def soap(owners, scal, g, gvec, second, lnew, rnew, xl, xr, back, m, mat, ema, vw, vf, vs, ve):
    slots = g.shape[0]
    f = jax.ShapeDtypeStruct
    hb = pl.BlockSpec(memory_space=pltpu.HBM)
    vm = pl.BlockSpec(memory_space=pltpu.VMEM)
    outs = [f((1, 1), F32)] * 3 + [f(x.shape, F32) for x in (mat, ema, m, second, lnew, rnew, xl, xr, vw, vf, vs, ve)]
    return pl.pallas_call(
        functools.partial(soap_kernel, slots),
        out_shape=outs,
        in_specs=[pl.BlockSpec(memory_space=pltpu.SMEM), vm, hb, vm, hb, hb, hb, vm, vm, hb, hb, hb, hb, vm, vm, vm, vm],
        out_specs=[vm] * 3 + [hb] * 6 + [vm] * 6,
        scratch_shapes=[
            pltpu.VMEM((slots, LANES, 2 * LANES), F32),
            pltpu.VMEM((slots, LANES, LANES), F32),
            pltpu.VMEM((slots, LANES, 2 * LANES), F32),
            pltpu.VMEM((slots, LANES, LANES), F32),
            pltpu.VMEM((slots, 2 * LANES, 3 * LANES), F32),
            pltpu.VMEM(mat.shape, F32),
            pltpu.VMEM(mat.shape, F32),
            pltpu.VMEM(m.shape, F32),
            *[pltpu.VMEM(x.shape, F32) for x in (g, m, back, mat, ema, second, lnew, rnew)],
            pltpu.SemaphoreType.DMA((6,)),
            pltpu.SemaphoreType.DMA((8,)),
        ],
        compiler_params=pltpu.CompilerParams(vmem_limit_bytes=62 * 2**20),
        name="soap",
    )(owners, scal, g, gvec, second, lnew, rnew, xl, xr, back, m, mat, ema, vw, vf, vs, ve)


def time_table():
    steps = np.arange(32, dtype=np.float32)
    halfway = TDIM // 2
    freqs = np.exp(-math.log(10000.0) * np.arange(halfway, dtype=np.float32) / (halfway - 1)).astype(np.float32)
    angles = (freqs[:, None] * steps[None, :]).astype(np.float32)
    offset = 0.008
    ratio = (steps + 1.0) / DSTEPS
    upper = np.cos((ratio + offset) / (1.0 + offset) * math.pi / 2) ** 2
    level = upper / math.cos(offset / (1.0 + offset) * math.pi / 2) ** 2
    level = np.clip(np.where(steps < DSTEPS, level, 0.0), 0.0, 1.0)
    levels = np.stack([np.sqrt(level), np.sqrt(1.0 - level)] + [np.zeros(32)] * 6)
    return np.concatenate([np.sin(angles), np.cos(angles), levels]).astype(np.float32)


def dot(a, b, ca=1, cb=0):
    return lax.dot_general(a, b, (((ca,), (cb,)), ((), ())), preferred_element_type=F32)


def mish_parts(v):
    e = jnp.exp(jnp.minimum(v, 20.0))
    n = e * (e + 2.0)
    r = pl.reciprocal(n + 2.0)
    return e, r, n * r


def mish_slope(v, e, r, t):
    return t + v * (4.0 * e * (e + 1.0)) * (r * r)


def gather_parts():
    taps = 2 * KERNEL
    bounds = [3, 3 + taps, UNITS + 3 - (OWNED - 1) * taps]
    while bounds[-1] < UNITS + 3:
        bounds.append(bounds[-1] + taps)
    return [(0, bounds[1])] + list(zip(bounds[1:-1], bounds[2:]))


def net_kernel(trajs, frames, groups, outer, inner, traj, noise, steps, valid, times, gmat, mat, vec, owners, mat_o, vec_o, loss_o, inverse_o,
               other, other_vec, shares_g, theirs, stage, mb, xin, xhat, h, skip, d, dskip, dy, dp, low, xt, s_one, s_two, mean, rstd, xsum, q_one, q_two,
               g_one, g_two, tb, dtb, noisy_t, noise_t, mask_t, dpl, acc, table, sem_c, sem_z, sem_y, sem_s, sem_x, sem_g):
    dpi = lax.axis_index("dp")
    a, b, c = place(outer, inner)
    piece = mat.shape[1]
    chunks = trajs // TILE
    rows_c = TILE * frames
    rows = trajs * frames
    taps = 2 * KERNEL
    part = 1.0 / (frames * (WIDTH // GROUPS))
    group = gmat[...].astype(BF16)
    core_peer = (dpi, spot(inner, a, b, 1 - c))
    in_peers = [(dpi, spot(inner, a, lax.rem(b + i, inner), c)) for i in range(1, inner)]
    out_peers = [(dpi, spot(inner, lax.rem(a + i, outer), b, c)) for i in range(1, outer)]
    odd = lax.rem(dpi, 2)
    twin_peer = (dpi + 1 - 2 * odd, spot(inner, a, b, c))
    greet([core_peer, twin_peer] + in_peers + out_peers)
    waits = []

    def send(src, dst, sems, index, peer):
        copy = pltpu.make_async_remote_copy(
            src_ref=src, dst_ref=dst, send_sem=sems.at[(0,) + index], recv_sem=sems.at[(1,) + index],
            device_id=peer, device_id_type=MESH)
        copy.start()
        waits.append(copy)
        return copy

    spans = [(0, taps), (taps * OWNED, UNITS), (taps, taps * OWNED)]
    first_copies = [send(vec, other_vec, sem_c, (3,), core_peer)]
    for k, (lo, hi) in enumerate(spans):
        first_copies.append(send(mat.at[pl.ds(lo, hi - lo)], other.at[pl.ds(lo, hi - lo)], sem_c, (k,), core_peer))
    parts = gather_parts()
    start_of = [3 if l == 0 else parts[l + 1][0] for l in range(OWNED)]
    time_at = parts[1][0]
    shares = [(lo, hi - lo, (hi - lo) * 3 // 10) for lo, hi in parts]
    source = {0: 0, 1: taps * OWNED}
    for g in range(2, len(parts)):
        source[g] = taps * (g - 1)
    cols = pl.ds(pl.multiple_of(c * LANES, LANES), LANES)
    state = {}

    def chip_rows(mine, theirs):
        upper = jnp.where(c == 0, mine, theirs)
        lower = jnp.where(c == 0, theirs, mine)
        return jnp.concatenate([upper, lower], axis=mine.ndim - 2)

    def region(g, kind, at_a, at_b):
        lo, count, side = shares[g]
        both = count - side
        if kind == "own":
            start, size = lo + odd * side, both
        elif kind == "lend":
            start, size = lo + odd * both, side
        else:
            start, size = lo + (1 - odd) * both, side
        return mb.at[pl.ds(start, size), at_a, at_b, :, cols]

    def build(g):
        lo, count, side = shares[g]
        hi = lo + count
        if g == 0:
            first_copies[0].wait_recv()
            first_copies[1].wait_recv()
            rows_v = chip_rows(vec[...], other_vec[...])
            for k, value in enumerate(split3(rows_v)):
                stage[k] = value.astype(mb.dtype)
            count -= 3
        elif g == 1:
            first_copies[2].wait_recv()
        elif g == 2:
            first_copies[3].wait_recv()
        at = source[g]
        stage[hi - count : hi] = chip_rows(mat[at : at + count], other[at : at + count]).astype(BF16).astype(mb.dtype)
        both = hi - lo - side
        mine = region(g, "own", a, b)
        mine[...] = stage[pl.ds(lo + odd * side, both), :, cols]
        state[g] = [send(mine, mine, sem_z, (g, k), p) for k, p in enumerate(out_peers)]

    def along(g):
        for copy in state[g]:
            copy.wait_recv()
        column = region(g, "own", slice(None), b)
        nexts = [send(column, column, sem_y, (g, k), p) for k, p in enumerate(in_peers)]
        state[g] = (nexts, [send(column, column, sem_s, (g, 0), core_peer)])

    def across(g):
        nexts, sib = state[g]
        for copy in nexts:
            copy.wait_recv()
        lent = region(g, "lend", slice(None), slice(None))
        twin = [send(lent, lent, sem_x, (g,), twin_peer)]
        for i in range(1, inner):
            column = region(g, "own", slice(None), lax.rem(b + i, inner))
            sib.append(send(column, column, sem_s, (g, i), core_peer))
        state[g] = (twin, sib)

    def beside(g):
        twin, sib = state[g]
        for copy in twin:
            copy.wait_recv()
        lent = region(g, "borrow", slice(None), slice(None))
        sib.append(send(lent, lent, sem_s, (g, inner), core_peer))
        state[g] = sib

    def whole(g):
        for copy in state[g]:
            copy.wait_recv()

    def chunk_of(n):
        return slice(n * TILE, (n + 1) * TILE)

    def flat(v):
        return v.reshape(rows_c, WIDTH)

    def wide(v):
        return v.reshape(frames, TILE, WIDTH)

    def row(index):
        return table[index : index + 1, :]

    def gain(l):
        return row(BASE + 3 + OWNED + l), row(BASE + 3 + 2 * OWNED + l)

    def tap(l, k):
        at = start_of[l] + 2 * k
        return mb[at : at + 2].reshape(WIDTH, WIDTH).astype(BF16)

    def lin(j):
        at = time_at + 2 * j
        return mb[at : at + 2].reshape(WIDTH, WIDTH).astype(BF16)

    def group_sum(v):
        count = v.shape[0]
        sums = dot(jnp.concatenate(split3(v), axis=0), group)
        return (sums[:count] + sums[count : 2 * count]) + sums[2 * count :]

    def loop(body, moves=()):
        for n in range(max(chunks, len(moves))):
            if n < len(moves):
                for act, g in moves[n]:
                    act(g)
            if n < chunks:
                body(n)

    def pass_one(l, n, x):
        at = chunk_of(n)
        xin[l, KERNEL // 2 : KERNEL // 2 + frames, at, :] = wide(x).astype(BF16)
        p = None
        for k in range(KERNEL):
            term = dot(flat(xin[l, k : k + frames, at, :]), tap(l, k))
            p = term if p is None else p + term
        p = wide(p + row(BASE + 3 + l))
        xhat[l, :, at, :] = p
        total = jnp.sum(p, axis=0)
        s_one[at, :] = total
        off = p - (total * (1.0 / frames))[None]
        s_two[at, :] = jnp.sum(off * off, axis=0)

    def stats(l):
        total = s_one[...]
        centre = group_sum(total) * part
        off = total * (1.0 / frames) - centre
        var = group_sum(s_two[...] + frames * off * off) * part
        scale = lax.rsqrt(var + NORM_EPS)
        mean[...] = centre
        rstd[l] = scale
        xsum[l] = frames * off * scale

    def normed(l, n):
        at = chunk_of(n)
        x = (xhat[l, :, at, :] - mean[at, :][None]) * rstd[l, at, :][None]
        xhat[l, :, at, :] = x
        g, s = gain(l)
        return x, x * g + s

    def pass_a(n, dm, x, v, pieces):
        at = chunk_of(n)
        slope = dm * mish_slope(v, *pieces)
        dy[:, at, :] = slope
        q_one[at, :] = jnp.sum(slope, axis=0)
        q_two[at, :] = jnp.sum(slope * x, axis=0)

    def pass_a_load(l, n, dm):
        x = xhat[l, :, chunk_of(n), :]
        g, s = gain(l)
        v = x * g + s
        pass_a(n, dm, x, v, mish_parts(v))

    def stats_back(l):
        g, s = gain(l)
        one, two = q_one[...], q_two[...]
        vec_o[BASE + 3 + OWNED + l : BASE + 4 + OWNED + l, :] = jnp.sum(two, axis=0, keepdims=True)
        vec_o[BASE + 3 + 2 * OWNED + l : BASE + 4 + 2 * OWNED + l, :] = jnp.sum(one, axis=0, keepdims=True)
        sums = group_sum(jnp.concatenate([one * g, two * g], axis=0)) * part
        first, second = sums[:trajs], sums[trajs:]
        g_one[...] = first
        g_two[...] = second
        dc = rstd[l] * (one * g - frames * first - xsum[l] * second)
        vec_o[BASE + 3 + l : BASE + 4 + l, :] = jnp.sum(dc, axis=0, keepdims=True)

    half_rows = LANES // 2
    trades = {}

    def put(block, value):
        for side in range(2):
            shares_g[side, block] = value[side * half_rows : (side + 1) * half_rows].astype(BF16)

    def trade(group, lo, hi):
        span = pl.ds(lo, hi - lo)
        trades[group] = send(shares_g.at[1 - c, span], theirs.at[span], sem_g, (group,), core_peer)

    def merge(group, lo, hi):
        trades[group].wait_recv()
        mat_o[lo:hi] = (shares_g[c, lo:hi].astype(F32) + theirs[lo:hi].astype(F32)).astype(BF16)

    build(0)
    build(1)
    build(2)
    vec_o[...] = jnp.zeros_like(vec_o)
    edge = jnp.zeros((OWNED, KERNEL // 2, trajs, WIDTH), BF16)
    xin[:, : KERNEL // 2] = edge
    xin[:, KERNEL // 2 + frames :] = edge
    dp[: KERNEL // 2] = edge[0]
    dp[KERNEL // 2 + frames :] = edge[0]
    acc[...] = jnp.zeros_like(acc)
    total = inverse_o.shape[0]
    slot = lax.broadcasted_iota(jnp.int32, (total, UNITS), 0)
    unit = lax.broadcasted_iota(jnp.int32, (total, UNITS), 1).astype(F32)
    inverse_o[...] = jnp.min(jnp.where(slot == owners[...], unit, float(UNITS)), axis=1, keepdims=True).astype(jnp.int32)
    stepid = lax.broadcasted_iota(jnp.int32, (32, trajs), 0)
    picked = mm(times[...], (stepid == steps[...]).astype(F32))
    emb = picked[:TDIM].astype(BF16)
    keep, add = picked[TDIM : TDIM + 1], picked[TDIM + 1 : TDIM + 2]
    for f in range(frames):
        at = slice(f * trajs, (f + 1) * trajs)
        raw = noise[:, f, :]
        noise_t[:, at] = raw
        noisy_t[:, at] = (keep * traj[:, f, :] + add * raw).astype(BF16)
        mask_t[:, at] = valid[f : f + 1, :].astype(F32)
    along(0)
    build(3)
    along(1)
    build(4)
    across(0)
    along(2)
    build(5)
    across(1)
    along(3)
    build(6)
    beside(0)
    across(2)
    along(4)
    beside(1)
    whole(0)
    full = [mb[k].reshape(VROWS, WIDTH).astype(F32) for k in range(3)]
    table[...] = (full[0] + full[1]) + full[2]
    low[...] = full[0].astype(BF16)
    w_in, w_head = low[:FEAT, :], low[FEAT : 2 * FEAT, :]
    h[...] = (dot(noisy_t[...], w_in, 0, 0) + row(BASE)).reshape(frames, trajs, WIDTH)

    def enter(n):
        pass_one(0, n, flat(h[:, chunk_of(n), :]))

    loop(enter, [[], [(across, 3)], [(along, 5)], [(beside, 2)]])
    across(4)
    whole(1)
    pre_time = dot(emb, mb[time_at + 2 * BLOCKS].reshape(TDIM, WIDTH).astype(BF16), 0, 0) + row(BASE + 1)
    time_parts = mish_parts(pre_time)
    temb = (pre_time * time_parts[2]).astype(BF16)
    time_slope = mish_slope(pre_time, *time_parts)
    for j in range(BLOCKS):
        tb[j] = dot(temb, lin(j)) + row(BASE + 3 + 3 * OWNED + j)
    moves = [[[], [(along, 6), (beside, 3)], [(across, 5)], [(beside, 4)]], [[(across, 6)], [], [(beside, 5)], []], [[], [(beside, 6)]], [], []]
    for l in range(OWNED - 1):
        stats(l)
        whole(l + 2)

        def forward(n, l=l):
            at = chunk_of(n)
            _, v = normed(l, n)
            m = v * mish_parts(v)[2]
            if l % 2 == 0:
                m = m + tb[l // 2, at, :][None]
            else:
                m = h[:, at, :] + m
                if l == 1:
                    skip[:, at, :] = m
                if l == 2 * BLOCKS - 3:
                    m = m + skip[:, at, :]
                h[:, at, :] = m
            pass_one(l + 1, n, flat(m))

        loop(forward, moves[l])
    stats(OWNED - 1)
    head_bias = table[BASE + 2 : BASE + 3, :]

    def settle(n):
        at = chunk_of(n)
        _, v = normed(OWNED - 1, n)
        dp[KERNEL // 2 : KERNEL // 2 + frames, at, :] = (h[:, at, :] + v * mish_parts(v)[2]).astype(BF16)

    loop(settle)
    top = dp[KERNEL // 2 : KERNEL // 2 + frames].reshape(rows, WIDTH)
    pick = lax.broadcasted_iota(jnp.int32, (FEAT, WIDTH), 0) == lax.broadcasted_iota(jnp.int32, (FEAT, WIDTH), 1)
    bias = jnp.sum(jnp.where(pick, head_bias, 0.0), axis=1, keepdims=True)
    err = dot(w_head, top, 1, 1) + bias - noise_t[...]
    weighted = mask_t[...] * err
    loss = jnp.sum(jnp.sum(weighted * err, axis=0, keepdims=True), axis=1, keepdims=True)
    count = FEAT * jnp.sum(mask_t[...], axis=1, keepdims=True)
    rowid = lax.broadcasted_iota(jnp.int32, (8, LANES), 0)
    loss_o[...] = jnp.where(rowid == 0, loss, jnp.where(rowid == 1, count, 0.0))
    grad = 2.0 * weighted
    g_bias = jnp.sum(grad, axis=1, keepdims=True)
    vec_o[BASE + 2 : BASE + 3, :] = jnp.sum(jnp.where(pick, g_bias, 0.0), axis=0, keepdims=True)
    dpl[...] = grad.astype(BF16)
    vec_o[FEAT : 2 * FEAT, :] = dot(dpl[...], top)
    d[...] = dot(dpl[...], w_head, 0, 0).reshape(frames, trajs, WIDTH)

    def turn(n):
        pass_a_load(OWNED - 1, n, d[:, chunk_of(n), :])

    loop(turn)
    def finish():
        d_in = d[...].reshape(rows, WIDTH)
        vec_o[BASE : BASE + 1, :] = jnp.sum(d_in, axis=0, keepdims=True)
        vec_o[:FEAT, :] = dot(noisy_t[...], d_in.astype(BF16))
        d_temb = None
        for j in range(BLOCKS):
            grads = dtb[j]
            vec_o[BASE + 3 + 3 * OWNED + j : BASE + 4 + 3 * OWNED + j, :] = jnp.sum(grads, axis=0, keepdims=True)
            grads = grads.astype(BF16)
            t_grad = dot(temb, grads, 0, 0)
            for half in range(2):
                put(taps * OWNED + 2 * j + half, t_grad[half * LANES : (half + 1) * LANES])
            term = dot(grads, lin(j), 1, 1)
            d_temb = term if d_temb is None else d_temb + term
        d_pre = d_temb * time_slope
        vec_o[BASE + 1 : BASE + 2, :] = jnp.sum(d_pre, axis=0, keepdims=True)
        put(UNITS - 1, dot(emb, d_pre.astype(BF16)))
        trade(OWNED, taps * OWNED, UNITS)

    for l in reversed(range(OWNED)):
        stats_back(l)

        def backward(n, l=l):
            g, s = gain(l)
            at = chunk_of(n)
            x = xhat[l, :, at, :]
            back = rstd[l, at, :][None] * (dy[:, at, :] * g - g_one[at, :][None] - x * g_two[at, :][None])
            dp[KERNEL // 2 : KERNEL // 2 + frames, at, :] = back.astype(BF16)
            dx = None
            for k in range(KERNEL):
                shift = KERNEL - 1 - k
                term = dot(flat(dp[shift : shift + frames, at, :]), tap(l, k), 1, 1)
                dx = term if dx is None else dx + term
            dx = wide(dx)
            if l % 2 == 1:
                dtb[l // 2, at, :] = jnp.sum(dx, axis=0)
                pass_a_load(l - 1, n, dx)
            else:
                dx = d[:, at, :] + dx
                if l == OWNED - 2:
                    dskip[:, at, :] = dx
                if l == 2:
                    dx = dx + dskip[:, at, :]
                d[:, at, :] = dx
                if l > 0:
                    pass_a_load(l - 1, n, dx)

        loop(backward)
        if l == 0:
            finish()
        xt[...] = xin[l, KERNEL // 2 : KERNEL // 2 + frames].reshape(rows, WIDTH).T
        for k in range(KERNEL):
            shift = KERNEL - 1 - k
            w_grad = dot(xt[...], dp[shift : shift + frames].reshape(rows, WIDTH))
            for half in range(2):
                put(taps * l + 2 * k + half, w_grad[half * LANES : (half + 1) * LANES])
        trade(l, taps * l, taps * (l + 1))

    mat_o[UNITS] = jnp.zeros((half_rows, WIDTH), BF16)
    for l in reversed(range(1, OWNED)):
        merge(l, taps * l, taps * (l + 1))
    merge(OWNED, taps * OWNED, UNITS)
    merge(0, 0, taps)
    for copy in waits:
        copy.wait_send()


def net(traj, noise, steps, valid, mat, vec, owners, total, groups, shards):
    outer, inner = split_shard(shards)
    feats, frames, trajs = traj.shape
    rows = frames * trajs
    piece = mat.shape[1]
    lane = np.arange(WIDTH) // (WIDTH // GROUPS)
    gmat = jnp.asarray((lane[:, None] == lane[None, :]).astype(np.float32))
    times = jnp.asarray(time_table())
    wire = BF16 if (2 * piece) % TILE == 0 else F32
    vm = pl.BlockSpec(memory_space=pltpu.VMEM)
    f = jax.ShapeDtypeStruct
    big = pltpu.VMEM((frames, trajs, WIDTH), F32)
    small = pltpu.VMEM((trajs, WIDTH), F32)
    padded = frames + KERNEL - 1
    dma = pltpu.SemaphoreType.DMA
    count = len(gather_parts())
    return pl.pallas_call(
        functools.partial(net_kernel, trajs, frames, groups, outer, inner),
        out_shape=[f((UNITS + 1, LANES // 2, WIDTH), BF16), f((VROWS, WIDTH), F32), f((8, LANES), F32), f((total, 1), jnp.int32)],
        in_specs=[vm] * 9,
        out_specs=[vm] * 4,
        scratch_shapes=[
            pltpu.VMEM((UNITS, piece, WIDTH), F32),
            pltpu.VMEM((piece, WIDTH), F32),
            pltpu.VMEM((2, UNITS, LANES // 2, WIDTH), BF16),
            pltpu.VMEM((UNITS, LANES // 2, WIDTH), BF16),
            pltpu.VMEM((UNITS + 3, 2 * piece, WIDTH), wire),
            pltpu.VMEM((UNITS + 3, outer, inner, 2 * piece, WIDTH), wire),
            pltpu.VMEM((OWNED, padded, trajs, WIDTH), BF16),
            pltpu.VMEM((OWNED, frames, trajs, WIDTH), F32),
            big, big, big, big, big,
            pltpu.VMEM((padded, trajs, WIDTH), BF16),
            pltpu.VMEM((VROWS, WIDTH), BF16),
            pltpu.VMEM((WIDTH, rows), BF16),
            small, small, small,
            pltpu.VMEM((OWNED, trajs, WIDTH), F32),
            pltpu.VMEM((OWNED, trajs, WIDTH), F32),
            small, small, small, small,
            pltpu.VMEM((BLOCKS, trajs, WIDTH), F32),
            pltpu.VMEM((BLOCKS, trajs, WIDTH), F32),
            pltpu.VMEM((feats, rows), BF16),
            pltpu.VMEM((feats, rows), F32),
            pltpu.VMEM((1, rows), F32),
            pltpu.VMEM((feats, rows), BF16),
            pltpu.VMEM((16, WIDTH), F32),
            pltpu.VMEM((VROWS, WIDTH), F32),
            dma((2, 4)), dma((2, count, outer - 1)), dma((2, count, max(inner - 1, 1))),
            dma((2, count, inner + 1)), dma((2, count)), dma((2, OWNED + 1)),
        ],
        compiler_params=pltpu.CompilerParams(collective_id=3, has_side_effects=True, vmem_limit_bytes=62 * 2**20),
        name="net",
    )(traj, noise, steps, valid, times, gmat, mat, vec, owners)


def body(
    trajectories,
    noise,
    timesteps,
    valid,
    owners,
    mat_weight,
    mat_ema,
    soap_first,
    soap_second,
    left_stat,
    right_stat,
    left_basis,
    right_basis,
    vec_weight,
    vec_first,
    vec_second,
    vec_ema,
):
    shards = lax.axis_size("shard")
    groups = lax.axis_size("dp")
    slots = soap_first.shape[0]
    mat_grad, vec_grad, scal, inverse = net(
        trajectories.transpose(2, 1, 0),
        noise.transpose(2, 1, 0),
        timesteps.reshape(1, -1),
        valid.T,
        mat_weight,
        vec_weight,
        owners.reshape(1, -1),
        shards * slots,
        groups,
        shards,
    )
    grads, grads_vec, scal, second, lnew, rnew, xl, xr, back = reduce_grads(
        inverse, mat_grad, vec_grad, scal, soap_first, soap_second, left_stat, right_stat, left_basis, right_basis, groups, shards
    )
    results = soap(
        owners, scal, grads, grads_vec, second, lnew, rnew, xl, xr, back,
        soap_first, mat_weight, mat_ema, vec_weight, vec_first, vec_second, vec_ema,
    )
    return tuple(x.reshape(()) for x in results[:3]) + tuple(results[3:])


def solution(mesh):
    placed = (
        P(("dp", "shard"), None, None),
        P(("dp", "shard"), None, None),
        P(("dp", "shard")),
        P(("dp", "shard"), None),
        P(),
        P(None, "shard", None),
        P(None, "shard", None),
        P("shard", None, None),
        P("shard", None, None),
        P("shard", None, None),
        P("shard", None, None),
        P("shard", None, None),
        P("shard", None, None),
        P("shard", None),
        P("shard", None),
        P("shard", None),
        P("shard", None),
    )
    return jax.shard_map(
        body,
        mesh=mesh,
        in_specs=placed,
        out_specs=(
            P(),
            P(),
            P(),
            P(None, "shard", None),
            P(None, "shard", None),
            P("shard", None, None),
            P("shard", None, None),
            P("shard", None, None),
            P("shard", None, None),
            P("shard", None, None),
            P("shard", None, None),
            P("shard", None),
            P("shard", None),
            P("shard", None),
            P("shard", None),
        ),
        check_vma=False,
    )
```

```python
import functools
import math

import jax
import jax.numpy as jnp
import numpy as np
from jax import lax
from jax.experimental import pallas as pl
from jax.experimental.pallas import tpu as pltpu
from jax.sharding import PartitionSpec as P

WIDTH = 256
KERNEL = 5
GROUPS = 8
TDIM = 128
FEAT = 23
BLOCKS = 3
DSTEPS = 20
STEP = 10
OWNED = 6
UNITS = 67
VROWS = 128

HIGH = lax.Precision.HIGHEST
BETA_ONE = 0.9
BETA_TWO = 0.95
ADAM_EPS = 1e-08
LEARN = 0.05
TABLE_LEARN = 0.25
DECAY = 0.01
CLIP = 0.05
EMA_RATE = 0.8
NORM_EPS = 1e-05
PANEL = 32
LANES = 128
PAD = 8
CHUNK = 8
TILE = 16
BASE = 2 * FEAT
F32 = jnp.float32
BF16 = jnp.bfloat16
MESH = pl.DeviceIdType.MESH


def mm(a, b, ca=1, cb=0):
    return lax.dot_general(a, b, (((ca,), (cb,)), ((), ())), precision=HIGH, preferred_element_type=F32)

def mm3(a, b, ca=1, cb=0):
    ah = a.astype(BF16)
    al = (a - ah.astype(F32)).astype(BF16)
    bh = b.astype(BF16)
    bl = (b - bh.astype(F32)).astype(BF16)
    d = (((ca,), (cb,)), ((), ()))

    def product(p, q):
        return lax.dot_general(p, q, d, preferred_element_type=F32)

    return product(ah, bh) + (product(ah, bl) + product(al, bh))


def split3(v):
    hi = v.astype(BF16)
    rest = v - hi.astype(F32)
    mid = rest.astype(BF16)
    last = (rest - mid.astype(F32)).astype(BF16)
    return hi, mid, last

def eliminate(held):
    lanes = lax.broadcasted_iota(jnp.int32, (8, LANES), 1)
    sub = lax.broadcasted_iota(jnp.int32, (8, LANES), 0)
    tall = PANEL // 8

    def lane(v, k):
        return jnp.broadcast_to(v[:, k : k + 1], (8, LANES))

    def combine(x0, x1, x2, x3, l10, l20, l30, l21, l31, l32):
        x1 = x1 - l10 * x0
        x2 = (x2 - l20 * x0) - l21 * x1
        x3 = ((x3 - l30 * x0) - l31 * x1) - l32 * x2
        return x0, x1, x2, x3

    for k in range(0, PANEL, 4):
        top, r = k // 8, k % 8
        for e in held:
            rows = [jnp.broadcast_to(e[top][r + i : r + i + 1, :], (8, LANES)) for i in range(4)]
            p = {(i, j): lane(rows[i], k + j) for i in range(4) for j in range(i, 4)}
            d0 = pl.reciprocal(p[0, 0])
            l10, l20, l30 = p[0, 1] * d0, p[0, 2] * d0, p[0, 3] * d0
            d1 = pl.reciprocal(p[1, 1] - p[0, 1] * l10)
            s12, s13 = p[1, 2] - p[0, 2] * l10, p[1, 3] - p[0, 3] * l10
            l21, l31 = s12 * d1, s13 * d1
            d2 = pl.reciprocal((p[2, 2] - p[0, 2] * l20) - s12 * l21)
            t23 = (p[2, 3] - p[0, 3] * l20) - s13 * l21
            l32 = t23 * d2
            d3 = pl.reciprocal(((p[3, 3] - p[0, 3] * l30) - s13 * l31) - t23 * l32)
            lower = (l10, l20, l30, l21, l31, l32)
            rows = combine(*rows, *lower)
            by = [x * y for x, y in zip(rows, (d0, d1, d2, d3))]
            for v in range(top, tall):
                columns = combine(*[lane(e[v], k + j) for j in range(4)], *lower)
                less = e[v]
                for x, y in zip(columns, by):
                    less = less - x * y
                if v == top:
                    kept = jnp.where(sub == r + 1, rows[1], e[v])
                    kept = jnp.where(sub == r + 2, rows[2], kept)
                    kept = jnp.where(sub == r + 3, rows[3], kept)
                    less = jnp.where(sub > r + 3, less, kept) if r == 0 else kept
                e[v] = less
    results = []
    for e in held:
        parts = []
        for v in range(tall):
            pivots = jnp.sum(jnp.where(lanes == sub + 8 * v, e[v], 0.0), axis=1, keepdims=True)
            parts.append(e[v] * lax.rsqrt(pivots))
        results.append(jnp.concatenate(parts, axis=0)[:, PANEL : 2 * PANEL])
    return results


def factor_panels(chains, start):
    rows = lax.broadcasted_iota(jnp.int32, (PANEL, LANES), 0)
    lanes = lax.broadcasted_iota(jnp.int32, (PANEL, LANES), 1)
    unit = jnp.where(lanes - PANEL == rows, 1.0, 0.0).astype(F32)
    shift = lax.rem(LANES - start, LANES)
    at = pl.ds(start, PANEL)
    held = []
    for z, out, s in chains:
        block = jnp.where(lanes < PANEL, pltpu.roll(z[s, at, :LANES], shift, 1), unit)
        held.append([block[8 * v : 8 * v + 8] for v in range(PANEL // 8)])
    panels = [mm(inverse, z[s, at, :]) for (z, out, s), inverse in zip(chains, eliminate(held))]
    for (z, out, s), done in zip(chains, panels):
        out[s, at, :] = done[:, LANES:]
    for (z, out, s), done in zip(chains, panels):
        hi, mid, last = split3(done)
        lhs = jnp.concatenate([hi, hi, mid, hi, last, mid], axis=0)[:, :LANES]
        rhs = jnp.concatenate([hi, mid, hi, last, hi, mid], axis=0)
        z[s] = z[s] - lax.dot_general(lhs, rhs, (((0,), (0,)), ((), ())), preferred_element_type=F32)


def factor_all(chains):
    def step(p, carry):
        factor_panels(chains, pl.multiple_of(p * PANEL, PANEL))
        return carry

    lax.fori_loop(0, LANES // PANEL, step, 0)


def split_shard(shards):
    return 4, shards // 8


def place(outer, inner):
    s = lax.axis_index("shard")
    return s // (2 * inner), lax.rem(s // 2, inner), lax.rem(s, 2)


def spot(inner, a, b, c):
    return (a * inner + b) * 2 + c


def greet(peers):
    barrier = pltpu.get_barrier_semaphore()
    for peer in peers:
        pl.semaphore_signal(barrier, inc=1, device_id=peer, device_id_type=MESH)
    pl.semaphore_wait(barrier, len(peers))


def reduce_kernel(groups, outer, inner, slots, shards, inverse, grad, vec, scal, m_h, v_h, ls_h, rs_h, lb_h, rb_h,
                  grad_h, vec_o, scal_o, second_h, lnew_h, rnew_h, xl_h, xr_h, back_h,
                  held, r_in_a, sum_a, r_dp_a, r_dp_b, sum_b, r_in_b, ready, r_out, final, landed, sc, turn, norms, sent, got,
                  w_core, w_in, w_dp, w_out, w_sum, m, v, ls, rs, lb, rb,
                  grad_o, second_o, lnew_o, rnew_o, xl_o, xr_o, back_o,
                  sem_in_a, sem_dp_a, sem_dp_b, sem_in_b, sem_out, sem_fin, sem_sc, sem_n, sem_u, sem_h, sem_p):
    d = lax.axis_index("dp")
    a, b, c = place(outer, inner)
    me = lax.axis_index("shard")
    rows = slots * LANES
    half = rows // 2
    piece = half // groups
    core_peer = (d, spot(inner, a, b, 1 - c))
    in_peers = [(d, spot(inner, a, lax.rem(b + i, inner), c)) for i in range(1, inner)]
    dp_peers = [(lax.rem(d + i, groups), me) for i in range(1, groups)]
    out_peers = [(d, spot(inner, lax.rem(a + i, outer), b, c)) for i in range(1, outer)]
    peers = [(d, lax.rem(me + i, shards)) for i in range(1, shards)]
    far = [(lax.rem(d + k, groups), lax.rem(me + i, shards)) for k in range(1, groups) for i in range(shards)]
    pulls = [pltpu.make_async_copy(src, dst, sem_h.at[k])
             for k, (src, dst) in enumerate(((lb_h, lb), (rb_h, rb), (m_h, m), (v_h, v), (ls_h, ls), (rs_h, rs)))]
    pushes = [pltpu.make_async_copy(src, dst, sem_p.at[k])
              for k, (src, dst) in enumerate(((second_o, second_h), (grad_o, grad_h), (lnew_o, lnew_h), (rnew_o, rnew_h),
                                              (xl_o, xl_h), (xr_o, xr_h), (back_o, back_h)))]
    for copy in pulls:
        copy.start()
    greet(peers + far)
    waits = []

    def send(src, dst, sems, index, peer):
        copy = pltpu.make_async_remote_copy(
            src_ref=src, dst_ref=dst, send_sem=sems.at[(0,) + index], recv_sem=sems.at[(1,) + index],
            device_id=peer, device_id_type=MESH)
        copy.start()
        waits.append(copy)
        return copy

    def load(aa, bb):
        first = spot(inner, aa, bb, 0) * slots
        return jnp.concatenate([grad[inverse[first + s, 0]] for s in range(2 * slots)], axis=0)

    order = [lax.rem(a + i, outer) for i in range(1, outer + 1)]
    sc[0, c] = scal[...]
    small = [send(sc.at[0, c], sc.at[0, c], sem_sc, (0, 0), core_peer),
             send(vec.at[:, :, 1 - c], w_core, sem_sc, (0, 3), core_peer)]
    in_a, dp_b, dp_a, in_b, out = {}, {}, {}, {}, {}

    def first_hop(i):
        for j in range(inner):
            at = i * inner + j
            held[at] = load(order[i], j)
        in_a[i] = [send(held.at[i * inner + lax.rem(b + k, inner), pl.ds(0, half)], r_in_a.at[i, k - 1], sem_in_a, (i, k - 1), in_peers[k - 1])
                   for k in range(1, inner)]
        dp_b[i] = [send(held.at[i * inner + j, pl.ds(pl.multiple_of(half + lax.rem(d + k, groups) * piece, TILE), piece)],
                        r_dp_b.at[i, j, k - 1], sem_dp_b, (i, j, k - 1), dp_peers[k - 1])
                   for k in range(1, groups) for j in range(inner)]

    def second_hop(i):
        for copy in in_a[i]:
            copy.wait_recv()
        total = held[i * inner + b, pl.ds(0, half)].astype(F32)
        for k in range(inner - 1):
            total = total + r_in_a[i, k].astype(F32)
        sum_a[i] = total.astype(BF16)
        dp_a[i] = [send(sum_a.at[i, pl.ds(pl.multiple_of(lax.rem(d + k, groups) * piece, TILE), piece)], r_dp_a.at[i, k - 1], sem_dp_a, (i, k - 1), dp_peers[k - 1])
                   for k in range(1, groups)]
        for copy in dp_b[i]:
            copy.wait_recv()
        for j in range(inner):
            total = held[i * inner + j, pl.ds(pl.multiple_of(half + d * piece, TILE), piece)].astype(F32)
            for k in range(groups - 1):
                total = total + r_dp_b[i, j, k].astype(F32)
            sum_b[i * inner + j] = total.astype(BF16)
        in_b[i] = [send(sum_b.at[i * inner + lax.rem(b + k, inner)], r_in_b.at[i, k - 1], sem_in_b, (i, k - 1), in_peers[k - 1])
                   for k in range(1, inner)]

    def third_hop(i):
        for copy in dp_a[i] + in_b[i]:
            copy.wait_recv()
        first = sum_a[i, pl.ds(pl.multiple_of(d * piece, TILE), piece)].astype(F32)
        for k in range(groups - 1):
            first = first + r_dp_a[i, k].astype(F32)
        second = sum_b[i * inner + b].astype(F32)
        for k in range(inner - 1):
            second = second + r_in_b[i, k].astype(F32)
        ready[i, 0:piece] = first.astype(BF16)
        ready[i, piece : 2 * piece] = second.astype(BF16)
        if i < outer - 1:
            out[i] = send(ready.at[i], r_out.at[i], sem_out, (i,), out_peers[i])

    def gathered(level, count):
        for copy in small:
            copy.wait_recv()
        total = sc[level, 0]
        for k in range(1, count):
            total = total + sc[level, k]
        return total

    first_hop(0)
    first_hop(1)
    total = gathered(0, 2)
    sc[1, b] = total
    w_sum[0] = vec[:, :, c] + w_core[...]
    small = [send(sc.at[1, b], sc.at[1, b], sem_sc, (1, k), p) for k, p in enumerate(in_peers)]
    small += [send(w_sum.at[0, :, lax.rem(b + k, inner)], w_in.at[k - 1], sem_sc, (1, 2 + k), in_peers[k - 1]) for k in range(1, inner)]
    second_hop(0)
    for i in range(2, outer):
        first_hop(i)
        second_hop(i - 1)
        third_hop(i - 2)
    total = gathered(1, inner)
    sc[2, d] = total
    summed = w_sum[0, :, b]
    for k in range(inner - 1):
        summed = summed + w_in[k]
    w_dp[d] = summed
    small = [send(sc.at[2, d], sc.at[2, d], sem_sc, (2, k), p) for k, p in enumerate(dp_peers)]
    small += [send(w_dp.at[d], w_dp.at[d], sem_sc, (2, 3 + k), p) for k, p in enumerate(dp_peers)]
    second_hop(outer - 1)
    third_hop(outer - 2)
    for copy in pulls:
        copy.wait()
    for s in range(slots):
        second_o[s] = mm3(mm3(lb[s], m[s], 0, 0), rb[s])
    total = gathered(2, groups)
    sc[3, a] = total
    summed = w_dp[0]
    for k in range(1, groups):
        summed = summed + w_dp[k]
    w_sum[1, :, 0] = summed
    small = [send(sc.at[3, a], sc.at[3, a], sem_sc, (3, k), p) for k, p in enumerate(out_peers)]
    small += [send(w_sum.at[1, lax.rem(a + k, outer), 0], w_out.at[k - 1], sem_sc, (3, 2 + k), out_peers[k - 1]) for k in range(1, outer)]
    third_hop(outer - 1)
    total = ready[outer - 1].astype(F32)
    for i in range(outer - 1):
        out[i].wait_recv()
        total = total + r_out[i].astype(F32)
    mine = total.astype(BF16)
    final[0] = mine[:piece]
    final[1] = mine[piece:]
    near = [(k, flip) for k in range(groups) for flip in range(2) if k or flip]
    last = []
    for n, (k, flip) in enumerate(near):
        core = lax.rem(c + flip, 2)
        target = (lax.rem(d + k, groups), spot(inner, a, b, core))
        last.append(send(final.at[core], landed.at[c, d], sem_fin, (n,), target))
    landed[c, d] = final[c]
    counts = gathered(3, outer)
    scale = 1.0 / counts[1:2, 0:1]
    table = w_sum[1, a, 0]
    for k in range(outer - 1):
        table = table + w_out[k]
    table = table * scale
    total = mine.astype(F32) * scale
    squares = jnp.sum(total * total) + jnp.where(d == 0, jnp.sum(table * table), 0.0)
    place_n = d * shards + me
    norms[place_n] = jnp.full((8, LANES), squares, F32)
    moves = [send(norms.at[place_n], norms.at[place_n], sem_n, (k,), p) for k, p in enumerate(peers + far)]
    for copy in last:
        copy.wait_recv()
    halves = [jnp.concatenate([landed[q, k] for k in range(groups)], axis=0).astype(F32) * scale for q in range(2)]
    quarter = LANES // 2
    for s in range(slots):
        slot = jnp.concatenate([halves[q][s * quarter : (s + 1) * quarter] for q in range(2)], axis=0)
        grad_o[s] = slot
        turn[s] = mm3(mm3(lb[s], slot, 0, 0), rb[s])
    for copy in moves:
        copy.wait_recv()
    total = norms[0]
    for k in range(1, groups * shards):
        total = total + norms[k]
    norm = jnp.sqrt(total)
    factor = jnp.minimum(1.0, CLIP / (norm + 1e-06))
    rowid = lax.broadcasted_iota(jnp.int32, (8, LANES), 0)
    scal_o[...] = jnp.where(rowid == 2, norm, counts)
    scale = factor[0:1, 0:1]
    vec_o[...] = table * scale
    for s in range(slots):
        turned = turn[s] * scale
        moment = BETA_ONE * second_o[s] + (1.0 - BETA_ONE) * turned
        second = BETA_TWO * v[s] + (1.0 - BETA_TWO) * turned * turned
        second_o[s] = second
        normed = moment / (1.0 - BETA_ONE**STEP) / (jnp.sqrt(second / (1.0 - BETA_TWO**STEP)) + ADAM_EPS)
        turn[s] = mm3(mm3(lb[s], normed), rb[s], 1, 1)
    width = back_o.shape[1]
    used = slots * width
    full = sent.shape[1]
    for t in range(shards):
        parts = [turn[s, t * width : (t + 1) * width, :] for s in range(slots)]
        if full > used:
            parts.append(jnp.zeros((full - used, WIDTH), F32))
        sent[t] = jnp.concatenate(parts, axis=0).astype(BF16)
    got[me] = sent[me]
    moves = [send(sent.at[p[1]], got.at[me], sem_u, (k,), p) for k, p in enumerate(peers)]
    pushes[0].start()
    for s in range(slots):
        slot = grad_o[s] * scale
        grad_o[s] = slot
        lnew = BETA_TWO * ls[s] + (1.0 - BETA_TWO) * mm3(slot, slot, 1, 1)
        rnew = BETA_TWO * rs[s] + (1.0 - BETA_TWO) * mm3(slot, slot, 0, 0)
        lnew_o[s] = lnew
        rnew_o[s] = rnew
        xl_o[s] = mm3(lb[s], lnew, 0, 1)
        xr_o[s] = mm3(rb[s], rnew, 0, 1)
    for copy in pushes[1:6]:
        copy.start()
    for copy in moves:
        copy.wait_recv()
    for t in range(shards):
        rows_t = got[t].astype(F32)
        for s in range(slots):
            back_o[t * slots + s] = rows_t[s * width : (s + 1) * width]
    pushes[6].start()
    for copy in waits:
        copy.wait_send()
    for copy in pushes:
        copy.wait()


def reduce_grads(inverse, grad, vec, scal, m, v, ls, rs, lb, rb, groups, shards):
    outer, inner = split_shard(shards)
    slots = m.shape[0]
    width = LANES // shards
    full = -(-slots * width // TILE) * TILE
    rows = slots * LANES
    half = rows // 2
    piece = half // groups
    f = jax.ShapeDtypeStruct
    hb = pl.BlockSpec(memory_space=pltpu.HBM)
    vm = pl.BlockSpec(memory_space=pltpu.VMEM)
    sm = pl.BlockSpec(memory_space=pltpu.SMEM)
    both = outer * inner
    table = vec.reshape(outer, inner, 2, width, WIDTH)

    def buf(*shape):
        return pltpu.VMEM(shape + (WIDTH,), BF16)

    def wide(*shape):
        return pltpu.VMEM(shape + (WIDTH,), F32)

    dma = pltpu.SemaphoreType.DMA
    peers_in, peers_dp = max(inner - 1, 1), max(groups - 1, 1)
    outs = [f(m.shape, F32), f((width, WIDTH), F32), f((8, LANES), F32)]
    outs += [f(x.shape, F32) for x in (v, ls, rs, lb, rb)] + [f((shards * slots, width, WIDTH), F32)]
    return pl.pallas_call(
        functools.partial(reduce_kernel, groups, outer, inner, slots, shards),
        out_shape=outs,
        in_specs=[sm] + [vm] * 3 + [hb] * 6,
        out_specs=[hb, vm, vm] + [hb] * 6,
        scratch_shapes=[
            buf(both, rows),
            buf(outer, peers_in, half), buf(outer, half), buf(outer, peers_dp, piece),
            buf(outer, inner, peers_dp, piece), buf(both, piece), buf(outer, peers_in, piece),
            buf(outer, 2 * piece), buf(outer - 1, 2 * piece), buf(2, piece), buf(2, groups, piece),
            pltpu.VMEM((4, 4, 8, LANES), F32),
            wide(slots, LANES), pltpu.VMEM((groups * shards, 8, LANES), F32), buf(shards, full), buf(shards, full),
            wide(outer, inner, width), wide(peers_in, outer, width), wide(groups, outer, width), wide(outer - 1, width),
            wide(2, outer, inner, width),
            *[pltpu.VMEM(x.shape, F32) for x in (m, v, ls, rs, lb, rb)],
            *[pltpu.VMEM(x.shape, F32) for x in (m, v, ls, rs, lb, rb)],
            pltpu.VMEM((shards * slots, width, WIDTH), F32),
            dma((2, outer, peers_in)), dma((2, outer, peers_dp)), dma((2, outer, inner, peers_dp)),
            dma((2, outer, peers_in)), dma((2, outer - 1)), dma((2, 2 * groups - 1)), dma((2, 4, 6)),
            dma((2, groups * shards - 1)), dma((2, shards - 1)), dma((6,)), dma((7,)),
        ],
        compiler_params=pltpu.CompilerParams(collective_id=1, has_side_effects=True, vmem_limit_bytes=62 * 2**20),
        name="reduce",
    )(inverse, grad, table, scal, m, v, ls, rs, lb, rb)


def soap_kernel(slots, owners, scal, g_h, gvec, second_i, lnew_i, rnew_i, xl, xr, back_h, m_i, mat_i, ema_i, vw, vf, vs, ve,
                loss_o, count_o, norm_o, mat_h, ema_h, m_h, v_h, ls_h, rs_h, lb_o, rb_o, vw_o, vf_o, vs_o, ve_o, zl, ol, zw, ow, xa, mat_o, ema_o, m_o, g, m, back, mat, ema, second, lnew, rnew, sem, sem_in):
    pulls = [pltpu.make_async_copy(src, dst, sem_in.at[k])
             for k, (src, dst) in enumerate(((second_i, second), (lnew_i, lnew), (rnew_i, rnew), (g_h, g), (m_i, m), (back_h, back), (mat_i, mat), (ema_i, ema)))]
    for copy in pulls:
        copy.start()
    outs = [pltpu.make_async_copy(src, dst, sem.at[k])
            for k, (src, dst) in enumerate(((second, v_h), (lnew, ls_h), (rnew, rs_h), (mat_o, mat_h), (ema_o, ema_h), (m_o, m_h)))]
    loss_o[...] = scal[0:1, 0:1]
    count_o[...] = scal[1:2, 0:1]
    norm_o[...] = scal[2:3, 0:1]
    eye = (lax.broadcasted_iota(jnp.int32, (LANES, LANES), 0) == lax.broadcasted_iota(jnp.int32, (LANES, LANES), 1)).astype(F32)
    for s in range(slots):
        zl[s, :, :LANES] = mm(xl[s], xl[s], 1, 1)
        zl[s, :, LANES:] = xl[s]
        gram = mm(xr[s], xr[s], 1, 1)
        zw[s, :, :LANES] = gram[:LANES, :LANES]
        zw[s, :, LANES:] = eye
        xa[s, :LANES, :LANES] = gram[:LANES, LANES:]
        xa[s, LANES:, :LANES] = gram[LANES:, LANES:]
        xa[s, :, LANES:] = xr[s]
    factor_all([(zw, ow, s) for s in range(slots)] + [(zl, ol, s) for s in range(slots)])
    for s in range(slots):
        lb_o[s] = ol[s].T
        done = mm(ow[s], xa[s, :LANES, :])
        rb_o[s, :, :LANES] = done[:, LANES:].T
        rest = xa[s, LANES:, :] - mm(done[:, :LANES], done, 0, 0)
        zw[s, :, :LANES] = rest[:, :LANES]
        zw[s, :, LANES:] = eye
        xa[s, LANES:, :] = rest
    for copy in pulls:
        copy.wait()
    for copy in outs[:3]:
        copy.start()
    for s in range(slots):
        m_o[s] = BETA_ONE * m[s] + (1.0 - BETA_ONE) * g[s]
    for unit in range(UNITS):
        new = mat[unit] * (1.0 - LEARN * DECAY) - LEARN * back[owners[unit]]
        mat_o[unit] = new
        ema_o[unit] = EMA_RATE * ema[unit] + (1.0 - EMA_RATE) * new
    for copy in outs[3:]:
        copy.start()
    factor_all([(zw, ow, s) for s in range(slots)])
    for s in range(slots):
        rb_o[s, :, LANES:] = mm(ow[s], xa[s, LANES:, LANES:]).T
    grad = gvec[...]
    first = BETA_ONE * vf[...] + (1.0 - BETA_ONE) * grad
    moment = BETA_TWO * vs[...] + (1.0 - BETA_TWO) * grad * grad
    step = first / (1.0 - BETA_ONE**STEP) / (jnp.sqrt(moment / (1.0 - BETA_TWO**STEP)) + ADAM_EPS)
    new = vw[...] * (1.0 - TABLE_LEARN * DECAY) - TABLE_LEARN * step
    vf_o[...] = first
    vs_o[...] = moment
    vw_o[...] = new
    ve_o[...] = EMA_RATE * ve[...] + (1.0 - EMA_RATE) * new
    for copy in outs:
        copy.wait()


def soap(owners, scal, g, gvec, second, lnew, rnew, xl, xr, back, m, mat, ema, vw, vf, vs, ve):
    slots = g.shape[0]
    f = jax.ShapeDtypeStruct
    hb = pl.BlockSpec(memory_space=pltpu.HBM)
    vm = pl.BlockSpec(memory_space=pltpu.VMEM)
    outs = [f((1, 1), F32)] * 3 + [f(x.shape, F32) for x in (mat, ema, m, second, lnew, rnew, xl, xr, vw, vf, vs, ve)]
    return pl.pallas_call(
        functools.partial(soap_kernel, slots),
        out_shape=outs,
        in_specs=[pl.BlockSpec(memory_space=pltpu.SMEM), vm, hb, vm, hb, hb, hb, vm, vm, hb, hb, hb, hb, vm, vm, vm, vm],
        out_specs=[vm] * 3 + [hb] * 6 + [vm] * 6,
        scratch_shapes=[
            pltpu.VMEM((slots, LANES, 2 * LANES), F32),
            pltpu.VMEM((slots, LANES, LANES), F32),
            pltpu.VMEM((slots, LANES, 2 * LANES), F32),
            pltpu.VMEM((slots, LANES, LANES), F32),
            pltpu.VMEM((slots, 2 * LANES, 3 * LANES), F32),
            pltpu.VMEM(mat.shape, F32),
            pltpu.VMEM(mat.shape, F32),
            pltpu.VMEM(m.shape, F32),
            *[pltpu.VMEM(x.shape, F32) for x in (g, m, back, mat, ema, second, lnew, rnew)],
            pltpu.SemaphoreType.DMA((6,)),
            pltpu.SemaphoreType.DMA((8,)),
        ],
        compiler_params=pltpu.CompilerParams(vmem_limit_bytes=62 * 2**20),
        name="soap",
    )(owners, scal, g, gvec, second, lnew, rnew, xl, xr, back, m, mat, ema, vw, vf, vs, ve)


def time_table():
    steps = np.arange(32, dtype=np.float32)
    halfway = TDIM // 2
    freqs = np.exp(-math.log(10000.0) * np.arange(halfway, dtype=np.float32) / (halfway - 1)).astype(np.float32)
    angles = (freqs[:, None] * steps[None, :]).astype(np.float32)
    offset = 0.008
    ratio = (steps + 1.0) / DSTEPS
    upper = np.cos((ratio + offset) / (1.0 + offset) * math.pi / 2) ** 2
    level = upper / math.cos(offset / (1.0 + offset) * math.pi / 2) ** 2
    level = np.clip(np.where(steps < DSTEPS, level, 0.0), 0.0, 1.0)
    levels = np.stack([np.sqrt(level), np.sqrt(1.0 - level)] + [np.zeros(32)] * 6)
    return np.concatenate([np.sin(angles), np.cos(angles), levels]).astype(np.float32)


def dot(a, b, ca=1, cb=0):
    return lax.dot_general(a, b, (((ca,), (cb,)), ((), ())), preferred_element_type=F32)


def mish_parts(v):
    e = jnp.exp(jnp.minimum(v, 20.0))
    n = e * (e + 2.0)
    r = pl.reciprocal(n + 2.0)
    return e, r, n * r


def mish_slope(v, e, r, t):
    return t + v * (4.0 * e * (e + 1.0)) * (r * r)


def gather_parts():
    taps = 2 * KERNEL
    bounds = [3, 3 + taps, UNITS + 3 - (OWNED - 1) * taps]
    while bounds[-1] < UNITS + 3:
        bounds.append(bounds[-1] + taps)
    return [(0, bounds[1])] + list(zip(bounds[1:-1], bounds[2:]))


def net_kernel(trajs, frames, groups, outer, inner, traj_h, noise_h, steps, valid, times, gmat, mat, vec, owners, mat_h, vec_o, loss_o, inverse_o,
               other, other_vec, shares_g, theirs, stage, mb, xin, xhat, h, skip, d, dskip, dy, dp, low, xt, s_one, s_two, mean, rstd, xsum, q_one, q_two,
               g_one, g_two, tb, dtb, noisy_t, noise_t, mask_t, dpl, acc, table, sem_c, sem_z, sem_y, sem_s, sem_x, sem_g, mat_o, traj, noise, sem_l):
    pulls = [pltpu.make_async_copy(traj_h, traj, sem_l.at[0]), pltpu.make_async_copy(noise_h, noise, sem_l.at[1])]
    for copy in pulls:
        copy.start()
    dpi = lax.axis_index("dp")
    a, b, c = place(outer, inner)
    piece = mat.shape[1]
    chunks = trajs // TILE
    rows_c = TILE * frames
    rows = trajs * frames
    taps = 2 * KERNEL
    part = 1.0 / (frames * (WIDTH // GROUPS))
    group = gmat[...].astype(BF16)
    core_peer = (dpi, spot(inner, a, b, 1 - c))
    in_peers = [(dpi, spot(inner, a, lax.rem(b + i, inner), c)) for i in range(1, inner)]
    out_peers = [(dpi, spot(inner, lax.rem(a + i, outer), b, c)) for i in range(1, outer)]
    odd = lax.rem(dpi, 2)
    twin_peer = (dpi + 1 - 2 * odd, spot(inner, a, b, c))
    greet([core_peer, twin_peer] + in_peers + out_peers)
    waits = []

    def send(src, dst, sems, index, peer):
        copy = pltpu.make_async_remote_copy(
            src_ref=src, dst_ref=dst, send_sem=sems.at[(0,) + index], recv_sem=sems.at[(1,) + index],
            device_id=peer, device_id_type=MESH)
        copy.start()
        waits.append(copy)
        return copy

    spans = [(0, taps), (taps * OWNED, UNITS), (taps, taps * OWNED)]
    first_copies = [send(vec, other_vec, sem_c, (3,), core_peer)]
    for k, (lo, hi) in enumerate(spans):
        first_copies.append(send(mat.at[pl.ds(lo, hi - lo)], other.at[pl.ds(lo, hi - lo)], sem_c, (k,), core_peer))
    parts = gather_parts()
    start_of = [3 if l == 0 else parts[l + 1][0] for l in range(OWNED)]
    time_at = parts[1][0]
    shares = [(lo, hi - lo, (hi - lo) * 3 // 10) for lo, hi in parts]
    source = {0: 0, 1: taps * OWNED}
    for g in range(2, len(parts)):
        source[g] = taps * (g - 1)
    cols = pl.ds(pl.multiple_of(c * LANES, LANES), LANES)
    state = {}

    def chip_rows(mine, theirs):
        upper = jnp.where(c == 0, mine, theirs)
        lower = jnp.where(c == 0, theirs, mine)
        return jnp.concatenate([upper, lower], axis=mine.ndim - 2)

    def region(g, kind, at_a, at_b):
        lo, count, side = shares[g]
        both = count - side
        if kind == "own":
            start, size = lo + odd * side, both
        elif kind == "lend":
            start, size = lo + odd * both, side
        else:
            start, size = lo + (1 - odd) * both, side
        return mb.at[pl.ds(start, size), at_a, at_b, :, cols]

    def build(g):
        lo, count, side = shares[g]
        hi = lo + count
        if g == 0:
            first_copies[0].wait_recv()
            first_copies[1].wait_recv()
            rows_v = chip_rows(vec[...], other_vec[...])
            for k, value in enumerate(split3(rows_v)):
                stage[k] = value.astype(mb.dtype)
            count -= 3
        elif g == 1:
            first_copies[2].wait_recv()
        elif g == 2:
            first_copies[3].wait_recv()
        at = source[g]
        stage[hi - count : hi] = chip_rows(mat[at : at + count], other[at : at + count]).astype(BF16).astype(mb.dtype)
        both = hi - lo - side
        mine = region(g, "own", a, b)
        mine[...] = stage[pl.ds(lo + odd * side, both), :, cols]
        state[g] = [send(mine, mine, sem_z, (g, k), p) for k, p in enumerate(out_peers)]

    def along(g):
        for copy in state[g]:
            copy.wait_recv()
        column = region(g, "own", slice(None), b)
        nexts = [send(column, column, sem_y, (g, k), p) for k, p in enumerate(in_peers)]
        state[g] = (nexts, [send(column, column, sem_s, (g, 0), core_peer)])

    def across(g):
        nexts, sib = state[g]
        for copy in nexts:
            copy.wait_recv()
        lent = region(g, "lend", slice(None), slice(None))
        twin = [send(lent, lent, sem_x, (g,), twin_peer)]
        for i in range(1, inner):
            column = region(g, "own", slice(None), lax.rem(b + i, inner))
            sib.append(send(column, column, sem_s, (g, i), core_peer))
        state[g] = (twin, sib)

    def beside(g):
        twin, sib = state[g]
        for copy in twin:
            copy.wait_recv()
        lent = region(g, "borrow", slice(None), slice(None))
        sib.append(send(lent, lent, sem_s, (g, inner), core_peer))
        state[g] = sib

    def whole(g):
        for copy in state[g]:
            copy.wait_recv()

    def chunk_of(n):
        return slice(n * TILE, (n + 1) * TILE)

    def flat(v):
        return v.reshape(rows_c, WIDTH)

    def wide(v):
        return v.reshape(frames, TILE, WIDTH)

    def row(index):
        return table[index : index + 1, :]

    def gain(l):
        return row(BASE + 3 + OWNED + l), row(BASE + 3 + 2 * OWNED + l)

    def tap(l, k):
        at = start_of[l] + 2 * k
        return mb[at : at + 2].reshape(WIDTH, WIDTH).astype(BF16)

    def lin(j):
        at = time_at + 2 * j
        return mb[at : at + 2].reshape(WIDTH, WIDTH).astype(BF16)

    def group_sum(v):
        count = v.shape[0]
        sums = dot(jnp.concatenate(split3(v), axis=0), group)
        return (sums[:count] + sums[count : 2 * count]) + sums[2 * count :]

    def loop(body, moves=()):
        for n in range(max(chunks, len(moves))):
            if n < len(moves):
                for act, g in moves[n]:
                    act(g)
            if n < chunks:
                body(n)

    def pass_one(l, n, x):
        at = chunk_of(n)
        xin[l, KERNEL // 2 : KERNEL // 2 + frames, at, :] = wide(x).astype(BF16)
        p = None
        for k in range(KERNEL):
            term = dot(flat(xin[l, k : k + frames, at, :]), tap(l, k))
            p = term if p is None else p + term
        p = wide(p + row(BASE + 3 + l))
        xhat[l, :, at, :] = p
        total = jnp.sum(p, axis=0)
        s_one[at, :] = total
        off = p - (total * (1.0 / frames))[None]
        s_two[at, :] = jnp.sum(off * off, axis=0)

    def stats(l):
        total = s_one[...]
        centre = group_sum(total) * part
        off = total * (1.0 / frames) - centre
        var = group_sum(s_two[...] + frames * off * off) * part
        scale = lax.rsqrt(var + NORM_EPS)
        mean[...] = centre
        rstd[l] = scale
        xsum[l] = frames * off * scale

    def normed(l, n):
        at = chunk_of(n)
        x = (xhat[l, :, at, :] - mean[at, :][None]) * rstd[l, at, :][None]
        xhat[l, :, at, :] = x
        g, s = gain(l)
        return x, x * g + s

    def pass_a(n, dm, x, v, pieces):
        at = chunk_of(n)
        slope = dm * mish_slope(v, *pieces)
        dy[:, at, :] = slope
        q_one[at, :] = jnp.sum(slope, axis=0)
        q_two[at, :] = jnp.sum(slope * x, axis=0)

    def pass_a_load(l, n, dm):
        x = xhat[l, :, chunk_of(n), :]
        g, s = gain(l)
        v = x * g + s
        pass_a(n, dm, x, v, mish_parts(v))

    def stats_back(l):
        g, s = gain(l)
        one, two = q_one[...], q_two[...]
        vec_o[BASE + 3 + OWNED + l : BASE + 4 + OWNED + l, :] = jnp.sum(two, axis=0, keepdims=True)
        vec_o[BASE + 3 + 2 * OWNED + l : BASE + 4 + 2 * OWNED + l, :] = jnp.sum(one, axis=0, keepdims=True)
        sums = group_sum(jnp.concatenate([one * g, two * g], axis=0)) * part
        first, second = sums[:trajs], sums[trajs:]
        g_one[...] = first
        g_two[...] = second
        dc = rstd[l] * (one * g - frames * first - xsum[l] * second)
        vec_o[BASE + 3 + l : BASE + 4 + l, :] = jnp.sum(dc, axis=0, keepdims=True)

    half_rows = LANES // 2
    trades = {}

    def put(block, value):
        for side in range(2):
            shares_g[side, block] = value[side * half_rows : (side + 1) * half_rows].astype(BF16)

    def trade(group, lo, hi):
        span = pl.ds(lo, hi - lo)
        trades[group] = send(shares_g.at[1 - c, span], theirs.at[span], sem_g, (group,), core_peer)

    def merge(group, lo, hi):
        trades[group].wait_recv()
        mat_o[lo:hi] = (shares_g[c, lo:hi].astype(F32) + theirs[lo:hi].astype(F32)).astype(BF16)

    build(0)
    build(1)
    build(2)
    vec_o[...] = jnp.zeros_like(vec_o)
    edge = jnp.zeros((OWNED, KERNEL // 2, trajs, WIDTH), BF16)
    xin[:, : KERNEL // 2] = edge
    xin[:, KERNEL // 2 + frames :] = edge
    dp[: KERNEL // 2] = edge[0]
    dp[KERNEL // 2 + frames :] = edge[0]
    acc[...] = jnp.zeros_like(acc)
    total = inverse_o.shape[0]
    slot = lax.broadcasted_iota(jnp.int32, (total, UNITS), 0)
    unit = lax.broadcasted_iota(jnp.int32, (total, UNITS), 1).astype(F32)
    inverse_o[...] = jnp.min(jnp.where(slot == owners[...], unit, float(UNITS)), axis=1, keepdims=True).astype(jnp.int32)
    stepid = lax.broadcasted_iota(jnp.int32, (32, trajs), 0)
    picked = mm(times[...], (stepid == steps[...]).astype(F32))
    emb = picked[:TDIM].astype(BF16)
    keep, add = picked[TDIM : TDIM + 1], picked[TDIM + 1 : TDIM + 2]
    for copy in pulls:
        copy.wait()
    for f in range(frames):
        at = slice(f * trajs, (f + 1) * trajs)
        raw = noise[:, f, :]
        noise_t[:, at] = raw
        noisy_t[:, at] = (keep * traj[:, f, :] + add * raw).astype(BF16)
        mask_t[:, at] = valid[f : f + 1, :].astype(F32)
    along(0)
    build(3)
    along(1)
    build(4)
    across(0)
    along(2)
    build(5)
    across(1)
    along(3)
    build(6)
    beside(0)
    across(2)
    along(4)
    beside(1)
    whole(0)
    full = [mb[k].reshape(VROWS, WIDTH).astype(F32) for k in range(3)]
    table[...] = (full[0] + full[1]) + full[2]
    low[...] = full[0].astype(BF16)
    w_in, w_head = low[:FEAT, :], low[FEAT : 2 * FEAT, :]
    h[...] = (dot(noisy_t[...], w_in, 0, 0) + row(BASE)).reshape(frames, trajs, WIDTH)

    def enter(n):
        pass_one(0, n, flat(h[:, chunk_of(n), :]))

    loop(enter, [[], [(across, 3)], [(along, 5)], [(beside, 2)]])
    across(4)
    whole(1)
    pre_time = dot(emb, mb[time_at + 2 * BLOCKS].reshape(TDIM, WIDTH).astype(BF16), 0, 0) + row(BASE + 1)
    time_parts = mish_parts(pre_time)
    temb = (pre_time * time_parts[2]).astype(BF16)
    time_slope = mish_slope(pre_time, *time_parts)
    for j in range(BLOCKS):
        tb[j] = dot(temb, lin(j)) + row(BASE + 3 + 3 * OWNED + j)
    moves = [[[], [(along, 6), (beside, 3)], [(across, 5)], [(beside, 4)]], [[(across, 6)], [], [(beside, 5)], []], [[], [(beside, 6)]], [], []]
    for l in range(OWNED - 1):
        stats(l)
        whole(l + 2)

        def forward(n, l=l):
            at = chunk_of(n)
            _, v = normed(l, n)
            m = v * mish_parts(v)[2]
            if l % 2 == 0:
                m = m + tb[l // 2, at, :][None]
            else:
                m = h[:, at, :] + m
                if l == 1:
                    skip[:, at, :] = m
                if l == 2 * BLOCKS - 3:
                    m = m + skip[:, at, :]
                h[:, at, :] = m
            pass_one(l + 1, n, flat(m))

        loop(forward, moves[l])
    stats(OWNED - 1)
    head_bias = table[BASE + 2 : BASE + 3, :]

    def settle(n):
        at = chunk_of(n)
        _, v = normed(OWNED - 1, n)
        dp[KERNEL // 2 : KERNEL // 2 + frames, at, :] = (h[:, at, :] + v * mish_parts(v)[2]).astype(BF16)

    loop(settle)
    top = dp[KERNEL // 2 : KERNEL // 2 + frames].reshape(rows, WIDTH)
    pick = lax.broadcasted_iota(jnp.int32, (FEAT, WIDTH), 0) == lax.broadcasted_iota(jnp.int32, (FEAT, WIDTH), 1)
    bias = jnp.sum(jnp.where(pick, head_bias, 0.0), axis=1, keepdims=True)
    err = dot(w_head, top, 1, 1) + bias - noise_t[...]
    weighted = mask_t[...] * err
    loss = jnp.sum(jnp.sum(weighted * err, axis=0, keepdims=True), axis=1, keepdims=True)
    count = FEAT * jnp.sum(mask_t[...], axis=1, keepdims=True)
    rowid = lax.broadcasted_iota(jnp.int32, (8, LANES), 0)
    loss_o[...] = jnp.where(rowid == 0, loss, jnp.where(rowid == 1, count, 0.0))
    grad = 2.0 * weighted
    g_bias = jnp.sum(grad, axis=1, keepdims=True)
    vec_o[BASE + 2 : BASE + 3, :] = jnp.sum(jnp.where(pick, g_bias, 0.0), axis=0, keepdims=True)
    dpl[...] = grad.astype(BF16)
    vec_o[FEAT : 2 * FEAT, :] = dot(dpl[...], top)
    d[...] = dot(dpl[...], w_head, 0, 0).reshape(frames, trajs, WIDTH)

    def turn(n):
        pass_a_load(OWNED - 1, n, d[:, chunk_of(n), :])

    loop(turn)
    def finish():
        d_in = d[...].reshape(rows, WIDTH)
        vec_o[BASE : BASE + 1, :] = jnp.sum(d_in, axis=0, keepdims=True)
        vec_o[:FEAT, :] = dot(noisy_t[...], d_in.astype(BF16))
        d_temb = None
        for j in range(BLOCKS):
            grads = dtb[j]
            vec_o[BASE + 3 + 3 * OWNED + j : BASE + 4 + 3 * OWNED + j, :] = jnp.sum(grads, axis=0, keepdims=True)
            grads = grads.astype(BF16)
            t_grad = dot(temb, grads, 0, 0)
            for half in range(2):
                put(taps * OWNED + 2 * j + half, t_grad[half * LANES : (half + 1) * LANES])
            term = dot(grads, lin(j), 1, 1)
            d_temb = term if d_temb is None else d_temb + term
        d_pre = d_temb * time_slope
        vec_o[BASE + 1 : BASE + 2, :] = jnp.sum(d_pre, axis=0, keepdims=True)
        put(UNITS - 1, dot(emb, d_pre.astype(BF16)))
        trade(OWNED, taps * OWNED, UNITS)

    for l in reversed(range(OWNED)):
        stats_back(l)

        def backward(n, l=l):
            g, s = gain(l)
            at = chunk_of(n)
            x = xhat[l, :, at, :]
            back = rstd[l, at, :][None] * (dy[:, at, :] * g - g_one[at, :][None] - x * g_two[at, :][None])
            dp[KERNEL // 2 : KERNEL // 2 + frames, at, :] = back.astype(BF16)
            dx = None
            for k in range(KERNEL):
                shift = KERNEL - 1 - k
                term = dot(flat(dp[shift : shift + frames, at, :]), tap(l, k), 1, 1)
                dx = term if dx is None else dx + term
            dx = wide(dx)
            if l % 2 == 1:
                dtb[l // 2, at, :] = jnp.sum(dx, axis=0)
                pass_a_load(l - 1, n, dx)
            else:
                dx = d[:, at, :] + dx
                if l == OWNED - 2:
                    dskip[:, at, :] = dx
                if l == 2:
                    dx = dx + dskip[:, at, :]
                d[:, at, :] = dx
                if l > 0:
                    pass_a_load(l - 1, n, dx)

        loop(backward)
        if l == 0:
            finish()
        xt[...] = xin[l, KERNEL // 2 : KERNEL // 2 + frames].reshape(rows, WIDTH).T
        for k in range(KERNEL):
            shift = KERNEL - 1 - k
            w_grad = dot(xt[...], dp[shift : shift + frames].reshape(rows, WIDTH))
            for half in range(2):
                put(taps * l + 2 * k + half, w_grad[half * LANES : (half + 1) * LANES])
        trade(l, taps * l, taps * (l + 1))

    mat_o[UNITS] = jnp.zeros((half_rows, WIDTH), BF16)
    for l in reversed(range(1, OWNED)):
        merge(l, taps * l, taps * (l + 1))
    merge(OWNED, taps * OWNED, UNITS)
    early = pltpu.make_async_copy(mat_o.at[pl.ds(taps, UNITS + 1 - taps)], mat_h.at[pl.ds(taps, UNITS + 1 - taps)], sem_l.at[2])
    early.start()
    merge(0, 0, taps)
    late = pltpu.make_async_copy(mat_o.at[pl.ds(0, taps)], mat_h.at[pl.ds(0, taps)], sem_l.at[3])
    late.start()
    early.wait()
    late.wait()
    for copy in waits:
        copy.wait_send()


def net(traj, noise, steps, valid, mat, vec, owners, total, groups, shards):
    outer, inner = split_shard(shards)
    feats, frames, trajs = traj.shape
    rows = frames * trajs
    piece = mat.shape[1]
    lane = np.arange(WIDTH) // (WIDTH // GROUPS)
    gmat = jnp.asarray((lane[:, None] == lane[None, :]).astype(np.float32))
    times = jnp.asarray(time_table())
    wire = BF16 if (2 * piece) % TILE == 0 else F32
    hb = pl.BlockSpec(memory_space=pltpu.HBM)
    vm = pl.BlockSpec(memory_space=pltpu.VMEM)
    f = jax.ShapeDtypeStruct
    big = pltpu.VMEM((frames, trajs, WIDTH), F32)
    small = pltpu.VMEM((trajs, WIDTH), F32)
    padded = frames + KERNEL - 1
    dma = pltpu.SemaphoreType.DMA
    count = len(gather_parts())
    return pl.pallas_call(
        functools.partial(net_kernel, trajs, frames, groups, outer, inner),
        out_shape=[f((UNITS + 1, LANES // 2, WIDTH), BF16), f((VROWS, WIDTH), F32), f((8, LANES), F32), f((total, 1), jnp.int32)],
        in_specs=[hb, hb] + [vm] * 7,
        out_specs=[hb] + [vm] * 3,
        scratch_shapes=[
            pltpu.VMEM((UNITS, piece, WIDTH), F32),
            pltpu.VMEM((piece, WIDTH), F32),
            pltpu.VMEM((2, UNITS, LANES // 2, WIDTH), BF16),
            pltpu.VMEM((UNITS, LANES // 2, WIDTH), BF16),
            pltpu.VMEM((UNITS + 3, 2 * piece, WIDTH), wire),
            pltpu.VMEM((UNITS + 3, outer, inner, 2 * piece, WIDTH), wire),
            pltpu.VMEM((OWNED, padded, trajs, WIDTH), BF16),
            pltpu.VMEM((OWNED, frames, trajs, WIDTH), F32),
            big, big, big, big, big,
            pltpu.VMEM((padded, trajs, WIDTH), BF16),
            pltpu.VMEM((VROWS, WIDTH), BF16),
            pltpu.VMEM((WIDTH, rows), BF16),
            small, small, small,
            pltpu.VMEM((OWNED, trajs, WIDTH), F32),
            pltpu.VMEM((OWNED, trajs, WIDTH), F32),
            small, small, small, small,
            pltpu.VMEM((BLOCKS, trajs, WIDTH), F32),
            pltpu.VMEM((BLOCKS, trajs, WIDTH), F32),
            pltpu.VMEM((feats, rows), BF16),
            pltpu.VMEM((feats, rows), F32),
            pltpu.VMEM((1, rows), F32),
            pltpu.VMEM((feats, rows), BF16),
            pltpu.VMEM((16, WIDTH), F32),
            pltpu.VMEM((VROWS, WIDTH), F32),
            dma((2, 4)), dma((2, count, outer - 1)), dma((2, count, max(inner - 1, 1))),
            dma((2, count, inner + 1)), dma((2, count)), dma((2, OWNED + 1)),
            pltpu.VMEM((UNITS + 1, LANES // 2, WIDTH), BF16),
            pltpu.VMEM(traj.shape, F32),
            pltpu.VMEM(traj.shape, F32),
            dma((4,)),
        ],
        compiler_params=pltpu.CompilerParams(collective_id=3, has_side_effects=True, vmem_limit_bytes=62 * 2**20),
        name="net",
    )(traj, noise, steps, valid, times, gmat, mat, vec, owners)


def body(
    trajectories,
    noise,
    timesteps,
    valid,
    owners,
    mat_weight,
    mat_ema,
    soap_first,
    soap_second,
    left_stat,
    right_stat,
    left_basis,
    right_basis,
    vec_weight,
    vec_first,
    vec_second,
    vec_ema,
):
    shards = lax.axis_size("shard")
    groups = lax.axis_size("dp")
    slots = soap_first.shape[0]
    mat_grad, vec_grad, scal, inverse = net(
        trajectories.transpose(2, 1, 0),
        noise.transpose(2, 1, 0),
        timesteps.reshape(1, -1),
        valid.T,
        mat_weight,
        vec_weight,
        owners.reshape(1, -1),
        shards * slots,
        groups,
        shards,
    )
    grads, grads_vec, scal, second, lnew, rnew, xl, xr, back = reduce_grads(
        inverse, mat_grad, vec_grad, scal, soap_first, soap_second, left_stat, right_stat, left_basis, right_basis, groups, shards
    )
    results = soap(
        owners, scal, grads, grads_vec, second, lnew, rnew, xl, xr, back,
        soap_first, mat_weight, mat_ema, vec_weight, vec_first, vec_second, vec_ema,
    )
    return tuple(x.reshape(()) for x in results[:3]) + tuple(results[3:])


def solution(mesh):
    placed = (
        P(("dp", "shard"), None, None),
        P(("dp", "shard"), None, None),
        P(("dp", "shard")),
        P(("dp", "shard"), None),
        P(),
        P(None, "shard", None),
        P(None, "shard", None),
        P("shard", None, None),
        P("shard", None, None),
        P("shard", None, None),
        P("shard", None, None),
        P("shard", None, None),
        P("shard", None, None),
        P("shard", None),
        P("shard", None),
        P("shard", None),
        P("shard", None),
    )
    return jax.shard_map(
        body,
        mesh=mesh,
        in_specs=placed,
        out_specs=(
            P(),
            P(),
            P(),
            P(None, "shard", None),
            P(None, "shard", None),
            P("shard", None, None),
            P("shard", None, None),
            P("shard", None, None),
            P("shard", None, None),
            P("shard", None, None),
            P("shard", None, None),
            P("shard", None),
            P("shard", None),
            P("shard", None),
            P("shard", None),
        ),
        check_vma=False,
    )
```
